32 devices in a mesh: section: 2 (over x), ctx: 2 (over core), shard: 8 (over z, y).
Axes of the slice: x: 2, y: 2, z: 4, core: 2. Of those that a mesh axis runs over, the one named last changes fastest.
Arguments:
- tokens: bfloat16 [2, 1024, 1600], P(None, ('ctx', 'shard')), may hold values from -6 to 6
- block_order: int32 [16, 2], replicated, may hold values from 0 to 31, as said below
- cotangent: bfloat16 [2, 1024, 1600], P(None, ('ctx', 'shard')), may hold values from -6 to 6
- first_gain: bfloat16 [2, 1600], P('section', 'shard'), may hold values from 0.099609375 to 1.8984375
- first_shift: bfloat16 [2, 1600], P('section', 'shard'), may hold values from -1.75 to 1.75
- query_key_value_weight: bfloat16 [2, 1600, 4800], P('section', 'shard'), may hold values from -0.15625 to 0.15625
- input_bias: bfloat16 [2, 3200], P('section', 'shard'), may hold values from -1.75 to 1.75
- attention_out_weight: bfloat16 [2, 1600, 1600], P('section', 'shard'), may hold values from -1.75 to 1.75
- attention_out_bias: bfloat16 [2, 1600], P('section', 'shard'), may hold values from -1.75 to 1.75
- second_gain: bfloat16 [2, 1600], P('section', 'shard'), may hold values from 0.099609375 to 1.8984375
- second_shift: bfloat16 [2, 1600], P('section', 'shard'), may hold values from -1.75 to 1.75
- widen_weight: bfloat16 [2, 1600, 6400], P('section', 'shard'), may hold values from -0.15625 to 0.15625
- widen_bias: bfloat16 [2, 6400], P('section', 'shard'), may hold values from -1.75 to 1.75
- narrow_weight: bfloat16 [2, 6400, 1600], P('section', 'shard'), may hold values from -0.078125 to 0.078125
- narrow_bias: bfloat16 [2, 1600], P('section', 'shard'), may hold values from -1.75 to 1.75
Outputs:
- layer_out: float32 [2, 2, 1024, 1600], P('section', None, ('ctx', 'shard'))
- d_in: float32 [2, 2, 1024, 1600], P('section', None, ('ctx', 'shard'))
- grad_first_gain: float32 [2, 1600], P('section', 'shard')
- grad_first_shift: float32 [2, 1600], P('section', 'shard')
- grad_input_weight: float32 [2, 1600, 4800], P('section', 'shard')
- grad_input_bias: float32 [2, 3200], P('section', 'shard')
- grad_output_weight: float32 [2, 1600, 1600], P('section', 'shard')
- grad_output_bias: float32 [2, 1600], P('section', 'shard')
- grad_second_gain: float32 [2, 1600], P('section', 'shard')
- grad_second_shift: float32 [2, 1600], P('section', 'shard')
- grad_expand_weight: float32 [2, 1600, 6400], P('section', 'shard')
- grad_expand_bias: float32 [2, 6400], P('section', 'shard')
- grad_reduce_weight: float32 [2, 6400, 1600], P('section', 'shard')
- grad_reduce_bias: float32 [2, 1600], P('section', 'shard')
The draws below stay inside these ranges and needn't reach their ends.
Inputs may be any that keep to these rules, and one draw needn't show every extreme that they name: `block_order`: row p names the two blocks of 32 positions in storage slot p: the first is below 16, the second equals 31 minus the first, and every block number occurs once in the table.
All inputs are finite; a program needn't handle non-finite values.
Results may differ from the reference program's by a relative error of at most 0.034.
Values may be sent and summed in bfloat16 or wider, within the bound.
A program may use at most 384 MiB of HBM per device.

```python
import math
import jax
import jax.numpy as jnp
from jax import lax

D = 1600
HEADS = 25
HD = 64
FF = 6400
SEQS = 2
GROUP = 16
L = 1024
BLK = 32


def draw_block_order(key, part):
    key = jax.random.fold_in(key, 7)
    shuffled = jax.random.permutation(key, GROUP).astype(jnp.int32)
    return jnp.stack([shuffled, 2 * GROUP - 1 - shuffled], axis=1).astype(jnp.int32)


def steps_of(own_key, extent, pieces, low, high):
    factor_of, own = 1.0, jax.random.fold_in(own_key, 6)
    for position, shards_of in pieces:
        draws = jnp.exp(jax.random.uniform(jax.random.fold_in(own, position), (shards_of,), jnp.float32, low / len(pieces), high / len(pieces)))
        factor_of = factor_of * jnp.repeat(draws, extent[position] // shards_of).reshape([-1 if axis == position else 1 for axis in range(len(extent))])
    return factor_of


def gaussian(rng, extent, deviation, limit, pieces=(), kind=jnp.bfloat16):
    result = deviation * jax.random.normal(rng, extent, jnp.float32)
    if pieces:
        result = result * steps_of(rng, extent, pieces, -0.22, 0.18)
    return jnp.clip(result, -limit, limit).astype(kind)


def setup_inputs(seed: int = 0) -> dict:
    seeds = jax.random.split(jax.random.key(seed), 16)
    tokens = gaussian(seeds[0], (SEQS, L, D), 1.0, 6.0, ((1, 16),))
    block_order = draw_block_order(jax.random.fold_in(seeds[15], 71), 0)
    cotangent = gaussian(seeds[2], (SEQS, L, D), 1.0, 6.0, ((1, 16),))
    first_gain = jnp.clip(1.0 + 0.18 * jax.random.normal(seeds[3], (2, D), jnp.float32), 0.099609375, 1.8984375).astype(jnp.bfloat16)
    first_shift = gaussian(seeds[4], (2, D), 0.3, 1.75, ((0, 2), (1, 8)))
    query_key_value_weight = gaussian(seeds[5], (2, D, 3 * D), D ** -0.5, 0.15625, ((0, 2), (1, 8)))
    input_bias = gaussian(seeds[6], (2, 2 * D), 0.3, 1.75, ((0, 2), (1, 8)))
    attention_out_weight = gaussian(seeds[7], (2, D, D), (max(1, D * 8 // L)) ** -0.5, 1.75, ((0, 2), (1, 8)))
    attention_out_bias = gaussian(seeds[8], (2, D), 0.3, 1.75, ((0, 2), (1, 8)))
    second_gain = jnp.clip(1.0 + 0.18 * jax.random.normal(seeds[9], (2, D), jnp.float32), 0.099609375, 1.8984375).astype(jnp.bfloat16)
    second_shift = gaussian(seeds[10], (2, D), 0.3, 1.75, ((0, 2), (1, 8)))
    widen_weight = gaussian(seeds[11], (2, D, FF), D ** -0.5, 0.15625, ((0, 2), (1, 8)))
    widen_bias = gaussian(seeds[12], (2, FF), 0.3, 1.75, ((0, 2), (1, 8)))
    narrow_weight = gaussian(seeds[13], (2, FF, D), FF ** -0.5, 0.078125, ((0, 2), (1, 8)))
    narrow_bias = gaussian(seeds[14], (2, D), 0.3, 1.75, ((0, 2), (1, 8)))
    return dict(tokens=tokens, block_order=block_order, cotangent=cotangent, first_gain=first_gain, first_shift=first_shift, query_key_value_weight=query_key_value_weight, input_bias=input_bias, attention_out_weight=attention_out_weight, attention_out_bias=attention_out_bias, second_gain=second_gain, second_shift=second_shift, widen_weight=widen_weight, widen_bias=widen_bias, narrow_weight=narrow_weight, narrow_bias=narrow_bias)


EPSILON = 1e-05
MASKED = -1e+30
EXACT_MATMUL = lax.Precision.HIGHEST

@jax.custom_vjp
def low(v):
    return lax.optimization_barrier(v.astype(jnp.bfloat16)).astype(jnp.float32)

@jax.custom_vjp
def low_back(v):
    return v

def low_keep(v):
    return (low(v), None)

def low_pass(kept, grad):
    return (grad,)

def back_keep(v):
    return (v, None)

def back_low(kept, grad):
    return (low(grad),)
low.defvjp(low_keep, low_pass)
low_back.defvjp(back_keep, back_low)

def layer_norm(values, norm_gain, norm_shift):
    center = values - lax.optimization_barrier(jnp.mean(values, axis=-1, keepdims=True))
    spread = lax.optimization_barrier(jnp.mean(center * center, axis=-1, keepdims=True))
    return center * lax.rsqrt(spread + EPSILON) * norm_gain + norm_shift

def gelu_tanh(values):
    return jax.nn.gelu(values, approximate=True)

def attention(queries, key_rows, values, places):
    span_rows = math.gcd(L, 512)
    query_blocks = queries.reshape(L // span_rows, span_rows, HEADS, HD)
    key_heads = key_rows.reshape(L, HEADS, HD)
    value_heads = values.reshape(L, HEADS, HD)
    place_blocks = places.reshape(L // span_rows, span_rows)

    def attend_block(current):
        query_block, place_block = current
        scores = low_back(jnp.einsum('qhd,khd->hqk', query_block, key_heads, precision=EXACT_MATMUL) * HD ** (-0.5))
        allowed = (place_block[:, None] >= places[None, :])[None]
        probs = jax.nn.softmax(jnp.where(allowed, scores, MASKED), axis=-1)
        return jnp.einsum('hqk,khd->qhd', low(probs), value_heads, precision=EXACT_MATMUL)
    return lax.map(jax.checkpoint(attend_block), (query_blocks, place_blocks)).reshape(L, D)

def layer(weights, input_to_layer, places):
    first_gain, first_shift, query_key_value_weight, input_bias, attention_out_weight, attention_out_bias, second_gain, second_shift, widen_weight, widen_bias, narrow_weight, narrow_bias = weights
    first_normalized = low(layer_norm(input_to_layer, first_gain, first_shift))
    attention_projected = jnp.einsum('knh,hw->knw', first_normalized, query_key_value_weight, precision=EXACT_MATMUL)
    queries = low(low_back(attention_projected[..., :D] + input_bias[:D]))
    key_rows = low(low_back(attention_projected[..., D:2 * D]))
    values = low(low_back(attention_projected[..., 2 * D:] + input_bias[D:]))
    attended = jax.vmap(attention, in_axes=(0, 0, 0, None))(queries, key_rows, values, places)
    attention_lower = low(low_back(attended))
    residual_stream = input_to_layer + low_back(jnp.einsum('knh,hw->knw', attention_lower, attention_out_weight, precision=EXACT_MATMUL) + attention_out_bias)
    second_normalized = low(layer_norm(residual_stream, second_gain, second_shift))
    hidden_before_gelu = low_back(jnp.einsum('knh,hw->knw', second_normalized, widen_weight, precision=EXACT_MATMUL) + widen_bias)
    hidden_units = low(gelu_tanh(hidden_before_gelu))
    return residual_stream + low_back(jnp.einsum('pxo,oc->pxc', hidden_units, narrow_weight, precision=EXACT_MATMUL) + narrow_bias)

def reference(tokens, block_order, cotangent, first_gain, first_shift, query_key_value_weight, input_bias, attention_out_weight, attention_out_bias, second_gain, second_shift, widen_weight, widen_bias, narrow_weight, narrow_bias):
    row_ids = jnp.arange(L, dtype=jnp.int32)
    order_flat = block_order.reshape(-1).astype(jnp.int32)
    places = (jnp.take(order_flat, row_ids // BLK) * BLK + row_ids % BLK).astype(jnp.int32)
    stacked = tuple((member.astype(jnp.float32) for member in (first_gain, first_shift, query_key_value_weight, input_bias, attention_out_weight, attention_out_bias, second_gain, second_shift, widen_weight, widen_bias, narrow_weight, narrow_bias)))
    lower = tuple((member[0] for member in stacked))
    upper = tuple((member[1] for member in stacked))
    input_to_layer = tokens.astype(jnp.float32)
    middle, pull_lower = jax.vjp(lambda weights, values: layer(weights, values, places), lower, input_to_layer)
    final, pull_upper = jax.vjp(lambda weights, values: layer(weights, values, places), upper, middle)
    upper_grads, middle_grad = pull_upper(cotangent.astype(jnp.float32))
    lower_grads, input_grad = pull_lower(middle_grad)
    grads = [jnp.stack([first_part, second_part]) for first_part, second_part in zip(lower_grads, upper_grads)]
    return (jnp.stack([middle, final]), jnp.stack([input_grad, middle_grad]), grads[0], grads[1], grads[2], grads[3], grads[4], grads[5], grads[6], grads[7], grads[8], grads[9], grads[10], grads[11])
```

```python
import functools

import jax
import jax.numpy as jnp
from jax import lax
from jax.experimental import pallas as pl
from jax.experimental.pallas import tpu as pltpu
from jax.sharding import PartitionSpec as P

HEADS = 25
HD = 64
EPSILON = 1e-05
MASKED = -1e30
LOG2E = 1.4426950408889634
GELU_A = 0.7978845608028654
GELU_B = 0.044715
MESH = pl.DeviceIdType.MESH
F32 = jnp.float32
BF16 = jnp.bfloat16
VMEM_SPEC = pl.BlockSpec(memory_space=pltpu.VMEM)
ANY_SPEC = pl.BlockSpec(memory_space=pl.ANY)
DMA = pltpu.SemaphoreType.DMA
VMEM_LIMIT = 56 * 2**20
HALVES = 2


def params(collective_id=None):
    if collective_id is None:
        return pltpu.CompilerParams(vmem_limit_bytes=VMEM_LIMIT)
    return pltpu.CompilerParams(
        collective_id=collective_id, has_side_effects=True, vmem_limit_bytes=VMEM_LIMIT
    )


def remote(src, dst, send_sem, recv_sem, device):
    return pltpu.make_async_remote_copy(
        src_ref=src,
        dst_ref=dst,
        send_sem=send_sem,
        recv_sem=recv_sem,
        device_id=device,
        device_id_type=MESH,
    )


class Place:
    def __init__(self, n):
        self.s = lax.axis_index("section")
        self.c = lax.axis_index("ctx")
        self.h = lax.axis_index("shard")
        self.n = n
        self.zn = n // 2
        self.y = lax.rem(self.h, 2)
        self.z = lax.div(self.h, 2)
        self.far_y = self.y + self.c - 2 * self.y * self.c

    def dev(self, z, y):
        return (self.s, self.c, z * 2 + y)

    @property
    def pair(self):
        return self.dev(self.z, 1 - self.y)

    @property
    def above(self):
        return self.dev(self.z + 1, self.y)

    @property
    def below(self):
        return self.dev(self.z - 1, self.y)

    @property
    def over(self):
        return (1 - self.s, self.c, self.h)

    @property
    def sibling(self):
        return (self.s, 1 - self.c, self.h)


def greet(p, line=False, spread=False, over=False, sibling=False):
    bar = pltpu.get_barrier_semaphore()
    peers = 0

    def signal(device):
        pl.semaphore_signal(bar, inc=1, device_id=device, device_id_type=MESH)

    if line:
        signal(p.pair)

        @pl.when(p.z < p.zn - 1)
        def _():
            signal(p.above)

        @pl.when(p.z > 0)
        def _():
            signal(p.below)

        peers = 1 + (p.z + p.zn - 1) // p.zn + (2 * p.zn - 2 - p.z) // p.zn
    if spread:
        for dz in range(1, p.zn):
            signal(p.dev(lax.rem(p.z + dz, p.zn), p.far_y))

        @pl.when(p.c == 1)
        def _():
            signal(p.dev(p.z, p.far_y))

        peers = peers + p.zn - 1 + p.c
    if over:
        signal(p.over)
        peers = peers + 1
    if sibling:
        signal(p.sibling)
        peers = peers + 1
    pl.semaphore_wait(bar, peers)


class Gather:
    def __init__(self, p, own_ref, out_ref, ss, rs, ls):
        self.p, self.own_ref, self.out_ref = p, own_ref, out_ref
        self.ss, self.rs, self.ls = ss, rs, ls
        self.hr = own_ref.shape[0] // HALVES

    def blk(self, half, zz, yy):
        row = (half * self.p.n + zz * 2 + yy) * self.hr
        return self.out_ref.at[pl.ds(pl.multiple_of(row, 16), self.hr)]

    def own(self, half):
        return self.own_ref.at[pl.ds(half * self.hr, self.hr)]

    def up(self, t, half, src):
        p = self.p
        sems = (self.ss.at[0, t, half], self.rs.at[0, t, half])
        return remote(src, self.blk(half, p.z - (t - 1), p.y), *sems, p.above)

    def down(self, t, half, src):
        p = self.p
        sems = (self.ss.at[1, t, half], self.rs.at[1, t, half])
        return remote(src, self.blk(half, p.z + (t - 1), p.y), *sems, p.below)

    def across(self, kind, t, half, zz, src):
        p = self.p
        sems = (self.ss.at[2 + kind, t, half], self.rs.at[2 + kind, t, half])
        return remote(src, self.blk(half, zz, p.y), *sems, p.pair)

    def local(self, half):
        p = self.p
        return pltpu.make_async_copy(
            self.own(half), self.blk(half, p.z, p.y), self.ls.at[half]
        )

    def start(self, halves=range(HALVES)):
        p = self.p
        for half in halves:
            src = self.own(half)

            @pl.when(p.z < p.zn - 1)
            def _():
                self.up(1, half, src).start()

            @pl.when(p.z > 0)
            def _():
                self.down(1, half, src).start()

            self.across(0, 0, half, p.z, src).start()
            self.local(half).start()

    def step(self, t, half):
        p = self.p
        z, zn = p.z, p.zn

        @pl.when(z >= t)
        def _():
            block = self.blk(half, z - t, p.y)
            self.up(t, half, block).wait_recv()
            if t < zn - 1:

                @pl.when(z < zn - 1)
                def _():
                    self.up(t + 1, half, block).start()

            self.across(0, t, half, z - t, block).start()

        @pl.when(z <= zn - 1 - t)
        def _():
            block = self.blk(half, z + t, p.y)
            self.down(t, half, block).wait_recv()
            if t < zn - 1:

                @pl.when(z > 0)
                def _():
                    self.down(t + 1, half, block).start()

            self.across(1, t, half, z + t, block).start()

    def steps(self):
        return [
            functools.partial(self.step, t, half)
            for t in range(1, self.p.zn)
            for half in range(HALVES)
        ]

    def finish(self):
        p = self.p
        z, zn = p.z, p.zn
        for half in range(HALVES):
            self.across(0, 0, half, z, self.own(half)).wait_recv()
            for t in range(1, zn):

                @pl.when(z >= t)
                def _():
                    self.across(0, t, half, z - t, self.own(half)).wait_recv()

                @pl.when(z <= zn - 1 - t)
                def _():
                    self.across(1, t, half, z + t, self.own(half)).wait_recv()

        for half in range(HALVES):
            self.local(half).wait()
            self.across(0, 0, half, z, self.own(half)).wait_send()
            for t in range(1, zn):

                @pl.when((z < zn - 1) & (z >= t - 1))
                def _():
                    self.up(t, half, self.own(half)).wait_send()

                @pl.when((z > 0) & (z <= zn - t))
                def _():
                    self.down(t, half, self.own(half)).wait_send()

                @pl.when(z >= t)
                def _():
                    self.across(0, t, half, z - t, self.own(half)).wait_send()

                @pl.when(z <= zn - 1 - t)
                def _():
                    self.across(1, t, half, z + t, self.own(half)).wait_send()


class Scatter:
    def __init__(self, p, part_ref, ybuf, rbuf, sbuf, ss, rs):
        self.p, self.part_ref = p, part_ref
        self.ybuf, self.rbuf, self.sbuf, self.ss, self.rs = ybuf, rbuf, sbuf, ss, rs
        self.hr = ybuf.shape[3]

    def blk(self, half, zz, yy):
        row = (half * self.p.n + zz * 2 + yy) * self.hr
        return self.part_ref.at[pl.ds(pl.multiple_of(row, 16), self.hr)]

    def across(self, k, t, half):
        p = self.p
        zz = p.z + t if k == 0 else p.z - t
        sems = (self.ss.at[k, t, half], self.rs.at[k, t, half])
        return remote(self.blk(half, zz, 1 - p.y), self.ybuf.at[k, t, half], *sems, p.pair)

    def along(self, k, t, half, slot):
        p = self.p
        sems = (self.ss.at[2 + k, t, half], self.rs.at[2 + k, slot, half])
        target = p.above if k == 0 else p.below
        return remote(self.sbuf.at[k, t, half], self.rbuf.at[k, slot, half], *sems, target)

    def ok(self, k, t):
        return self.p.z <= self.p.zn - 1 - t if k == 0 else self.p.z >= t

    def has(self, k):
        return self.p.z > 0 if k == 0 else self.p.z < self.p.zn - 1

    def start(self):
        for t in range(self.p.zn - 1, 0, -1):
            for half in range(HALVES):
                for k in range(2):

                    @pl.when(self.ok(k, t))
                    def _():
                        self.across(k, t, half).start()

        for half in range(HALVES):
            self.across(0, 0, half).start()

    def step(self, t, half, k):
        p = self.p
        zz = p.z + t if k == 0 else p.z - t

        @pl.when(self.ok(k, t))
        def _():
            self.across(k, t, half).wait_recv()
            total = self.blk(half, zz, p.y)[...].astype(F32)
            total = total + self.ybuf[k, t, half].astype(F32)
            if t < p.zn - 1:

                @pl.when(self.has(k))
                def _():
                    self.along(k, t, half, t).wait_recv()
                    more = total + self.rbuf[k, t, half].astype(F32)
                    self.sbuf[k, t, half] = more.astype(BF16)

                @pl.when(jnp.logical_not(self.has(k)))
                def _():
                    self.sbuf[k, t, half] = total.astype(BF16)

            else:
                self.sbuf[k, t, half] = total.astype(BF16)
            self.along(k, t, half, t - 1).start()

    def steps(self):
        return [
            functools.partial(self.step, t, half, k)
            for t in range(self.p.zn - 1, 0, -1)
            for half in range(HALVES)
            for k in range(2)
        ]

    def result(self, half):
        p = self.p
        self.across(0, 0, half).wait_recv()
        for k in range(2):

            @pl.when(self.has(k))
            def _():
                self.along(k, 0, half, 0).wait_recv()

            @pl.when(jnp.logical_not(self.has(k)))
            def _():
                self.rbuf[k, 0, half] = jnp.zeros(self.rbuf.shape[3:], BF16)

        total = self.blk(half, p.z, p.y)[...].astype(F32) + self.ybuf[0, 0, half].astype(F32)
        return total + self.rbuf[0, 0, half].astype(F32) + self.rbuf[1, 0, half].astype(F32)

    def finish(self):
        for half in range(HALVES):
            self.across(0, 0, half).wait_send()
            for t in range(1, self.p.zn):
                for k in range(2):

                    @pl.when(self.ok(k, t))
                    def _():
                        self.across(k, t, half).wait_send()
                        self.along(k, t, half, t - 1).wait_send()


class Spread:
    def __init__(self, p, src, dst, ss, rs, ls):
        self.p, self.src, self.dst, self.ss, self.rs, self.ls = p, src, dst, ss, rs, ls

    def source(self, dz):
        return lax.rem(self.p.z + self.p.zn - dz, self.p.zn) * 2 + self.p.far_y

    def out(self, dz):
        p = self.p
        target = lax.rem(p.z + dz, p.zn) * 2 + p.far_y
        sems = (self.ss.at[0, dz], self.rs.at[0, dz])
        return remote(self.src.at[target], self.dst.at[p.s, p.h], *sems, (p.s, p.c, target))

    def aside(self, dz):
        block = self.dst.at[self.p.s, self.source(dz)]
        return remote(block, block, self.ss.at[1, dz], self.rs.at[1, dz], self.p.sibling)

    def cross(self, dz):
        block = self.dst.at[self.p.s, self.source(dz)]
        return remote(block, block, self.ss.at[2, dz], self.rs.at[2, dz], self.p.over)

    def cross_own(self):
        p = self.p
        sems = (self.ss.at[2, 0], self.rs.at[2, 0])
        return remote(self.src.at[p.h], self.dst.at[p.s, p.h], *sems, p.over)

    def cross_aside(self, dz):
        block = self.dst.at[1 - self.p.s, self.source(dz)]
        return remote(block, block, self.ss.at[3, dz], self.rs.at[3, dz], self.p.sibling)

    def local(self):
        p = self.p
        return pltpu.make_async_copy(self.src.at[p.h], self.dst.at[p.s, p.h], self.ls)

    def start(self):
        @pl.when(self.p.c == 1)
        def _():
            self.out(0).start()

        @pl.when(self.p.c == 0)
        def _():
            self.cross_own().start()

        for dz in range(1, self.p.zn):
            self.out(dz).start()
        self.local().start()

    def arrived(self, dz):
        self.out(dz).wait_recv()
        self.cross(dz).start()
        self.aside(dz).start()

    def crossed(self, dz):
        self.cross(dz).wait_recv()
        self.cross_aside(dz).start()

    def first(self):
        @pl.when(self.p.c == 1)
        def _():
            self.arrived(0)

    def steps(self):
        found = [self.first]
        found += [functools.partial(self.arrived, dz) for dz in range(1, self.p.zn)]
        return found + [functools.partial(self.crossed, dz) for dz in range(self.p.zn)]

    def finish(self):
        self.local().wait()

        @pl.when(self.p.c == 0)
        def _():
            self.aside(0).wait_recv()
            self.cross_own().wait_send()

        @pl.when(self.p.c == 1)
        def _():
            self.out(0).wait_send()
            self.aside(0).wait_send()
            self.cross(0).wait_send()

        for dz in range(self.p.zn):
            if dz:
                self.aside(dz).wait_recv()
                self.aside(dz).wait_send()
                self.out(dz).wait_send()
                self.cross(dz).wait_send()
            self.cross_aside(dz).wait_recv()
            self.cross_aside(dz).wait_send()


class RowSwap:
    def __init__(self, p, src, dst, ss, rs, ls):
        self.p, self.src, self.dst, self.ss, self.rs, self.ls = p, src, dst, ss, rs, ls
        self.split = src.shape[0] % 32 == 0

    def piece(self, which):
        if not self.split:
            return self.src, self.dst.at[which]
        half = self.src.shape[0] // 2
        rows = pl.ds(pl.multiple_of(self.p.c * half, 16), half)
        return self.src.at[rows], self.dst.at[which, rows]

    def cross(self):
        src, dst = self.piece(self.p.s)
        return remote(src, dst, self.ss.at[0], self.rs.at[0], self.p.over)

    def aside(self):
        block = self.piece(1 - self.p.s)[1]
        return remote(block, block, self.ss.at[1], self.rs.at[1], self.p.sibling)

    def local(self):
        return pltpu.make_async_copy(self.src, self.dst.at[self.p.s], self.ls)

    def start(self):
        self.cross().start()
        self.local().start()

    def step(self):
        self.cross().wait_recv()
        if self.split:
            self.aside().start()

    def finish(self):
        self.local().wait()
        self.cross().wait_send()
        if self.split:
            self.aside().wait_recv()
            self.aside().wait_send()


class Cross:
    def __init__(self, p, src, dst, ss, rs, source):
        self.p, self.source = p, source
        self.copy = remote(src, dst, ss, rs, p.over)

    def start(self):
        @pl.when(self.p.s == self.source)
        def _():
            self.copy.start()

    def finish(self):
        @pl.when(self.p.s == self.source)
        def _():
            self.copy.wait_send()

        @pl.when(self.p.s != self.source)
        def _():
            self.copy.wait_recv()


def greet_all(p):
    bar = pltpu.get_barrier_semaphore()
    for a in range(2):
        for b in range(p.n):
            if (a, b) != (0, 0):
                other = (lax.rem(p.s + a, 2), p.c, lax.rem(p.h + b, p.n))
                pl.semaphore_signal(bar, inc=1, device_id=other, device_id_type=MESH)
    pl.semaphore_signal(bar, inc=1, device_id=p.sibling, device_id_type=MESH)
    pl.semaphore_wait(bar, 2 * p.n)


def others(n):
    return [(a, b) for a in range(2) for b in range(n) if (a, b) != (0, 0)]


def start_kernel(n, tok_ref, pack_ref, qkv_ref, out_ref, *refs):
    tok_all, pack_all, qkv_all, out_all = refs[:4]
    g_ss, g_rs, g_ls, p_ss, p_rs, a_ss, a_rs, o_ss, o_rs, l_sem = refs[4:]
    p = Place(n)
    s, c, h = p.s, p.c, p.h
    greet_all(p)

    def pack_copy(a, b):
        target = (lax.rem(s + a, 2), c, lax.rem(h + b, n))
        return remote(pack_ref, pack_all.at[s, h], p_ss.at[a, b], p_rs.at[a, b], target)

    for a, b in others(n):
        pack_copy(a, b).start()
    pack_own = pltpu.make_async_copy(pack_ref, pack_all.at[s, h], l_sem.at[0])
    pack_own.start()
    tokens = Gather(p, tok_ref, tok_all, g_ss, g_rs, g_ls)
    qkv = Spread(p, qkv_ref, qkv_all, a_ss, a_rs, l_sem.at[1])
    out = RowSwap(p, out_ref, out_all, o_ss, o_rs, l_sem.at[2])
    tokens.start()
    qkv.start()
    out.start()
    qkv_steps = qkv.steps()
    for step in tokens.steps():
        step()
        if qkv_steps:
            qkv_steps.pop(0)()
    for step in qkv_steps:
        step()
    out.step()
    pack_own.wait()
    for a, b in others(n):
        pack_copy(a, b).wait_recv()
        pack_copy(a, b).wait_send()
    tokens.finish()
    qkv.finish()
    out.finish()


def start_call(n, tok, pack, qkv, out):
    rows, width = tok.shape
    zn = n // 2
    shapes = [
        jax.ShapeDtypeStruct((n * rows, width), BF16),
        jax.ShapeDtypeStruct((2, n) + pack.shape, BF16),
        jax.ShapeDtypeStruct((2,) + qkv.shape, BF16),
        jax.ShapeDtypeStruct((2,) + out.shape, BF16),
    ]
    return pl.pallas_call(
        functools.partial(start_kernel, n),
        out_shape=shapes,
        in_specs=[ANY_SPEC] * 4,
        out_specs=[ANY_SPEC] * 4,
        scratch_shapes=[
            DMA((4, zn, HALVES)),
            DMA((4, zn, HALVES)),
            DMA((HALVES,)),
            DMA((2, n)),
            DMA((2, n)),
            DMA((4, zn)),
            DMA((4, zn)),
            DMA((2,)),
            DMA((2,)),
            DMA((3,)),
        ],
        compiler_params=params(0),
        name="start",
    )(tok, pack, qkv, out)


def lay_out_kernel(low, share, qkv_ref, widen_ref, out_ref, narrow_ref, *outs):
    qkv_to, widen_to, out_to, narrow_to = outs
    n, padded, hide = widen_to.shape
    width = qkv_ref.shape[1] // 3
    sh = qkv_to.shape[2] // 3
    gap = padded - share
    for j in range(n):
        for t in range(3):
            first = t * width + HD * low[j]
            qkv_to[j, :share, t * sh : (t + 1) * sh] = qkv_ref[:, first : first + sh]
        widen_to[j, :share] = widen_ref[:, j * hide : (j + 1) * hide]
        if gap:
            qkv_to[j, share:] = jnp.zeros((gap, 3 * sh), BF16)
            widen_to[j, share:] = jnp.zeros((gap, hide), BF16)
    spread = []
    for ref in (out_ref, narrow_ref):
        rows = ref.shape[0]
        pieces = []
        for j in range(n):
            pieces.append(ref[:, j * share : (j + 1) * share])
            if gap:
                pieces.append(jnp.zeros((rows, gap), BF16))
        spread.append(jnp.concatenate(pieces, axis=1))
    narrow_to[...] = spread[1]
    out_to[...] = spread[0]


def lay_out_call(low, slots, padded, qkv, widen, out, narrow):
    n = len(low)
    share, hidden = widen.shape
    sh = slots * HD
    return pl.pallas_call(
        functools.partial(lay_out_kernel, low, share),
        out_shape=[
            jax.ShapeDtypeStruct((n, padded, 3 * sh), BF16),
            jax.ShapeDtypeStruct((n, padded, hidden // n), BF16),
            jax.ShapeDtypeStruct((share, n * padded), BF16),
            jax.ShapeDtypeStruct((narrow.shape[0], n * padded), BF16),
        ],
        in_specs=[VMEM_SPEC] * 4,
        out_specs=[VMEM_SPEC] * 4,
        compiler_params=params(),
        name="lay_out",
    )(qkv, widen, out, narrow)


def settle_kernel(low, share, qkv_ref, widen_ref, out_ref, narrow_ref, *outs):
    qkv_to, widen_to, out_to, narrow_to = outs
    n, padded, hide = widen_ref.shape
    width = qkv_to.shape[1] // 3
    sh = qkv_ref.shape[2] // 3
    qkv_to[...] = jnp.zeros_like(qkv_to)
    for j in range(n):
        for t in range(3):
            first = t * width + HD * low[j]
            qkv_to[:, first : first + sh] += qkv_ref[j, :share, t * sh : (t + 1) * sh].astype(F32)
    for j in range(n):
        widen_to[:, j * hide : (j + 1) * hide] = widen_ref[j, :share].astype(F32)
        for ref, to in ((out_ref, out_to), (narrow_ref, narrow_to)):
            piece = ref[: to.shape[0], j * padded : j * padded + share]
            to[:, j * share : (j + 1) * share] = piece.astype(F32)


def settle_call(low, share, qkv, widen, out, narrow):
    n, _, hide = widen.shape
    width = n * share
    return pl.pallas_call(
        functools.partial(settle_kernel, low, share),
        out_shape=[
            jax.ShapeDtypeStruct((share, 3 * width), F32),
            jax.ShapeDtypeStruct((share, n * hide), F32),
            jax.ShapeDtypeStruct((share, width), F32),
            jax.ShapeDtypeStruct((hide, width), F32),
        ],
        in_specs=[VMEM_SPEC] * 4,
        out_specs=[VMEM_SPEC] * 4,
        compiler_params=params(),
        name="settle",
    )(qkv, widen, out, narrow)


def unit_rows(values, mask, width):
    center = (values - jnp.sum(values, axis=-1, keepdims=True) * (1.0 / width)) * mask
    spread = jnp.sum(center * center, axis=-1, keepdims=True) * (1.0 / width)
    scale = lax.rsqrt(spread + EPSILON)
    return center * scale, scale


def norm_back(grad, unit, scale, gain, width):
    inner = grad * gain
    mean = jnp.sum(inner, axis=-1, keepdims=True) * (1.0 / width)
    along = jnp.sum(inner * unit, axis=-1, keepdims=True) * (1.0 / width)
    return (inner - mean - unit * along) * scale


FORWARD_KINDS = ("mid", "end")


def phase_kernel(n, kind, width, side, *refs):
    forward = kind in FORWARD_KINDS
    gathers = kind != "first"
    ins = 6 if forward else 5
    outs = (1 if forward else 2) + (1 if gathers else 0)
    in_refs, refs = refs[:ins], refs[ins:]
    if side:
        side_in, refs = refs[0], refs[1:]
    out_refs, refs = refs[:outs], refs[outs:]
    if side:
        side_out, refs = refs[0], refs[1:]
    ybuf, rbuf, sbuf, s_ss, s_rs = refs[:5]
    refs = refs[5:]
    if gathers:
        own, g_ss, g_rs, g_ls = refs[:4]
        refs = refs[4:]
    p = Place(n)
    greet(p, line=True, over=bool(side), sibling=side == "swap")
    scatter = Scatter(p, in_refs[0], ybuf, rbuf, sbuf, s_ss, s_rs)
    scatter.start()
    job = None
    if side == "swap":
        job = RowSwap(p, side_in, side_out, *refs[:3])
        job.start()
    elif side:
        job = Cross(p, side_in, side_out, *refs[:2], int(side[-1]))
        job.start()
    gather = None
    if gathers:
        gather = Gather(p, own, out_refs[-1], g_ss, g_rs, g_ls)
    for step in scatter.steps():
        step()
    hr = ybuf.shape[3]
    sums = [jnp.zeros((1, in_refs[0].shape[1]), F32)] * 3
    for half in range(HALVES):
        rows = slice(half * hr, (half + 1) * hr)
        total = scatter.result(half)
        if forward:
            value = in_refs[1][rows] + (total + in_refs[2][...])
            out_refs[0][rows] = value
            gain, shift, mask = (ref[...] for ref in in_refs[3:])
            own[rows] = (unit_rows(value, mask, width)[0] * gain + shift).astype(BF16)
        else:
            base, grad, gain, mask = in_refs[1][rows], in_refs[2][rows], in_refs[3], in_refs[4]
            unit, scale = unit_rows(base, mask[...], width)
            value = grad + norm_back(total, unit, scale, gain[...], width)
            out_refs[0][rows] = value
            low = value.astype(BF16)
            if gathers:
                own[rows] = low
            for item, term in enumerate((total * unit, total, low.astype(F32))):
                sums[item] = sums[item] + jnp.sum(term, axis=0, keepdims=True)
        if gathers:
            gather.start([half])
    if not forward:
        out_refs[1][...] = jnp.concatenate(sums, axis=0)
    if gathers:
        for step in gather.steps():
            step()
    if side == "swap":
        job.step()
    if gathers:
        gather.finish()
    scatter.finish()
    if job is not None:
        job.finish()


def scatter_scratch(n, rows, full):
    zn = n // 2
    return [pltpu.VMEM((2, zn, HALVES, rows // HALVES, full), BF16)] * 3 + [
        DMA((4, zn, HALVES)),
        DMA((4, zn, HALVES)),
    ]


def gather_scratch(n):
    zn = n // 2
    return [DMA((4, zn, HALVES)), DMA((4, zn, HALVES)), DMA((HALVES,))]


def phase_call(n, kind, collective_id, width, part, *local, side=None, carried=None):
    total_rows, full = part.shape
    rows = total_rows // n
    forward = kind in FORWARD_KINDS
    gathers = kind != "first"
    shapes = [jax.ShapeDtypeStruct((rows, full), F32)]
    if not forward:
        shapes.append(jax.ShapeDtypeStruct((3, full), F32))
    scratch = scatter_scratch(n, rows, full)
    if gathers:
        shapes.append(jax.ShapeDtypeStruct((total_rows, full), BF16))
        scratch += [pltpu.VMEM((rows, full), BF16)] + gather_scratch(n)
    in_specs = [VMEM_SPEC] * (1 + len(local))
    out_specs = [VMEM_SPEC] * len(shapes)
    args = (part,) + local
    if side:
        args += (carried,)
        in_specs.append(ANY_SPEC)
        out_specs.append(ANY_SPEC)
        lead = (2,) if side == "swap" else ()
        shapes.append(jax.ShapeDtypeStruct(lead + carried.shape, BF16))
        scratch += [DMA((2,)), DMA((2,)), DMA] if side == "swap" else [DMA, DMA]
    return pl.pallas_call(
        functools.partial(phase_kernel, n, kind, width, side),
        out_shape=shapes,
        in_specs=in_specs,
        out_specs=out_specs,
        scratch_shapes=scratch,
        compiler_params=params(collective_id),
        name="phase_" + kind,
    )(*args)


def dot_t(a, b):
    return lax.dot_general(a, b, (((1,), (1,)), ((), ())), preferred_element_type=F32)


def dot_n(a, b):
    return lax.dot_general(a, b, (((1,), (0,)), ((), ())), preferred_element_type=F32)


def in_blocks(rows, step, chunk, between):
    count = rows // step
    if count <= 2:
        for b in range(count):
            chunk(b * step, between)
    else:

        def body(b, carry):
            chunk(pl.multiple_of(b * step, step), [])
            return carry

        lax.fori_loop(0, count, body, 0)


def run_next(between):
    if between:
        between.pop(0)()


def attend_kernel(n, slots, step, side, own_ref, kpos_ref, qpos_ref, carried, *refs):
    att_ref, low_ref, lse_ref, oth_ref, carried_to, kv_ss, kv_rs = refs[:7]
    p = Place(n)
    rows = own_ref.shape[0]
    sh = slots * HD
    power = HD**-0.5 * LOG2E
    if side == "spread":
        greet(p, spread=True, over=True, sibling=True)
    else:
        greet(p, line=True, sibling=True)
    swap = remote(own_ref.at[:, pl.ds(sh, 2 * sh)], oth_ref, kv_ss, kv_rs, p.sibling)
    swap.start()
    job = (Spread if side == "spread" else Gather)(p, carried, carried_to, *refs[7:])
    job.start()
    swap.wait_recv()

    def at(base, slot):
        return slice(base + slot * HD, base + (slot + 1) * HD)

    def chunk(first, between):
        q_rows = pl.ds(first, step)
        qpos = qpos_ref[:, q_rows]
        for slot in range(slots):
            queries = own_ref[q_rows, at(0, slot)]
            keys = (own_ref[:, at(sh, slot)], oth_ref[:, at(0, slot)])
            values = (own_ref[:, at(2 * sh, slot)], oth_ref[:, at(sh, slot)])
            scores = []
            for part in range(2):
                allowed = kpos_ref[part * rows : (part + 1) * rows] <= qpos
                scores.append(jnp.where(allowed, dot_t(keys[part], queries), MASKED))
            top = jnp.maximum(
                jnp.max(scores[0], axis=0, keepdims=True), jnp.max(scores[1], axis=0, keepdims=True)
            )
            total = jnp.zeros_like(top)
            weighted = jnp.zeros((HD, step), F32)
            exps = []
            for part in range(2):
                e = jnp.exp2((scores[part] - top) * power)
                total = total + jnp.sum(e, axis=0, keepdims=True)
                exps.append(e)
            inverse = 1.0 / total
            for part in range(2):
                probs = (exps[part] * inverse).astype(BF16)
                weighted = weighted + dot_n(values[part].T, probs)
            att_ref[at(0, slot), q_rows] = weighted
            low_ref[q_rows, at(0, slot)] = weighted.T.astype(BF16)
            lse_ref[slot : slot + 1, q_rows] = top * power + jnp.log(total) * LOG2E
            run_next(between)

    between = job.steps()
    in_blocks(rows, step, chunk, between)
    for rest in between:
        rest()
    swap.wait_send()
    job.finish()


def attend_call(n, collective_id, slots, qkv, kpos, qpos, side, carried):
    rows = qkv.shape[0]
    zn = n // 2
    sh = slots * HD
    step = min(rows, 256)
    if side == "spread":
        moved = jax.ShapeDtypeStruct((2,) + carried.shape, BF16)
        scratch = [DMA((4, zn)), DMA((4, zn)), DMA]
    else:
        moved = jax.ShapeDtypeStruct((n * carried.shape[0], carried.shape[1]), BF16)
        scratch = gather_scratch(n)
    return pl.pallas_call(
        functools.partial(attend_kernel, n, slots, step, side),
        out_shape=[
            jax.ShapeDtypeStruct((sh, rows), F32),
            jax.ShapeDtypeStruct((rows, sh), BF16),
            jax.ShapeDtypeStruct((slots, rows), F32),
            jax.ShapeDtypeStruct((rows, 2 * sh), BF16),
            moved,
        ],
        in_specs=[VMEM_SPEC] * 3 + [ANY_SPEC],
        out_specs=[VMEM_SPEC] * 4 + [ANY_SPEC],
        scratch_shapes=[DMA, DMA] + scratch,
        compiler_params=params(collective_id),
        name="attend_" + side,
    )(qkv, kpos, qpos, carried)


def attend_back_kernel(n, slots, step, last, *refs):
    own_ref, oth_ref, grad_ref, att_ref, lse_ref, kpos_ref, qpos_ref = refs[:7]
    refs = refs[7:]
    if last:
        part_ref, base_ref, bias_ref = refs[:3]
        refs = refs[3:]
    triple_ref, refs = refs[0], refs[1:]
    if last:
        value_ref, refs = refs[0], refs[1:]
    dq_t, dkv_own, dkv_oth, came, kv_ss, kv_rs = refs[:6]
    p = Place(n)
    rows = own_ref.shape[0]
    sh = slots * HD
    scale = HD**-0.5
    greet(p, line=last, sibling=True)
    between = []
    if last:
        scatter = Scatter(p, part_ref, *refs[6:])
        scatter.start()
        between = scatter.steps()

    def at(base, slot):
        return slice(base + slot * HD, base + (slot + 1) * HD)

    dq_t[...] = jnp.zeros_like(dq_t)
    swap = remote(dkv_oth, came, kv_ss, kv_rs, p.sibling)
    for part in (1, 0):
        dkv = (dkv_own, dkv_oth)[part]
        src = (own_ref, oth_ref)[part]
        base = (sh, 0)[part]
        dkv[...] = jnp.zeros_like(dkv)

        def chunk(first, between):
            q_rows = pl.ds(first, step)
            qpos = qpos_ref[:, q_rows]
            for slot in range(slots):
                queries = own_ref[q_rows, at(0, slot)]
                grads = grad_ref[q_rows, at(0, slot)]
                keys, values = src[:, at(base, slot)], src[:, at(base + sh, slot)]
                lse = lse_ref[slot : slot + 1, q_rows]
                correction = jnp.sum(
                    grads.astype(F32).T * att_ref[at(0, slot), q_rows], axis=0, keepdims=True
                )
                allowed = kpos_ref[part * rows : (part + 1) * rows] <= qpos
                scores = dot_t(keys, queries)
                probs = jnp.where(allowed, jnp.exp2(scores * (scale * LOG2E) - lse), 0.0)
                prob_grad = dot_t(values, grads)
                score_grad = (probs * (prob_grad - correction)).astype(BF16)
                dkv[:, at(0, slot)] += dot_n(score_grad, queries) * scale
                dkv[:, at(sh, slot)] += dot_n(probs.astype(BF16), grads)
                dq_t[at(0, slot), q_rows] += dot_n(keys.T, score_grad)
                run_next(between)

        in_blocks(rows, step, chunk, between)
        if part:
            swap.start()
    triple_ref[:, :sh] = (dq_t[...].T * scale).astype(BF16)
    for rest in between:
        rest()
    if last:
        hr = base_ref.shape[0] // HALVES
        for half in range(HALVES):
            part_rows = slice(half * hr, (half + 1) * hr)
            total = scatter.result(half)
            value_ref[part_rows] = base_ref[part_rows] + (total + bias_ref[...])
        scatter.finish()
    swap.wait_recv()
    triple_ref[:, sh:] = (dkv_own[...] + came[...]).astype(BF16)
    swap.wait_send()


def attend_back_call(n, collective_id, slots, *args, last=()):
    qkv = args[0]
    rows = qkv.shape[0]
    sh = slots * HD
    step = min(rows, 256)
    shapes = [jax.ShapeDtypeStruct((rows, 3 * sh), BF16)]
    scratch = [pltpu.VMEM((sh, rows), F32)] + [pltpu.VMEM((rows, 2 * sh), F32)] * 3
    scratch += [DMA, DMA]
    if last:
        shapes.append(jax.ShapeDtypeStruct(last[1].shape, F32))
        scratch += scatter_scratch(n, *last[1].shape)
    return pl.pallas_call(
        functools.partial(attend_back_kernel, n, slots, step, bool(last)),
        out_shape=shapes,
        in_specs=[VMEM_SPEC] * (len(args) + len(last)),
        out_specs=[VMEM_SPEC] * len(shapes),
        scratch_shapes=scratch,
        compiler_params=params(collective_id),
        name="attend_back",
    )(*args, *last)


def fold_kernel(n, count, *refs):
    blocks, rows = refs[:2]
    blocks_to, rows_to = refs[2:4]
    blocks_in, rows_in, ss, rs = refs[4:]
    p = Place(n)
    zn = p.zn
    greet(p, sibling=True)
    near_y = 1 - p.far_y
    half = rows_to.shape[0]

    def mine(first):
        return pl.ds(pl.multiple_of(first * half, 8), half)

    copies = [
        remote(blocks.at[z * 2 + near_y], blocks_in.at[z], ss.at[z], rs.at[z], p.sibling)
        for z in range(zn)
    ]
    copies.append(remote(rows.at[mine(1 - p.c)], rows_in, ss.at[zn], rs.at[zn], p.sibling))
    for copy in copies:
        copy.start()
    for z in range(zn):
        copies[z].wait_recv()
        own = blocks[z * 2 + p.far_y].astype(F32)
        blocks_to[z] = (own + blocks_in[z].astype(F32)).astype(BF16)
    copies[zn].wait_recv()
    rows_to[...] = (rows[mine(p.c)].astype(F32) + rows_in[...].astype(F32)).astype(BF16)
    for copy in copies:
        copy.wait_send()


def fold_call(n, collective_id, blocks, rows):
    zn = n // 2
    halves = (rows.shape[0] // 2, rows.shape[1])
    some = (zn,) + blocks.shape[1:]
    return pl.pallas_call(
        functools.partial(fold_kernel, n, 1),
        out_shape=[jax.ShapeDtypeStruct(some, BF16), jax.ShapeDtypeStruct(halves, BF16)],
        in_specs=[VMEM_SPEC] * 2,
        out_specs=[VMEM_SPEC] * 2,
        scratch_shapes=[
            pltpu.VMEM(some, BF16),
            pltpu.VMEM(halves, BF16),
            DMA((zn + 1,)),
            DMA((zn + 1,)),
        ],
        compiler_params=params(collective_id),
        name="fold",
    )(blocks, rows)


def finish_kernel(n, *refs):
    widen, narrow, qkv, qkv_far, out, out_far, vec, streams = refs[:8]
    widen_to, narrow_to, qkv_to, out_to, vec_to, streams_to = refs[8:14]
    qkv_in, qkv_sum, out_in, out_sum, vec_in, vec_sum, vec_sib = refs[14:21]
    a_ss, a_rs, x_ss, x_rs, v_ss, v_rs, r_ss, r_rs, ls = refs[21:]
    p = Place(n)
    s, c, h, z, zn = p.s, p.c, p.h, p.z, p.zn
    greet_all(p)

    def vec_copy(a, b):
        l, i = lax.rem(s + a, 2), lax.rem(h + b, n)
        return remote(vec.at[l, i], vec_in.at[s, h], v_ss.at[a, b], v_rs.at[a, b], (l, c, i))

    def x_block(dz):
        far = lax.rem(z + dz, zn)
        return remote(qkv_far.at[far], qkv_in.at[far], x_ss.at[dz], x_rs.at[dz], p.over)

    out_cross = remote(out_far, out_in, x_ss.at[zn], x_rs.at[zn], p.over)
    stream_cross = remote(streams, streams_to, x_ss.at[zn + 1], x_rs.at[zn + 1], p.over)
    spreads = ((widen, widen_to), (qkv_sum, qkv_to))

    def send(w, dz):
        far = lax.rem(z + dz, zn)
        src, dst = spreads[w]
        target = (s, c, far * 2 + p.far_y)
        return remote(src.at[far], dst.at[h], a_ss.at[0, w, dz], a_rs.at[0, w, dz], target)

    def keep(w):
        src, dst = spreads[w]
        return pltpu.make_async_copy(src.at[z], dst.at[h], ls.at[w])

    def aside(w, dz):
        block = spreads[w][1].at[lax.rem(z + zn - dz, zn) * 2 + p.far_y]
        return remote(block, block, a_ss.at[1, w, dz], a_rs.at[1, w, dz], p.sibling)

    def start_zero(w):
        @pl.when(c == 1)
        def _():
            send(w, 0).start()

        @pl.when(c == 0)
        def _():
            keep(w).start()

    def row_copies(w, src, dst):
        half = src.shape[0]
        piece = dst.at[pl.ds(pl.multiple_of(c * half, 8), half)]
        return (
            pltpu.make_async_copy(src, piece, ls.at[2 + w]),
            remote(src, piece, r_ss.at[w], r_rs.at[w], p.sibling),
        )

    order = list(range(1, zn)) + [0]
    for dz in order:
        x_block(dz).start()
    out_cross.start()
    stream_cross.start()
    for a, b in others(n):
        vec_copy(a, b).start()
    for dz in range(1, zn):
        send(0, dz).start()
    start_zero(0)
    narrow_copies = row_copies(0, narrow, narrow_to)
    for copy in narrow_copies:
        copy.start()
    for dz in order:
        x_block(dz).wait_recv()
        far = lax.rem(z + dz, zn)
        qkv_sum[far] = (qkv[far].astype(F32) + qkv_in[far].astype(F32)).astype(BF16)
        if dz:
            send(1, dz).start()
        else:
            start_zero(1)
    out_cross.wait_recv()
    out_sum[...] = (out[...].astype(F32) + out_in[...].astype(F32)).astype(BF16)
    out_copies = row_copies(1, out_sum, out_to)
    for copy in out_copies:
        copy.start()
    total = vec[s, h]
    for a, b in others(n):
        vec_copy(a, b).wait_recv()
        total = total + vec_in[lax.rem(s + a, 2), lax.rem(h + n - b, n)]
    vec_sum[...] = total
    vec_share = remote(vec_sum, vec_sib, r_ss.at[2], r_rs.at[2], p.sibling)
    vec_share.start()
    for w in range(2):

        @pl.when(c == 1)
        def _():
            send(w, 0).wait_recv()

        @pl.when(c == 0)
        def _():
            keep(w).wait()

        for dz in range(zn):
            if dz:
                send(w, dz).wait_recv()
            aside(w, dz).start()
    vec_share.wait_recv()
    vec_to[...] = total + vec_sib[...]
    vec_share.wait_send()
    for w in range(2):

        @pl.when(c == 1)
        def _():
            send(w, 0).wait_send()

        for dz in range(zn):
            if dz:
                send(w, dz).wait_send()
            aside(w, dz).wait_recv()
            aside(w, dz).wait_send()
    for copies in (narrow_copies, out_copies):
        copies[0].wait()
        copies[1].wait_recv()
        copies[1].wait_send()
    for a, b in others(n):
        vec_copy(a, b).wait_send()
    for dz in range(zn):
        x_block(dz).wait_send()
    out_cross.wait_send()
    stream_cross.wait_recv()
    stream_cross.wait_send()


def finish_call(n, collective_id, widen, narrow, qkv, qkv_far, out, out_far, vec, streams):
    zn = n // 2
    piece = vec.shape[2:]
    return pl.pallas_call(
        functools.partial(finish_kernel, n),
        out_shape=[
            jax.ShapeDtypeStruct((n,) + widen.shape[1:], BF16),
            jax.ShapeDtypeStruct((2 * narrow.shape[0], narrow.shape[1]), BF16),
            jax.ShapeDtypeStruct((n,) + qkv.shape[1:], BF16),
            jax.ShapeDtypeStruct((2 * out.shape[0], out.shape[1]), BF16),
            jax.ShapeDtypeStruct(piece, F32),
            jax.ShapeDtypeStruct(streams.shape, BF16),
        ],
        in_specs=[VMEM_SPEC] * 8,
        out_specs=[ANY_SPEC] * 4 + [VMEM_SPEC] * 2,
        scratch_shapes=[
            pltpu.VMEM(qkv.shape, BF16),
            pltpu.VMEM(qkv.shape, BF16),
            pltpu.VMEM(out.shape, BF16),
            pltpu.VMEM(out.shape, BF16),
            pltpu.VMEM((2, n) + piece, F32),
            pltpu.VMEM(piece, F32),
            pltpu.VMEM(piece, F32),
            DMA((2, 2, zn)),
            DMA((2, 2, zn)),
            DMA((zn + 2,)),
            DMA((zn + 2,)),
            DMA((2, n)),
            DMA((2, n)),
            DMA((3,)),
            DMA((3,)),
            DMA((4,)),
        ],
        compiler_params=params(collective_id),
        name="finish",
    )(widen, narrow, qkv, qkv_far, out, out_far, vec, streams)


def windows(width, n):
    share = width // n
    low = [j * share // HD for j in range(n)]
    slots = max(((j + 1) * share - 1) // HD - low[j] + 1 for j in range(n))
    return [min(first, HEADS - slots) for first in low], slots


def pick(table, index):
    return lax.dynamic_index_in_dim(table, index, 0, keepdims=False)


def on_device(n, tokens, block_order, cotangent, *vectors_and_weights):
    (
        first_gain,
        first_shift,
        qkv_weight,
        input_bias,
        out_weight,
        out_bias,
        second_gain,
        second_shift,
        widen_weight,
        widen_bias,
        narrow_weight,
        narrow_bias,
    ) = (member[0] for member in vectors_and_weights)
    s = lax.axis_index("section")
    c = lax.axis_index("ctx")
    h = lax.axis_index("shard")
    _, rows, width = tokens.shape
    hidden = widen_weight.shape[1]
    share = width // n
    hide = hidden // n
    padded = -(-share // 16) * 16
    full = n * padded
    low, slots = windows(width, n)
    sh = slots * HD
    total_rows = n * rows
    half_rows = rows // HALVES

    def pad_features(values):
        lead = values.shape[:-1]
        parts = values.reshape(lead + (n, share))
        parts = jnp.pad(parts, [(0, 0)] * len(lead) + [(0, 0), (0, padded - share)])
        return parts.reshape(lead + (full,))

    def cut_features(values):
        lead = values.shape[:-1]
        return values.reshape(lead + (n, padded))[..., :share].reshape(lead + (width,))

    mask = pad_features(jnp.ones((1, width), F32))
    offsets = jnp.array([j * share - HD * low[j] for j in range(n)], jnp.int32)
    offset = pick(offsets, h)

    qkv_send, widen_send, out_rows, narrow_send = lay_out_call(
        low, slots, padded, qkv_weight, widen_weight, out_weight, narrow_weight
    )
    out_send = lax.dynamic_update_slice(
        jnp.zeros((sh, full), BF16), out_rows, (offset, jnp.int32(0))
    )
    lanes = max(-(-hide // 128) * 128, -(-2 * share // 128) * 128)

    def lane(vector):
        return jnp.pad(vector, (0, lanes - vector.shape[0]))

    pack = jnp.stack(
        [
            lane(member)
            for member in (
                first_gain,
                first_shift,
                out_bias,
                second_gain,
                second_shift,
                narrow_bias,
                input_bias,
                widen_bias,
            )
        ]
    )
    pack = jnp.pad(pack, [(0, 8), (0, 0)])
    own_tokens = pad_features(jnp.where(s == 0, tokens[0], tokens[1]))
    own_cot = pad_features(jnp.where(s == 0, cotangent[0], cotangent[1]))
    tok_all, packs, qkv_all, out_all = start_call(n, own_tokens, pack, qkv_send, out_send)

    order = block_order.reshape(2, n, HALVES).transpose(0, 2, 1)
    places = order[..., None] * half_rows + jnp.arange(half_rows, dtype=jnp.int32)
    places = places.reshape(2, total_rows)
    own_places = jnp.where(c == 0, places[0], places[1])
    oth_places = jnp.where(c == 0, places[1], places[0])
    kpos = jnp.concatenate([own_places, oth_places])[:, None]
    qpos = own_places[None, :]

    layers = []
    for layer in range(2):
        vec = packs[layer].astype(F32)

        def feature(row):
            return jnp.pad(vec[:, row, :share], [(0, 0), (0, padded - share)]).reshape(1, full)

        bias = vec[:, 6, : 2 * share].reshape(2, width)
        bias_windows = jnp.stack([bias[:, HD * f : HD * f + sh] for f in low])
        bias_own = pick(bias_windows, h)
        qkv_bias = jnp.concatenate([bias_own[0], jnp.zeros((sh,), F32), bias_own[1]])
        layers.append(
            dict(
                gain1=feature(0),
                shift1=feature(1),
                out_bias=feature(2),
                gain2=feature(3),
                shift2=feature(4),
                narrow_bias=feature(5),
                qkv_bias=qkv_bias,
                widen_bias=pick(vec[:, 7, :hide], h),
                qkv=qkv_all[layer].reshape(full, 3 * sh),
                out=out_all[layer],
            )
        )

    x = own_tokens.astype(F32)
    unit = unit_rows(tok_all.astype(F32), mask, width)[0]
    normed = (unit * layers[0]["gain1"] + layers[0]["shift1"]).astype(BF16)
    stored = []
    layer_outs = []
    for layer in range(2):
        w = layers[layer]
        qkv = (dot_n(normed, w["qkv"]) + w["qkv_bias"]).astype(BF16)
        side, carried = ("gather", own_cot) if layer else ("spread", widen_send)
        att, att_low, lse, other, moved = attend_call(
            n, 1 + layer, slots, qkv, kpos, qpos, side, carried
        )
        if layer:
            out_low_all = moved
        else:
            for member in range(2):
                layers[member]["widen"] = moved[member].reshape(full, hide)
        part = dot_n(att_low, w["out"]).astype(BF16)
        found = phase_call(
            n,
            "mid",
            3 + layer,
            width,
            part,
            x,
            w["out_bias"],
            w["gain2"],
            w["shift2"],
            mask,
            side=None if layer else "swap",
            carried=narrow_send,
        )
        residual, normed_two = found[:2]
        if not layer:
            for member in range(2):
                layers[member]["narrow"] = found[2][member]
        hidden_pre = dot_n(normed_two, w["widen"]) + w["widen_bias"]
        act = jnp.tanh(GELU_A * (hidden_pre + GELU_B * hidden_pre**3))
        hidden_low = (0.5 * hidden_pre * (1.0 + act)).astype(BF16)
        part = dot_n(hidden_low, w["narrow"]).astype(BF16)
        stored.append((x, normed, qkv, other, att, att_low, lse, residual, normed_two))
        stored[-1] += (hidden_pre, hidden_low)
        if layer == 0:
            nxt = layers[1]
            x, normed = phase_call(
                n,
                "end",
                5,
                width,
                part,
                residual,
                w["narrow_bias"],
                nxt["gain1"],
                nxt["shift1"],
                mask,
            )
            layer_outs.append(x)
        else:
            last = (part, residual, w["narrow_bias"])

    def over_rows(a, b):
        found = lax.dot_general(a, b, (((0,), (0,)), ((), ())), preferred_element_type=F32)
        return found.astype(BF16)

    def column_sums(values):
        return jnp.sum(values.astype(F32), axis=0)

    out_grad = own_cot.astype(F32)
    out_sums = column_sums(own_cot)[None]
    vec_grads, d_ins, early, late, came = {}, {}, {}, {}, {}
    for layer in (1, 0):
        w = layers[layer]
        x, normed, qkv, other, att, att_low, lse, residual, normed_two = stored[layer][:9]
        hidden_pre, hidden_low = stored[layer][9:]
        hidden_grad = dot_t(out_low_all, w["narrow"])
        square = hidden_pre * hidden_pre
        act = jnp.tanh(GELU_A * (hidden_pre + GELU_B * hidden_pre * square))
        slope = 0.5 * (1.0 + act) + 0.5 * hidden_pre * (1.0 - act * act) * GELU_A * (
            1.0 + 3.0 * GELU_B * square
        )
        pre_grad = (hidden_grad * slope).astype(BF16)
        part = dot_t(pre_grad, w["widen"]).astype(BF16)
        early[layer] = fold_call(
            n,
            7 + layer,
            over_rows(normed_two, pre_grad).reshape(n, padded, hide),
            jnp.pad(over_rows(hidden_low, out_low_all), [(0, -hide % 32), (0, 0)]),
        )
        source = f"cross{1 - layer}"
        resid_grad, sums_two, resid_low_all, narrow_came = phase_call(
            n,
            "resid",
            9 + layer,
            width,
            part,
            residual,
            out_grad,
            w["gain2"],
            mask,
            side=source,
            carried=early[layer][1],
        )
        att_grad = dot_t(resid_low_all, w["out"]).astype(BF16)
        found = attend_back_call(
            n,
            11 + layer,
            slots,
            qkv,
            other,
            att_grad,
            att,
            lse,
            kpos,
            qpos,
            last=last if layer else (),
        )
        triple = found[0]
        if layer:
            layer_outs.append(found[1])
        part = dot_t(triple, w["qkv"]).astype(BF16)
        found = phase_call(
            n,
            "input" if layer else "first",
            13 + layer,
            width,
            part,
            x,
            resid_grad,
            w["gain1"],
            mask,
            side=source,
            carried=early[layer][0],
        )
        d_in, sums_one = found[:2]
        d_ins[layer] = d_in
        came[layer] = (found[-1], narrow_came)
        out_full = over_rows(att_low, resid_low_all)
        late[layer] = fold_call(
            n,
            15 + layer,
            over_rows(normed, triple).reshape(n, padded, 3 * sh),
            lax.dynamic_slice_in_dim(jnp.pad(out_full, [(0, sh), (0, 0)]), offset, sh, 0),
        )
        triple_sums = column_sums(triple)
        spots = [
            jnp.pad(
                jnp.stack([triple_sums[:sh], triple_sums[2 * sh :]]),
                [(0, 0), (HD * f, width - sh - HD * f)],
            )
            for f in low
        ]
        slot_sums = pick(jnp.stack(spots), h)
        hide_sums = jnp.where(
            jnp.arange(n, dtype=jnp.int32)[:, None] == h, column_sums(pre_grad)[None], 0.0
        )
        features = jnp.concatenate([sums_one[:2], sums_two[2:], sums_two[:2], out_sums])
        features = features.reshape(6, n, padded).transpose(1, 0, 2)
        vec_grads[layer] = jnp.concatenate(
            [
                jnp.pad(features, [(0, 0), (0, 0), (0, lanes - padded)]),
                jnp.pad(slot_sums.reshape(n, 1, 2 * share), [(0, 0), (0, 0), (0, lanes - 2 * share)]),
                jnp.pad(hide_sums[:, None], [(0, 0), (0, 0), (0, lanes - hide)]),
            ],
            axis=1,
        )
        out_grad = d_in
        out_sums = sums_one[2:]
        if layer:
            out_low_all = found[2]

    def own(first, second):
        return jnp.where(s == 0, first, second)

    def added(item):
        return own(
            early[0][item].astype(F32) + came[0][item].astype(F32),
            early[1][item].astype(F32) + came[1][item].astype(F32),
        ).astype(BF16)

    streams = jnp.stack(
        [own(layer_outs[1], layer_outs[0]), own(d_ins[1], d_ins[0])]
    ).astype(BF16)
    widen_back, narrow_back, qkv_back, out_back, vec, streams_came = finish_call(
        n,
        17,
        added(0),
        added(1),
        own(late[0][0], late[1][0]),
        own(late[1][0], late[0][0]),
        own(late[0][1], late[1][1]),
        own(late[1][1], late[0][1]),
        jnp.stack([vec_grads[0], vec_grads[1]]),
        streams,
    )
    grads = settle_call(low, share, qkv_back, widen_back, out_back, narrow_back)
    qkv_grad, widen_grad, out_grad_w, narrow_grad = grads

    def joined(mine, theirs):
        theirs = theirs.astype(F32)
        return cut_features(jnp.stack([own(mine, theirs), own(theirs, mine)]))[None]

    layer_out = joined(own(layer_outs[0], layer_outs[1]), streams_came[0])
    d_in = joined(own(d_ins[0], d_ins[1]), streams_came[1])

    def vector(row, size):
        return vec[row, :size][None]

    return (
        layer_out,
        d_in,
        vector(0, share),
        vector(1, share),
        qkv_grad[None],
        vector(6, 2 * share),
        out_grad_w[None],
        vector(2, share),
        vector(3, share),
        vector(4, share),
        widen_grad[None],
        vector(7, hide),
        narrow_grad[None],
        vector(5, share),
    )


def solution(mesh):
    rows = P(None, ("ctx", "shard"), None)
    vector = P("section", "shard")
    matrix = P("section", "shard", None)
    order = (
        vector,
        vector,
        matrix,
        vector,
        matrix,
        vector,
        vector,
        vector,
        matrix,
        vector,
        matrix,
        vector,
    )
    streams = P("section", None, ("ctx", "shard"), None)
    return jax.shard_map(
        functools.partial(on_device, mesh.shape["shard"]),
        mesh=mesh,
        in_specs=(rows, P(), rows) + order,
        out_specs=(streams, streams) + order,
        check_vma=False,
    )
```

```python
import functools

import jax
import jax.numpy as jnp
import numpy as np
from jax import lax
from jax.experimental import pallas as pl
from jax.experimental.pallas import tpu as pltpu
from jax.sharding import PartitionSpec as P

HEADS = 25
HD = 64
EPSILON = 1e-05
MASKED = -1e30
LOG2E = 1.4426950408889634
GELU_A = 0.7978845608028654
GELU_B = 0.044715
MESH = pl.DeviceIdType.MESH
F32 = jnp.float32
BF16 = jnp.bfloat16
VMEM_SPEC = pl.BlockSpec(memory_space=pltpu.VMEM)
ANY_SPEC = pl.BlockSpec(memory_space=pl.ANY)
DMA = pltpu.SemaphoreType.DMA
VMEM_LIMIT = 60 * 2**20
HALVES = 2


def params(collective_id=None):
    if collective_id is None:
        return pltpu.CompilerParams(vmem_limit_bytes=VMEM_LIMIT)
    return pltpu.CompilerParams(
        collective_id=collective_id, has_side_effects=True, vmem_limit_bytes=VMEM_LIMIT
    )


def remote(src, dst, send_sem, recv_sem, device):
    return pltpu.make_async_remote_copy(
        src_ref=src,
        dst_ref=dst,
        send_sem=send_sem,
        recv_sem=recv_sem,
        device_id=device,
        device_id_type=MESH,
    )


class Place:
    def __init__(self, n):
        self.s = lax.axis_index("section")
        self.c = lax.axis_index("ctx")
        self.h = lax.axis_index("shard")
        self.n = n
        self.zn = n // 2
        self.y = lax.rem(self.h, 2)
        self.z = lax.div(self.h, 2)
        self.far_y = self.y + self.c - 2 * self.y * self.c

    def flip(self, k):
        found = self.z
        for bit in range(self.zn.bit_length()):
            if k >> bit & 1:
                found = found + (1 - 2 * lax.rem(self.z // 2**bit, 2)) * 2**bit
        return found

    def dev(self, z, y):
        return (self.s, self.c, z * 2 + y)

    @property
    def pair(self):
        return self.dev(self.z, 1 - self.y)

    @property
    def above(self):
        return self.dev(self.z + 1, self.y)

    @property
    def below(self):
        return self.dev(self.z - 1, self.y)

    @property
    def over(self):
        return (1 - self.s, self.c, self.h)

    @property
    def sibling(self):
        return (self.s, 1 - self.c, self.h)


def greet(p, line=False, spread=False, over=False, sibling=False):
    bar = pltpu.get_barrier_semaphore()
    peers = 0

    def signal(device):
        pl.semaphore_signal(bar, inc=1, device_id=device, device_id_type=MESH)

    if line:
        signal(p.pair)

        @pl.when(p.z < p.zn - 1)
        def _():
            signal(p.above)

        @pl.when(p.z > 0)
        def _():
            signal(p.below)

        peers = 1 + (p.z + p.zn - 1) // p.zn + (2 * p.zn - 2 - p.z) // p.zn
    if spread:
        for dz in range(1, p.zn):
            signal(p.dev(lax.rem(p.z + dz, p.zn), p.far_y))

        @pl.when(p.c == 1)
        def _():
            signal(p.dev(p.z, p.far_y))

        peers = peers + p.zn - 1 + p.c
    if over:
        signal(p.over)
        peers = peers + 1
    if sibling:
        signal(p.sibling)
        peers = peers + 1
    pl.semaphore_wait(bar, peers)


class Gather:
    def __init__(self, p, own_ref, out_ref, ss, rs, ls):
        self.p, self.own_ref, self.out_ref = p, own_ref, out_ref
        self.ss, self.rs, self.ls = ss, rs, ls
        self.hr = own_ref.shape[0] // HALVES

    def blk(self, half, zz, yy):
        row = (half * self.p.n + zz * 2 + yy) * self.hr
        return self.out_ref.at[pl.ds(pl.multiple_of(row, 16), self.hr)]

    def own(self, half):
        return self.own_ref.at[pl.ds(half * self.hr, self.hr)]

    def up(self, t, half, src):
        p = self.p
        sems = (self.ss.at[0, t, half], self.rs.at[0, t, half])
        return remote(src, self.blk(half, p.z - (t - 1), p.y), *sems, p.above)

    def down(self, t, half, src):
        p = self.p
        sems = (self.ss.at[1, t, half], self.rs.at[1, t, half])
        return remote(src, self.blk(half, p.z + (t - 1), p.y), *sems, p.below)

    def across(self, kind, t, half, zz, src):
        p = self.p
        sems = (self.ss.at[2 + kind, t, half], self.rs.at[2 + kind, t, half])
        return remote(src, self.blk(half, zz, p.y), *sems, p.pair)

    def local(self, half):
        p = self.p
        return pltpu.make_async_copy(
            self.own(half), self.blk(half, p.z, p.y), self.ls.at[half]
        )

    def start(self, halves=range(HALVES)):
        p = self.p
        for half in halves:
            src = self.own(half)

            @pl.when(p.z < p.zn - 1)
            def _():
                self.up(1, half, src).start()

            @pl.when(p.z > 0)
            def _():
                self.down(1, half, src).start()

            self.across(0, 0, half, p.z, src).start()
            self.local(half).start()

    def step(self, t, half):
        p = self.p
        z, zn = p.z, p.zn

        @pl.when(z >= t)
        def _():
            block = self.blk(half, z - t, p.y)
            self.up(t, half, block).wait_recv()
            if t < zn - 1:

                @pl.when(z < zn - 1)
                def _():
                    self.up(t + 1, half, block).start()

            self.across(0, t, half, z - t, block).start()

        @pl.when(z <= zn - 1 - t)
        def _():
            block = self.blk(half, z + t, p.y)
            self.down(t, half, block).wait_recv()
            if t < zn - 1:

                @pl.when(z > 0)
                def _():
                    self.down(t + 1, half, block).start()

            self.across(1, t, half, z + t, block).start()

    def steps(self):
        return [
            functools.partial(self.step, t, half)
            for t in range(1, self.p.zn)
            for half in range(HALVES)
        ]

    def finish(self):
        p = self.p
        z, zn = p.z, p.zn
        for half in range(HALVES):
            self.across(0, 0, half, z, self.own(half)).wait_recv()
            for t in range(1, zn):

                @pl.when(z >= t)
                def _():
                    self.across(0, t, half, z - t, self.own(half)).wait_recv()

                @pl.when(z <= zn - 1 - t)
                def _():
                    self.across(1, t, half, z + t, self.own(half)).wait_recv()

        for half in range(HALVES):
            self.local(half).wait()
            self.across(0, 0, half, z, self.own(half)).wait_send()
            for t in range(1, zn):

                @pl.when((z < zn - 1) & (z >= t - 1))
                def _():
                    self.up(t, half, self.own(half)).wait_send()

                @pl.when((z > 0) & (z <= zn - t))
                def _():
                    self.down(t, half, self.own(half)).wait_send()

                @pl.when(z >= t)
                def _():
                    self.across(0, t, half, z - t, self.own(half)).wait_send()

                @pl.when(z <= zn - 1 - t)
                def _():
                    self.across(1, t, half, z + t, self.own(half)).wait_send()


class Scatter:
    def __init__(self, p, part_ref, ybuf, rbuf, sbuf, ss, rs):
        self.p, self.part_ref = p, part_ref
        self.ybuf, self.rbuf, self.sbuf, self.ss, self.rs = ybuf, rbuf, sbuf, ss, rs
        self.hr = ybuf.shape[2]

    def blk(self, half, zz, yy):
        row = (half * self.p.n + zz * 2 + yy) * self.hr
        return self.part_ref.at[pl.ds(pl.multiple_of(row, 16), self.hr)]

    def goal(self, k, t):
        return self.p.z + t if k == 0 else self.p.z - t

    def across(self, k, t, half):
        p = self.p
        zz = self.goal(k, t)
        sems = (self.ss.at[k, t, half], self.rs.at[k, t, half])
        return remote(self.blk(half, zz, 1 - p.y), self.ybuf.at[zz, half], *sems, p.pair)

    def along(self, k, t, half, slot):
        p = self.p
        zz = self.goal(k, t)
        sems = (self.ss.at[2 + k, t, half], self.rs.at[2 + k, slot, half])
        target = p.above if k == 0 else p.below
        return remote(self.sbuf.at[zz, half], self.rbuf.at[zz + 1 - k, half], *sems, target)

    def ok(self, k, t):
        return self.p.z <= self.p.zn - 1 - t if k == 0 else self.p.z >= t

    def has(self, k):
        return self.p.z > 0 if k == 0 else self.p.z < self.p.zn - 1

    def start(self):
        for t in range(self.p.zn - 1, 0, -1):
            for half in range(HALVES):
                for k in range(2):

                    @pl.when(self.ok(k, t))
                    def _():
                        self.across(k, t, half).start()

        for half in range(HALVES):
            self.across(0, 0, half).start()

    def step(self, t, half, k):
        p = self.p
        zz = self.goal(k, t)

        @pl.when(self.ok(k, t))
        def _():
            self.across(k, t, half).wait_recv()
            total = self.blk(half, zz, p.y)[...].astype(F32)
            total = total + self.ybuf[zz, half].astype(F32)
            if t < p.zn - 1:

                @pl.when(self.has(k))
                def _():
                    self.along(k, t, half, t).wait_recv()
                    more = total + self.rbuf[zz + 1 - k, half].astype(F32)
                    self.sbuf[zz, half] = more.astype(BF16)

                @pl.when(jnp.logical_not(self.has(k)))
                def _():
                    self.sbuf[zz, half] = total.astype(BF16)

            else:
                self.sbuf[zz, half] = total.astype(BF16)
            self.along(k, t, half, t - 1).start()

    def steps(self):
        return [
            functools.partial(self.step, t, half, k)
            for t in range(self.p.zn - 1, 0, -1)
            for half in range(HALVES)
            for k in range(2)
        ]

    def result(self, half):
        p = self.p
        z = p.z
        self.across(0, 0, half).wait_recv()
        for k in range(2):

            @pl.when(self.has(k))
            def _():
                self.along(k, 0, half, 0).wait_recv()

            @pl.when(jnp.logical_not(self.has(k)))
            def _():
                self.rbuf[z + 1 - k, half] = jnp.zeros(self.rbuf.shape[2:], BF16)

        total = self.blk(half, z, p.y)[...].astype(F32) + self.ybuf[z, half].astype(F32)
        return total + self.rbuf[z + 1, half].astype(F32) + self.rbuf[z, half].astype(F32)

    def finish(self):
        for half in range(HALVES):
            self.across(0, 0, half).wait_send()
            for t in range(1, self.p.zn):
                for k in range(2):

                    @pl.when(self.ok(k, t))
                    def _():
                        self.across(k, t, half).wait_send()
                        self.along(k, t, half, t - 1).wait_send()


class Spread:
    def __init__(self, p, src, dst, ss, rs, ls):
        self.p, self.src, self.dst, self.ss, self.rs, self.ls = p, src, dst, ss, rs, ls

    def source(self, dz):
        return self.p.flip(dz) * 2 + self.p.far_y

    def out(self, dz):
        p = self.p
        target = self.source(dz)
        sems = (self.ss.at[0, dz], self.rs.at[0, dz])
        return remote(self.src.at[target], self.dst.at[p.s, p.h], *sems, (p.s, p.c, target))

    def aside(self, dz):
        block = self.dst.at[self.p.s, self.source(dz)]
        return remote(block, block, self.ss.at[1, dz], self.rs.at[1, dz], self.p.sibling)

    def cross(self, dz):
        block = self.dst.at[self.p.s, self.source(dz)]
        return remote(block, block, self.ss.at[2, dz], self.rs.at[2, dz], self.p.over)

    def cross_own(self):
        p = self.p
        sems = (self.ss.at[2, 0], self.rs.at[2, 0])
        return remote(self.src.at[p.h], self.dst.at[p.s, p.h], *sems, p.over)

    def cross_aside(self, dz):
        block = self.dst.at[1 - self.p.s, self.source(dz)]
        return remote(block, block, self.ss.at[3, dz], self.rs.at[3, dz], self.p.sibling)

    def local(self):
        p = self.p
        return pltpu.make_async_copy(self.src.at[p.h], self.dst.at[p.s, p.h], self.ls)

    def start(self):
        @pl.when(self.p.c == 1)
        def _():
            self.out(0).start()

        @pl.when(self.p.c == 0)
        def _():
            self.cross_own().start()

        for dz in range(1, min(3, self.p.zn)):
            self.out(dz).start()
        self.local().start()

    def arrived(self, dz):
        if 3 <= dz + 2 < self.p.zn:
            self.out(dz + 1).wait_send()
            self.out(dz + 2).start()
        self.out(dz).wait_recv()
        self.cross(dz).start()
        self.aside(dz).start()

    def crossed(self, dz):
        self.cross(dz).wait_recv()
        self.cross_aside(dz).start()

    def first(self):
        @pl.when(self.p.c == 1)
        def _():
            self.arrived(0)

    def steps(self):
        found = [self.first]
        found += [functools.partial(self.arrived, dz) for dz in range(1, self.p.zn)]
        return found + [functools.partial(self.crossed, dz) for dz in range(self.p.zn)]

    def finish(self):
        self.local().wait()

        @pl.when(self.p.c == 0)
        def _():
            self.aside(0).wait_recv()
            self.cross_own().wait_send()

        @pl.when(self.p.c == 1)
        def _():
            self.out(0).wait_send()
            self.aside(0).wait_send()
            self.cross(0).wait_send()

        for dz in range(self.p.zn):
            if dz:
                self.aside(dz).wait_recv()
                self.aside(dz).wait_send()
                if dz == 1 or dz == self.p.zn - 1:
                    self.out(dz).wait_send()
                self.cross(dz).wait_send()
            self.cross_aside(dz).wait_recv()
            self.cross_aside(dz).wait_send()


class RowSwap:
    def __init__(self, p, src, dst, ss, rs, ls):
        self.p, self.src, self.dst, self.ss, self.rs, self.ls = p, src, dst, ss, rs, ls
        self.split = src.shape[0] % 32 == 0

    def piece(self, which):
        count = self.src.shape[0]
        if not self.split:
            return self.src, self.dst.at[which, pl.ds(0, count)]
        half = count // 2
        rows = pl.ds(pl.multiple_of(self.p.c * half, 16), half)
        return self.src.at[rows], self.dst.at[which, rows]

    def cross(self):
        src, dst = self.piece(self.p.s)
        return remote(src, dst, self.ss.at[0], self.rs.at[0], self.p.over)

    def aside(self):
        block = self.piece(1 - self.p.s)[1]
        return remote(block, block, self.ss.at[1], self.rs.at[1], self.p.sibling)

    def local(self):
        rows = pl.ds(0, self.src.shape[0])
        return pltpu.make_async_copy(self.src, self.dst.at[self.p.s, rows], self.ls)

    def start(self):
        self.cross().start()
        self.local().start()

    def step(self):
        self.cross().wait_recv()
        if self.split:
            self.aside().start()

    def finish(self):
        self.local().wait()
        self.cross().wait_send()
        if self.split:
            self.aside().wait_recv()
            self.aside().wait_send()


class Cross:
    def __init__(self, p, src, dst, ss, rs, source):
        self.p, self.source = p, source
        self.copy = remote(src, dst, ss, rs, p.over)

    def start(self):
        @pl.when(self.p.s == self.source)
        def _():
            self.copy.start()

    def finish(self):
        @pl.when(self.p.s == self.source)
        def _():
            self.copy.wait_send()

        @pl.when(self.p.s != self.source)
        def _():
            self.copy.wait_recv()


class Fold:
    def __init__(self, p, src, came, out, ss, rs):
        self.p, self.src, self.came, self.out, self.ss, self.rs = p, src, came, out, ss, rs
        self.count = out.shape[0]
        self.size = out.shape[1]

    def rows(self, item, near):
        p = self.p
        if self.count == 1:
            index = 1 - p.c if near else p.c
        else:
            index = item * 2 + (1 - p.far_y if near else p.far_y)
        return pl.ds(pl.multiple_of(index * self.size, 16), self.size)

    def copy(self, item):
        src = self.src.at[self.rows(item, True)]
        sems = (self.ss.at[item], self.rs.at[item])
        return remote(src, self.came.at[item], *sems, self.p.sibling)

    def start(self):
        for item in range(self.count):
            self.copy(item).start()

    def step(self, item):
        self.copy(item).wait_recv()
        own = self.src[self.rows(item, False)].astype(F32)
        self.out[item] = (own + self.came[item].astype(F32)).astype(BF16)

    def steps(self):
        return [functools.partial(self.step, item) for item in range(self.count)]

    def finish(self):
        for item in range(self.count):
            self.copy(item).wait_send()


def fold_scratch(source, out):
    return [pltpu.VMEM(source, BF16), pltpu.VMEM(out, BF16), DMA((out[0],)), DMA((out[0],))]


def product(a_ref, b_ref, to_ref):
    rows = to_ref.shape[0]

    def step(first, size):
        found = lax.dot_general(
            a_ref[:, first : first + size],
            b_ref[...],
            (((0,), (0,)), ((), ())),
            preferred_element_type=F32,
        )
        to_ref[first : first + size] = found.astype(BF16)

    return [
        functools.partial(step, first, min(256, rows - first)) for first in range(0, rows, 256)
    ]


def home_rows(a_ref, b_ref, to_ref, low, share):
    found = lax.dot_general(
        a_ref[...], b_ref[...], (((0,), (0,)), ((), ())), preferred_element_type=F32
    )
    h = lax.axis_index("shard")
    shift = 0
    for j, first in enumerate(low):
        shift = shift + jnp.where(h == j, (HD * first - j * share) % found.shape[0], 0)
    to_ref[...] = pltpu.roll(found, shift, 0).astype(BF16)


def in_turn(steps, work, each=1):
    for step in steps:
        for _ in range(each):
            run_next(work)
        step()


def by_halves(scatter, gather, rows_step, work, each=1):
    in_turn(scatter.steps(), work, each)
    for half in range(HALVES):
        rows_step(half)
        if gather is not None:
            gather.start([half])
    if gather is not None:
        in_turn(gather.steps(), work, each)


def fetch(src, dst, sem):
    copy = pltpu.make_async_copy(src, dst, sem)
    copy.start()
    return copy


def row_blocks(rows, step):
    size = min(rows, 256)
    count = rows // size
    if count <= 2:
        for b in range(count):
            step(b * size, size)
    else:

        def body(b, carry):
            step(pl.multiple_of(b * size, size), size)
            return carry

        lax.fori_loop(0, count, body, 0)


def gelu_parts(values):
    square = values * values
    return jnp.tanh(GELU_A * (values + GELU_B * values * square)), square


def greet_all(p):
    bar = pltpu.get_barrier_semaphore()
    for a in range(2):
        for b in range(p.n):
            if (a, b) != (0, 0):
                other = (lax.rem(p.s + a, 2), p.c, lax.rem(p.h + b, p.n))
                pl.semaphore_signal(bar, inc=1, device_id=other, device_id_type=MESH)
    pl.semaphore_signal(bar, inc=1, device_id=p.sibling, device_id_type=MESH)
    pl.semaphore_wait(bar, 2 * p.n)


def others(n):
    return [(a, b) for a in range(2) for b in range(n) if (a, b) != (0, 0)]


def start_kernel(n, low, width, tok_ref, pack_ref, qkv_ref, out_ref, mask_ref, *refs):
    normed_to, found_to, qkv_all, out_all, feats_to, qkv_bias, widen_bias = refs[:7]
    tok_all, pack_all, g_ss, g_rs, g_ls, p_ss, p_rs, a_ss, a_rs, o_ss, o_rs, l_sem = refs[7:]
    p = Place(n)
    s, c, h = p.s, p.c, p.h
    greet_all(p)

    def pack_copy(a, b):
        target = (lax.rem(s + a, 2), c, lax.rem(h + b, n))
        return remote(pack_ref, pack_all.at[s, h], p_ss.at[a, b], p_rs.at[a, b], target)

    tokens = Gather(p, tok_ref, tok_all, g_ss, g_rs, g_ls)
    qkv = Spread(p, qkv_ref, qkv_all, a_ss, a_rs, l_sem.at[1])
    out = RowSwap(p, out_ref, out_all, o_ss, o_rs, l_sem.at[2])
    pack_own = pltpu.make_async_copy(pack_ref, pack_all.at[s, h], l_sem.at[0])
    tokens.start()
    qkv.start()
    for a, b in others(n):
        pack_copy(a, b).start()
    pack_own.start()
    out.start()
    qkv_steps = qkv.steps()
    for step in tokens.steps():
        step()
        if qkv_steps:
            qkv_steps.pop(0)()
    tokens.finish()
    pack_own.wait()
    for a, b in others(n):
        pack_copy(a, b).wait_recv()
    sh = qkv_ref.shape[2] // 3
    share = width // n
    padded = qkv_ref.shape[1]
    for layer in range(2):
        pieces = [pack_all[layer, j] for j in range(n)]
        feats_to[layer] = jnp.concatenate([m[:, :padded] for m in pieces], axis=1).astype(F32)
        bias = jnp.concatenate([m[6:7, : 2 * share] for m in pieces], axis=1).astype(F32)
        found = jnp.zeros((1, 2 * sh), F32)
        wide = jnp.zeros((1, widen_bias.shape[2]), F32)
        for j in range(n):
            first = HD * low[j]
            spots = [bias[:, k * width + first : k * width + first + sh] for k in range(2)]
            found = jnp.where(h == j, jnp.concatenate(spots, axis=1), found)
            own = pieces[j][7:8, : wide.shape[1]].astype(F32)
            wide = jnp.where(h == j, own, wide)
        qkv_bias[layer] = jnp.concatenate(
            [found[:, :sh], jnp.zeros((1, sh), F32), found[:, sh:]], axis=1
        )
        widen_bias[layer] = wide
    unit = unit_rows(tok_all[...].astype(F32), mask_ref[...], width)[0]
    normed_to[...] = (unit * feats_to[0, 0:1] + feats_to[0, 1:2]).astype(BF16)
    for step in qkv_steps:
        step()
    out.step()
    qkv.finish()
    weight = qkv_all[0].reshape(n * padded, 3 * sh)
    found_to[...] = (dot_n(normed_to[...], weight) + qkv_bias[0]).astype(BF16)
    for a, b in others(n):
        pack_copy(a, b).wait_send()
    out.finish()


def start_call(n, low, width, hide, tok, pack, qkv, out, mask):
    rows, full = tok.shape
    zn = n // 2
    shapes = [
        jax.ShapeDtypeStruct((n * rows, full), BF16),
        jax.ShapeDtypeStruct((n * rows, qkv.shape[2]), BF16),
        jax.ShapeDtypeStruct((2,) + qkv.shape, BF16),
        jax.ShapeDtypeStruct((2,) + out.shape, BF16),
        jax.ShapeDtypeStruct((2, 16, full), F32),
        jax.ShapeDtypeStruct((2, 1, qkv.shape[2]), F32),
        jax.ShapeDtypeStruct((2, 1, hide), F32),
    ]
    return pl.pallas_call(
        functools.partial(start_kernel, n, low, width),
        out_shape=shapes,
        in_specs=[VMEM_SPEC] * 5,
        out_specs=[VMEM_SPEC] * 7,
        scratch_shapes=[
            pltpu.VMEM((n * rows, full), BF16),
            pltpu.VMEM((2, n) + pack.shape, BF16),
            DMA((4, zn, HALVES)),
            DMA((4, zn, HALVES)),
            DMA((HALVES,)),
            DMA((2, n)),
            DMA((2, n)),
            DMA((4, zn)),
            DMA((4, zn)),
            DMA((2,)),
            DMA((2,)),
            DMA((3,)),
        ],
        compiler_params=params(0),
        name="start",
    )(tok, pack, qkv, out, mask)


def with_gaps(values, n, padded):
    rows, width = values.shape
    share = width // n
    pieces = []
    for j in range(n):
        pieces.append(values[:, j * share : (j + 1) * share])
        if padded > share:
            pieces.append(jnp.zeros((rows, padded - share), values.dtype))
    return jnp.concatenate(pieces, axis=1)


def lay_out_kernel(low, qkv_ref, widen_ref, out_ref, narrow_ref, tok_ref, cot_ref, *refs):
    vectors, outs = refs[:8], refs[8:]
    qkv_to, widen_to, out_to, narrow_to, pack_to, tok_to, x_to, cot_to, grad_to, sums_to = outs
    n, padded, hide_full = widen_to.shape
    share, hidden = widen_ref.shape
    hide = hidden // n
    width = qkv_ref.shape[1] // 3
    sh = qkv_to.shape[2] // 3
    gap = padded - share
    s = lax.axis_index("section")
    h = lax.axis_index("shard")
    for j in range(n):
        for t in range(3):
            first = t * width + HD * low[j]
            qkv_to[j, :share, t * sh : (t + 1) * sh] = qkv_ref[:, first : first + sh]
        widen_to[j, :share, :hide] = widen_ref[:, j * hide : (j + 1) * hide]
        if hide_full > hide:
            widen_to[j, :share, hide:] = jnp.zeros((share, hide_full - hide), BF16)
        if gap:
            qkv_to[j, share:] = jnp.zeros((gap, 3 * sh), BF16)
            widen_to[j, share:] = jnp.zeros((gap, hide_full), BF16)
    narrow_to[:hide] = with_gaps(narrow_ref[...], n, padded)
    extra = narrow_to.shape[0] - hide
    if extra:
        narrow_to[hide:] = jnp.zeros((extra, n * padded), BF16)
    offset = 0
    for j in range(n):
        offset = offset + jnp.where(h == j, j * share - HD * low[j], 0)
    rows = with_gaps(out_ref[...].astype(F32), n, padded)
    rows = jnp.concatenate([rows, jnp.zeros((sh - share, n * padded), F32)], axis=0)
    out_to[...] = pltpu.roll(rows, offset, 0).astype(BF16)
    lanes = pack_to.shape[1]
    members = []
    for ref in vectors:
        member = ref[...].astype(F32)
        members.append(
            jnp.concatenate([member, jnp.zeros((1, lanes - member.shape[1]), F32)], axis=1)
        )
    members.append(jnp.zeros((8, lanes), F32))
    pack_to[...] = jnp.concatenate(members, axis=0).astype(BF16)
    for ref, low_to, full_to in ((tok_ref, tok_to, x_to), (cot_ref, cot_to, grad_to)):
        values = with_gaps(ref[s], n, padded)
        low_to[...] = values
        full_to[...] = values.astype(F32)
    sums_to[...] = jnp.sum(grad_to[...], axis=0, keepdims=True)


def lay_out_call(low, slots, padded, qkv, widen, out, narrow, tokens, cotangent, *vectors):
    n = len(low)
    share, hidden = widen.shape
    sh = slots * HD
    full = n * padded
    rows = tokens.shape[1]
    lanes = max(-(-hidden // n // 128) * 128, -(-2 * share // 128) * 128)
    return pl.pallas_call(
        functools.partial(lay_out_kernel, low),
        out_shape=[
            jax.ShapeDtypeStruct((n, padded, 3 * sh), BF16),
            jax.ShapeDtypeStruct((n, padded, -(-hidden // n // 128) * 128), BF16),
            jax.ShapeDtypeStruct((sh, full), BF16),
            jax.ShapeDtypeStruct((-(-narrow.shape[0] // 16) * 16, full), BF16),
            jax.ShapeDtypeStruct((16, lanes), BF16),
            jax.ShapeDtypeStruct((rows, full), BF16),
            jax.ShapeDtypeStruct((rows, full), F32),
            jax.ShapeDtypeStruct((rows, full), BF16),
            jax.ShapeDtypeStruct((rows, full), F32),
            jax.ShapeDtypeStruct((1, full), F32),
        ],
        in_specs=[VMEM_SPEC] * (6 + len(vectors)),
        out_specs=[VMEM_SPEC] * 10,
        compiler_params=params(),
        name="lay_out",
    )(qkv, widen, out, narrow, tokens, cotangent, *vectors)


def settle_kernel(low, sizes, qkv_ref, widen_ref, out_ref, narrow_ref, vec_ref, came_ref, *refs):
    streams, (qkv_to, widen_to, out_to, narrow_to, *outs) = refs[:4], refs[4:]
    stream_to, vectors = outs[:2], outs[2:]
    n, padded, _ = widen_ref.shape
    share = out_to.shape[0]
    hide = narrow_to.shape[0]
    width = qkv_to.shape[1] // 3
    sh = qkv_ref.shape[2] // 3
    s = lax.axis_index("section")

    def without_gaps(values):
        pieces = [values[:, j * padded : j * padded + share] for j in range(n)]
        return jnp.concatenate(pieces, axis=1)

    qkv_to[...] = jnp.zeros_like(qkv_to)
    for j in range(n):
        for t in range(3):
            first = t * width + HD * low[j]
            qkv_to[:, first : first + sh] += qkv_ref[j, :share, t * sh : (t + 1) * sh].astype(F32)
        widen_to[:, j * hide : (j + 1) * hide] = widen_ref[j, :share, :hide].astype(F32)
    for ref, to in ((out_ref, out_to), (narrow_ref, narrow_to)):
        to[...] = without_gaps(ref[: to.shape[0]].astype(F32))
    for item, to in enumerate(stream_to):
        first, second = (ref[...] for ref in streams[2 * item : 2 * item + 2])
        to[s] = without_gaps(jnp.where(s == 0, first, second))
        to[1 - s] = without_gaps(came_ref[item].astype(F32))
    for row, (size, to) in enumerate(zip(sizes, vectors)):
        to[...] = vec_ref[row : row + 1, :size]


def settle_call(low, share, hide, qkv, widen, out, narrow, vec, came, *streams):
    n = widen.shape[0]
    width = n * share
    rows = came.shape[1]
    sizes = [share] * 6 + [2 * share, hide]
    return pl.pallas_call(
        functools.partial(settle_kernel, low, sizes),
        out_shape=[
            jax.ShapeDtypeStruct((share, 3 * width), F32),
            jax.ShapeDtypeStruct((share, n * hide), F32),
            jax.ShapeDtypeStruct((share, width), F32),
            jax.ShapeDtypeStruct((hide, width), F32),
            jax.ShapeDtypeStruct((2, rows, width), F32),
            jax.ShapeDtypeStruct((2, rows, width), F32),
        ]
        + [jax.ShapeDtypeStruct((1, size), F32) for size in sizes],
        in_specs=[VMEM_SPEC] * 10,
        out_specs=[VMEM_SPEC] * 14,
        compiler_params=params(),
        name="settle",
    )(qkv, widen, out, narrow, vec, came, *streams)


def unit_rows(values, mask, width):
    center = (values - jnp.sum(values, axis=-1, keepdims=True) * (1.0 / width)) * mask
    spread = jnp.sum(center * center, axis=-1, keepdims=True) * (1.0 / width)
    scale = lax.rsqrt(spread + EPSILON)
    return center * scale, scale


def norm_back(grad, unit, scale, gain, width):
    inner = grad * gain
    mean = jnp.sum(inner, axis=-1, keepdims=True) * (1.0 / width)
    along = jnp.sum(inner * unit, axis=-1, keepdims=True) * (1.0 / width)
    return (inner - mean - unit * along) * scale


def forward_kernel(n, width, layer, side, *refs):
    middle = layer is not None
    part, base, bias, gain, shift, mask = refs[:6]
    refs = refs[6:]
    if middle:
        widen_all, narrow_in, widen_bias, refs = refs[0], refs[1], refs[2], refs[3:]
    value_to, low_all, refs = refs[0], refs[1], refs[2:]
    if middle:
        pre_to, hidden_to, part_to, refs = refs[0], refs[1], refs[2], refs[3:]
    if side:
        side_out, refs = refs[0], refs[1:]
    own, g_ss, g_rs, g_ls = refs[5:9]
    p = Place(n)
    greet(p, line=True, over=side, sibling=side)
    scatter = Scatter(p, part, *refs[:5])
    scatter.start()
    loads = []
    if middle:
        widen, load_sems, rest = refs[9], refs[10], refs[11:]
        loads.append(fetch(widen_all.at[layer], widen, load_sems.at[0]))
        if side:
            job = RowSwap(p, narrow_in, side_out, *rest)
            job.start()
            filled = narrow_in.shape[0]
            for member in range(2):
                if side_out.shape[1] > filled:
                    spare = (side_out.shape[1] - filled, side_out.shape[2])
                    side_out[member, filled:] = jnp.zeros(spare, BF16)
            narrow = side_out.at[layer]
        else:
            narrow = rest[0]
            loads.append(fetch(narrow_in.at[layer], narrow, load_sems.at[1]))
    gather = Gather(p, own, low_all, g_ss, g_rs, g_ls)
    hr = own.shape[0] // HALVES

    def rows_step(half):
        rows = slice(half * hr, (half + 1) * hr)
        value = base[rows] + (scatter.result(half) + bias[...])
        value_to[rows] = value
        own[rows] = (unit_rows(value, mask[...], width)[0] * gain[...] + shift[...]).astype(BF16)

    by_halves(scatter, gather, rows_step, [])
    if side:
        job.step()
    gather.finish()
    for load in loads:
        load.wait()
    if side:
        job.finish()
    if middle:

        def block(first, size):
            rows = pl.ds(first, size)
            weight = widen[...].reshape(low_all.shape[1], widen.shape[2])
            pre = dot_n(low_all[rows], weight) + widen_bias[...]
            pre_to[rows] = pre
            hidden = (0.5 * pre * (1.0 + gelu_parts(pre)[0])).astype(BF16)
            hidden_to[rows] = hidden
            part_to[rows] = dot_n(hidden, narrow[...]).astype(BF16)

        row_blocks(low_all.shape[0], block)
    scatter.finish()


def scatter_scratch(n, rows, full):
    zn = n // 2
    piece = (HALVES, rows // HALVES, full)
    return [
        pltpu.VMEM((zn,) + piece, BF16),
        pltpu.VMEM((zn + 1,) + piece, BF16),
        pltpu.VMEM((zn,) + piece, BF16),
        DMA((4, zn, HALVES)),
        DMA((4, zn, HALVES)),
    ]


def gather_scratch(n):
    zn = n // 2
    return [DMA((4, zn, HALVES)), DMA((4, zn, HALVES)), DMA((HALVES,))]


def forward_call(n, collective_id, width, part, *local, layer=None, feed=(), carry=False):
    total_rows, full = part.shape
    rows = total_rows // n
    shapes = [
        jax.ShapeDtypeStruct((rows, full), F32),
        jax.ShapeDtypeStruct((total_rows, full), BF16),
    ]
    scratch = scatter_scratch(n, rows, full)
    scratch += [pltpu.VMEM((rows, full), BF16)] + gather_scratch(n)
    in_specs = [VMEM_SPEC] * (1 + len(local))
    if layer is not None:
        widen, narrow, _ = feed
        hide = widen.shape[3]
        in_specs += [ANY_SPEC, VMEM_SPEC if carry else ANY_SPEC, VMEM_SPEC]
        shapes += [
            jax.ShapeDtypeStruct((total_rows, hide), F32),
            jax.ShapeDtypeStruct((total_rows, hide), BF16),
            jax.ShapeDtypeStruct((total_rows, full), BF16),
        ]
        scratch += [pltpu.VMEM(widen.shape[1:], BF16), DMA((2,))]
        if carry:
            shapes.append(jax.ShapeDtypeStruct((2, hide, full), BF16))
            scratch += [DMA((2,)), DMA((2,)), DMA]
        else:
            scratch.append(pltpu.VMEM((hide, full), BF16))
    return pl.pallas_call(
        functools.partial(forward_kernel, n, width, layer, carry),
        out_shape=shapes,
        in_specs=in_specs,
        out_specs=[VMEM_SPEC] * len(shapes),
        scratch_shapes=scratch,
        compiler_params=params(collective_id),
        name="forward_rows",
    )(part, *local, *feed)


def back_rows(scatter, half, base, grad, gain, mask, width):
    hr = scatter.hr
    rows = slice(half * hr, (half + 1) * hr)
    total = scatter.result(half)
    unit, scale = unit_rows(base[rows], mask[...], width)
    value = grad[rows] + norm_back(total, unit, scale, gain[...], width)
    low = value.astype(BF16)
    terms = (total * unit, total, low.astype(F32))
    return rows, value, low, [jnp.sum(term, axis=0, keepdims=True) for term in terms]


def resid_kernel(n, width, layer, *refs):
    base, grad, gain, mask, normed, hidden_pre, hidden, outs, widen_all, narrow_all = refs[:10]
    value_to, sums_to, low_all, wide_to, wide_came, slim_to, pre_sums = refs[10:17]
    refs = refs[17:]
    own, g_ss, g_rs, g_ls = refs[5:9]
    wide, wide_in, wide_ss, wide_rs, slim, slim_in, slim_ss, slim_rs, x_ss, x_rs = refs[9:19]
    part, pre, widen, narrow, load_sems = refs[19:]
    p = Place(n)
    loads = [
        fetch(narrow_all.at[layer], narrow, load_sems.at[0]),
        fetch(widen_all.at[layer], widen, load_sems.at[1]),
    ]
    greet(p, line=True, over=True, sibling=True)
    for load in loads:
        load.wait()

    def block(first, size):
        rows = pl.ds(first, size)
        values = hidden_pre[rows]
        act, square = gelu_parts(values)
        slope = 0.5 * (1.0 + act) + 0.5 * values * (1.0 - act * act) * GELU_A * (
            1.0 + 3.0 * GELU_B * square
        )
        found = (dot_t(outs[rows], narrow[...]) * slope).astype(BF16)
        pre[rows] = found
        weight = widen[...].reshape(part.shape[1], widen.shape[2])
        part[rows] = dot_t(found, weight).astype(BF16)

    row_blocks(part.shape[0], block)
    scatter = Scatter(p, part, *refs[:5])
    scatter.start()
    gather = Gather(p, own, low_all, g_ss, g_rs, g_ls)
    wide_fold = Fold(p, wide, wide_in, wide_to, wide_ss, wide_rs)
    slim_fold = Fold(p, slim, slim_in, slim_to, slim_ss, slim_rs)
    cross = Cross(p, wide_to, wide_came, x_ss, x_rs, 1 - layer)

    def pre_sum():
        pre_sums[...] = jnp.sum(pre[...].astype(F32), axis=0, keepdims=True)

    for step in product(normed, pre, wide):
        step()
    wide_fold.start()
    work = product(hidden, outs, slim) + wide_fold.steps() + [cross.start, slim_fold.start, pre_sum]
    work += slim_fold.steps()
    sums = []

    def rows_step(half):
        rows, value, low, terms = back_rows(scatter, half, base, grad, gain, mask, width)
        value_to[rows] = value
        own[rows] = low
        sums.append(jnp.concatenate(terms, axis=0))

    by_halves(scatter, gather, rows_step, work, 3)
    sums_to[...] = sum(sums)
    for rest in work:
        rest()
    gather.finish()
    scatter.finish()
    for job in (wide_fold, slim_fold, cross):
        job.finish()


def resid_call(n, collective_id, width, layer, hide, *args):
    base, normed, hidden = args[0], args[4], args[6]
    widen, narrow = args[8:]
    rows = base.shape[0]
    total_rows, full = normed.shape
    zn = n // 2
    wide = (zn, full // n, hidden.shape[1])
    half = -(-hide // 32) * 16
    slim = (1, half, full)
    return pl.pallas_call(
        functools.partial(resid_kernel, n, width, layer),
        out_shape=[
            jax.ShapeDtypeStruct((rows, full), F32),
            jax.ShapeDtypeStruct((3, full), F32),
            jax.ShapeDtypeStruct((total_rows, full), BF16),
            jax.ShapeDtypeStruct(wide, BF16),
            jax.ShapeDtypeStruct(wide, BF16),
            jax.ShapeDtypeStruct(slim, BF16),
            jax.ShapeDtypeStruct((1, hidden.shape[1]), F32),
        ],
        in_specs=[VMEM_SPEC] * 8 + [ANY_SPEC] * 2,
        out_specs=[VMEM_SPEC] * 7,
        scratch_shapes=scatter_scratch(n, rows, full)
        + [pltpu.VMEM((rows, full), BF16)]
        + gather_scratch(n)
        + fold_scratch((full, hidden.shape[1]), wide)
        + fold_scratch((2 * half, full), slim)
        + [DMA, DMA]
        + [
            pltpu.VMEM((total_rows, full), BF16),
            pltpu.VMEM(hidden.shape, BF16),
            pltpu.VMEM(widen.shape[1:], BF16),
            pltpu.VMEM(narrow.shape[1:], BF16),
            DMA((2,)),
        ],
        compiler_params=params(collective_id),
        name="back_resid",
    )(*args)


def input_kernel(n, width, source, low, *refs):
    part, base, grad, gain, mask, normed, triple, att, resid, slim = refs[:10]
    value_to, sums_to, low_all, qkv_to, out_to, slim_came, triple_sums = refs[10:17]
    refs = refs[17:]
    own, g_ss, g_rs, g_ls = refs[5:9]
    qkv, qkv_in, qkv_ss, qkv_rs, out, out_in, out_ss, out_rs, x_ss, x_rs = refs[9:]
    p = Place(n)
    greet(p, line=True, over=True, sibling=True)
    scatter = Scatter(p, part, *refs[:5])
    scatter.start()
    cross = Cross(p, slim, slim_came, x_ss, x_rs, source)
    cross.start()
    gather = Gather(p, own, low_all, g_ss, g_rs, g_ls)
    qkv_fold = Fold(p, qkv, qkv_in, qkv_to, qkv_ss, qkv_rs)
    out_fold = Fold(p, out, out_in, out_to, out_ss, out_rs)

    def triple_sum():
        triple_sums[...] = jnp.sum(triple[...].astype(F32), axis=0, keepdims=True)

    work = product(normed, triple, qkv) + [qkv_fold.start]
    work += [functools.partial(home_rows, att, resid, out, low, width // n), out_fold.start]
    work += qkv_fold.steps() + [triple_sum] + out_fold.steps()
    sums = []

    def rows_step(half):
        rows, value, lower, terms = back_rows(scatter, half, base, grad, gain, mask, width)
        value_to[rows] = value
        own[rows] = lower
        sums.append(jnp.concatenate(terms, axis=0))

    by_halves(scatter, gather, rows_step, work, 2)
    sums_to[...] = sum(sums)
    for rest in work:
        rest()
    gather.finish()
    scatter.finish()
    for job in (qkv_fold, out_fold, cross):
        job.finish()


def input_call(n, collective_id, width, source, low, part, base, grad, gain, mask, *operands):
    normed, triple, att, resid, slim = operands
    total_rows, full = part.shape
    rows = total_rows // n
    zn = n // 2
    qkv = (zn, full // n, triple.shape[1])
    out = (1, att.shape[1] // 2, full)
    return pl.pallas_call(
        functools.partial(input_kernel, n, width, source, low),
        out_shape=[
            jax.ShapeDtypeStruct((rows, full), F32),
            jax.ShapeDtypeStruct((3, full), F32),
            jax.ShapeDtypeStruct((total_rows, full), BF16),
            jax.ShapeDtypeStruct(qkv, BF16),
            jax.ShapeDtypeStruct(out, BF16),
            jax.ShapeDtypeStruct(slim.shape, BF16),
            jax.ShapeDtypeStruct((1, triple.shape[1]), F32),
        ],
        in_specs=[VMEM_SPEC] * 10,
        out_specs=[VMEM_SPEC] * 7,
        scratch_shapes=scatter_scratch(n, rows, full)
        + [pltpu.VMEM((rows, full), BF16)]
        + gather_scratch(n)
        + fold_scratch((full, triple.shape[1]), qkv)
        + fold_scratch((att.shape[1], full), out)
        + [DMA, DMA],
        compiler_params=params(collective_id),
        name="back_input",
    )(part, base, grad, gain, mask, *operands)


def finale_kernel(n, width, low, *refs):
    part, base, grad, gain, mask, normed, triple, att, resid = refs[:9]
    wides, wide_cames, slims, slim_came, qkv_far, out_far, vecs = (
        refs[9:11],
        refs[11:13],
        refs[13:15],
        refs[15],
        refs[16],
        refs[17],
        refs[18:25],
    )
    layer_outs, upper_d_in, refs = refs[25:27], refs[27], refs[28:]
    value_to, wide_to, slim_to, qkv_to, out_to, vec_to, streams_to = refs[:7]
    refs = refs[7:]
    qkv, qkv_fold_in, qkv_ss, qkv_rs, out, out_fold_in, out_ss, out_rs = refs[5:13]
    qkv_own, qkv_in, qkv_sum, out_own, out_in, out_sum = refs[13:19]
    wide_sum, slim_in, slim_sum, vec, vec_in, vec_sum, vec_sib, streams = refs[19:27]
    a_ss, a_rs, x_ss, x_rs, v_ss, v_rs, r_ss, r_rs, ls = refs[27:]
    p = Place(n)
    s, c, h, z, zn = p.s, p.c, p.h, p.z, p.zn
    share = width // n
    greet_all(p)
    scatter = Scatter(p, part, *refs[:5])
    scatter.start()

    @pl.when(s == 0)
    def _():
        wide_sum[...] = (wides[0][...].astype(F32) + wide_cames[0][...].astype(F32)).astype(BF16)

    @pl.when(s == 1)
    def _():
        wide_sum[...] = (wides[1][...].astype(F32) + wide_cames[1][...].astype(F32)).astype(BF16)

    spreads = ((wide_sum, wide_to), (qkv_sum, qkv_to))

    def send(w, k):
        far = p.flip(k)
        src, dst = spreads[w]
        target = (s, c, far * 2 + p.far_y)
        return remote(src.at[far], dst.at[h], a_ss.at[0, w, k], a_rs.at[0, w, k], target)

    def keep(w):
        src, dst = spreads[w]
        return pltpu.make_async_copy(src.at[z], dst.at[h], ls.at[w])

    def aside(w, k):
        block = spreads[w][1].at[p.flip(k) * 2 + p.far_y]
        return remote(block, block, a_ss.at[1, w, k], a_rs.at[1, w, k], p.sibling)

    def start_zero(w):
        @pl.when(c == 1)
        def _():
            send(w, 0).start()

        @pl.when(c == 0)
        def _():
            keep(w).start()

    def x_block(k, src=qkv_far):
        far = p.flip(k)
        return remote(src.at[far], qkv_in.at[far], x_ss.at[k], x_rs.at[k], p.over)

    def out_cross(src=out_far):
        return remote(src, out_in, x_ss.at[zn], x_rs.at[zn], p.over)

    stream_cross = remote(streams, streams_to, x_ss.at[zn + 1], x_rs.at[zn + 1], p.over)
    slim_cross = Cross(p, slims[0], slim_in, x_ss.at[zn + 2], x_rs.at[zn + 2], 1)

    def start_far():
        @pl.when(s == 0)
        def _():
            for k in range(zn):
                x_block(k).start()
            out_cross().start()

    def start_own(k):
        @pl.when(s == 1)
        def _():
            x_block(k, qkv_own).start()

    def start_own_out():
        @pl.when(s == 1)
        def _():
            out_cross(out_own).start()

    qkv_fold = Fold(p, qkv, qkv_fold_in, qkv_own, qkv_ss, qkv_rs)
    out_fold = Fold(p, out, out_fold_in, out_own, out_ss, out_rs)

    start_zero(0)
    for k in range(1, zn):
        send(0, k).start()
    start_far()
    for step in product(normed, triple, qkv):
        step()
    qkv_fold.start()
    work = [functools.partial(home_rows, att, resid, out, low, share), out_fold.start]
    work += qkv_fold.steps()
    work += [functools.partial(start_own, k) for k in list(range(1, zn)) + [0]]
    work += out_fold.steps() + [start_own_out, slim_cross.start]
    sums = []

    def rows_step(half):
        rows, value, lower, terms = back_rows(scatter, half, base, grad, gain, mask, width)
        value_to[rows] = value
        sums.append(jnp.concatenate(terms, axis=0))

    by_halves(scatter, None, rows_step, work, 3)
    for rest in work:
        rest()

    streams[0] = jnp.where(s == 0, layer_outs[1][...], layer_outs[0][...]).astype(BF16)
    streams[1] = jnp.where(s == 0, upper_d_in[...], value_to[...]).astype(BF16)
    stream_cross.start()

    ones = (sum(sums), vecs[0][...])
    twos, triples, pres = vecs[1:3], (None, vecs[3]), vecs[4:6]
    lanes = vec.shape[3]
    padded = base.shape[1] // n
    sh = triple.shape[1] // 3
    for layer in range(2):
        one, two = ones[layer], twos[layer][...]
        outs = vecs[6][...] if layer else ones[1][2:3]
        features = jnp.concatenate([one[0:2], two[2:3], two[0:2], outs], axis=0)
        if layer:
            found = triples[1][...]
        else:
            found = jnp.sum(triple[...].astype(F32), axis=0, keepdims=True)
        bias = jnp.zeros((1, 2 * width), F32)
        for j, first in enumerate(low):
            spots = []
            for begin in (0, 2 * sh):
                spots += [
                    jnp.zeros((1, HD * first), F32),
                    found[:, begin : begin + sh],
                    jnp.zeros((1, width - sh - HD * first), F32),
                ]
            spots = [spot for spot in spots if spot.shape[1]]
            bias = jnp.where(h == j, jnp.concatenate(spots, axis=1), bias)
        for i in range(n):
            pieces = [
                features[:, i * padded : (i + 1) * padded],
                bias[:, i * 2 * share : (i + 1) * 2 * share],
                jnp.where(h == i, pres[layer][...], 0.0),
            ]
            wide_pieces = []
            for piece in pieces:
                rows, size = piece.shape
                if size < lanes:
                    piece = jnp.concatenate([piece, jnp.zeros((rows, lanes - size), F32)], axis=1)
                wide_pieces.append(piece)
            vec[layer, i] = jnp.concatenate(wide_pieces, axis=0)

    def vec_copy(a, b):
        l, i = lax.rem(s + a, 2), lax.rem(h + b, n)
        return remote(vec.at[l, i], vec_in.at[s, h], v_ss.at[a, b], v_rs.at[a, b], (l, c, i))

    for a, b in others(n):
        vec_copy(a, b).start()

    def add(to, index, first, second, came):
        @pl.when(s == 0)
        def _():
            to[index] = (first[index].astype(F32) + came[index].astype(F32)).astype(BF16)

        @pl.when(s == 1)
        def _():
            to[index] = (second[index].astype(F32) + came[index].astype(F32)).astype(BF16)

    for k in list(range(1, zn)) + [0]:
        x_block(k).wait_recv()
        add(qkv_sum, p.flip(k), qkv_own, qkv_far, qkv_in)
        if k:
            send(1, k).start()
        else:
            start_zero(1)
    out_cross().wait_recv()
    add(out_sum, 0, out_own, out_far, out_in)

    @pl.when(s == 0)
    def _():
        slim_cross.copy.wait_recv()
        slim_sum[0] = (slims[0][0].astype(F32) + slim_in[0].astype(F32)).astype(BF16)

    @pl.when(s == 1)
    def _():
        slim_cross.copy.wait_send()
        slim_sum[0] = (slims[1][0].astype(F32) + slim_came[0].astype(F32)).astype(BF16)

    def row_copies(w, src, dst):
        half = src.shape[1]
        piece = dst.at[pl.ds(pl.multiple_of(c * half, 16), half)]
        return (
            pltpu.make_async_copy(src.at[0], piece, ls.at[2 + w]),
            remote(src.at[0], piece, r_ss.at[w], r_rs.at[w], p.sibling),
        )

    copies = row_copies(0, slim_sum, slim_to) + row_copies(1, out_sum, out_to)
    for copy in copies:
        copy.start()
    total = vec[s, h]
    for a, b in others(n):
        vec_copy(a, b).wait_recv()
        total = total + vec_in[lax.rem(s + a, 2), lax.rem(h + n - b, n)]
    vec_sum[...] = total
    vec_share = remote(vec_sum, vec_sib, r_ss.at[2], r_rs.at[2], p.sibling)
    vec_share.start()
    for w in range(2):

        @pl.when(c == 1)
        def _():
            send(w, 0).wait_recv()

        @pl.when(c == 0)
        def _():
            keep(w).wait()

        for k in range(zn):
            if k:
                send(w, k).wait_recv()
            aside(w, k).start()
    vec_share.wait_recv()
    vec_to[...] = total + vec_sib[...]
    vec_share.wait_send()
    for w in range(2):

        @pl.when(c == 1)
        def _():
            send(w, 0).wait_send()

        for k in range(zn):
            if k:
                send(w, k).wait_send()
            aside(w, k).wait_recv()
            aside(w, k).wait_send()
    for w in range(2):
        copies[2 * w].wait()
        copies[2 * w + 1].wait_recv()
        copies[2 * w + 1].wait_send()
    for a, b in others(n):
        vec_copy(a, b).wait_send()
    for k in range(zn):
        x_block(k).wait_send()
    out_cross().wait_send()
    stream_cross.wait_recv()
    stream_cross.wait_send()
    for job in (scatter, qkv_fold, out_fold):
        job.finish()


def finale_call(n, collective_id, width, low, *args):
    part, triple, att = args[0], args[6], args[7]
    wide, slim, lanes = args[9].shape, args[13].shape, args[22].shape[1]
    total_rows, full = part.shape
    rows = total_rows // n
    zn = n // 2
    qkv = (zn, full // n, triple.shape[1])
    out = (1, att.shape[1] // 2, full)
    return pl.pallas_call(
        functools.partial(finale_kernel, n, width, low),
        out_shape=[
            jax.ShapeDtypeStruct((rows, full), F32),
            jax.ShapeDtypeStruct((n,) + wide[1:], BF16),
            jax.ShapeDtypeStruct((2 * slim[1], full), BF16),
            jax.ShapeDtypeStruct((n,) + qkv[1:], BF16),
            jax.ShapeDtypeStruct((2 * out[1], full), BF16),
            jax.ShapeDtypeStruct((8, lanes), F32),
            jax.ShapeDtypeStruct((2, rows, full), BF16),
        ],
        in_specs=[VMEM_SPEC] * len(args),
        out_specs=[VMEM_SPEC] + [ANY_SPEC] * 4 + [VMEM_SPEC] * 2,
        scratch_shapes=scatter_scratch(n, rows, full)
        + fold_scratch((full, triple.shape[1]), qkv)
        + fold_scratch((att.shape[1], full), out)
        + [pltpu.VMEM(qkv, BF16)] * 3
        + [pltpu.VMEM(out, BF16)] * 3
        + [
            pltpu.VMEM(wide, BF16),
            pltpu.VMEM(slim, BF16),
            pltpu.VMEM(slim, BF16),
            pltpu.VMEM((2, n, 8, lanes), F32),
            pltpu.VMEM((2, n, 8, lanes), F32),
            pltpu.VMEM((8, lanes), F32),
            pltpu.VMEM((8, lanes), F32),
            pltpu.VMEM((2, rows, full), BF16),
            DMA((2, 2, zn)),
            DMA((2, 2, zn)),
            DMA((zn + 3,)),
            DMA((zn + 3,)),
            DMA((2, n)),
            DMA((2, n)),
            DMA((3,)),
            DMA((3,)),
            DMA((4,)),
        ],
        compiler_params=params(collective_id),
        name="finale",
    )(*args)


def dot_t(a, b):
    return lax.dot_general(a, b, (((1,), (1,)), ((), ())), preferred_element_type=F32)


def dot_n(a, b):
    return lax.dot_general(a, b, (((1,), (0,)), ((), ())), preferred_element_type=F32)


def in_blocks(rows, step, chunk, between):
    count = rows // step
    if count <= 2:
        for b in range(count):
            chunk(b * step, rows // 2 if (b + 1) * step <= rows // 2 else rows, between)
    else:

        def body(b, carry, keys):
            chunk(pl.multiple_of(b * step, step), keys, [])
            return carry

        middle = count // 2 if count % 2 == 0 else 0
        lax.fori_loop(0, middle, functools.partial(body, keys=rows // 2), 0)
        lax.fori_loop(middle, count, functools.partial(body, keys=rows), 0)


def run_next(between):
    if between:
        between.pop(0)()


def attend_kernel(n, slots, step, layer, side, *refs):
    kpos_ref, qpos_ref, carried, out_all = refs[:4]
    refs = refs[4:]
    if layer:
        normed, qkv_all, qkv_bias = refs[:3]
        refs = refs[3:]
    else:
        own_ref, refs = refs[0], refs[1:]
    att_ref, low_ref, lse_ref, oth_ref, part_to, carried_to = refs[:6]
    refs = refs[6:]
    if layer:
        own_ref, refs = refs[0], refs[1:]
    kv_ss, kv_rs, out_weight, load_sems = refs[:4]
    refs = refs[4:]
    if layer:
        qkv_weight, refs = refs[0], refs[1:]
        qkv_load = fetch(qkv_all.at[layer], qkv_weight, load_sems.at[1])
    out_load = fetch(out_all.at[layer], out_weight, load_sems.at[0])
    p = Place(n)
    rows = own_ref.shape[0]
    sh = slots * HD
    power = HD**-0.5 * LOG2E
    if side == "spread":
        greet(p, spread=True, over=True, sibling=True)
    else:
        greet(p, line=True, sibling=True)
    job = (Spread if side == "spread" else Gather)(p, carried, carried_to, *refs)
    job.start()
    if layer:
        qkv_load.wait()

        def project(first, size):
            some = pl.ds(first, size)
            weight = qkv_weight[...].reshape(normed.shape[1], 3 * sh)
            own_ref[some] = (dot_n(normed[some], weight) + qkv_bias[...]).astype(BF16)

        row_blocks(rows, project)
    swap = remote(own_ref.at[:, pl.ds(sh, 2 * sh)], oth_ref, kv_ss, kv_rs, p.sibling)
    swap.start()
    swap.wait_recv()

    def at(base, slot):
        return slice(base + slot * HD, base + (slot + 1) * HD)

    def chunk(first, seen, between):
        q_rows = pl.ds(first, step)
        qpos = qpos_ref[:, q_rows]
        for slot in range(slots):
            queries = own_ref[q_rows, at(0, slot)]
            keys = (own_ref[:seen, at(sh, slot)], oth_ref[:seen, at(0, slot)])
            values = (own_ref[:seen, at(2 * sh, slot)], oth_ref[:seen, at(sh, slot)])
            scores = []
            for part in range(2):
                allowed = kpos_ref[part * rows : part * rows + seen] <= qpos
                scores.append(jnp.where(allowed, dot_t(keys[part], queries), MASKED))
            top = jnp.maximum(
                jnp.max(scores[0], axis=0, keepdims=True), jnp.max(scores[1], axis=0, keepdims=True)
            )
            total = jnp.zeros_like(top)
            weighted = jnp.zeros((HD, step), F32)
            exps = []
            for part in range(2):
                e = jnp.exp2((scores[part] - top) * power)
                total = total + jnp.sum(e, axis=0, keepdims=True)
                exps.append(e)
            inverse = 1.0 / total
            for part in range(2):
                probs = (exps[part] * inverse).astype(BF16)
                weighted = weighted + dot_n(values[part].T, probs)
            att_ref[at(0, slot), q_rows] = weighted
            low_ref[q_rows, at(0, slot)] = weighted.T.astype(BF16)
            lse_ref[slot : slot + 1, q_rows] = top * power + jnp.log(total) * LOG2E
            run_next(between)

    between = job.steps()
    in_blocks(rows, step, chunk, between)
    out_load.wait()

    def give(first, size):
        some = pl.ds(first, size)
        part_to[some] = dot_n(low_ref[some], out_weight[...]).astype(BF16)

    row_blocks(rows, give)
    for rest in between:
        rest()
    swap.wait_send()
    job.finish()


def attend_call(n, collective_id, slots, layer, side, kpos, qpos, carried, out_all, *source):
    rows = qpos.shape[1]
    zn = n // 2
    sh = slots * HD
    full = out_all.shape[2]
    step = min(rows, 256)
    if side == "spread":
        moved = jax.ShapeDtypeStruct((2,) + carried.shape, BF16)
        scratch = [DMA((4, zn)), DMA((4, zn)), DMA]
    else:
        moved = jax.ShapeDtypeStruct((n * carried.shape[0], carried.shape[1]), BF16)
        scratch = gather_scratch(n)
    shapes = [
        jax.ShapeDtypeStruct((sh, rows), F32),
        jax.ShapeDtypeStruct((rows, sh), BF16),
        jax.ShapeDtypeStruct((slots, rows), F32),
        jax.ShapeDtypeStruct((rows, 2 * sh), BF16),
        jax.ShapeDtypeStruct((rows, full), BF16),
        moved,
    ]
    in_specs = [VMEM_SPEC] * 3 + [ANY_SPEC, VMEM_SPEC]
    kept = [DMA, DMA, pltpu.VMEM((sh, full), BF16), DMA((2,))]
    if layer:
        in_specs += [ANY_SPEC, VMEM_SPEC]
        shapes.append(jax.ShapeDtypeStruct((rows, 3 * sh), BF16))
        kept.append(pltpu.VMEM(source[1].shape[1:], BF16))
    return pl.pallas_call(
        functools.partial(attend_kernel, n, slots, step, layer, side),
        out_shape=shapes,
        in_specs=in_specs,
        out_specs=[VMEM_SPEC] * len(shapes),
        scratch_shapes=kept + scratch,
        compiler_params=params(collective_id),
        name="attend_" + side,
    )(kpos, qpos, carried, out_all, *source)


def attend_back_kernel(n, slots, step, layer, last, *refs):
    own_ref, oth_ref, resid, att_ref, lse_ref, kpos_ref, qpos_ref, out_all, qkv_all = refs[:9]
    refs = refs[9:]
    if last:
        part_ref, base_ref, bias_ref = refs[:3]
        refs = refs[3:]
    triple_ref, part_to, refs = refs[0], refs[1], refs[2:]
    if last:
        value_ref, refs = refs[0], refs[1:]
    dq_t, dkv_own, dkv_oth, came, kv_ss, kv_rs = refs[:6]
    grad_ref, out_weight, qkv_weight, load_sems = refs[6:10]
    out_load = fetch(out_all.at[layer], out_weight, load_sems.at[0])
    qkv_load = fetch(qkv_all.at[layer], qkv_weight, load_sems.at[1])
    p = Place(n)
    rows = own_ref.shape[0]
    sh = slots * HD
    scale = HD**-0.5
    greet(p, line=last, sibling=True)
    between = []
    if last:
        scatter = Scatter(p, part_ref, *refs[10:])
        scatter.start()
        between = scatter.steps()
    out_load.wait()

    def enter(first, size):
        some = pl.ds(first, size)
        grad_ref[some] = dot_t(resid[some], out_weight[...]).astype(BF16)

    row_blocks(rows, enter)

    def at(base, slot):
        return slice(base + slot * HD, base + (slot + 1) * HD)

    dq_t[...] = jnp.zeros_like(dq_t)
    swap = remote(dkv_oth, came, kv_ss, kv_rs, p.sibling)
    for part in (1, 0):
        dkv = (dkv_own, dkv_oth)[part]
        src = (own_ref, oth_ref)[part]
        base = (sh, 0)[part]
        dkv[...] = jnp.zeros_like(dkv)

        def chunk(first, seen, between):
            q_rows = pl.ds(first, step)
            qpos = qpos_ref[:, q_rows]
            for slot in range(slots):
                queries = own_ref[q_rows, at(0, slot)]
                grads = grad_ref[q_rows, at(0, slot)]
                keys, values = src[:seen, at(base, slot)], src[:seen, at(base + sh, slot)]
                lse = lse_ref[slot : slot + 1, q_rows]
                correction = jnp.sum(
                    grads.astype(F32).T * att_ref[at(0, slot), q_rows], axis=0, keepdims=True
                )
                allowed = kpos_ref[part * rows : part * rows + seen] <= qpos
                scores = dot_t(keys, queries)
                probs = jnp.where(allowed, jnp.exp2(scores * (scale * LOG2E) - lse), 0.0)
                prob_grad = dot_t(values, grads)
                score_grad = (probs * (prob_grad - correction)).astype(BF16)
                dkv[:seen, at(0, slot)] += dot_n(score_grad, queries) * scale
                dkv[:seen, at(sh, slot)] += dot_n(probs.astype(BF16), grads)
                dq_t[at(0, slot), q_rows] += dot_n(keys.T, score_grad)
                run_next(between)

        in_blocks(rows, step, chunk, between)
        if part:
            swap.start()
    triple_ref[:, :sh] = (dq_t[...].T * scale).astype(BF16)

    def finish_last():
        for rest in between:
            rest()
        hr = base_ref.shape[0] // HALVES
        for half in range(HALVES):
            part_rows = slice(half * hr, (half + 1) * hr)
            total = scatter.result(half)
            value_ref[part_rows] = base_ref[part_rows] + (total + bias_ref[...])
        scatter.finish()

    swap.wait_recv()
    triple_ref[:, sh:] = (dkv_own[...] + came[...]).astype(BF16)
    qkv_load.wait()

    def leave(first, size):
        some = pl.ds(first, size)
        weight = qkv_weight[...].reshape(part_to.shape[1], 3 * sh)
        part_to[some] = dot_t(triple_ref[some], weight).astype(BF16)

    row_blocks(rows, leave)
    if last:
        finish_last()
    swap.wait_send()


def attend_back_call(n, collective_id, slots, layer, *args, last=()):
    qkv, out_all, qkv_all = args[0], args[7], args[8]
    rows = qkv.shape[0]
    sh = slots * HD
    full = out_all.shape[2]
    step = min(rows, 256)
    shapes = [
        jax.ShapeDtypeStruct((rows, 3 * sh), BF16),
        jax.ShapeDtypeStruct((rows, full), BF16),
    ]
    scratch = [pltpu.VMEM((sh, rows), F32)] + [pltpu.VMEM((rows, 2 * sh), F32)] * 3
    scratch += [DMA, DMA]
    scratch += [
        pltpu.VMEM((rows, sh), BF16),
        pltpu.VMEM((sh, full), BF16),
        pltpu.VMEM(qkv_all.shape[1:], BF16),
        DMA((2,)),
    ]
    if last:
        shapes.append(jax.ShapeDtypeStruct(last[1].shape, F32))
        scratch += scatter_scratch(n, *last[1].shape)
    return pl.pallas_call(
        functools.partial(attend_back_kernel, n, slots, step, layer, bool(last)),
        out_shape=shapes,
        in_specs=[VMEM_SPEC] * 7 + [ANY_SPEC] * 2 + [VMEM_SPEC] * len(last),
        out_specs=[VMEM_SPEC] * len(shapes),
        scratch_shapes=scratch,
        compiler_params=params(collective_id),
        name="attend_back",
    )(*args, *last)


def windows(width, n):
    share = width // n
    low = [j * share // HD for j in range(n)]
    slots = max(((j + 1) * share - 1) // HD - low[j] + 1 for j in range(n))
    return [min(first, HEADS - slots) for first in low], slots


def on_device(n, tokens, block_order, cotangent, *vectors_and_weights):
    (
        first_gain,
        first_shift,
        qkv_weight,
        input_bias,
        out_weight,
        out_bias,
        second_gain,
        second_shift,
        widen_weight,
        widen_bias,
        narrow_weight,
        narrow_bias,
    ) = (member[0] for member in vectors_and_weights)
    c = lax.axis_index("ctx")
    _, rows, width = tokens.shape
    hidden = widen_weight.shape[1]
    share = width // n
    hide = hidden // n
    padded = -(-share // 16) * 16
    full = n * padded
    low, slots = windows(width, n)
    sh = slots * HD
    total_rows = n * rows
    half_rows = rows // HALVES

    mask = jnp.asarray(np.arange(full)[None] % padded < share, F32)
    qkv_send, widen_send, out_send, narrow_send, pack, own_tokens, x, own_cot, out_grad, out_sums = (
        lay_out_call(
            low,
            slots,
            padded,
            qkv_weight,
            widen_weight,
            out_weight,
            narrow_weight,
            tokens,
            cotangent,
            first_gain[None],
            first_shift[None],
            out_bias[None],
            second_gain[None],
            second_shift[None],
            narrow_bias[None],
            input_bias[None],
            widen_bias[None],
        )
    )
    hide_full = widen_send.shape[2]
    normed, qkv, qkv_all, out_all, feats, qkv_bias, widen_biases = start_call(
        n, low, width, widen_send.shape[2], own_tokens, pack, qkv_send, out_send, mask
    )

    order = block_order.reshape(2, n, HALVES).transpose(0, 2, 1)
    places = order[..., None] * half_rows + jnp.arange(half_rows, dtype=jnp.int32)
    places = places.reshape(2, total_rows)
    own_places = jnp.where(c == 0, places[0], places[1])
    oth_places = jnp.where(c == 0, places[1], places[0])
    kpos = jnp.concatenate([own_places, oth_places])[:, None]
    qpos = own_places[None, :]

    layers = [
        dict(
            gain1=feats[layer, 0:1],
            shift1=feats[layer, 1:2],
            out_bias=feats[layer, 2:3],
            gain2=feats[layer, 3:4],
            shift2=feats[layer, 4:5],
            narrow_bias=feats[layer, 5:6],
            qkv_bias=qkv_bias[layer],
            widen_bias=widen_biases[layer],
        )
        for layer in range(2)
    ]

    stored = []
    layer_outs = []
    for layer in range(2):
        w = layers[layer]
        if layer:
            found = attend_call(
                n, 2, slots, 1, "gather", kpos, qpos, own_cot, out_all, normed, qkv_all, w["qkv_bias"]
            )
            out_low_all, qkv = found[5:]
        else:
            found = attend_call(n, 1, slots, 0, "spread", kpos, qpos, widen_send, out_all, qkv)
            widen_all = found[5]
        att, att_low, lse, other, part = found[:5]
        found = forward_call(
            n,
            3 + layer,
            width,
            part,
            x,
            w["out_bias"],
            w["gain2"],
            w["shift2"],
            mask,
            layer=layer,
            feed=(widen_all, narrow_all if layer else narrow_send, w["widen_bias"]),
            carry=not layer,
        )
        residual, normed_two, hidden_pre, hidden_low, part = found[:5]
        stored.append((x, normed, qkv, other, att, att_low, lse, residual, normed_two))
        stored[-1] += (hidden_pre, hidden_low)
        if layer == 0:
            narrow_all = found[5]
            nxt = layers[1]
            x, normed = forward_call(
                n,
                5,
                width,
                part,
                residual,
                w["narrow_bias"],
                nxt["gain1"],
                nxt["shift1"],
                mask,
            )
            layer_outs.append(x)
        else:
            last = (part, residual, w["narrow_bias"])

    found = {}
    for layer in (1, 0):
        w = layers[layer]
        x, normed, qkv, other, att, att_low, lse, residual, normed_two = stored[layer][:9]
        hidden_pre, hidden_low = stored[layer][9:]
        resid_grad, sums_two, resid_low_all, wide, wide_came, slim, pre_sums = resid_call(
            n,
            7 + layer,
            width,
            layer,
            hide,
            residual,
            out_grad,
            w["gain2"],
            mask,
            normed_two,
            hidden_pre,
            hidden_low,
            out_low_all,
            widen_all,
            narrow_all,
        )
        back = attend_back_call(
            n,
            9 + layer,
            slots,
            layer,
            qkv,
            other,
            resid_low_all,
            att,
            lse,
            kpos,
            qpos,
            out_all,
            qkv_all,
            last=last if layer else (),
        )
        triple, part = back[:2]
        local = (part, x, resid_grad, w["gain1"], mask, normed, triple, att_low, resid_low_all)
        found[layer] = (wide, wide_came, slim, sums_two, pre_sums)
        if layer:
            layer_outs.append(back[2])
            upper_d_in, sums_one, out_low_all, qkv_grad, out_rows, slim_came, triple_sums = (
                input_call(n, 11, width, 0, low, *local, slim)
            )
            out_grad = upper_d_in
    lower, upper = found[0], found[1]
    d_in, widen_back, narrow_back, qkv_back, out_back, vec, came = finale_call(
        n,
        12,
        width,
        low,
        *local,
        lower[0],
        upper[0],
        lower[1],
        upper[1],
        lower[2],
        upper[2],
        slim_came,
        qkv_grad,
        out_rows,
        sums_one,
        lower[3],
        upper[3],
        triple_sums,
        lower[4],
        upper[4],
        out_sums,
        *layer_outs,
        upper_d_in,
    )
    settled = settle_call(
        low,
        share,
        hide,
        qkv_back,
        widen_back,
        out_back,
        narrow_back,
        vec,
        came,
        *layer_outs,
        d_in,
        upper_d_in,
    )
    qkv_out, widen_out, out_out, narrow_out, layer_out, d_out = (m[None] for m in settled[:6])
    gain1, shift1, out_b, gain2, shift2, narrow_b, input_b, widen_b = settled[6:]
    return (
        layer_out,
        d_out,
        gain1,
        shift1,
        qkv_out,
        input_b,
        out_out,
        out_b,
        gain2,
        shift2,
        widen_out,
        widen_b,
        narrow_out,
        narrow_b,
    )


def solution(mesh):
    rows = P(None, ("ctx", "shard"), None)
    vector = P("section", "shard")
    matrix = P("section", "shard", None)
    order = (
        vector,
        vector,
        matrix,
        vector,
        matrix,
        vector,
        vector,
        vector,
        matrix,
        vector,
        matrix,
        vector,
    )
    streams = P("section", None, ("ctx", "shard"), None)
    return jax.shard_map(
        functools.partial(on_device, mesh.shape["shard"]),
        mesh=mesh,
        in_specs=(rows, P(), rows) + order,
        out_specs=(streams, streams) + order,
        check_vma=False,
    )
```

```python
import functools

import jax
import jax.numpy as jnp
import numpy as np
from jax import lax
from jax.experimental import pallas as pl
from jax.experimental.pallas import tpu as pltpu
from jax.sharding import PartitionSpec as P

HEADS = 25
HD = 64
EPSILON = 1e-05
MASKED = -1e30
LOG2E = 1.4426950408889634
GELU_A = 0.7978845608028654
GELU_B = 0.044715
MESH = pl.DeviceIdType.MESH
F32 = jnp.float32
BF16 = jnp.bfloat16
VMEM_SPEC = pl.BlockSpec(memory_space=pltpu.VMEM)
ANY_SPEC = pl.BlockSpec(memory_space=pl.ANY)
DMA = pltpu.SemaphoreType.DMA
VMEM_LIMIT = 60 * 2**20
HALVES = 2


def params(collective_id=None):
    if collective_id is None:
        return pltpu.CompilerParams(vmem_limit_bytes=VMEM_LIMIT)
    return pltpu.CompilerParams(
        collective_id=collective_id, has_side_effects=True, vmem_limit_bytes=VMEM_LIMIT
    )


def remote(src, dst, send_sem, recv_sem, device):
    return pltpu.make_async_remote_copy(
        src_ref=src,
        dst_ref=dst,
        send_sem=send_sem,
        recv_sem=recv_sem,
        device_id=device,
        device_id_type=MESH,
    )


class Place:
    def __init__(self, n):
        self.s = lax.axis_index("section")
        self.c = lax.axis_index("ctx")
        self.h = lax.axis_index("shard")
        self.n = n
        self.zn = n // 2
        self.y = lax.rem(self.h, 2)
        self.z = lax.div(self.h, 2)
        self.far_y = self.y + self.c - 2 * self.y * self.c

    def flip(self, k):
        found = self.z
        for bit in range(self.zn.bit_length()):
            if k >> bit & 1:
                found = found + (1 - 2 * lax.rem(self.z // 2**bit, 2)) * 2**bit
        return found

    def dev(self, z, y):
        return (self.s, self.c, z * 2 + y)

    @property
    def pair(self):
        return self.dev(self.z, 1 - self.y)

    @property
    def above(self):
        return self.dev(self.z + 1, self.y)

    @property
    def below(self):
        return self.dev(self.z - 1, self.y)

    @property
    def over(self):
        return (1 - self.s, self.c, self.h)

    @property
    def sibling(self):
        return (self.s, 1 - self.c, self.h)


def greet(p, line=False, spread=False, over=False, sibling=False):
    bar = pltpu.get_barrier_semaphore()
    peers = 0

    def signal(device):
        pl.semaphore_signal(bar, inc=1, device_id=device, device_id_type=MESH)

    if line:
        signal(p.pair)

        @pl.when(p.z < p.zn - 1)
        def _():
            signal(p.above)

        @pl.when(p.z > 0)
        def _():
            signal(p.below)

        peers = 1 + (p.z + p.zn - 1) // p.zn + (2 * p.zn - 2 - p.z) // p.zn
    if spread:
        for dz in range(1, p.zn):
            signal(p.dev(lax.rem(p.z + dz, p.zn), p.far_y))

        @pl.when(p.c == 1)
        def _():
            signal(p.dev(p.z, p.far_y))

        peers = peers + p.zn - 1 + p.c
    if over:
        signal(p.over)
        peers = peers + 1
    if sibling:
        signal(p.sibling)
        peers = peers + 1
    pl.semaphore_wait(bar, peers)


class Gather:
    def __init__(self, p, own_ref, out_ref, ss, rs, ls):
        self.p, self.own_ref, self.out_ref = p, own_ref, out_ref
        self.ss, self.rs, self.ls = ss, rs, ls
        self.hr = own_ref.shape[0] // HALVES

    def blk(self, half, zz, yy):
        row = (half * self.p.n + zz * 2 + yy) * self.hr
        return self.out_ref.at[pl.ds(pl.multiple_of(row, 16), self.hr)]

    def own(self, half):
        return self.own_ref.at[pl.ds(half * self.hr, self.hr)]

    def up(self, t, half, src):
        p = self.p
        sems = (self.ss.at[0, t, half], self.rs.at[0, t, half])
        return remote(src, self.blk(half, p.z - (t - 1), p.y), *sems, p.above)

    def down(self, t, half, src):
        p = self.p
        sems = (self.ss.at[1, t, half], self.rs.at[1, t, half])
        return remote(src, self.blk(half, p.z + (t - 1), p.y), *sems, p.below)

    def across(self, kind, t, half, zz, src):
        p = self.p
        sems = (self.ss.at[2 + kind, t, half], self.rs.at[2 + kind, t, half])
        return remote(src, self.blk(half, zz, p.y), *sems, p.pair)

    def local(self, half):
        p = self.p
        return pltpu.make_async_copy(
            self.own(half), self.blk(half, p.z, p.y), self.ls.at[half]
        )

    def start(self, halves=range(HALVES)):
        p = self.p
        for half in halves:
            src = self.own(half)

            @pl.when(p.z < p.zn - 1)
            def _():
                self.up(1, half, src).start()

            @pl.when(p.z > 0)
            def _():
                self.down(1, half, src).start()

            self.across(0, 0, half, p.z, src).start()
            self.local(half).start()

    def step(self, t, half):
        p = self.p
        z, zn = p.z, p.zn

        @pl.when(z >= t)
        def _():
            block = self.blk(half, z - t, p.y)
            self.up(t, half, block).wait_recv()
            if t < zn - 1:

                @pl.when(z < zn - 1)
                def _():
                    self.up(t + 1, half, block).start()

            self.across(0, t, half, z - t, block).start()

        @pl.when(z <= zn - 1 - t)
        def _():
            block = self.blk(half, z + t, p.y)
            self.down(t, half, block).wait_recv()
            if t < zn - 1:

                @pl.when(z > 0)
                def _():
                    self.down(t + 1, half, block).start()

            self.across(1, t, half, z + t, block).start()

    def steps(self):
        return [
            functools.partial(self.step, t, half)
            for t in range(1, self.p.zn)
            for half in range(HALVES)
        ]

    def finish(self):
        p = self.p
        z, zn = p.z, p.zn
        for half in range(HALVES):
            self.across(0, 0, half, z, self.own(half)).wait_recv()
            for t in range(1, zn):

                @pl.when(z >= t)
                def _():
                    self.across(0, t, half, z - t, self.own(half)).wait_recv()

                @pl.when(z <= zn - 1 - t)
                def _():
                    self.across(1, t, half, z + t, self.own(half)).wait_recv()

        for half in range(HALVES):
            self.local(half).wait()
            self.across(0, 0, half, z, self.own(half)).wait_send()
            for t in range(1, zn):

                @pl.when((z < zn - 1) & (z >= t - 1))
                def _():
                    self.up(t, half, self.own(half)).wait_send()

                @pl.when((z > 0) & (z <= zn - t))
                def _():
                    self.down(t, half, self.own(half)).wait_send()

                @pl.when(z >= t)
                def _():
                    self.across(0, t, half, z - t, self.own(half)).wait_send()

                @pl.when(z <= zn - 1 - t)
                def _():
                    self.across(1, t, half, z + t, self.own(half)).wait_send()


class Scatter:
    def __init__(self, p, part_ref, ybuf, rbuf, sbuf, ss, rs):
        self.p, self.part_ref = p, part_ref
        self.ybuf, self.rbuf, self.sbuf, self.ss, self.rs = ybuf, rbuf, sbuf, ss, rs
        self.hr = ybuf.shape[2]

    def blk(self, half, zz, yy):
        row = (half * self.p.n + zz * 2 + yy) * self.hr
        return self.part_ref.at[pl.ds(pl.multiple_of(row, 16), self.hr)]

    def goal(self, k, t):
        return self.p.z + t if k == 0 else self.p.z - t

    def across(self, k, t, half):
        p = self.p
        zz = self.goal(k, t)
        sems = (self.ss.at[k, t, half], self.rs.at[k, t, half])
        return remote(self.blk(half, zz, 1 - p.y), self.ybuf.at[zz, half], *sems, p.pair)

    def along(self, k, t, half, slot):
        p = self.p
        zz = self.goal(k, t)
        sems = (self.ss.at[2 + k, t, half], self.rs.at[2 + k, slot, half])
        target = p.above if k == 0 else p.below
        return remote(self.sbuf.at[zz, half], self.rbuf.at[zz + 1 - k, half], *sems, target)

    def ok(self, k, t):
        return self.p.z <= self.p.zn - 1 - t if k == 0 else self.p.z >= t

    def has(self, k):
        return self.p.z > 0 if k == 0 else self.p.z < self.p.zn - 1

    def start(self):
        for t in range(self.p.zn - 1, 0, -1):
            for half in range(HALVES):
                for k in range(2):

                    @pl.when(self.ok(k, t))
                    def _():
                        self.across(k, t, half).start()

        for half in range(HALVES):
            self.across(0, 0, half).start()

    def step(self, t, half, k):
        p = self.p
        zz = self.goal(k, t)

        @pl.when(self.ok(k, t))
        def _():
            self.across(k, t, half).wait_recv()
            total = self.blk(half, zz, p.y)[...].astype(F32)
            total = total + self.ybuf[zz, half].astype(F32)
            if t < p.zn - 1:

                @pl.when(self.has(k))
                def _():
                    self.along(k, t, half, t).wait_recv()
                    more = total + self.rbuf[zz + 1 - k, half].astype(F32)
                    self.sbuf[zz, half] = more.astype(BF16)

                @pl.when(jnp.logical_not(self.has(k)))
                def _():
                    self.sbuf[zz, half] = total.astype(BF16)

            else:
                self.sbuf[zz, half] = total.astype(BF16)
            self.along(k, t, half, t - 1).start()

    def steps(self):
        return [
            functools.partial(self.step, t, half, k)
            for t in range(self.p.zn - 1, 0, -1)
            for half in range(HALVES)
            for k in range(2)
        ]

    def result(self, half):
        p = self.p
        z = p.z
        self.across(0, 0, half).wait_recv()
        for k in range(2):

            @pl.when(self.has(k))
            def _():
                self.along(k, 0, half, 0).wait_recv()

            @pl.when(jnp.logical_not(self.has(k)))
            def _():
                self.rbuf[z + 1 - k, half] = jnp.zeros(self.rbuf.shape[2:], BF16)

        total = self.blk(half, z, p.y)[...].astype(F32) + self.ybuf[z, half].astype(F32)
        return total + self.rbuf[z + 1, half].astype(F32) + self.rbuf[z, half].astype(F32)

    def finish(self):
        for half in range(HALVES):
            self.across(0, 0, half).wait_send()
            for t in range(1, self.p.zn):
                for k in range(2):

                    @pl.when(self.ok(k, t))
                    def _():
                        self.across(k, t, half).wait_send()
                        self.along(k, t, half, t - 1).wait_send()


class Spread:
    def __init__(self, p, src, dst, ss, rs, ls):
        self.p, self.src, self.dst, self.ss, self.rs, self.ls = p, src, dst, ss, rs, ls

    def source(self, dz):
        return self.p.flip(dz) * 2 + self.p.far_y

    def out(self, dz):
        p = self.p
        target = self.source(dz)
        sems = (self.ss.at[0, dz], self.rs.at[0, dz])
        return remote(self.src.at[target], self.dst.at[p.s, p.h], *sems, (p.s, p.c, target))

    def aside(self, dz):
        block = self.dst.at[self.p.s, self.source(dz)]
        return remote(block, block, self.ss.at[1, dz], self.rs.at[1, dz], self.p.sibling)

    def cross(self, dz):
        block = self.dst.at[self.p.s, self.source(dz)]
        return remote(block, block, self.ss.at[2, dz], self.rs.at[2, dz], self.p.over)

    def cross_own(self):
        p = self.p
        sems = (self.ss.at[2, 0], self.rs.at[2, 0])
        return remote(self.src.at[p.h], self.dst.at[p.s, p.h], *sems, p.over)

    def cross_aside(self, dz):
        block = self.dst.at[1 - self.p.s, self.source(dz)]
        return remote(block, block, self.ss.at[3, dz], self.rs.at[3, dz], self.p.sibling)

    def local(self):
        p = self.p
        return pltpu.make_async_copy(self.src.at[p.h], self.dst.at[p.s, p.h], self.ls)

    def start(self):
        @pl.when(self.p.c == 1)
        def _():
            self.out(0).start()

        @pl.when(self.p.c == 0)
        def _():
            self.cross_own().start()

        for dz in range(1, min(3, self.p.zn)):
            self.out(dz).start()
        self.local().start()

    def arrived(self, dz):
        if 3 <= dz + 2 < self.p.zn:
            self.out(dz + 1).wait_send()
            self.out(dz + 2).start()
        self.out(dz).wait_recv()
        self.cross(dz).start()
        self.aside(dz).start()

    def crossed(self, dz):
        self.cross(dz).wait_recv()
        self.cross_aside(dz).start()

    def first(self):
        @pl.when(self.p.c == 1)
        def _():
            self.arrived(0)

    def steps(self):
        found = [self.first]
        found += [functools.partial(self.arrived, dz) for dz in range(1, self.p.zn)]
        return found + [functools.partial(self.crossed, dz) for dz in range(self.p.zn)]

    def finish(self):
        self.local().wait()

        @pl.when(self.p.c == 0)
        def _():
            self.aside(0).wait_recv()
            self.cross_own().wait_send()

        @pl.when(self.p.c == 1)
        def _():
            self.out(0).wait_send()
            self.aside(0).wait_send()
            self.cross(0).wait_send()

        for dz in range(self.p.zn):
            if dz:
                self.aside(dz).wait_recv()
                self.aside(dz).wait_send()
                if dz == 1 or dz == self.p.zn - 1:
                    self.out(dz).wait_send()
                self.cross(dz).wait_send()
            self.cross_aside(dz).wait_recv()
            self.cross_aside(dz).wait_send()


class RowSwap:
    def __init__(self, p, src, dst, ss, rs, ls):
        self.p, self.src, self.dst, self.ss, self.rs, self.ls = p, src, dst, ss, rs, ls
        self.split = src.shape[0] % 32 == 0

    def piece(self, which):
        count = self.src.shape[0]
        if not self.split:
            return self.src, self.dst.at[which, pl.ds(0, count)]
        half = count // 2
        rows = pl.ds(pl.multiple_of(self.p.c * half, 16), half)
        return self.src.at[rows], self.dst.at[which, rows]

    def cross(self):
        src, dst = self.piece(self.p.s)
        return remote(src, dst, self.ss.at[0], self.rs.at[0], self.p.over)

    def aside(self):
        block = self.piece(1 - self.p.s)[1]
        return remote(block, block, self.ss.at[1], self.rs.at[1], self.p.sibling)

    def local(self):
        rows = pl.ds(0, self.src.shape[0])
        return pltpu.make_async_copy(self.src, self.dst.at[self.p.s, rows], self.ls)

    def start(self):
        self.cross().start()
        self.local().start()

    def step(self):
        self.cross().wait_recv()
        if self.split:
            self.aside().start()

    def finish(self):
        self.local().wait()
        self.cross().wait_send()
        if self.split:
            self.aside().wait_recv()
            self.aside().wait_send()


class Cross:
    def __init__(self, p, src, dst, ss, rs, source):
        self.p, self.source = p, source
        self.copy = remote(src, dst, ss, rs, p.over)

    def start(self):
        @pl.when(self.p.s == self.source)
        def _():
            self.copy.start()

    def finish(self):
        @pl.when(self.p.s == self.source)
        def _():
            self.copy.wait_send()

        @pl.when(self.p.s != self.source)
        def _():
            self.copy.wait_recv()


class Home:
    def __init__(self, p, src, dst, ss, rs, ls):
        self.p, self.src, self.dst, self.ss, self.rs, self.ls = p, src, dst, ss, rs, ls

    def send(self, k):
        p = self.p
        far = p.flip(k)
        target = (p.s, p.c, far * 2 + p.far_y)
        sems = (self.ss.at[0, k], self.rs.at[0, k])
        return remote(self.src.at[far], self.dst.at[p.h], *sems, target)

    def keep(self):
        return pltpu.make_async_copy(self.src.at[self.p.z], self.dst.at[self.p.h], self.ls)

    def aside(self, k):
        block = self.dst.at[self.p.flip(k) * 2 + self.p.far_y]
        return remote(block, block, self.ss.at[1, k], self.rs.at[1, k], self.p.sibling)

    def start(self, k):
        if k:
            self.send(k).start()
            return

        @pl.when(self.p.c == 1)
        def _():
            self.send(0).start()

        @pl.when(self.p.c == 0)
        def _():
            self.keep().start()

    def arrived(self, k):
        if k:
            self.send(k).wait_recv()
        else:

            @pl.when(self.p.c == 1)
            def _():
                self.send(0).wait_recv()

            @pl.when(self.p.c == 0)
            def _():
                self.keep().wait()

        self.aside(k).start()

    def steps(self):
        return [functools.partial(self.arrived, k) for k in range(self.p.zn)]

    def finish(self):
        @pl.when(self.p.c == 1)
        def _():
            self.send(0).wait_send()

        for k in range(self.p.zn):
            if k:
                self.send(k).wait_send()
            self.aside(k).wait_recv()
            self.aside(k).wait_send()


def add_home(p, to, index, first, first_came, second, second_came):
    pairs = ((first, first_came), (second, second_came))
    for section, (own, came) in enumerate(pairs):

        @pl.when(p.s == section)
        def _():
            to[index] = (own[index].astype(F32) + came[index].astype(F32)).astype(BF16)


class Fold:
    def __init__(self, p, src, came, out, ss, rs):
        self.p, self.src, self.came, self.out, self.ss, self.rs = p, src, came, out, ss, rs
        self.count = out.shape[0]
        self.size = out.shape[1]

    def rows(self, item, near):
        p = self.p
        if self.count == 1:
            index = 1 - p.c if near else p.c
        else:
            index = item * 2 + (1 - p.far_y if near else p.far_y)
        return pl.ds(pl.multiple_of(index * self.size, 16), self.size)

    def copy(self, item):
        src = self.src.at[self.rows(item, True)]
        sems = (self.ss.at[item], self.rs.at[item])
        return remote(src, self.came.at[item], *sems, self.p.sibling)

    def start(self):
        for item in range(self.count):
            self.copy(item).start()

    def step(self, item):
        self.copy(item).wait_recv()
        own = self.src[self.rows(item, False)].astype(F32)
        self.out[item] = (own + self.came[item].astype(F32)).astype(BF16)

    def steps(self):
        return [functools.partial(self.step, item) for item in range(self.count)]

    def finish(self):
        for item in range(self.count):
            self.copy(item).wait_send()


def fold_scratch(source, out):
    return [pltpu.VMEM(source, BF16), pltpu.VMEM(out, BF16), DMA((out[0],)), DMA((out[0],))]


def product(a_ref, b_ref, to_ref):
    rows = to_ref.shape[0]

    def step(first, size):
        found = lax.dot_general(
            a_ref[:, first : first + size],
            b_ref[...],
            (((0,), (0,)), ((), ())),
            preferred_element_type=F32,
        )
        to_ref[first : first + size] = found.astype(BF16)

    return [
        functools.partial(step, first, min(256, rows - first)) for first in range(0, rows, 256)
    ]


def home_rows(a_ref, b_ref, to_ref, low, share):
    found = lax.dot_general(
        a_ref[...], b_ref[...], (((0,), (0,)), ((), ())), preferred_element_type=F32
    )
    h = lax.axis_index("shard")
    shift = 0
    for j, first in enumerate(low):
        shift = shift + jnp.where(h == j, (HD * first - j * share) % found.shape[0], 0)
    to_ref[...] = pltpu.roll(found, shift, 0).astype(BF16)


def in_turn(steps, work, each=1):
    for step in steps:
        for _ in range(each):
            run_next(work)
        step()


def by_halves(scatter, gather, rows_step, work, each=1):
    in_turn(scatter.steps(), work, each)
    for half in range(HALVES):
        rows_step(half)
        if gather is not None:
            gather.start([half])
    if gather is not None:
        in_turn(gather.steps(), work, each)


def fetch(src, dst, sem):
    copy = pltpu.make_async_copy(src, dst, sem)
    copy.start()
    return copy


class Staging:
    def __init__(self):
        self.loads, self.stores, self.running = {}, {}, []

    def need(self, *items):
        for item in items:
            self.loads.pop(item).wait()

    def done(self, *items):
        for item in items:
            self.running.append(fetch(*self.stores.pop(item)))

    def end(self):
        self.done(*list(self.stores))
        for copy in self.running:
            copy.wait()


def staged_call(body, name, collective_id, args, shapes, scratch, late=(), plain=(), early=(), raw=()):
    late, early = tuple(late), tuple(early)
    n_in, n_out, n_scratch = len(args), len(shapes), len(scratch)

    def run(*refs):
        ins, outs = list(refs[:n_in]), list(refs[n_in : n_in + n_out])
        rest = refs[n_in + n_out :]
        own, rest = rest[:n_scratch], rest[n_scratch:]
        staged_in, rest = rest[: len(late)], rest[len(late) :]
        staged_out, sems = rest[: len(early)], rest[len(early) :]
        io = Staging()
        for x, item in enumerate(late):
            io.loads[item] = fetch(ins[item], staged_in[x], sems[0].at[x])
            ins[item] = staged_in[x]
        for x, item in enumerate(early):
            io.stores[item] = (staged_out[x], outs[item], sems[1].at[x])
            outs[item] = staged_out[x]
        body(io, *ins, *outs, *own)
        io.end()

    stages = [pltpu.VMEM(args[item].shape, args[item].dtype) for item in late]
    stages += [pltpu.VMEM(shapes[item].shape, shapes[item].dtype) for item in early]
    stages += [DMA((max(len(late), 1),)), DMA((max(len(early), 1),))]
    return pl.pallas_call(
        run,
        out_shape=shapes,
        in_specs=[ANY_SPEC if i in late + tuple(plain) else VMEM_SPEC for i in range(n_in)],
        out_specs=[ANY_SPEC if i in early + tuple(raw) else VMEM_SPEC for i in range(n_out)],
        scratch_shapes=list(scratch) + stages,
        compiler_params=params(collective_id),
        name=name,
    )(*args)


def row_blocks(rows, step):
    size = min(rows, 256)
    count = rows // size
    if count <= 2:
        for b in range(count):
            step(b * size, size)
    else:

        def body(b, carry):
            step(pl.multiple_of(b * size, size), size)
            return carry

        lax.fori_loop(0, count, body, 0)


def gelu_parts(values):
    square = values * values
    return jnp.tanh(GELU_A * (values + GELU_B * values * square)), square


def greet_all(p):
    bar = pltpu.get_barrier_semaphore()
    for a in range(2):
        for b in range(p.n):
            if (a, b) != (0, 0):
                other = (lax.rem(p.s + a, 2), p.c, lax.rem(p.h + b, p.n))
                pl.semaphore_signal(bar, inc=1, device_id=other, device_id_type=MESH)
    pl.semaphore_signal(bar, inc=1, device_id=p.sibling, device_id_type=MESH)
    pl.semaphore_wait(bar, 2 * p.n)


def others(n):
    return [(a, b) for a in range(2) for b in range(n) if (a, b) != (0, 0)]


def with_gaps(values, n, padded):
    rows, width = values.shape
    share = width // n
    pieces = []
    for j in range(n):
        pieces.append(values[:, j * share : (j + 1) * share])
        if padded > share:
            pieces.append(jnp.zeros((rows, padded - share), values.dtype))
    return jnp.concatenate(pieces, axis=1)


def lay_vectors(vectors, pack_to):
    lanes = pack_to.shape[1]
    members = []
    for ref in vectors:
        member = ref[...].astype(F32)
        members.append(
            jnp.concatenate([member, jnp.zeros((1, lanes - member.shape[1]), F32)], axis=1)
        )
    members.append(jnp.zeros((8, lanes), F32))
    pack_to[...] = jnp.concatenate(members, axis=0).astype(BF16)


def lay_first(low, qkv_ref, qkv_to):
    n, padded, triple = qkv_to.shape
    share = qkv_ref.shape[0]
    width = qkv_ref.shape[1] // 3
    sh = triple // 3
    for j in range(n):
        for t in range(3):
            first = t * width + HD * low[j]
            qkv_to[j, :share, t * sh : (t + 1) * sh] = qkv_ref[:, first : first + sh]
        if padded > share:
            qkv_to[j, share:] = jnp.zeros((padded - share, triple), BF16)


def lay_rows(low, out_ref, out_to):
    share = out_ref.shape[0]
    sh, full = out_to.shape
    n = len(low)
    h = lax.axis_index("shard")
    offset = 0
    for j in range(n):
        offset = offset + jnp.where(h == j, j * share - HD * low[j], 0)
    rows = with_gaps(out_ref[...].astype(F32), n, full // n)
    rows = jnp.concatenate([rows, jnp.zeros((sh - share, full), F32)], axis=0)
    out_to[...] = pltpu.roll(rows, offset, 0).astype(BF16)


def lay_widen(j, widen_ref, widen_to):
    n, padded, hide_full = widen_to.shape
    share, hidden = widen_ref.shape
    hide = hidden // n
    widen_to[j, :share, :hide] = widen_ref[:, j * hide : (j + 1) * hide]
    if hide_full > hide:
        widen_to[j, :share, hide:] = jnp.zeros((share, hide_full - hide), BF16)
    if padded > share:
        widen_to[j, share:] = jnp.zeros((padded - share, hide_full), BF16)


def lay_narrow(first, size, n, narrow_ref, narrow_to):
    rows = slice(first, first + size)
    narrow_to[rows] = with_gaps(narrow_ref[rows], n, narrow_to.shape[1] // n)


def spread_vectors(n, low, width, pack_all, feats_to, qkv_bias, widen_bias):
    h = lax.axis_index("shard")
    sh = qkv_bias.shape[2] // 3
    share = width // n
    padded = feats_to.shape[2] // n
    for layer in range(2):
        pieces = [pack_all[layer, j] for j in range(n)]
        feats_to[layer] = jnp.concatenate([m[:, :padded] for m in pieces], axis=1).astype(F32)
        bias = jnp.concatenate([m[6:7, : 2 * share] for m in pieces], axis=1).astype(F32)
        found = jnp.zeros((1, 2 * sh), F32)
        wide = jnp.zeros((1, widen_bias.shape[2]), F32)
        for j in range(n):
            first = HD * low[j]
            spots = [bias[:, k * width + first : k * width + first + sh] for k in range(2)]
            found = jnp.where(h == j, jnp.concatenate(spots, axis=1), found)
            own = pieces[j][7:8, : wide.shape[1]].astype(F32)
            wide = jnp.where(h == j, own, wide)
        qkv_bias[layer] = jnp.concatenate(
            [found[:, :sh], jnp.zeros((1, sh), F32), found[:, sh:]], axis=1
        )
        widen_bias[layer] = wide


def open_kernel(n, low, width, slots, step, io, *refs):
    tok_ref, cot_ref, vectors, refs = refs[0], refs[1], refs[2:10], refs[10:]
    qkv_ref, out_ref, widen_ref, narrow_ref, mask, kpos_ref, qpos_ref = refs[:7]
    refs = refs[7:]
    narrow_to, x_to, cot_to, grad_to, sums_to, normed_to, own_ref, qkv_all, out_all = refs[:9]
    feats_to, qkv_bias, widen_bias, att_ref, low_ref, lse_ref, oth_ref, part_to = refs[9:17]
    widen_all, refs = refs[17], refs[18:]
    tok_own, pack, qkv_send, out_rows, widen_raw, narrow_raw, widen_send = refs[:7]
    tok_all, pack_all, refs = refs[7], refs[8], refs[9:]
    g_ss, g_rs, g_ls, p_ss, p_rs, a_ss, a_rs, w_ss, w_rs, o_ss, o_rs, l_sem = refs[:12]
    kv_ss, kv_rs = refs[12:]
    p = Place(n)
    s, c, h = p.s, p.c, p.h
    widen_load = fetch(widen_ref, widen_raw, l_sem.at[4])
    narrow_load = fetch(narrow_ref, narrow_raw, l_sem.at[5])
    padded = qkv_send.shape[1]
    tok_own[...] = with_gaps(tok_ref[s], n, padded)
    greet_all(p)

    def pack_copy(a, b):
        target = (lax.rem(s + a, 2), c, lax.rem(h + b, n))
        return remote(pack, pack_all.at[s, h], p_ss.at[a, b], p_rs.at[a, b], target)

    tokens = Gather(p, tok_own, tok_all, g_ss, g_rs, g_ls)
    qkv = Spread(p, qkv_send, qkv_all, a_ss, a_rs, l_sem.at[1])
    widen = Spread(p, widen_send, widen_all, w_ss, w_rs, l_sem.at[3])
    out = RowSwap(p, out_rows, out_all, o_ss, o_rs, l_sem.at[2])
    pack_own = pltpu.make_async_copy(pack, pack_all.at[s, h], l_sem.at[0])
    tokens.start()
    io.need(10)
    lay_first(low, qkv_ref, qkv_send)
    qkv.start()
    lay_vectors(vectors, pack)
    for a, b in others(n):
        pack_copy(a, b).start()
    pack_own.start()

    def start_out():
        io.need(1, 11)
        lay_rows(low, out_ref, out_rows)
        out.start()

    def lay_cot():
        values = with_gaps(cot_ref[s], n, padded)
        cot_to[...] = values
        grad_to[...] = values.astype(F32)
        sums_to[...] = jnp.sum(grad_to[...], axis=0, keepdims=True)
        x_to[...] = tok_own[...].astype(F32)

    hide = narrow_ref.shape[0]
    work = [start_out, widen_load.wait]
    work += [functools.partial(lay_widen, j, widen_raw, widen_send) for j in range(n)]
    work += [lay_cot, narrow_load.wait]
    work += [
        functools.partial(lay_narrow, first, min(208, hide - first), n, narrow_raw, narrow_to)
        for first in range(0, hide, 208)
    ]
    qkv_steps = qkv.steps()
    for token_step in tokens.steps():
        run_next(work)
        run_next(work)
        token_step()
        run_next(qkv_steps)
    for rest in work:
        rest()
    extra = narrow_to.shape[0] - hide
    if extra:
        narrow_to[hide:] = jnp.zeros((extra, n * padded), BF16)
    io.done(0)
    tokens.finish()
    widen.start()
    pack_own.wait()
    for a, b in others(n):
        pack_copy(a, b).wait_recv()
    spread_vectors(n, low, width, pack_all, feats_to, qkv_bias, widen_bias)

    def first_norm(first, size):
        some = pl.ds(first, size)
        unit = unit_rows(tok_all[some].astype(F32), mask[...], width)[0]
        normed_to[some] = (unit * feats_to[0, 0:1] + feats_to[0, 1:2]).astype(BF16)

    rows = tok_all.shape[0]
    row_blocks(rows, first_norm)
    io.done(5)
    for rest in qkv_steps:
        rest()
    qkv.finish()
    io.done(7)
    sh = slots * HD

    def project(first, size):
        some = pl.ds(first, size)
        weight = qkv_all[0].reshape(n * padded, 3 * sh)
        own_ref[some] = (dot_n(normed_to[some], weight) + qkv_bias[0]).astype(BF16)

    row_blocks(rows, project)
    swap = remote(own_ref.at[:, pl.ds(sh, 2 * sh)], oth_ref, kv_ss, kv_rs, p.sibling)
    swap.start()
    swap.wait_recv()
    out.step()
    between = widen.steps()
    chunk = attention(slots, step, own_ref, oth_ref, kpos_ref, qpos_ref, att_ref, low_ref, lse_ref)
    in_blocks(rows, step, chunk, between)
    out.finish()
    io.done(6, 8, 12, 13, 15)

    def give(first, size):
        some = pl.ds(first, size)
        part_to[some] = dot_n(low_ref[some], out_all[0]).astype(BF16)

    row_blocks(rows, give)
    io.done(16)
    for rest in between:
        rest()
    for a, b in others(n):
        pack_copy(a, b).wait_send()
    swap.wait_send()
    widen.finish()


def open_call(n, low, slots, padded, tokens, cotangent, vectors, weights, mask, kpos, qpos):
    qkv, out, widen, narrow = weights
    share, hidden = widen.shape
    width = n * share
    hide = hidden // n
    hide_full = -(-hide // 128) * 128
    sh = slots * HD
    full = n * padded
    rows = tokens.shape[1]
    total = n * rows
    zn = n // 2
    lanes = max(hide_full, -(-2 * share // 128) * 128)
    blocks = (n, padded, 3 * sh)
    wide = (n, padded, hide_full)

    def low_type(*shape):
        return jax.ShapeDtypeStruct(shape, BF16)

    def full_type(*shape):
        return jax.ShapeDtypeStruct(shape, F32)

    return staged_call(
        functools.partial(open_kernel, n, low, width, slots, min(total, 256)),
        "open",
        0,
        (tokens, cotangent, *vectors, qkv, out, widen, narrow, mask, kpos, qpos),
        [
            low_type(-(-hide // 16) * 16, full),
            full_type(rows, full),
            low_type(rows, full),
            full_type(rows, full),
            full_type(1, full),
            low_type(total, full),
            low_type(total, 3 * sh),
            low_type(2, *blocks),
            low_type(2, sh, full),
            full_type(2, 16, full),
            full_type(2, 1, 3 * sh),
            full_type(2, 1, hide_full),
            full_type(sh, total),
            low_type(total, sh),
            full_type(slots, total),
            low_type(total, 2 * sh),
            low_type(total, full),
            low_type(2, *wide),
        ],
        [
            pltpu.VMEM((rows, full), BF16),
            pltpu.VMEM((16, lanes), BF16),
            pltpu.VMEM(blocks, BF16),
            pltpu.VMEM((sh, full), BF16),
            pltpu.VMEM(widen.shape, BF16),
            pltpu.VMEM(narrow.shape, BF16),
            pltpu.VMEM(wide, BF16),
            pltpu.VMEM((total, full), BF16),
            pltpu.VMEM((2, n, 16, lanes), BF16),
        ]
        + gather_scratch(n)
        + [DMA((2, n))] * 2
        + [DMA((4, zn))] * 4
        + [DMA((2,))] * 2
        + [DMA((6,)), DMA, DMA],
        late=(1, 10, 11),
        plain=(12, 13),
        early=(0, 5, 6, 7, 8, 12, 13, 15, 16),
        raw=(17,),
    )


def settle_kernel(low, sizes, *refs):
    sources, vec_ref, came_ref, streams, refs = refs[:4], refs[4], refs[5], refs[6:10], refs[10:]
    outs, stream_to, vectors, refs = refs[:4], refs[4:6], refs[6:14], refs[14:]
    loaded, made, in_sem, out_sem = refs[:4], refs[4:8], refs[8], refs[9]
    qkv_ref, widen_ref, out_ref, narrow_ref = loaded
    qkv_to, widen_to, out_to, narrow_to = made
    order = (3, 1, 0, 2)
    loads = {i: fetch(sources[i], loaded[i], in_sem.at[i]) for i in order}
    n, padded, _ = widen_ref.shape
    share = out_to.shape[0]
    hide = narrow_to.shape[0]
    width = qkv_to.shape[1] // 3
    sh = qkv_ref.shape[2] // 3
    s = lax.axis_index("section")

    def without_gaps(values):
        pieces = [values[:, j * padded : j * padded + share] for j in range(n)]
        return jnp.concatenate(pieces, axis=1)

    def lay_rows_back(ref, to):
        to[...] = without_gaps(ref[: to.shape[0]].astype(F32))

    def lay_qkv_back():
        qkv_to[...] = jnp.zeros_like(qkv_to)
        for j in range(n):
            for t in range(3):
                first = t * width + HD * low[j]
                block = qkv_ref[j, :share, t * sh : (t + 1) * sh]
                qkv_to[:, first : first + sh] += block.astype(F32)

    def lay_widen_back():
        for j in range(n):
            widen_to[:, j * hide : (j + 1) * hide] = widen_ref[j, :share, :hide].astype(F32)

    makers = (
        lay_qkv_back,
        lay_widen_back,
        functools.partial(lay_rows_back, out_ref, out_to),
        functools.partial(lay_rows_back, narrow_ref, narrow_to),
    )
    for item, to in enumerate(stream_to):
        first, second = (ref[...] for ref in streams[2 * item : 2 * item + 2])
        to[s] = without_gaps(jnp.where(s == 0, first, second))
        to[1 - s] = without_gaps(came_ref[item].astype(F32))
    for row, (size, to) in enumerate(zip(sizes, vectors)):
        to[...] = vec_ref[row : row + 1, :size]
    stores = []
    for i in order:
        loads[i].wait()
        makers[i]()
        stores.append(fetch(made[i], outs[i], out_sem.at[i]))
    for store in stores:
        store.wait()


def settle_call(low, share, hide, qkv, widen, out, narrow, vec, came, *streams):
    n = widen.shape[0]
    width = n * share
    rows = came.shape[1]
    sizes = [share] * 6 + [2 * share, hide]
    big = [(share, 3 * width), (share, n * hide), (share, width), (hide, width)]
    return pl.pallas_call(
        functools.partial(settle_kernel, low, sizes),
        out_shape=[jax.ShapeDtypeStruct(shape, F32) for shape in big]
        + [
            jax.ShapeDtypeStruct((2, rows, width), F32),
            jax.ShapeDtypeStruct((2, rows, width), F32),
        ]
        + [jax.ShapeDtypeStruct((1, size), F32) for size in sizes],
        in_specs=[ANY_SPEC] * 4 + [VMEM_SPEC] * 6,
        out_specs=[ANY_SPEC] * 4 + [VMEM_SPEC] * 10,
        scratch_shapes=[pltpu.VMEM(m.shape, BF16) for m in (qkv, widen, out, narrow)]
        + [pltpu.VMEM(shape, F32) for shape in big]
        + [DMA((4,)), DMA((4,))],
        compiler_params=params(),
        name="settle",
    )(qkv, widen, out, narrow, vec, came, *streams)


def unit_rows(values, mask, width):
    center = (values - jnp.sum(values, axis=-1, keepdims=True) * (1.0 / width)) * mask
    spread = jnp.sum(center * center, axis=-1, keepdims=True) * (1.0 / width)
    scale = lax.rsqrt(spread + EPSILON)
    return center * scale, scale


def norm_back(grad, unit, scale, gain, width):
    inner = grad * gain
    mean = jnp.sum(inner, axis=-1, keepdims=True) * (1.0 / width)
    along = jnp.sum(inner * unit, axis=-1, keepdims=True) * (1.0 / width)
    return (inner - mean - unit * along) * scale


def forward_kernel(n, width, layer, side, io, *refs):
    middle = layer is not None
    part, base, feats, mask = refs[:4]
    refs = refs[4:]
    if middle:
        bias, gain, shift = (feats[layer, row : row + 1] for row in (2, 3, 4))
        widen_all, narrow_in, widen_bias, refs = refs[0], refs[1], refs[2], refs[3:]
    else:
        bias, gain, shift = feats[0, 5:6], feats[1, 0:1], feats[1, 1:2]
    value_to, low_all, refs = refs[0], refs[1], refs[2:]
    if middle:
        pre_to, hidden_to, part_to, refs = refs[0], refs[1], refs[2], refs[3:]
    if side:
        side_out, refs = refs[0], refs[1:]
    own, g_ss, g_rs, g_ls = refs[5:9]
    p = Place(n)
    greet(p, line=True, over=side, sibling=side)
    scatter = Scatter(p, part, *refs[:5])
    scatter.start()
    loads = []
    if middle:
        widen, load_sems, rest = refs[9], refs[10], refs[11:]
        loads.append(fetch(widen_all.at[layer], widen, load_sems.at[0]))
        if side:
            io.need(5)
            job = RowSwap(p, narrow_in, side_out, *rest)
            job.start()
            filled = narrow_in.shape[0]
            for member in range(2):
                if side_out.shape[1] > filled:
                    spare = (side_out.shape[1] - filled, side_out.shape[2])
                    side_out[member, filled:] = jnp.zeros(spare, BF16)
            narrow = side_out.at[layer]
        else:
            narrow = rest[0]
            loads.append(fetch(narrow_in.at[layer], narrow, load_sems.at[1]))
    gather = Gather(p, own, low_all, g_ss, g_rs, g_ls)
    hr = own.shape[0] // HALVES

    def rows_step(half):
        rows = slice(half * hr, (half + 1) * hr)
        value = base[rows] + (scatter.result(half) + bias)
        value_to[rows] = value
        own[rows] = (unit_rows(value, mask[...], width)[0] * gain + shift).astype(BF16)

    by_halves(scatter, gather, rows_step, [])
    if side:
        job.step()
    gather.finish()
    for load in loads:
        load.wait()
    if side:
        job.finish()
        io.done(5)
    if middle:
        io.done(1)

        def block(first, size):
            rows = pl.ds(first, size)
            weight = widen[...].reshape(low_all.shape[1], widen.shape[2])
            pre = dot_n(low_all[rows], weight) + widen_bias[layer]
            pre_to[rows] = pre
            hidden = (0.5 * pre * (1.0 + gelu_parts(pre)[0])).astype(BF16)
            hidden_to[rows] = hidden
            part_to[rows] = dot_n(hidden, narrow[...]).astype(BF16)

        row_blocks(low_all.shape[0], block)
    scatter.finish()


def scatter_scratch(n, rows, full):
    zn = n // 2
    piece = (HALVES, rows // HALVES, full)
    return [
        pltpu.VMEM((zn,) + piece, BF16),
        pltpu.VMEM((zn + 1,) + piece, BF16),
        pltpu.VMEM((zn,) + piece, BF16),
        DMA((4, zn, HALVES)),
        DMA((4, zn, HALVES)),
    ]


def gather_scratch(n):
    zn = n // 2
    return [DMA((4, zn, HALVES)), DMA((4, zn, HALVES)), DMA((HALVES,))]


def forward_call(n, collective_id, width, part, *local, layer=None, feed=(), carry=False):
    total_rows, full = part.shape
    rows = total_rows // n
    shapes = [
        jax.ShapeDtypeStruct((rows, full), F32),
        jax.ShapeDtypeStruct((total_rows, full), BF16),
    ]
    scratch = scatter_scratch(n, rows, full)
    scratch += [pltpu.VMEM((rows, full), BF16)] + gather_scratch(n)
    if layer is not None:
        widen, narrow, _ = feed
        hide = widen.shape[3]
        shapes += [
            jax.ShapeDtypeStruct((total_rows, hide), F32),
            jax.ShapeDtypeStruct((total_rows, hide), BF16),
            jax.ShapeDtypeStruct((total_rows, full), BF16),
        ]
        scratch += [pltpu.VMEM(widen.shape[1:], BF16), DMA((2,))]
        if carry:
            shapes.append(jax.ShapeDtypeStruct((2, hide, full), BF16))
            scratch += [DMA((2,)), DMA((2,)), DMA]
        else:
            scratch.append(pltpu.VMEM((hide, full), BF16))
    middle = layer is not None
    return staged_call(
        functools.partial(forward_kernel, n, width, layer, carry),
        "forward_rows",
        collective_id,
        (part, *local, *feed),
        shapes,
        scratch,
        late=(5,) if carry else (),
        plain=((4,) if carry else (4, 5)) if middle else (),
        early=((1, 2, 3, 4, 5) if carry else (1, 2, 3, 4)) if middle else (),
        raw=() if middle else (1,),
    )


def back_rows(scatter, half, base, grad, gain, mask, width):
    hr = scatter.hr
    rows = slice(half * hr, (half + 1) * hr)
    total = scatter.result(half)
    unit, scale = unit_rows(base[rows], mask[...], width)
    value = grad[rows] + norm_back(total, unit, scale, gain, width)
    low = value.astype(BF16)
    terms = (total * unit, total, low.astype(F32))
    return rows, value, low, [jnp.sum(term, axis=0, keepdims=True) for term in terms]


def resid_kernel(n, width, layer, io, *refs):
    base, grad, feats, mask, normed, hidden_pre, hidden, outs, widen_all, narrow_all = refs[:10]
    gain = feats[layer, 3:4]
    value_to, sums_to, low_all, wide_to, wide_came, slim_to, pre_sums = refs[10:17]
    refs = refs[17:]
    own, g_ss, g_rs, g_ls = refs[5:9]
    wide, wide_in, wide_ss, wide_rs, slim, slim_in, slim_ss, slim_rs, x_ss, x_rs = refs[9:19]
    part, pre, widen, narrow, load_sems = refs[19:]
    p = Place(n)
    loads = [
        fetch(narrow_all.at[layer], narrow, load_sems.at[0]),
        fetch(widen_all.at[layer], widen, load_sems.at[1]),
    ]
    greet(p, line=True, over=True, sibling=True)
    for load in loads:
        load.wait()
    io.need(5, 7)

    def block(first, size):
        rows = pl.ds(first, size)
        values = hidden_pre[rows]
        act, square = gelu_parts(values)
        slope = 0.5 * (1.0 + act) + 0.5 * values * (1.0 - act * act) * GELU_A * (
            1.0 + 3.0 * GELU_B * square
        )
        found = (dot_t(outs[rows], narrow[...]) * slope).astype(BF16)
        pre[rows] = found
        weight = widen[...].reshape(part.shape[1], widen.shape[2])
        part[rows] = dot_t(found, weight).astype(BF16)

    row_blocks(part.shape[0], block)
    scatter = Scatter(p, part, *refs[:5])
    scatter.start()
    gather = Gather(p, own, low_all, g_ss, g_rs, g_ls)
    wide_fold = Fold(p, wide, wide_in, wide_to, wide_ss, wide_rs)
    slim_fold = Fold(p, slim, slim_in, slim_to, slim_ss, slim_rs)
    cross = Cross(p, wide_to, wide_came, x_ss, x_rs, 1 - layer)

    def pre_sum():
        pre_sums[...] = jnp.sum(pre[...].astype(F32), axis=0, keepdims=True)

    io.need(4, 6)
    for step in product(normed, pre, wide):
        step()
    wide_fold.start()

    def wide_done():
        cross.start()
        io.done(3)

    work = product(hidden, outs, slim) + wide_fold.steps() + [wide_done, slim_fold.start, pre_sum]
    work += slim_fold.steps() + [functools.partial(io.done, 5)]
    sums = []

    def rows_step(half):
        rows, value, low, terms = back_rows(scatter, half, base, grad, gain, mask, width)
        value_to[rows] = value
        own[rows] = low
        sums.append(jnp.concatenate(terms, axis=0))

    by_halves(scatter, gather, rows_step, work, 3)
    sums_to[...] = sum(sums)
    for rest in work:
        rest()
    gather.finish()
    scatter.finish()
    for job in (wide_fold, slim_fold, cross):
        job.finish()


def resid_call(n, collective_id, width, layer, hide, *args):
    base, normed, hidden = args[0], args[4], args[6]
    widen, narrow = args[8:]
    rows = base.shape[0]
    total_rows, full = normed.shape
    zn = n // 2
    wide = (zn, full // n, hidden.shape[1])
    half = -(-hide // 32) * 16
    slim = (1, half, full)
    return staged_call(
        functools.partial(resid_kernel, n, width, layer),
        "back_resid",
        collective_id,
        args,
        [
            jax.ShapeDtypeStruct((rows, full), F32),
            jax.ShapeDtypeStruct((3, full), F32),
            jax.ShapeDtypeStruct((total_rows, full), BF16),
            jax.ShapeDtypeStruct(wide, BF16),
            jax.ShapeDtypeStruct(wide, BF16),
            jax.ShapeDtypeStruct(slim, BF16),
            jax.ShapeDtypeStruct((1, hidden.shape[1]), F32),
        ],
        scatter_scratch(n, rows, full)
        + [pltpu.VMEM((rows, full), BF16)]
        + gather_scratch(n)
        + fold_scratch((full, hidden.shape[1]), wide)
        + fold_scratch((2 * half, full), slim)
        + [DMA, DMA]
        + [
            pltpu.VMEM((total_rows, full), BF16),
            pltpu.VMEM(hidden.shape, BF16),
            pltpu.VMEM(widen.shape[1:], BF16),
            pltpu.VMEM(narrow.shape[1:], BF16),
            DMA((2,)),
        ],
        late=(4, 5, 6, 7),
        plain=(8, 9),
        early=(3, 5),
        raw=(2, 4),
    )


def input_kernel(n, width, source, low, io, *refs):
    part, base, grad, feats, mask, normed, triple, att, resid, slim = refs[:10]
    gain = feats[1, 0:1]
    value_to, sums_to, low_all, qkv_to, out_to, slim_came, triple_sums = refs[10:17]
    refs = refs[17:]
    own, g_ss, g_rs, g_ls = refs[5:9]
    qkv, qkv_in, qkv_ss, qkv_rs, out, out_in, out_ss, out_rs, x_ss, x_rs = refs[9:]
    p = Place(n)
    greet(p, line=True, over=True, sibling=True)
    scatter = Scatter(p, part, *refs[:5])
    scatter.start()
    cross = Cross(p, slim, slim_came, x_ss, x_rs, source)
    cross.start()
    gather = Gather(p, own, low_all, g_ss, g_rs, g_ls)
    qkv_fold = Fold(p, qkv, qkv_in, qkv_to, qkv_ss, qkv_rs)
    out_fold = Fold(p, out, out_in, out_to, out_ss, out_rs)

    def triple_sum():
        triple_sums[...] = jnp.sum(triple[...].astype(F32), axis=0, keepdims=True)

    work = [functools.partial(io.need, 5, 6)] + product(normed, triple, qkv)
    work += [qkv_fold.start, functools.partial(io.need, 7, 8)]
    work += [functools.partial(home_rows, att, resid, out, low, width // n), out_fold.start]
    work += qkv_fold.steps() + [functools.partial(io.done, 3), triple_sum]
    work += out_fold.steps() + [functools.partial(io.done, 4)]
    sums = []

    def rows_step(half):
        rows, value, lower, terms = back_rows(scatter, half, base, grad, gain, mask, width)
        value_to[rows] = value
        own[rows] = lower
        sums.append(jnp.concatenate(terms, axis=0))

    by_halves(scatter, gather, rows_step, work, 2)
    sums_to[...] = sum(sums)
    for rest in work:
        rest()
    gather.finish()
    scatter.finish()
    for job in (qkv_fold, out_fold, cross):
        job.finish()


def input_call(n, collective_id, width, source, low, part, base, grad, feats, mask, *operands):
    normed, triple, att, resid, slim = operands
    total_rows, full = part.shape
    rows = total_rows // n
    zn = n // 2
    qkv = (zn, full // n, triple.shape[1])
    out = (1, att.shape[1] // 2, full)
    return staged_call(
        functools.partial(input_kernel, n, width, source, low),
        "back_input",
        collective_id,
        (part, base, grad, feats, mask) + operands,
        [
            jax.ShapeDtypeStruct((rows, full), F32),
            jax.ShapeDtypeStruct((3, full), F32),
            jax.ShapeDtypeStruct((total_rows, full), BF16),
            jax.ShapeDtypeStruct(qkv, BF16),
            jax.ShapeDtypeStruct(out, BF16),
            jax.ShapeDtypeStruct(slim.shape, BF16),
            jax.ShapeDtypeStruct((1, triple.shape[1]), F32),
        ],
        scatter_scratch(n, rows, full)
        + [pltpu.VMEM((rows, full), BF16)]
        + gather_scratch(n)
        + fold_scratch((full, triple.shape[1]), qkv)
        + fold_scratch((att.shape[1], full), out)
        + [DMA, DMA],
        late=(5, 6, 7, 8),
        plain=(9,),
        early=(3, 4),
        raw=(2, 5),
    )


def finale_kernel(n, width, low, io, *refs):
    part, base, grad, feats, mask, normed, triple, att, resid = refs[:9]
    slims, slim_cames, qkv_far, out_far, vecs = refs[9:11], refs[11:13], refs[13], refs[14], refs[15:22]
    layer_outs, upper_d_in, refs = refs[22:24], refs[24], refs[25:]
    value_to, slim_to, qkv_to, out_to, vec_to, streams_to = refs[:6]
    refs = refs[6:]
    qkv, qkv_fold_in, qkv_ss, qkv_rs, out, out_fold_in, out_ss, out_rs = refs[5:13]
    qkv_own, qkv_in, qkv_sum, out_own, out_in, out_sum = refs[13:19]
    slim_sum, slim_pair, vec, vec_in, vec_sum, vec_sib, streams = refs[19:26]
    a_ss, a_rs, x_ss, x_rs, v_ss, v_rs, r_ss, r_rs, ls = refs[26:]
    p = Place(n)
    s, c, h, z, zn = p.s, p.c, p.h, p.z, p.zn
    share = width // n
    greet_all(p)
    scatter = Scatter(p, part, *refs[:5])
    scatter.start()

    slim_loads = [
        (
            pltpu.make_async_copy(slims[layer], slim_pair.at[0], ls.at[1]),
            pltpu.make_async_copy(slim_cames[layer], slim_pair.at[1], ls.at[4]),
        )
        for layer in range(2)
    ]
    for section, loads in enumerate(slim_loads):

        @pl.when(s == section)
        def _():
            for load in loads:
                load.start()

    back = Home(p, qkv_sum, qkv_to, a_ss, a_rs, ls.at[0])

    def x_block(k, src=qkv_far):
        far = p.flip(k)
        return remote(src.at[far], qkv_in.at[far], x_ss.at[k], x_rs.at[k], p.over)

    def out_cross(src=out_far):
        return remote(src, out_in, x_ss.at[zn], x_rs.at[zn], p.over)

    stream_cross = remote(streams, streams_to, x_ss.at[zn + 1], x_rs.at[zn + 1], p.over)

    def start_far():
        @pl.when(s == 0)
        def _():
            for k in range(zn):
                x_block(k).start()
            out_cross().start()

    def start_own(k):
        @pl.when(s == 1)
        def _():
            x_block(k, qkv_own).start()

    def start_own_out():
        @pl.when(s == 1)
        def _():
            out_cross(out_own).start()

    qkv_fold = Fold(p, qkv, qkv_fold_in, qkv_own, qkv_ss, qkv_rs)
    out_fold = Fold(p, out, out_fold_in, out_own, out_ss, out_rs)

    io.need(13, 14)
    start_far()
    io.need(5, 6)
    for step in product(normed, triple, qkv):
        step()
    qkv_fold.start()
    io.need(7, 8)
    work = [functools.partial(home_rows, att, resid, out, low, share), out_fold.start]
    work += qkv_fold.steps()
    work += [functools.partial(start_own, k) for k in list(range(1, zn)) + [0]]
    work += out_fold.steps() + [start_own_out]
    sums = []

    def rows_step(half):
        rows, value, lower, terms = back_rows(scatter, half, base, grad, feats[0, 0:1], mask, width)
        value_to[rows] = value
        sums.append(jnp.concatenate(terms, axis=0))

    by_halves(scatter, None, rows_step, work, 3)
    for rest in work:
        rest()

    io.need(22, 23, 24)
    streams[0] = jnp.where(s == 0, layer_outs[1][...], layer_outs[0][...]).astype(BF16)
    streams[1] = jnp.where(s == 0, upper_d_in[...], value_to[...]).astype(BF16)
    io.done(0)
    stream_cross.start()

    ones = (sum(sums), vecs[0][...])
    twos, triples, pres = vecs[1:3], (None, vecs[3]), vecs[4:6]
    lanes = vec.shape[3]
    padded = base.shape[1] // n
    sh = triple.shape[1] // 3
    for layer in range(2):
        one, two = ones[layer], twos[layer][...]
        outs = vecs[6][...] if layer else ones[1][2:3]
        features = jnp.concatenate([one[0:2], two[2:3], two[0:2], outs], axis=0)
        if layer:
            found = triples[1][...]
        else:
            found = jnp.sum(triple[...].astype(F32), axis=0, keepdims=True)
        bias = jnp.zeros((1, 2 * width), F32)
        for j, first in enumerate(low):
            spots = []
            for begin in (0, 2 * sh):
                spots += [
                    jnp.zeros((1, HD * first), F32),
                    found[:, begin : begin + sh],
                    jnp.zeros((1, width - sh - HD * first), F32),
                ]
            spots = [spot for spot in spots if spot.shape[1]]
            bias = jnp.where(h == j, jnp.concatenate(spots, axis=1), bias)
        for i in range(n):
            pieces = [
                features[:, i * padded : (i + 1) * padded],
                bias[:, i * 2 * share : (i + 1) * 2 * share],
                jnp.where(h == i, pres[layer][...], 0.0),
            ]
            wide_pieces = []
            for piece in pieces:
                rows, size = piece.shape
                if size < lanes:
                    piece = jnp.concatenate([piece, jnp.zeros((rows, lanes - size), F32)], axis=1)
                wide_pieces.append(piece)
            vec[layer, i] = jnp.concatenate(wide_pieces, axis=0)

    def vec_copy(a, b):
        l, i = lax.rem(s + a, 2), lax.rem(h + b, n)
        return remote(vec.at[l, i], vec_in.at[s, h], v_ss.at[a, b], v_rs.at[a, b], (l, c, i))

    for a, b in others(n):
        vec_copy(a, b).start()

    for k in list(range(1, zn)) + [0]:
        x_block(k).wait_recv()
        add_home(p, qkv_sum, p.flip(k), qkv_own, qkv_in, qkv_far, qkv_in)
        back.start(k)
    out_cross().wait_recv()
    add_home(p, out_sum, 0, out_own, out_in, out_far, out_in)
    for load in slim_loads[0]:
        load.wait()
    slim_sum[0] = (slim_pair[0, 0].astype(F32) + slim_pair[1, 0].astype(F32)).astype(BF16)

    def row_copies(w, src, dst):
        half = src.shape[1]
        piece = dst.at[pl.ds(pl.multiple_of(c * half, 16), half)]
        return (
            pltpu.make_async_copy(src.at[0], piece, ls.at[2 + w]),
            remote(src.at[0], piece, r_ss.at[w], r_rs.at[w], p.sibling),
        )

    copies = row_copies(0, slim_sum, slim_to) + row_copies(1, out_sum, out_to)
    for copy in copies:
        copy.start()
    total = vec[s, h]
    for a, b in others(n):
        vec_copy(a, b).wait_recv()
        total = total + vec_in[lax.rem(s + a, 2), lax.rem(h + n - b, n)]
    vec_sum[...] = total
    vec_share = remote(vec_sum, vec_sib, r_ss.at[2], r_rs.at[2], p.sibling)
    vec_share.start()
    for step in back.steps():
        step()
    vec_share.wait_recv()
    vec_to[...] = total + vec_sib[...]
    vec_share.wait_send()
    back.finish()
    for w in range(2):
        copies[2 * w].wait()
        copies[2 * w + 1].wait_recv()
        copies[2 * w + 1].wait_send()
    for a, b in others(n):
        vec_copy(a, b).wait_send()
    for k in range(zn):
        x_block(k).wait_send()
    out_cross().wait_send()
    stream_cross.wait_recv()
    stream_cross.wait_send()
    for job in (scatter, qkv_fold, out_fold):
        job.finish()


def finale_call(n, collective_id, width, low, *args):
    part, triple, att = args[0], args[6], args[7]
    slim, lanes = args[9].shape, args[19].shape[1]
    total_rows, full = part.shape
    rows = total_rows // n
    zn = n // 2
    qkv = (zn, full // n, triple.shape[1])
    out = (1, att.shape[1] // 2, full)
    return staged_call(
        functools.partial(finale_kernel, n, width, low),
        "finale",
        collective_id,
        args,
        [
            jax.ShapeDtypeStruct((rows, full), F32),
            jax.ShapeDtypeStruct((2 * slim[1], full), BF16),
            jax.ShapeDtypeStruct((n,) + qkv[1:], BF16),
            jax.ShapeDtypeStruct((2 * out[1], full), BF16),
            jax.ShapeDtypeStruct((8, lanes), F32),
            jax.ShapeDtypeStruct((2, rows, full), BF16),
        ],
        scatter_scratch(n, rows, full)
        + fold_scratch((full, triple.shape[1]), qkv)
        + fold_scratch((att.shape[1], full), out)
        + [pltpu.VMEM(qkv, BF16)] * 3
        + [pltpu.VMEM(out, BF16)] * 3
        + [
            pltpu.VMEM(slim, BF16),
            pltpu.VMEM((2,) + slim, BF16),
            pltpu.VMEM((2, n, 8, lanes), F32),
            pltpu.VMEM((2, n, 8, lanes), F32),
            pltpu.VMEM((8, lanes), F32),
            pltpu.VMEM((8, lanes), F32),
            pltpu.VMEM((2, rows, full), BF16),
            DMA((2, zn)),
            DMA((2, zn)),
            DMA((zn + 2,)),
            DMA((zn + 2,)),
            DMA((2, n)),
            DMA((2, n)),
            DMA((3,)),
            DMA((3,)),
            DMA((5,)),
        ],
        late=(5, 6, 7, 8, 13, 14, 22, 23, 24),
        plain=(9, 10, 11, 12),
        early=(0,),
        raw=(1, 2, 3, 5),
    )


def dot_t(a, b):
    return lax.dot_general(a, b, (((1,), (1,)), ((), ())), preferred_element_type=F32)


def dot_n(a, b):
    return lax.dot_general(a, b, (((1,), (0,)), ((), ())), preferred_element_type=F32)


def in_blocks(rows, step, chunk, between):
    count = rows // step
    if count <= 2:
        for b in range(count):
            chunk(b * step, rows // 2 if (b + 1) * step <= rows // 2 else rows, between)
    else:

        def body(b, carry, keys):
            chunk(pl.multiple_of(b * step, step), keys, [])
            return carry

        middle = count // 2 if count % 2 == 0 else 0
        lax.fori_loop(0, middle, functools.partial(body, keys=rows // 2), 0)
        lax.fori_loop(middle, count, functools.partial(body, keys=rows), 0)


def run_next(between):
    if between:
        between.pop(0)()


def attention(slots, step, own_ref, oth_ref, kpos_ref, qpos_ref, att_ref, low_ref, lse_ref):
    rows = own_ref.shape[0]
    sh = slots * HD
    power = HD**-0.5 * LOG2E

    def at(base, slot):
        return slice(base + slot * HD, base + (slot + 1) * HD)

    def chunk(first, seen, between):
        q_rows = pl.ds(first, step)
        qpos = qpos_ref[:, q_rows]
        for slot in range(slots):
            queries = own_ref[q_rows, at(0, slot)]
            keys = (own_ref[:seen, at(sh, slot)], oth_ref[:seen, at(0, slot)])
            values = (own_ref[:seen, at(2 * sh, slot)], oth_ref[:seen, at(sh, slot)])
            scores = []
            for part in range(2):
                allowed = kpos_ref[part * rows : part * rows + seen] <= qpos
                scores.append(jnp.where(allowed, dot_t(keys[part], queries), MASKED))
            top = jnp.maximum(
                jnp.max(scores[0], axis=0, keepdims=True), jnp.max(scores[1], axis=0, keepdims=True)
            )
            total = jnp.zeros_like(top)
            weighted = jnp.zeros((HD, step), F32)
            exps = []
            for part in range(2):
                e = jnp.exp2((scores[part] - top) * power)
                total = total + jnp.sum(e, axis=0, keepdims=True)
                exps.append(e)
            inverse = 1.0 / total
            for part in range(2):
                probs = (exps[part] * inverse).astype(BF16)
                weighted = weighted + dot_n(values[part].T, probs)
            att_ref[at(0, slot), q_rows] = weighted
            low_ref[q_rows, at(0, slot)] = weighted.T.astype(BF16)
            lse_ref[slot : slot + 1, q_rows] = top * power + jnp.log(total) * LOG2E
            run_next(between)

    return chunk


def attend_kernel(n, slots, step, layer, io, *refs):
    kpos_ref, qpos_ref, carried, out_all, normed, qkv_all, qkv_bias = refs[:7]
    att_ref, low_ref, lse_ref, oth_ref, part_to, carried_to, own_ref = refs[7:14]
    kv_ss, kv_rs, out_weight, qkv_weight, load_sems = refs[14:19]
    qkv_load = fetch(qkv_all.at[layer], qkv_weight, load_sems.at[1])
    out_load = fetch(out_all.at[layer], out_weight, load_sems.at[0])
    p = Place(n)
    rows = own_ref.shape[0]
    sh = slots * HD
    greet(p, line=True, sibling=True)
    job = Gather(p, carried, carried_to, *refs[19:])
    job.start()
    qkv_load.wait()
    io.need(4)
    between = job.steps()

    def project(first, size):
        some = pl.ds(first, size)
        weight = qkv_weight[...].reshape(normed.shape[1], 3 * sh)
        own_ref[some] = (dot_n(normed[some], weight) + qkv_bias[layer]).astype(BF16)

    row_blocks(rows, project)
    swap = remote(own_ref.at[:, pl.ds(sh, 2 * sh)], oth_ref, kv_ss, kv_rs, p.sibling)
    swap.start()
    run_next(between)
    run_next(between)
    swap.wait_recv()
    chunk = attention(slots, step, own_ref, oth_ref, kpos_ref, qpos_ref, att_ref, low_ref, lse_ref)
    in_blocks(rows, step, chunk, between)
    out_load.wait()

    def give(first, size):
        some = pl.ds(first, size)
        part_to[some] = dot_n(low_ref[some], out_weight[...]).astype(BF16)

    row_blocks(rows, give)
    io.done(0, 1, 4, 6)
    for rest in between:
        rest()
    swap.wait_send()
    job.finish()


def attend_call(n, collective_id, slots, layer, kpos, qpos, carried, out_all, *source):
    rows = qpos.shape[1]
    sh = slots * HD
    full = out_all.shape[2]
    return staged_call(
        functools.partial(attend_kernel, n, slots, min(rows, 256), layer),
        "attend",
        collective_id,
        (kpos, qpos, carried, out_all, *source),
        [
            jax.ShapeDtypeStruct((sh, rows), F32),
            jax.ShapeDtypeStruct((rows, sh), BF16),
            jax.ShapeDtypeStruct((slots, rows), F32),
            jax.ShapeDtypeStruct((rows, 2 * sh), BF16),
            jax.ShapeDtypeStruct((rows, full), BF16),
            jax.ShapeDtypeStruct((n * carried.shape[0], full), BF16),
            jax.ShapeDtypeStruct((rows, 3 * sh), BF16),
        ],
        [
            DMA,
            DMA,
            pltpu.VMEM((sh, full), BF16),
            pltpu.VMEM(source[1].shape[1:], BF16),
            DMA((2,)),
        ]
        + gather_scratch(n),
        late=(4,),
        plain=(3, 5),
        early=(0, 1, 4, 6),
        raw=(5,),
    )


def attend_back_kernel(n, slots, step, layer, last, home, io, *refs):
    own_ref, oth_ref, resid, att_ref, lse_ref, kpos_ref, qpos_ref, out_all, qkv_all = refs[:9]
    refs = refs[9:]
    if last:
        part_ref, base_ref, feats = refs[:3]
        refs = refs[3:]
    if home:
        wides, slim, refs = refs[:4], refs[4], refs[5:]
    triple_ref, part_to, refs = refs[0], refs[1], refs[2:]
    if last:
        value_ref, refs = refs[0], refs[1:]
    if home:
        wide_to, slim_came, refs = refs[0], refs[1], refs[2:]
    dq_t, dkv_own, dkv_oth, came, kv_ss, kv_rs = refs[:6]
    grad_ref, out_weight, qkv_weight, load_sems = refs[6:10]
    out_load = fetch(out_all.at[layer], out_weight, load_sems.at[0])
    qkv_load = fetch(qkv_all.at[layer], qkv_weight, load_sems.at[1])
    p = Place(n)
    rows = own_ref.shape[0]
    sh = slots * HD
    scale = HD**-0.5
    greet(p, line=last, sibling=True, spread=home, over=home)
    between = []
    if last:
        scatter = Scatter(p, part_ref, *refs[10:])
        scatter.start()
        between = scatter.steps()
    if home:
        wide_sum, wide_pair, a_ss, a_rs, ls, x_ss, x_rs = refs[10:]
        wide_loads = [
            [
                pltpu.make_async_copy(wides[2 * layer + i], wide_pair.at[i], ls.at[1 + i])
                for i in range(2)
            ]
            for layer in range(2)
        ]
        for section, loads in enumerate(wide_loads):

            @pl.when(p.s == section)
            def _():
                for load in loads:
                    load.start()

        cross = Cross(p, slim, slim_came, x_ss, x_rs, 1)
        cross.start()
        back = Home(p, wide_sum, wide_to, a_ss, a_rs, ls.at[0])
        for load in wide_loads[0]:
            load.wait()
        for k in list(range(1, p.zn)) + [0]:
            far = p.flip(k)
            total = wide_pair[0, far].astype(F32) + wide_pair[1, far].astype(F32)
            wide_sum[far] = total.astype(BF16)
            back.start(k)
        between = back.steps()
    io.need(2)
    out_load.wait()

    def enter(first, size):
        some = pl.ds(first, size)
        grad_ref[some] = dot_t(resid[some], out_weight[...]).astype(BF16)

    row_blocks(rows, enter)
    io.need(0, 1, 3)

    def at(base, slot):
        return slice(base + slot * HD, base + (slot + 1) * HD)

    dq_t[...] = jnp.zeros_like(dq_t)
    swap = remote(dkv_oth, came, kv_ss, kv_rs, p.sibling)
    for part in (1, 0):
        dkv = (dkv_own, dkv_oth)[part]
        src = (own_ref, oth_ref)[part]
        base = (sh, 0)[part]
        dkv[...] = jnp.zeros_like(dkv)

        def chunk(first, seen, between):
            q_rows = pl.ds(first, step)
            qpos = qpos_ref[:, q_rows]
            for slot in range(slots):
                queries = own_ref[q_rows, at(0, slot)]
                grads = grad_ref[q_rows, at(0, slot)]
                keys, values = src[:seen, at(base, slot)], src[:seen, at(base + sh, slot)]
                lse = lse_ref[slot : slot + 1, q_rows]
                correction = jnp.sum(
                    grads.astype(F32).T * att_ref[at(0, slot), q_rows], axis=0, keepdims=True
                )
                allowed = kpos_ref[part * rows : part * rows + seen] <= qpos
                scores = dot_t(keys, queries)
                probs = jnp.where(allowed, jnp.exp2(scores * (scale * LOG2E) - lse), 0.0)
                prob_grad = dot_t(values, grads)
                score_grad = (probs * (prob_grad - correction)).astype(BF16)
                dkv[:seen, at(0, slot)] += dot_n(score_grad, queries) * scale
                dkv[:seen, at(sh, slot)] += dot_n(probs.astype(BF16), grads)
                dq_t[at(0, slot), q_rows] += dot_n(keys.T, score_grad)
                run_next(between)

        in_blocks(rows, step, chunk, between)
        if part:
            swap.start()
    triple_ref[:, :sh] = (dq_t[...].T * scale).astype(BF16)

    def finish_last():
        for rest in between:
            rest()
        hr = base_ref.shape[0] // HALVES
        for half in range(HALVES):
            part_rows = slice(half * hr, (half + 1) * hr)
            total = scatter.result(half)
            value_ref[part_rows] = base_ref[part_rows] + (total + feats[1, 5:6])
        scatter.finish()

    swap.wait_recv()
    triple_ref[:, sh:] = (dkv_own[...] + came[...]).astype(BF16)
    qkv_load.wait()

    def leave(first, size):
        some = pl.ds(first, size)
        weight = qkv_weight[...].reshape(part_to.shape[1], 3 * sh)
        part_to[some] = dot_t(triple_ref[some], weight).astype(BF16)

    io.done(0)
    row_blocks(rows, leave)
    io.done(1)
    if last:
        finish_last()
    if home:
        for rest in between:
            rest()
        back.finish()
        cross.finish()
    swap.wait_send()


def attend_back_call(n, collective_id, slots, layer, *args, last=(), home=()):
    qkv, out_all, qkv_all = args[0], args[7], args[8]
    rows = qkv.shape[0]
    sh = slots * HD
    full = out_all.shape[2]
    step = min(rows, 256)
    shapes = [
        jax.ShapeDtypeStruct((rows, 3 * sh), BF16),
        jax.ShapeDtypeStruct((rows, full), BF16),
    ]
    scratch = [pltpu.VMEM((sh, rows), F32)] + [pltpu.VMEM((rows, 2 * sh), F32)] * 3
    scratch += [DMA, DMA]
    scratch += [
        pltpu.VMEM((rows, sh), BF16),
        pltpu.VMEM((sh, full), BF16),
        pltpu.VMEM(qkv_all.shape[1:], BF16),
        DMA((2,)),
    ]
    if last:
        shapes.append(jax.ShapeDtypeStruct(last[1].shape, F32))
        scratch += scatter_scratch(n, *last[1].shape)
    if home:
        wide, slim = home[0].shape, home[4].shape
        shapes += [
            jax.ShapeDtypeStruct((n,) + wide[1:], BF16),
            jax.ShapeDtypeStruct(slim, BF16),
        ]
        scratch += [pltpu.VMEM(wide, BF16), pltpu.VMEM((2,) + wide, BF16)]
        scratch += [DMA((2, n // 2)), DMA((2, n // 2)), DMA((3,)), DMA, DMA]
    return staged_call(
        functools.partial(attend_back_kernel, n, slots, step, layer, bool(last), bool(home)),
        "attend_back",
        collective_id,
        args + tuple(last) + tuple(home),
        shapes,
        scratch,
        late=(0, 1, 2, 3),
        plain=(7, 8) + (tuple(range(9, 14)) if home else ()),
        early=(0, 1),
        raw=(2, 3) if home else (),
    )


def windows(width, n):
    share = width // n
    low = [j * share // HD for j in range(n)]
    slots = max(((j + 1) * share - 1) // HD - low[j] + 1 for j in range(n))
    return [min(first, HEADS - slots) for first in low], slots


def on_device(n, tokens, block_order, cotangent, *vectors_and_weights):
    (
        first_gain,
        first_shift,
        qkv_weight,
        input_bias,
        out_weight,
        out_bias,
        second_gain,
        second_shift,
        widen_weight,
        widen_bias,
        narrow_weight,
        narrow_bias,
    ) = (member[0] for member in vectors_and_weights)
    c = lax.axis_index("ctx")
    _, rows, width = tokens.shape
    hidden = widen_weight.shape[1]
    share = width // n
    hide = hidden // n
    padded = -(-share // 16) * 16
    full = n * padded
    low, slots = windows(width, n)
    sh = slots * HD
    total_rows = n * rows
    half_rows = rows // HALVES

    mask = jnp.asarray(np.arange(full)[None] % padded < share, F32)
    order = block_order.reshape(2, n, HALVES).transpose(0, 2, 1)
    places = order[..., None] * half_rows + jnp.arange(half_rows, dtype=jnp.int32)
    places = places.reshape(2, total_rows)
    own_places = jnp.where(c == 0, places[0], places[1])
    oth_places = jnp.where(c == 0, places[1], places[0])
    kpos = jnp.concatenate([own_places, oth_places])[:, None]
    qpos = own_places[None, :]

    (
        narrow_send,
        x,
        own_cot,
        out_grad,
        out_sums,
        normed,
        qkv,
        qkv_all,
        out_all,
        feats,
        qkv_bias,
        widen_biases,
        *attended,
        widen_all,
    ) = open_call(
        n,
        low,
        slots,
        padded,
        tokens,
        cotangent,
        [
            member[None]
            for member in (
                first_gain,
                first_shift,
                out_bias,
                second_gain,
                second_shift,
                narrow_bias,
                input_bias,
                widen_bias,
            )
        ],
        (qkv_weight, out_weight, widen_weight, narrow_weight),
        mask,
        kpos,
        qpos,
    )
    stored = []
    layer_outs = []
    for layer in range(2):
        if layer:
            *attended, out_low_all, qkv = attend_call(
                n, 2, slots, 1, kpos, qpos, own_cot, out_all, normed, qkv_all, qkv_bias
            )
        att, att_low, lse, other, part = attended
        found = forward_call(
            n,
            3 + layer,
            width,
            part,
            x,
            feats,
            mask,
            layer=layer,
            feed=(widen_all, narrow_all if layer else narrow_send, widen_biases),
            carry=not layer,
        )
        residual, normed_two, hidden_pre, hidden_low, part = found[:5]
        stored.append((x, normed, qkv, other, att, att_low, lse, residual, normed_two))
        stored[-1] += (hidden_pre, hidden_low)
        if layer == 0:
            narrow_all = found[5]
            x, normed = forward_call(n, 5, width, part, residual, feats, mask)
            layer_outs.append(x)
        else:
            last = (part, residual, feats)

    found = {}
    for layer in (1, 0):
        x, normed, qkv, other, att, att_low, lse, residual, normed_two = stored[layer][:9]
        hidden_pre, hidden_low = stored[layer][9:]
        resid_grad, sums_two, resid_low_all, wide, wide_came, slim, pre_sums = resid_call(
            n,
            7 + layer,
            width,
            layer,
            hide,
            residual,
            out_grad,
            feats,
            mask,
            normed_two,
            hidden_pre,
            hidden_low,
            out_low_all,
            widen_all,
            narrow_all,
        )
        back = attend_back_call(
            n,
            9 + layer,
            slots,
            layer,
            qkv,
            other,
            resid_low_all,
            att,
            lse,
            kpos,
            qpos,
            out_all,
            qkv_all,
            last=last if layer else (),
            home=() if layer else (wide, wide_came) + found[1][:2] + (slim,),
        )
        triple, part = back[:2]
        local = (part, x, resid_grad, feats, mask, normed, triple, att_low, resid_low_all)
        found[layer] = (wide, wide_came, slim, sums_two, pre_sums)
        if layer:
            layer_outs.append(back[2])
            upper_d_in, sums_one, out_low_all, qkv_grad, out_rows, slim_came, triple_sums = (
                input_call(n, 11, width, 0, low, *local, slim)
            )
            out_grad = upper_d_in
    lower, upper = found[0], found[1]
    widen_back, slim_back = back[2:]
    d_in, narrow_back, qkv_back, out_back, vec, came = finale_call(
        n,
        12,
        width,
        low,
        *local,
        lower[2],
        upper[2],
        slim_back,
        slim_came,
        qkv_grad,
        out_rows,
        sums_one,
        lower[3],
        upper[3],
        triple_sums,
        lower[4],
        upper[4],
        out_sums,
        *layer_outs,
        upper_d_in,
    )
    settled = settle_call(
        low,
        share,
        hide,
        qkv_back,
        widen_back,
        out_back,
        narrow_back,
        vec,
        came,
        *layer_outs,
        d_in,
        upper_d_in,
    )
    qkv_out, widen_out, out_out, narrow_out, layer_out, d_out = (m[None] for m in settled[:6])
    gain1, shift1, out_b, gain2, shift2, narrow_b, input_b, widen_b = settled[6:]
    return (
        layer_out,
        d_out,
        gain1,
        shift1,
        qkv_out,
        input_b,
        out_out,
        out_b,
        gain2,
        shift2,
        widen_out,
        widen_b,
        narrow_out,
        narrow_b,
    )


def solution(mesh):
    rows = P(None, ("ctx", "shard"), None)
    vector = P("section", "shard")
    matrix = P("section", "shard", None)
    order = (
        vector,
        vector,
        matrix,
        vector,
        matrix,
        vector,
        vector,
        vector,
        matrix,
        vector,
        matrix,
        vector,
    )
    streams = P("section", None, ("ctx", "shard"), None)
    return jax.shard_map(
        functools.partial(on_device, mesh.shape["shard"]),
        mesh=mesh,
        in_specs=(rows, P(), rows) + order,
        out_specs=(streams, streams) + order,
        check_vma=False,
    )
```

```python
import functools

import jax
import jax.numpy as jnp
import numpy as np
from jax import lax
from jax.experimental import pallas as pl
from jax.experimental.pallas import tpu as pltpu
from jax.sharding import PartitionSpec as P

HEADS = 25
HD = 64
EPSILON = 1e-05
MASKED = -1e30
LOG2E = 1.4426950408889634
GELU_A = 0.7978845608028654
GELU_B = 0.044715
MESH = pl.DeviceIdType.MESH
F32 = jnp.float32
BF16 = jnp.bfloat16
VMEM_SPEC = pl.BlockSpec(memory_space=pltpu.VMEM)
ANY_SPEC = pl.BlockSpec(memory_space=pl.ANY)
DMA = pltpu.SemaphoreType.DMA
VMEM_LIMIT = 60 * 2**20
HALVES = 2


def params(collective_id=None):
    if collective_id is None:
        return pltpu.CompilerParams(vmem_limit_bytes=VMEM_LIMIT)
    return pltpu.CompilerParams(
        collective_id=collective_id, has_side_effects=True, vmem_limit_bytes=VMEM_LIMIT
    )


def remote(src, dst, send_sem, recv_sem, device):
    return pltpu.make_async_remote_copy(
        src_ref=src,
        dst_ref=dst,
        send_sem=send_sem,
        recv_sem=recv_sem,
        device_id=device,
        device_id_type=MESH,
    )


class Place:
    def __init__(self, n):
        self.s = lax.axis_index("section")
        self.c = lax.axis_index("ctx")
        self.h = lax.axis_index("shard")
        self.n = n
        self.zn = n // 2
        self.y = lax.rem(self.h, 2)
        self.z = lax.div(self.h, 2)
        self.far_y = self.y + self.c - 2 * self.y * self.c

    def flip(self, k):
        found = self.z
        for bit in range(self.zn.bit_length()):
            if k >> bit & 1:
                found = found + (1 - 2 * lax.rem(self.z // 2**bit, 2)) * 2**bit
        return found

    def dev(self, z, y):
        return (self.s, self.c, z * 2 + y)

    @property
    def pair(self):
        return self.dev(self.z, 1 - self.y)

    @property
    def above(self):
        return self.dev(self.z + 1, self.y)

    @property
    def below(self):
        return self.dev(self.z - 1, self.y)

    @property
    def over(self):
        return (1 - self.s, self.c, self.h)

    @property
    def sibling(self):
        return (self.s, 1 - self.c, self.h)


def greet(p, line=False, spread=False, over=False, sibling=False):
    bar = pltpu.get_barrier_semaphore()
    peers = 0

    def signal(device):
        pl.semaphore_signal(bar, inc=1, device_id=device, device_id_type=MESH)

    if line:
        signal(p.pair)

        @pl.when(p.z < p.zn - 1)
        def _():
            signal(p.above)

        @pl.when(p.z > 0)
        def _():
            signal(p.below)

        peers = 1 + (p.z + p.zn - 1) // p.zn + (2 * p.zn - 2 - p.z) // p.zn
    if spread:
        for dz in range(1, p.zn):
            signal(p.dev(lax.rem(p.z + dz, p.zn), p.far_y))

        @pl.when(p.c == 1)
        def _():
            signal(p.dev(p.z, p.far_y))

        peers = peers + p.zn - 1 + p.c
    if over:
        signal(p.over)
        peers = peers + 1
    if sibling:
        signal(p.sibling)
        peers = peers + 1
    pl.semaphore_wait(bar, peers)


class Gather:
    def __init__(self, p, own_ref, out_ref, ss, rs, ls):
        self.p, self.own_ref, self.out_ref = p, own_ref, out_ref
        self.ss, self.rs, self.ls = ss, rs, ls
        self.hr = own_ref.shape[0] // HALVES

    def blk(self, half, zz, yy):
        row = (half * self.p.n + zz * 2 + yy) * self.hr
        return self.out_ref.at[pl.ds(pl.multiple_of(row, 16), self.hr)]

    def own(self, half):
        return self.own_ref.at[pl.ds(half * self.hr, self.hr)]

    def up(self, t, half, src):
        p = self.p
        sems = (self.ss.at[0, t, half], self.rs.at[0, t, half])
        return remote(src, self.blk(half, p.z - (t - 1), p.y), *sems, p.above)

    def down(self, t, half, src):
        p = self.p
        sems = (self.ss.at[1, t, half], self.rs.at[1, t, half])
        return remote(src, self.blk(half, p.z + (t - 1), p.y), *sems, p.below)

    def across(self, kind, t, half, zz, src):
        p = self.p
        sems = (self.ss.at[2 + kind, t, half], self.rs.at[2 + kind, t, half])
        return remote(src, self.blk(half, zz, p.y), *sems, p.pair)

    def local(self, half):
        p = self.p
        return pltpu.make_async_copy(
            self.own(half), self.blk(half, p.z, p.y), self.ls.at[half]
        )

    def start(self, halves=range(HALVES)):
        p = self.p
        for half in halves:
            src = self.own(half)

            @pl.when(p.z < p.zn - 1)
            def _():
                self.up(1, half, src).start()

            @pl.when(p.z > 0)
            def _():
                self.down(1, half, src).start()

            self.across(0, 0, half, p.z, src).start()
            self.local(half).start()

    def step(self, t, half):
        p = self.p
        z, zn = p.z, p.zn

        @pl.when(z >= t)
        def _():
            block = self.blk(half, z - t, p.y)
            self.up(t, half, block).wait_recv()
            if t < zn - 1:

                @pl.when(z < zn - 1)
                def _():
                    self.up(t + 1, half, block).start()

            self.across(0, t, half, z - t, block).start()

        @pl.when(z <= zn - 1 - t)
        def _():
            block = self.blk(half, z + t, p.y)
            self.down(t, half, block).wait_recv()
            if t < zn - 1:

                @pl.when(z > 0)
                def _():
                    self.down(t + 1, half, block).start()

            self.across(1, t, half, z + t, block).start()

    def steps(self):
        return [
            functools.partial(self.step, t, half)
            for t in range(1, self.p.zn)
            for half in range(HALVES)
        ]

    def finish(self):
        p = self.p
        z, zn = p.z, p.zn
        for half in range(HALVES):
            self.across(0, 0, half, z, self.own(half)).wait_recv()
            for t in range(1, zn):

                @pl.when(z >= t)
                def _():
                    self.across(0, t, half, z - t, self.own(half)).wait_recv()

                @pl.when(z <= zn - 1 - t)
                def _():
                    self.across(1, t, half, z + t, self.own(half)).wait_recv()

        for half in range(HALVES):
            self.local(half).wait()
            self.across(0, 0, half, z, self.own(half)).wait_send()
            for t in range(1, zn):

                @pl.when((z < zn - 1) & (z >= t - 1))
                def _():
                    self.up(t, half, self.own(half)).wait_send()

                @pl.when((z > 0) & (z <= zn - t))
                def _():
                    self.down(t, half, self.own(half)).wait_send()

                @pl.when(z >= t)
                def _():
                    self.across(0, t, half, z - t, self.own(half)).wait_send()

                @pl.when(z <= zn - 1 - t)
                def _():
                    self.across(1, t, half, z + t, self.own(half)).wait_send()


class Scatter:
    def __init__(self, p, part_ref, ybuf, rbuf, sbuf, ss, rs):
        self.p, self.part_ref = p, part_ref
        self.ybuf, self.rbuf, self.sbuf, self.ss, self.rs = ybuf, rbuf, sbuf, ss, rs
        self.hr = ybuf.shape[2]

    def blk(self, half, zz, yy):
        row = (half * self.p.n + zz * 2 + yy) * self.hr
        return self.part_ref.at[pl.ds(pl.multiple_of(row, 16), self.hr)]

    def goal(self, k, t):
        return self.p.z + t if k == 0 else self.p.z - t

    def across(self, k, t, half):
        p = self.p
        zz = self.goal(k, t)
        sems = (self.ss.at[k, t, half], self.rs.at[k, t, half])
        return remote(self.blk(half, zz, 1 - p.y), self.ybuf.at[zz, half], *sems, p.pair)

    def along(self, k, t, half, slot):
        p = self.p
        zz = self.goal(k, t)
        sems = (self.ss.at[2 + k, t, half], self.rs.at[2 + k, slot, half])
        target = p.above if k == 0 else p.below
        return remote(self.sbuf.at[zz, half], self.rbuf.at[zz + 1 - k, half], *sems, target)

    def ok(self, k, t):
        return self.p.z <= self.p.zn - 1 - t if k == 0 else self.p.z >= t

    def has(self, k):
        return self.p.z > 0 if k == 0 else self.p.z < self.p.zn - 1

    def start(self):
        for t in range(self.p.zn - 1, 0, -1):
            for half in range(HALVES):
                for k in range(2):

                    @pl.when(self.ok(k, t))
                    def _():
                        self.across(k, t, half).start()

        for half in range(HALVES):
            self.across(0, 0, half).start()

    def step(self, t, half, k):
        p = self.p
        zz = self.goal(k, t)

        @pl.when(self.ok(k, t))
        def _():
            self.across(k, t, half).wait_recv()
            total = self.blk(half, zz, p.y)[...].astype(F32)
            total = total + self.ybuf[zz, half].astype(F32)
            if t < p.zn - 1:

                @pl.when(self.has(k))
                def _():
                    self.along(k, t, half, t).wait_recv()
                    more = total + self.rbuf[zz + 1 - k, half].astype(F32)
                    self.sbuf[zz, half] = more.astype(BF16)

                @pl.when(jnp.logical_not(self.has(k)))
                def _():
                    self.sbuf[zz, half] = total.astype(BF16)

            else:
                self.sbuf[zz, half] = total.astype(BF16)
            self.along(k, t, half, t - 1).start()

    def steps(self):
        return [
            functools.partial(self.step, t, half, k)
            for t in range(self.p.zn - 1, 0, -1)
            for half in range(HALVES)
            for k in range(2)
        ]

    def result(self, half):
        p = self.p
        z = p.z
        self.across(0, 0, half).wait_recv()
        for k in range(2):

            @pl.when(self.has(k))
            def _():
                self.along(k, 0, half, 0).wait_recv()

            @pl.when(jnp.logical_not(self.has(k)))
            def _():
                self.rbuf[z + 1 - k, half] = jnp.zeros(self.rbuf.shape[2:], BF16)

        total = self.blk(half, z, p.y)[...].astype(F32) + self.ybuf[z, half].astype(F32)
        return total + self.rbuf[z + 1, half].astype(F32) + self.rbuf[z, half].astype(F32)

    def finish(self):
        for half in range(HALVES):
            self.across(0, 0, half).wait_send()
            for t in range(1, self.p.zn):
                for k in range(2):

                    @pl.when(self.ok(k, t))
                    def _():
                        self.across(k, t, half).wait_send()
                        self.along(k, t, half, t - 1).wait_send()


class Spread:
    def __init__(self, p, src, dst, ss, rs, ls):
        self.p, self.src, self.dst, self.ss, self.rs, self.ls = p, src, dst, ss, rs, ls

    def source(self, dz):
        return self.p.flip(dz) * 2 + self.p.far_y

    def out(self, dz):
        p = self.p
        target = self.source(dz)
        sems = (self.ss.at[0, dz], self.rs.at[0, dz])
        return remote(self.src.at[target], self.dst.at[p.s, p.h], *sems, (p.s, p.c, target))

    def aside(self, dz):
        block = self.dst.at[self.p.s, self.source(dz)]
        return remote(block, block, self.ss.at[1, dz], self.rs.at[1, dz], self.p.sibling)

    def cross(self, dz):
        block = self.dst.at[self.p.s, self.source(dz)]
        return remote(block, block, self.ss.at[2, dz], self.rs.at[2, dz], self.p.over)

    def cross_own(self):
        p = self.p
        sems = (self.ss.at[2, 0], self.rs.at[2, 0])
        return remote(self.src.at[p.h], self.dst.at[p.s, p.h], *sems, p.over)

    def cross_aside(self, dz):
        block = self.dst.at[1 - self.p.s, self.source(dz)]
        return remote(block, block, self.ss.at[3, dz], self.rs.at[3, dz], self.p.sibling)

    def local(self):
        p = self.p
        return pltpu.make_async_copy(self.src.at[p.h], self.dst.at[p.s, p.h], self.ls)

    def start(self):
        @pl.when(self.p.c == 1)
        def _():
            self.out(0).start()

        @pl.when(self.p.c == 0)
        def _():
            self.cross_own().start()

        for dz in range(1, min(3, self.p.zn)):
            self.out(dz).start()
        self.local().start()

    def arrived(self, dz):
        if 3 <= dz + 2 < self.p.zn:
            self.out(dz + 1).wait_send()
            self.out(dz + 2).start()
        self.out(dz).wait_recv()
        self.cross(dz).start()
        self.aside(dz).start()

    def crossed(self, dz):
        self.cross(dz).wait_recv()
        self.cross_aside(dz).start()

    def first(self):
        @pl.when(self.p.c == 1)
        def _():
            self.arrived(0)

    def steps(self):
        found = [self.first]
        found += [functools.partial(self.arrived, dz) for dz in range(1, self.p.zn)]
        return found + [functools.partial(self.crossed, dz) for dz in range(self.p.zn)]

    def finish(self):
        self.local().wait()

        @pl.when(self.p.c == 0)
        def _():
            self.aside(0).wait_recv()
            self.cross_own().wait_send()

        @pl.when(self.p.c == 1)
        def _():
            self.out(0).wait_send()
            self.aside(0).wait_send()
            self.cross(0).wait_send()

        for dz in range(self.p.zn):
            if dz:
                self.aside(dz).wait_recv()
                self.aside(dz).wait_send()
                if dz == 1 or dz == self.p.zn - 1:
                    self.out(dz).wait_send()
                self.cross(dz).wait_send()
            self.cross_aside(dz).wait_recv()
            self.cross_aside(dz).wait_send()


class RowSwap:
    def __init__(self, p, src, dst, ss, rs, ls):
        self.p, self.src, self.dst, self.ss, self.rs, self.ls = p, src, dst, ss, rs, ls
        self.split = src.shape[0] % 32 == 0

    def piece(self, which):
        count = self.src.shape[0]
        if not self.split:
            return self.src, self.dst.at[which, pl.ds(0, count)]
        half = count // 2
        rows = pl.ds(pl.multiple_of(self.p.c * half, 16), half)
        return self.src.at[rows], self.dst.at[which, rows]

    def cross(self):
        src, dst = self.piece(self.p.s)
        return remote(src, dst, self.ss.at[0], self.rs.at[0], self.p.over)

    def aside(self):
        block = self.piece(1 - self.p.s)[1]
        return remote(block, block, self.ss.at[1], self.rs.at[1], self.p.sibling)

    def local(self):
        rows = pl.ds(0, self.src.shape[0])
        return pltpu.make_async_copy(self.src, self.dst.at[self.p.s, rows], self.ls)

    def start(self):
        self.cross().start()
        self.local().start()

    def step(self):
        self.cross().wait_recv()
        if self.split:
            self.aside().start()

    def finish(self):
        self.local().wait()
        self.cross().wait_send()
        if self.split:
            self.aside().wait_recv()
            self.aside().wait_send()


class Cross:
    def __init__(self, p, src, dst, ss, rs, source):
        self.p, self.source = p, source
        self.copy = remote(src, dst, ss, rs, p.over)

    def start(self):
        @pl.when(self.p.s == self.source)
        def _():
            self.copy.start()

    def finish(self):
        @pl.when(self.p.s == self.source)
        def _():
            self.copy.wait_send()

        @pl.when(self.p.s != self.source)
        def _():
            self.copy.wait_recv()


class Home:
    def __init__(self, p, src, dst, ss, rs, ls):
        self.p, self.src, self.dst, self.ss, self.rs, self.ls = p, src, dst, ss, rs, ls

    def send(self, k):
        p = self.p
        far = p.flip(k)
        target = (p.s, p.c, far * 2 + p.far_y)
        sems = (self.ss.at[0, k], self.rs.at[0, k])
        return remote(self.src.at[far], self.dst.at[p.h], *sems, target)

    def keep(self):
        return pltpu.make_async_copy(self.src.at[self.p.z], self.dst.at[self.p.h], self.ls)

    def aside(self, k):
        block = self.dst.at[self.p.flip(k) * 2 + self.p.far_y]
        return remote(block, block, self.ss.at[1, k], self.rs.at[1, k], self.p.sibling)

    def start(self, k):
        if k:
            self.send(k).start()
            return

        @pl.when(self.p.c == 1)
        def _():
            self.send(0).start()

        @pl.when(self.p.c == 0)
        def _():
            self.keep().start()

    def arrived(self, k):
        if k:
            self.send(k).wait_recv()
        else:

            @pl.when(self.p.c == 1)
            def _():
                self.send(0).wait_recv()

            @pl.when(self.p.c == 0)
            def _():
                self.keep().wait()

        self.aside(k).start()

    def steps(self):
        return [functools.partial(self.arrived, k) for k in range(self.p.zn)]

    def finish(self):
        @pl.when(self.p.c == 1)
        def _():
            self.send(0).wait_send()

        for k in range(self.p.zn):
            if k:
                self.send(k).wait_send()
            self.aside(k).wait_recv()
            self.aside(k).wait_send()


def add_home(p, to, index, first, first_came, second, second_came):
    pairs = ((first, first_came), (second, second_came))
    for section, (own, came) in enumerate(pairs):

        @pl.when(p.s == section)
        def _():
            to[index] = (own[index].astype(F32) + came[index].astype(F32)).astype(BF16)


class Fold:
    def __init__(self, p, src, came, out, ss, rs):
        self.p, self.src, self.came, self.out, self.ss, self.rs = p, src, came, out, ss, rs
        self.count = out.shape[0]
        self.size = out.shape[1]

    def rows(self, item, near):
        p = self.p
        if self.count == 1:
            index = 1 - p.c if near else p.c
        else:
            index = item * 2 + (1 - p.far_y if near else p.far_y)
        return pl.ds(pl.multiple_of(index * self.size, 16), self.size)

    def copy(self, item):
        src = self.src.at[self.rows(item, True)]
        sems = (self.ss.at[item], self.rs.at[item])
        return remote(src, self.came.at[item], *sems, self.p.sibling)

    def start(self):
        for item in range(self.count):
            self.copy(item).start()

    def step(self, item):
        self.copy(item).wait_recv()
        own = self.src[self.rows(item, False)].astype(F32)
        self.out[item] = (own + self.came[item].astype(F32)).astype(BF16)

    def steps(self):
        return [functools.partial(self.step, item) for item in range(self.count)]

    def finish(self):
        for item in range(self.count):
            self.copy(item).wait_send()


def fold_scratch(source, out):
    return [pltpu.VMEM(source, BF16), pltpu.VMEM(out, BF16), DMA((out[0],)), DMA((out[0],))]


def product(a_ref, b_ref, to_ref):
    rows = to_ref.shape[0]

    def step(first, size):
        found = lax.dot_general(
            a_ref[:, first : first + size],
            b_ref[...],
            (((0,), (0,)), ((), ())),
            preferred_element_type=F32,
        )
        to_ref[first : first + size] = found.astype(BF16)

    return [
        functools.partial(step, first, min(256, rows - first)) for first in range(0, rows, 256)
    ]


def home_rows(a_ref, b_ref, to_ref, low, share):
    found = lax.dot_general(
        a_ref[...], b_ref[...], (((0,), (0,)), ((), ())), preferred_element_type=F32
    )
    h = lax.axis_index("shard")
    shift = 0
    for j, first in enumerate(low):
        shift = shift + jnp.where(h == j, (HD * first - j * share) % found.shape[0], 0)
    to_ref[...] = pltpu.roll(found, shift, 0).astype(BF16)


def in_turn(steps, work, each=1):
    for step in steps:
        for _ in range(each):
            run_next(work)
        step()


def by_halves(scatter, gather, rows_step, work, each=1):
    in_turn(scatter.steps(), work, each)
    for half in range(HALVES):
        rows_step(half)
        if gather is not None:
            gather.start([half])
    if gather is not None:
        in_turn(gather.steps(), work, each)


def fetch(src, dst, sem):
    copy = pltpu.make_async_copy(src, dst, sem)
    copy.start()
    return copy


class Staging:
    def __init__(self):
        self.loads, self.stores, self.running = {}, {}, []

    def need(self, *items):
        for item in items:
            self.loads.pop(item).wait()

    def done(self, *items):
        for item in items:
            self.running.append(fetch(*self.stores.pop(item)))

    def end(self):
        self.done(*list(self.stores))
        for copy in self.running:
            copy.wait()


def staged_call(
    body, name, collective_id, args, shapes, scratch, late=(), plain=(), early=(), raw=(), layers={}
):
    late, early = tuple(late), tuple(early)
    n_in, n_out, n_scratch = len(args), len(shapes), len(scratch)

    def run(*refs):
        ins, outs = list(refs[:n_in]), list(refs[n_in : n_in + n_out])
        rest = refs[n_in + n_out :]
        own, rest = rest[:n_scratch], rest[n_scratch:]
        staged_in, rest = rest[: len(late)], rest[len(late) :]
        staged_out, sems = rest[: len(early)], rest[len(early) :]
        io = Staging()
        for x, item in enumerate(late):
            src = ins[item].at[layers[item]] if item in layers else ins[item]
            io.loads[item] = fetch(src, staged_in[x], sems[0].at[x])
            ins[item] = staged_in[x]
        for x, item in enumerate(early):
            io.stores[item] = (staged_out[x], outs[item], sems[1].at[x])
            outs[item] = staged_out[x]
        body(io, *ins, *outs, *own)
        io.end()

    stages = [
        pltpu.VMEM(args[item].shape[1 if item in layers else 0 :], args[item].dtype) for item in late
    ]
    stages += [pltpu.VMEM(shapes[item].shape, shapes[item].dtype) for item in early]
    stages += [DMA((max(len(late), 1),)), DMA((max(len(early), 1),))]
    return pl.pallas_call(
        run,
        out_shape=shapes,
        in_specs=[ANY_SPEC if i in late + tuple(plain) else VMEM_SPEC for i in range(n_in)],
        out_specs=[ANY_SPEC if i in early + tuple(raw) else VMEM_SPEC for i in range(n_out)],
        scratch_shapes=list(scratch) + stages,
        compiler_params=params(collective_id),
        name=name,
    )(*args)


def row_blocks(rows, step):
    size = min(rows, 256)
    count = rows // size
    if count <= 2:
        for b in range(count):
            step(b * size, size)
    else:

        def body(b, carry):
            step(pl.multiple_of(b * size, size), size)
            return carry

        lax.fori_loop(0, count, body, 0)


def gelu_parts(values):
    square = values * values
    return jnp.tanh(GELU_A * (values + GELU_B * values * square)), square


def greet_all(p):
    bar = pltpu.get_barrier_semaphore()
    for a in range(2):
        for b in range(p.n):
            if (a, b) != (0, 0):
                other = (lax.rem(p.s + a, 2), p.c, lax.rem(p.h + b, p.n))
                pl.semaphore_signal(bar, inc=1, device_id=other, device_id_type=MESH)
    pl.semaphore_signal(bar, inc=1, device_id=p.sibling, device_id_type=MESH)
    pl.semaphore_wait(bar, 2 * p.n)


def others(n):
    return [(a, b) for a in range(2) for b in range(n) if (a, b) != (0, 0)]


def with_gaps(values, n, padded):
    rows, width = values.shape
    share = width // n
    pieces = []
    for j in range(n):
        pieces.append(values[:, j * share : (j + 1) * share])
        if padded > share:
            pieces.append(jnp.zeros((rows, padded - share), values.dtype))
    return jnp.concatenate(pieces, axis=1)


def lay_vectors(vectors, pack_to):
    lanes = pack_to.shape[1]
    members = []
    for ref in vectors:
        member = ref[...].astype(F32)
        members.append(
            jnp.concatenate([member, jnp.zeros((1, lanes - member.shape[1]), F32)], axis=1)
        )
    members.append(jnp.zeros((8, lanes), F32))
    pack_to[...] = jnp.concatenate(members, axis=0).astype(BF16)


def lay_first(low, qkv_ref, qkv_to):
    n, padded, triple = qkv_to.shape
    share = qkv_ref.shape[0]
    width = qkv_ref.shape[1] // 3
    sh = triple // 3
    for j in range(n):
        for t in range(3):
            first = t * width + HD * low[j]
            qkv_to[j, :share, t * sh : (t + 1) * sh] = qkv_ref[:, first : first + sh]
        if padded > share:
            qkv_to[j, share:] = jnp.zeros((padded - share, triple), BF16)


def lay_rows(low, out_ref, out_to):
    share = out_ref.shape[0]
    sh, full = out_to.shape
    n = len(low)
    h = lax.axis_index("shard")
    offset = 0
    for j in range(n):
        offset = offset + jnp.where(h == j, j * share - HD * low[j], 0)
    rows = with_gaps(out_ref[...].astype(F32), n, full // n)
    rows = jnp.concatenate([rows, jnp.zeros((sh - share, full), F32)], axis=0)
    out_to[...] = pltpu.roll(rows, offset, 0).astype(BF16)


def lay_widen(j, widen_ref, widen_to):
    n, padded, hide_full = widen_to.shape
    share, hidden = widen_ref.shape
    hide = hidden // n
    widen_to[j, :share, :hide] = widen_ref[:, j * hide : (j + 1) * hide]
    if hide_full > hide:
        widen_to[j, :share, hide:] = jnp.zeros((share, hide_full - hide), BF16)
    if padded > share:
        widen_to[j, share:] = jnp.zeros((padded - share, hide_full), BF16)


def lay_narrow(first, size, n, narrow_ref, narrow_to):
    rows = slice(first, first + size)
    narrow_to[rows] = with_gaps(narrow_ref[rows], n, narrow_to.shape[1] // n)


def spread_vectors(n, low, width, pack_all, feats_to, qkv_bias, widen_bias):
    h = lax.axis_index("shard")
    sh = qkv_bias.shape[2] // 3
    share = width // n
    padded = feats_to.shape[2] // n
    for layer in range(2):
        pieces = [pack_all[layer, j] for j in range(n)]
        feats_to[layer] = jnp.concatenate([m[:, :padded] for m in pieces], axis=1).astype(F32)
        bias = jnp.concatenate([m[6:7, : 2 * share] for m in pieces], axis=1).astype(F32)
        found = jnp.zeros((1, 2 * sh), F32)
        wide = jnp.zeros((1, widen_bias.shape[2]), F32)
        for j in range(n):
            first = HD * low[j]
            spots = [bias[:, k * width + first : k * width + first + sh] for k in range(2)]
            found = jnp.where(h == j, jnp.concatenate(spots, axis=1), found)
            own = pieces[j][7:8, : wide.shape[1]].astype(F32)
            wide = jnp.where(h == j, own, wide)
        qkv_bias[layer] = jnp.concatenate(
            [found[:, :sh], jnp.zeros((1, sh), F32), found[:, sh:]], axis=1
        )
        widen_bias[layer] = wide


def feed_forward(low_all, widen, narrow, widen_bias, pre_to, hidden_to, part_to):
    def block(first, size):
        rows = pl.ds(first, size)
        weight = widen[...].reshape(low_all.shape[1], widen.shape[2])
        pre = dot_n(low_all[rows], weight) + widen_bias
        pre_to[rows] = pre
        hidden = (0.5 * pre * (1.0 + gelu_parts(pre)[0])).astype(BF16)
        hidden_to[rows] = hidden
        part_to[rows] = dot_n(hidden, narrow[...]).astype(BF16)

    row_blocks(low_all.shape[0], block)


def open_kernel(n, low, width, slots, step, io, *refs):
    tok_ref, cot_ref, vectors, refs = refs[0], refs[1], refs[2:10], refs[10:]
    qkv_ref, out_ref, widen_ref, narrow_ref, mask, kpos_ref, qpos_ref = refs[:7]
    refs = refs[7:]
    x_to, cot_to, grad_to, sums_to, normed_to, own_ref, qkv_all, out_all = refs[:8]
    feats_to, qkv_bias, widen_bias, att_ref, low_ref, lse_ref, oth_ref, widen_all = refs[8:16]
    value_to, tok_all, pre_to, hidden_to, part_to, narrow_all = refs[16:22]
    refs = refs[22:]
    tok_own, pack, qkv_send, out_rows, widen_raw, narrow_raw, widen_send, narrow_to = refs[:8]
    pack_all, widen, refs = refs[8], refs[9], refs[10:]
    g_ss, g_rs, g_ls, p_ss, p_rs, a_ss, a_rs, w_ss, w_rs, o_ss, o_rs, l_sem = refs[:12]
    kv_ss, kv_rs, n_ss, n_rs, refs = refs[12], refs[13], refs[14], refs[15], refs[16:]
    scatter_refs, (second_ss, second_rs, second_ls) = refs[:5], refs[5:]
    p = Place(n)
    s, c, h = p.s, p.c, p.h
    widen_load = fetch(widen_ref, widen_raw, l_sem.at[4])
    narrow_load = fetch(narrow_ref, narrow_raw, l_sem.at[5])
    padded = qkv_send.shape[1]
    tok_own[...] = with_gaps(tok_ref[s], n, padded)
    greet_all(p)

    def pack_copy(a, b):
        target = (lax.rem(s + a, 2), c, lax.rem(h + b, n))
        return remote(pack, pack_all.at[s, h], p_ss.at[a, b], p_rs.at[a, b], target)

    tokens = Gather(p, tok_own, tok_all, g_ss, g_rs, g_ls)
    qkv = Spread(p, qkv_send, qkv_all, a_ss, a_rs, l_sem.at[1])
    wide = Spread(p, widen_send, widen_all, w_ss, w_rs, l_sem.at[3])
    narrow = RowSwap(p, narrow_to, narrow_all, n_ss, n_rs, l_sem.at[6])
    out = RowSwap(p, out_rows, out_all, o_ss, o_rs, l_sem.at[2])
    pack_own = pltpu.make_async_copy(pack, pack_all.at[s, h], l_sem.at[0])
    tokens.start()
    io.need(10)
    lay_first(low, qkv_ref, qkv_send)
    qkv.start()
    lay_vectors(vectors, pack)
    for a, b in others(n):
        pack_copy(a, b).start()
    pack_own.start()

    def start_out():
        io.need(1, 11)
        lay_rows(low, out_ref, out_rows)
        out.start()

    def lay_cot():
        values = with_gaps(cot_ref[s], n, padded)
        cot_to[...] = values
        grad_to[...] = values.astype(F32)
        sums_to[...] = jnp.sum(grad_to[...], axis=0, keepdims=True)
        x_to[...] = tok_own[...].astype(F32)

    hide = narrow_ref.shape[0]
    work = [start_out, widen_load.wait]
    work += [functools.partial(lay_widen, j, widen_raw, widen_send) for j in range(n)]
    work += [lay_cot, narrow_load.wait]
    work += [
        functools.partial(lay_narrow, first, min(208, hide - first), n, narrow_raw, narrow_to)
        for first in range(0, hide, 208)
    ]
    qkv_steps = qkv.steps()
    for token_step in tokens.steps():
        run_next(work)
        run_next(work)
        token_step()
        run_next(qkv_steps)
    for rest in work:
        rest()
    extra = narrow_to.shape[0] - hide
    if extra:
        narrow_to[hide:] = jnp.zeros((extra, n * padded), BF16)
    for member in range(2):
        if narrow_all.shape[1] > narrow_to.shape[0]:
            spare = (narrow_all.shape[1] - narrow_to.shape[0], n * padded)
            narrow_all[member, narrow_to.shape[0] :] = jnp.zeros(spare, BF16)
    tokens.finish()
    wide.start()
    pack_own.wait()
    for a, b in others(n):
        pack_copy(a, b).wait_recv()
    spread_vectors(n, low, width, pack_all, feats_to, qkv_bias, widen_bias)

    normed = part_to

    def first_norm(first, size):
        some = pl.ds(first, size)
        unit = unit_rows(tok_all[some].astype(F32), mask[...], width)[0]
        normed[some] = (unit * feats_to[0, 0:1] + feats_to[0, 1:2]).astype(BF16)

    rows = tok_all.shape[0]
    row_blocks(rows, first_norm)
    normed_store = fetch(normed, normed_to, l_sem.at[7])
    for rest in qkv_steps:
        rest()
    qkv.finish()
    narrow.start()
    io.done(6)
    sh = slots * HD

    def project(first, size):
        some = pl.ds(first, size)
        weight = qkv_all[0].reshape(n * padded, 3 * sh)
        own_ref[some] = (dot_n(normed[some], weight) + qkv_bias[0]).astype(BF16)

    row_blocks(rows, project)
    swap = remote(own_ref.at[:, pl.ds(sh, 2 * sh)], oth_ref, kv_ss, kv_rs, p.sibling)
    swap.start()
    swap.wait_recv()
    out.step()
    wide_steps = wide.steps()
    chunk = attention(slots, step, own_ref, oth_ref, kpos_ref, qpos_ref, att_ref, low_ref, lse_ref)
    in_blocks(rows, step, chunk, [])
    out.finish()
    io.done(5, 7, 11, 12, 14)
    normed_store.wait()

    def give(first, size):
        some = pl.ds(first, size)
        part_to[some] = dot_n(low_ref[some], out_all[0]).astype(BF16)

    row_blocks(rows, give)

    scatter = Scatter(p, part_to, *scatter_refs)
    scatter.start()
    arrivals, crossings = wide_steps[: p.zn], wide_steps[p.zn :]
    early = len(arrivals) // 2
    for arrive in arrivals[:early]:
        arrive()
    second = Gather(p, tok_own, tok_all, second_ss, second_rs, second_ls)
    hr = tok_own.shape[0] // HALVES

    def rows_step(half):
        some = slice(half * hr, (half + 1) * hr)
        value = x_to[some] + (scatter.result(half) + feats_to[0, 2:3])
        value_to[some] = value
        unit = unit_rows(value, mask[...], width)[0]
        tok_own[some] = (unit * feats_to[0, 3:4] + feats_to[0, 4:5]).astype(BF16)

    by_halves(scatter, None, lambda half: None, [])
    for arrive in arrivals[early:]:
        arrive()
    for half in range(HALVES):
        rows_step(half)
        second.start([half])
    for second_step in second.steps():
        second_step()
    narrow.step()
    for crossing in crossings:
        crossing()
    second.finish()
    scatter.finish()
    for a, b in others(n):
        pack_copy(a, b).wait_send()
    swap.wait_send()
    narrow.finish()
    wide.finish()
    load = fetch(widen_all.at[0], widen, l_sem.at[4])
    io.done(17, 21)
    load.wait()
    feed_forward(tok_all, widen, narrow_all.at[0], widen_bias[0], pre_to, hidden_to, part_to)


def open_call(n, low, slots, padded, tokens, cotangent, vectors, weights, mask, kpos, qpos):
    qkv, out, widen, narrow = weights
    share, hidden = widen.shape
    width = n * share
    hide = hidden // n
    hide_full = -(-hide // 128) * 128
    sh = slots * HD
    full = n * padded
    rows = tokens.shape[1]
    total = n * rows
    zn = n // 2
    lanes = max(hide_full, -(-2 * share // 128) * 128)
    blocks = (n, padded, 3 * sh)
    wide = (n, padded, hide_full)

    def low_type(*shape):
        return jax.ShapeDtypeStruct(shape, BF16)

    def full_type(*shape):
        return jax.ShapeDtypeStruct(shape, F32)

    return staged_call(
        functools.partial(open_kernel, n, low, width, slots, min(total, 256)),
        "open",
        0,
        (tokens, cotangent, *vectors, qkv, out, widen, narrow, mask, kpos, qpos),
        [
            full_type(rows, full),
            low_type(rows, full),
            full_type(rows, full),
            full_type(1, full),
            low_type(total, full),
            low_type(total, 3 * sh),
            low_type(2, *blocks),
            low_type(2, sh, full),
            full_type(2, 16, full),
            full_type(2, 1, 3 * sh),
            full_type(2, 1, hide_full),
            full_type(sh, total),
            low_type(total, sh),
            full_type(slots, total),
            low_type(total, 2 * sh),
            low_type(2, *wide),
            full_type(rows, full),
            low_type(total, full),
            full_type(total, hide_full),
            low_type(total, hide_full),
            low_type(total, full),
            low_type(2, hide_full, full),
        ],
        [
            pltpu.VMEM((rows, full), BF16),
            pltpu.VMEM((16, lanes), BF16),
            pltpu.VMEM(blocks, BF16),
            pltpu.VMEM((sh, full), BF16),
            pltpu.VMEM(widen.shape, BF16),
            pltpu.VMEM(narrow.shape, BF16),
            pltpu.VMEM(wide, BF16),
            pltpu.VMEM((-(-hide // 16) * 16, full), BF16),
            pltpu.VMEM((2, n, 16, lanes), BF16),
            pltpu.VMEM(wide, BF16),
        ]
        + gather_scratch(n)
        + [DMA((2, n))] * 2
        + [DMA((4, zn))] * 4
        + [DMA((2,))] * 2
        + [DMA((8,)), DMA, DMA, DMA((2,)), DMA((2,))]
        + scatter_scratch(n, rows, full)
        + gather_scratch(n),
        late=(1, 10, 11),
        plain=(12, 13),
        early=(5, 6, 7, 11, 12, 14, 17, 18, 19, 20, 21),
        raw=(4, 15),
    )


def settle_kernel(low, sizes, *refs):
    sources, vec_ref, came_ref, streams, refs = refs[:4], refs[4], refs[5], refs[6:10], refs[10:]
    outs, stream_to, vectors, refs = refs[:4], refs[4:6], refs[6:14], refs[14:]
    loaded, made, in_sem, out_sem = refs[:4], refs[4:8], refs[8], refs[9]
    qkv_ref, widen_ref, out_ref, narrow_ref = loaded
    qkv_to, widen_to, out_to, narrow_to = made
    order = (3, 1, 0, 2)
    loads = {i: fetch(sources[i], loaded[i], in_sem.at[i]) for i in order}
    n, padded, _ = widen_ref.shape
    share = out_to.shape[0]
    hide = narrow_to.shape[0]
    width = qkv_to.shape[1] // 3
    sh = qkv_ref.shape[2] // 3
    s = lax.axis_index("section")

    def without_gaps(values):
        pieces = [values[:, j * padded : j * padded + share] for j in range(n)]
        return jnp.concatenate(pieces, axis=1)

    def lay_rows_back(ref, to):
        to[...] = without_gaps(ref[: to.shape[0]]).astype(F32)

    def lay_qkv_back():
        qkv_to[...] = jnp.zeros_like(qkv_to)
        for j in range(n):
            for t in range(3):
                first = t * width + HD * low[j]
                block = qkv_ref[j, :share, t * sh : (t + 1) * sh]
                qkv_to[:, first : first + sh] += block.astype(F32)

    def lay_widen_back():
        pieces = [widen_ref[j, :share, :hide] for j in range(n)]
        widen_to[...] = jnp.concatenate(pieces, axis=1).astype(F32)

    makers = (
        lay_qkv_back,
        lay_widen_back,
        functools.partial(lay_rows_back, out_ref, out_to),
        functools.partial(lay_rows_back, narrow_ref, narrow_to),
    )
    for item, to in enumerate(stream_to):
        first, second = (ref[...] for ref in streams[2 * item : 2 * item + 2])
        to[s] = without_gaps(jnp.where(s == 0, first, second))
        to[1 - s] = without_gaps(came_ref[item].astype(F32))
    for row, (size, to) in enumerate(zip(sizes, vectors)):
        to[...] = vec_ref[row : row + 1, :size]
    stores = []
    for i in order:
        loads[i].wait()
        makers[i]()
        stores.append(fetch(made[i], outs[i], out_sem.at[i]))
    for store in stores:
        store.wait()


def settle_call(low, share, hide, qkv, widen, out, narrow, vec, came, *streams):
    n = widen.shape[0]
    width = n * share
    rows = came.shape[1]
    sizes = [share] * 6 + [2 * share, hide]
    big = [(share, 3 * width), (share, n * hide), (share, width), (hide, width)]
    return pl.pallas_call(
        functools.partial(settle_kernel, low, sizes),
        out_shape=[jax.ShapeDtypeStruct(shape, F32) for shape in big]
        + [
            jax.ShapeDtypeStruct((2, rows, width), F32),
            jax.ShapeDtypeStruct((2, rows, width), F32),
        ]
        + [jax.ShapeDtypeStruct((1, size), F32) for size in sizes],
        in_specs=[ANY_SPEC] * 4 + [VMEM_SPEC] * 6,
        out_specs=[ANY_SPEC] * 4 + [VMEM_SPEC] * 10,
        scratch_shapes=[pltpu.VMEM(m.shape, BF16) for m in (qkv, widen, out, narrow)]
        + [pltpu.VMEM(shape, F32) for shape in big]
        + [DMA((4,)), DMA((4,))],
        compiler_params=params(),
        name="settle",
    )(qkv, widen, out, narrow, vec, came, *streams)


def unit_rows(values, mask, width):
    center = (values - jnp.sum(values, axis=-1, keepdims=True) * (1.0 / width)) * mask
    spread = jnp.sum(center * center, axis=-1, keepdims=True) * (1.0 / width)
    scale = lax.rsqrt(spread + EPSILON)
    return center * scale, scale


def norm_back(grad, unit, scale, gain, width):
    inner = grad * gain
    mean = jnp.sum(inner, axis=-1, keepdims=True) * (1.0 / width)
    along = jnp.sum(inner * unit, axis=-1, keepdims=True) * (1.0 / width)
    return (inner - mean - unit * along) * scale


def forward_kernel(n, width, layer, io, *refs):
    middle = layer is not None
    part, base, feats, mask = refs[:4]
    refs = refs[4:]
    if middle:
        bias, gain, shift = (feats[layer, row : row + 1] for row in (2, 3, 4))
        widen_all, narrow_all, widen_bias, refs = refs[0], refs[1], refs[2], refs[3:]
    else:
        bias, gain, shift = feats[0, 5:6], feats[1, 0:1], feats[1, 1:2]
    value_to, low_all, refs = refs[0], refs[1], refs[2:]
    if middle:
        pre_to, hidden_to, part_to, refs = refs[0], refs[1], refs[2], refs[3:]
    own, g_ss, g_rs, g_ls = refs[5:9]
    p = Place(n)
    greet(p, line=True)
    scatter = Scatter(p, part, *refs[:5])
    scatter.start()
    loads = []
    if middle:
        widen, narrow, load_sems = refs[9:]
        loads.append(fetch(widen_all.at[layer], widen, load_sems.at[0]))
        loads.append(fetch(narrow_all.at[layer], narrow, load_sems.at[1]))
    gather = Gather(p, own, low_all, g_ss, g_rs, g_ls)
    hr = own.shape[0] // HALVES

    def rows_step(half):
        rows = slice(half * hr, (half + 1) * hr)
        value = base[rows] + (scatter.result(half) + bias)
        value_to[rows] = value
        own[rows] = (unit_rows(value, mask[...], width)[0] * gain + shift).astype(BF16)

    by_halves(scatter, gather, rows_step, [])
    gather.finish()
    for load in loads:
        load.wait()
    if middle:
        io.done(1)
        feed_forward(low_all, widen, narrow, widen_bias[layer], pre_to, hidden_to, part_to)
    scatter.finish()


def scatter_scratch(n, rows, full):
    zn = n // 2
    piece = (HALVES, rows // HALVES, full)
    return [
        pltpu.VMEM((zn,) + piece, BF16),
        pltpu.VMEM((zn + 1,) + piece, BF16),
        pltpu.VMEM((zn,) + piece, BF16),
        DMA((4, zn, HALVES)),
        DMA((4, zn, HALVES)),
    ]


def gather_scratch(n):
    zn = n // 2
    return [DMA((4, zn, HALVES)), DMA((4, zn, HALVES)), DMA((HALVES,))]


def forward_call(n, collective_id, width, part, *local, layer=None, feed=()):
    total_rows, full = part.shape
    rows = total_rows // n
    shapes = [
        jax.ShapeDtypeStruct((rows, full), F32),
        jax.ShapeDtypeStruct((total_rows, full), BF16),
    ]
    scratch = scatter_scratch(n, rows, full)
    scratch += [pltpu.VMEM((rows, full), BF16)] + gather_scratch(n)
    middle = layer is not None
    if middle:
        widen, narrow, _ = feed
        hide = widen.shape[3]
        shapes += [
            jax.ShapeDtypeStruct((total_rows, hide), F32),
            jax.ShapeDtypeStruct((total_rows, hide), BF16),
            jax.ShapeDtypeStruct((total_rows, full), BF16),
        ]
        scratch += [pltpu.VMEM(widen.shape[1:], BF16), pltpu.VMEM((hide, full), BF16), DMA((2,))]
    return staged_call(
        functools.partial(forward_kernel, n, width, layer),
        "forward_rows",
        collective_id,
        (part, *local, *feed),
        shapes,
        scratch,
        plain=(4, 5) if middle else (),
        early=(1, 2, 3, 4) if middle else (),
        raw=() if middle else (1,),
    )


def back_rows(scatter, half, base, grad, gain, mask, width):
    hr = scatter.hr
    rows = slice(half * hr, (half + 1) * hr)
    total = scatter.result(half)
    unit, scale = unit_rows(base[rows], mask[...], width)
    value = grad[rows] + norm_back(total, unit, scale, gain, width)
    low = value.astype(BF16)
    terms = (total * unit, total, low.astype(F32))
    return rows, value, low, [jnp.sum(term, axis=0, keepdims=True) for term in terms]


def resid_kernel(n, width, layer, io, *refs):
    base, grad, feats, mask, normed, hidden_pre, hidden, outs, widen, narrow = refs[:10]
    gain = feats[layer, 3:4]
    value_to, sums_to, low_all, wide_to, wide_came, slim_to, pre_sums = refs[10:17]
    refs = refs[17:]
    own, g_ss, g_rs, g_ls = refs[5:9]
    wide, wide_in, wide_ss, wide_rs, slim, slim_in, slim_ss, slim_rs, x_ss, x_rs = refs[9:19]
    part, pre = refs[19:]
    p = Place(n)
    greet(p, line=True, over=True, sibling=True)
    io.need(9, 7, 5)

    def inner(first, size):
        rows = pl.ds(first, size)
        values = hidden_pre[rows]
        act, square = gelu_parts(values)
        slope = 0.5 * (1.0 + act) + 0.5 * values * (1.0 - act * act) * GELU_A * (
            1.0 + 3.0 * GELU_B * square
        )
        found = (dot_t(outs[rows], narrow[...]) * slope).astype(BF16)
        pre[rows] = found

    def outer(first, size):
        rows = pl.ds(first, size)
        weight = widen[...].reshape(part.shape[1], widen.shape[2])
        part[rows] = dot_t(pre[rows], weight).astype(BF16)

    row_blocks(part.shape[0], inner)
    io.need(8)
    row_blocks(part.shape[0], outer)
    scatter = Scatter(p, part, *refs[:5])
    scatter.start()
    gather = Gather(p, own, low_all, g_ss, g_rs, g_ls)
    wide_fold = Fold(p, wide, wide_in, wide_to, wide_ss, wide_rs)
    slim_fold = Fold(p, slim, slim_in, slim_to, slim_ss, slim_rs)
    cross = Cross(p, wide_to, wide_came, x_ss, x_rs, 1 - layer)

    def pre_sum():
        pre_sums[...] = jnp.sum(pre[...].astype(F32), axis=0, keepdims=True)

    io.need(4, 6)
    for step in product(normed, pre, wide):
        step()
    wide_fold.start()

    def wide_done():
        cross.start()
        io.done(3)

    work = product(hidden, outs, slim) + wide_fold.steps() + [wide_done, slim_fold.start, pre_sum]
    work += slim_fold.steps() + [functools.partial(io.done, 5)]
    sums = []

    def rows_step(half):
        rows, value, low, terms = back_rows(scatter, half, base, grad, gain, mask, width)
        value_to[rows] = value
        own[rows] = low
        sums.append(jnp.concatenate(terms, axis=0))

    by_halves(scatter, gather, rows_step, work, 3)
    sums_to[...] = sum(sums)
    for rest in work:
        rest()
    gather.finish()
    scatter.finish()
    for job in (wide_fold, slim_fold, cross):
        job.finish()


def resid_call(n, collective_id, width, layer, hide, *args):
    base, normed, hidden = args[0], args[4], args[6]
    rows = base.shape[0]
    total_rows, full = normed.shape
    zn = n // 2
    wide = (zn, full // n, hidden.shape[1])
    half = -(-hide // 32) * 16
    slim = (1, half, full)
    return staged_call(
        functools.partial(resid_kernel, n, width, layer),
        "back_resid",
        collective_id,
        args,
        [
            jax.ShapeDtypeStruct((rows, full), F32),
            jax.ShapeDtypeStruct((3, full), F32),
            jax.ShapeDtypeStruct((total_rows, full), BF16),
            jax.ShapeDtypeStruct(wide, BF16),
            jax.ShapeDtypeStruct(wide, BF16),
            jax.ShapeDtypeStruct(slim, BF16),
            jax.ShapeDtypeStruct((1, hidden.shape[1]), F32),
        ],
        scatter_scratch(n, rows, full)
        + [pltpu.VMEM((rows, full), BF16)]
        + gather_scratch(n)
        + fold_scratch((full, hidden.shape[1]), wide)
        + fold_scratch((2 * half, full), slim)
        + [DMA, DMA]
        + [
            pltpu.VMEM((total_rows, full), BF16),
            pltpu.VMEM(hidden.shape, BF16),
        ],
        late=(9, 7, 5, 8, 4, 6),
        layers={8: layer, 9: layer},
        early=(3, 5),
        raw=(2, 4),
    )


def input_kernel(n, width, source, low, io, *refs):
    part, base, grad, feats, mask, normed, triple, att, resid, slim = refs[:10]
    gain = feats[1, 0:1]
    value_to, sums_to, low_all, qkv_to, out_to, slim_came, triple_sums = refs[10:17]
    refs = refs[17:]
    own, g_ss, g_rs, g_ls = refs[5:9]
    qkv, qkv_in, qkv_ss, qkv_rs, out, out_in, out_ss, out_rs, x_ss, x_rs = refs[9:]
    p = Place(n)
    greet(p, line=True, over=True, sibling=True)
    scatter = Scatter(p, part, *refs[:5])
    scatter.start()
    cross = Cross(p, slim, slim_came, x_ss, x_rs, source)
    cross.start()
    gather = Gather(p, own, low_all, g_ss, g_rs, g_ls)
    qkv_fold = Fold(p, qkv, qkv_in, qkv_to, qkv_ss, qkv_rs)
    out_fold = Fold(p, out, out_in, out_to, out_ss, out_rs)

    def triple_sum():
        triple_sums[...] = jnp.sum(triple[...].astype(F32), axis=0, keepdims=True)

    work = [functools.partial(io.need, 5, 6)] + product(normed, triple, qkv)
    work += [qkv_fold.start, functools.partial(io.need, 7, 8)]
    work += [functools.partial(home_rows, att, resid, out, low, width // n), out_fold.start]
    work += qkv_fold.steps() + [functools.partial(io.done, 3), triple_sum]
    work += out_fold.steps() + [functools.partial(io.done, 4)]
    sums = []

    def rows_step(half):
        rows, value, lower, terms = back_rows(scatter, half, base, grad, gain, mask, width)
        value_to[rows] = value
        own[rows] = lower
        sums.append(jnp.concatenate(terms, axis=0))

    by_halves(scatter, gather, rows_step, work, 2)
    sums_to[...] = sum(sums)
    for rest in work:
        rest()
    gather.finish()
    scatter.finish()
    for job in (qkv_fold, out_fold, cross):
        job.finish()


def input_call(n, collective_id, width, source, low, part, base, grad, feats, mask, *operands):
    normed, triple, att, resid, slim = operands
    total_rows, full = part.shape
    rows = total_rows // n
    zn = n // 2
    qkv = (zn, full // n, triple.shape[1])
    out = (1, att.shape[1] // 2, full)
    return staged_call(
        functools.partial(input_kernel, n, width, source, low),
        "back_input",
        collective_id,
        (part, base, grad, feats, mask) + operands,
        [
            jax.ShapeDtypeStruct((rows, full), F32),
            jax.ShapeDtypeStruct((3, full), F32),
            jax.ShapeDtypeStruct((total_rows, full), BF16),
            jax.ShapeDtypeStruct(qkv, BF16),
            jax.ShapeDtypeStruct(out, BF16),
            jax.ShapeDtypeStruct(slim.shape, BF16),
            jax.ShapeDtypeStruct((1, triple.shape[1]), F32),
        ],
        scatter_scratch(n, rows, full)
        + [pltpu.VMEM((rows, full), BF16)]
        + gather_scratch(n)
        + fold_scratch((full, triple.shape[1]), qkv)
        + fold_scratch((att.shape[1], full), out)
        + [DMA, DMA],
        late=(5, 6, 7, 8),
        plain=(9,),
        early=(3, 4),
        raw=(2, 5),
    )


def finale_kernel(n, width, low, io, *refs):
    part, base, grad, feats, mask, normed, triple, att, resid = refs[:9]
    slims, slim_cames, qkv_far, out_far, vecs = refs[9:11], refs[11:13], refs[13], refs[14], refs[15:22]
    layer_outs, upper_d_in, wides, refs = refs[22:24], refs[24], refs[25:29], refs[29:]
    value_to, slim_to, qkv_to, out_to, vec_to, streams_to, wide_to = refs[:7]
    refs = refs[7:]
    qkv, qkv_fold_in, qkv_ss, qkv_rs, out, out_fold_in, out_ss, out_rs = refs[5:13]
    qkv_own, qkv_in, qkv_sum, out_own, out_in, out_sum = refs[13:19]
    slim_sum, slim_pair, vec, vec_in, vec_sum, vec_sib, streams = refs[19:26]
    a_ss, a_rs, x_ss, x_rs, v_ss, v_rs, r_ss, r_rs, ls = refs[26:35]
    wide_sum, wide_pair, w_ss, w_rs = refs[35:]
    p = Place(n)
    s, c, h, z, zn = p.s, p.c, p.h, p.z, p.zn
    share = width // n
    greet_all(p)
    scatter = Scatter(p, part, *refs[:5])
    scatter.start()

    first = slim_cames[0].shape[1]
    rest = slim_pair.shape[2] - first
    choices = (
        (
            (wides[0], wide_pair.at[0], 5),
            (wides[1], wide_pair.at[1], 6),
            (slims[0], slim_pair.at[0], 1),
            (slim_cames[0], slim_pair.at[1, :, pl.ds(0, first)], 4),
        ),
        (
            (wides[2], wide_pair.at[0], 5),
            (wides[3], wide_pair.at[1], 6),
            (slims[1], slim_pair.at[0], 1),
            (slim_cames[1].at[:, pl.ds(0, first)], slim_pair.at[1, :, pl.ds(0, first)], 4),
            (slim_cames[1].at[:, pl.ds(first, rest)], slim_pair.at[1, :, pl.ds(first, rest)], 7),
        ),
    )
    for section, chosen in enumerate(choices):

        @pl.when(s == section)
        def _():
            for src, dst, item in chosen:
                pltpu.make_async_copy(src, dst, ls.at[item]).start()

    def chosen_wait(item):
        src, dst, sem = choices[0][item]
        pltpu.make_async_copy(src, dst, ls.at[sem]).wait()

    slim_cross = remote(
        slims[0].at[:, pl.ds(first, rest)],
        slim_pair.at[1, :, pl.ds(first, rest)],
        x_ss.at[zn + 2],
        x_rs.at[zn + 2],
        p.over,
    )
    wide_back = Home(p, wide_sum, wide_to, w_ss, w_rs, ls.at[8])
    chosen_wait(0)
    chosen_wait(1)
    for k in list(range(1, zn)) + [0]:
        far = p.flip(k)
        total = wide_pair[0, far].astype(F32) + wide_pair[1, far].astype(F32)
        wide_sum[far] = total.astype(BF16)
        wide_back.start(k)
    back = Home(p, qkv_sum, qkv_to, a_ss, a_rs, ls.at[0])

    def x_block(k, src=qkv_far):
        far = p.flip(k)
        return remote(src.at[far], qkv_in.at[far], x_ss.at[k], x_rs.at[k], p.over)

    def out_cross(src=out_far):
        return remote(src, out_in, x_ss.at[zn], x_rs.at[zn], p.over)

    stream_cross = remote(streams, streams_to, x_ss.at[zn + 1], x_rs.at[zn + 1], p.over)

    def start_far():
        @pl.when(s == 0)
        def _():
            for k in range(zn):
                x_block(k).start()
            out_cross().start()

    def start_own(k):
        @pl.when(s == 1)
        def _():
            x_block(k, qkv_own).start()

    def start_own_out():
        @pl.when(s == 1)
        def _():
            out_cross(out_own).start()

    qkv_fold = Fold(p, qkv, qkv_fold_in, qkv_own, qkv_ss, qkv_rs)
    out_fold = Fold(p, out, out_fold_in, out_own, out_ss, out_rs)

    io.need(13, 14)
    start_far()
    io.need(5, 6)
    for step in product(normed, triple, qkv):
        step()
    qkv_fold.start()
    io.need(7, 8)
    work = [functools.partial(home_rows, att, resid, out, low, share), out_fold.start]
    work += qkv_fold.steps()
    work += [functools.partial(start_own, k) for k in list(range(1, zn)) + [0]]
    work += out_fold.steps() + [start_own_out]
    sums = []

    def rows_step(half):
        rows, value, lower, terms = back_rows(scatter, half, base, grad, feats[0, 0:1], mask, width)
        value_to[rows] = value
        sums.append(jnp.concatenate(terms, axis=0))

    by_halves(scatter, None, rows_step, work, 3)
    for rest in work:
        rest()

    io.need(22, 23, 24)
    streams[0] = jnp.where(s == 0, layer_outs[1][...], layer_outs[0][...]).astype(BF16)
    streams[1] = jnp.where(s == 0, upper_d_in[...], value_to[...]).astype(BF16)
    io.done(0)
    stream_cross.start()

    ones = (sum(sums), vecs[0][...])
    twos, triples, pres = vecs[1:3], (None, vecs[3]), vecs[4:6]
    lanes = vec.shape[3]
    padded = base.shape[1] // n
    sh = triple.shape[1] // 3
    for layer in range(2):
        one, two = ones[layer], twos[layer][...]
        outs = vecs[6][...] if layer else ones[1][2:3]
        features = jnp.concatenate([one[0:2], two[2:3], two[0:2], outs], axis=0)
        if layer:
            found = triples[1][...]
        else:
            found = jnp.sum(triple[...].astype(F32), axis=0, keepdims=True)
        bias = jnp.zeros((1, 2 * width), F32)
        for j, first in enumerate(low):
            spots = []
            for begin in (0, 2 * sh):
                spots += [
                    jnp.zeros((1, HD * first), F32),
                    found[:, begin : begin + sh],
                    jnp.zeros((1, width - sh - HD * first), F32),
                ]
            spots = [spot for spot in spots if spot.shape[1]]
            bias = jnp.where(h == j, jnp.concatenate(spots, axis=1), bias)
        for i in range(n):
            pieces = [
                features[:, i * padded : (i + 1) * padded],
                bias[:, i * 2 * share : (i + 1) * 2 * share],
                jnp.where(h == i, pres[layer][...], 0.0),
            ]
            wide_pieces = []
            for piece in pieces:
                rows, size = piece.shape
                if size < lanes:
                    piece = jnp.concatenate([piece, jnp.zeros((rows, lanes - size), F32)], axis=1)
                wide_pieces.append(piece)
            vec[layer, i] = jnp.concatenate(wide_pieces, axis=0)

    def vec_copy(a, b):
        l, i = lax.rem(s + a, 2), lax.rem(h + b, n)
        return remote(vec.at[l, i], vec_in.at[s, h], v_ss.at[a, b], v_rs.at[a, b], (l, c, i))

    for a, b in others(n):
        vec_copy(a, b).start()

    for k in list(range(1, zn)) + [0]:
        x_block(k).wait_recv()
        add_home(p, qkv_sum, p.flip(k), qkv_own, qkv_in, qkv_far, qkv_in)
        back.start(k)
    out_cross().wait_recv()
    add_home(p, out_sum, 0, out_own, out_in, out_far, out_in)
    for k in range(zn):
        x_block(k).wait_send()
    chosen_wait(2)
    chosen_wait(3)

    @pl.when(s == 1)
    def _():
        slim_cross.start()
        src, dst, sem = choices[1][4]
        pltpu.make_async_copy(src, dst, ls.at[sem]).wait()

    for step in wide_back.steps():
        step()

    @pl.when(s == 0)
    def _():
        slim_cross.wait_recv()

    slim_sum[0] = (slim_pair[0, 0].astype(F32) + slim_pair[1, 0].astype(F32)).astype(BF16)

    def row_copies(w, src, dst):
        half = src.shape[1]
        piece = dst.at[pl.ds(pl.multiple_of(c * half, 16), half)]
        return (
            pltpu.make_async_copy(src.at[0], piece, ls.at[2 + w]),
            remote(src.at[0], piece, r_ss.at[w], r_rs.at[w], p.sibling),
        )

    copies = row_copies(0, slim_sum, slim_to) + row_copies(1, out_sum, out_to)
    for copy in copies:
        copy.start()
    total = vec[s, h]
    for a, b in others(n):
        vec_copy(a, b).wait_recv()
        total = total + vec_in[lax.rem(s + a, 2), lax.rem(h + n - b, n)]
    vec_sum[...] = total
    vec_share = remote(vec_sum, vec_sib, r_ss.at[2], r_rs.at[2], p.sibling)
    vec_share.start()
    for step in back.steps():
        step()
    vec_share.wait_recv()
    vec_to[...] = total + vec_sib[...]
    vec_share.wait_send()
    back.finish()
    wide_back.finish()

    @pl.when(s == 1)
    def _():
        slim_cross.wait_send()

    for w in range(2):
        copies[2 * w].wait()
        copies[2 * w + 1].wait_recv()
        copies[2 * w + 1].wait_send()
    for a, b in others(n):
        vec_copy(a, b).wait_send()
    out_cross().wait_send()
    stream_cross.wait_recv()
    stream_cross.wait_send()
    for job in (scatter, qkv_fold, out_fold):
        job.finish()


def finale_call(n, collective_id, width, low, *args):
    part, triple, att = args[0], args[6], args[7]
    slim, lanes, wide = args[9].shape, args[19].shape[1], args[25].shape
    total_rows, full = part.shape
    rows = total_rows // n
    zn = n // 2
    qkv = (zn, full // n, triple.shape[1])
    out = (1, att.shape[1] // 2, full)
    return staged_call(
        functools.partial(finale_kernel, n, width, low),
        "finale",
        collective_id,
        args,
        [
            jax.ShapeDtypeStruct((rows, full), F32),
            jax.ShapeDtypeStruct((2 * slim[1], full), BF16),
            jax.ShapeDtypeStruct((n,) + qkv[1:], BF16),
            jax.ShapeDtypeStruct((2 * out[1], full), BF16),
            jax.ShapeDtypeStruct((8, lanes), F32),
            jax.ShapeDtypeStruct((2, rows, full), BF16),
            jax.ShapeDtypeStruct((n,) + wide[1:], BF16),
        ],
        scatter_scratch(n, rows, full)
        + fold_scratch((full, triple.shape[1]), qkv)
        + fold_scratch((att.shape[1], full), out)
        + [pltpu.VMEM(qkv, BF16)] * 3
        + [pltpu.VMEM(out, BF16)] * 3
        + [
            pltpu.VMEM(slim, BF16),
            pltpu.VMEM((2,) + slim, BF16),
            pltpu.VMEM((2, n, 8, lanes), F32),
            pltpu.VMEM((2, n, 8, lanes), F32),
            pltpu.VMEM((8, lanes), F32),
            pltpu.VMEM((8, lanes), F32),
            pltpu.VMEM((2, rows, full), BF16),
            DMA((2, zn)),
            DMA((2, zn)),
            DMA((zn + 3,)),
            DMA((zn + 3,)),
            DMA((2, n)),
            DMA((2, n)),
            DMA((3,)),
            DMA((3,)),
            DMA((9,)),
            pltpu.VMEM(wide, BF16),
            pltpu.VMEM((2,) + wide, BF16),
            DMA((2, zn)),
            DMA((2, zn)),
        ],
        late=(5, 6, 7, 8, 13, 14, 22, 23, 24),
        plain=(9, 10, 11, 12, 25, 26, 27, 28),
        early=(0,),
        raw=(1, 2, 3, 5, 6),
    )


def dot_t(a, b):
    return lax.dot_general(a, b, (((1,), (1,)), ((), ())), preferred_element_type=F32)


def dot_n(a, b):
    return lax.dot_general(a, b, (((1,), (0,)), ((), ())), preferred_element_type=F32)


def in_blocks(rows, step, chunk, between):
    count = rows // step
    if count <= 2:
        for b in range(count):
            chunk(b * step, rows // 2 if (b + 1) * step <= rows // 2 else rows, between)
    else:

        def body(b, carry, keys):
            chunk(pl.multiple_of(b * step, step), keys, [])
            return carry

        middle = count // 2 if count % 2 == 0 else 0
        lax.fori_loop(0, middle, functools.partial(body, keys=rows // 2), 0)
        lax.fori_loop(middle, count, functools.partial(body, keys=rows), 0)


def run_next(between):
    if between:
        between.pop(0)()


def attention(slots, step, own_ref, oth_ref, kpos_ref, qpos_ref, att_ref, low_ref, lse_ref):
    rows = own_ref.shape[0]
    sh = slots * HD
    power = HD**-0.5 * LOG2E

    def at(base, slot):
        return slice(base + slot * HD, base + (slot + 1) * HD)

    def chunk(first, seen, between):
        q_rows = pl.ds(first, step)
        qpos = qpos_ref[:, q_rows]
        for slot in range(slots):
            queries = own_ref[q_rows, at(0, slot)]
            keys = (own_ref[:seen, at(sh, slot)], oth_ref[:seen, at(0, slot)])
            values = (own_ref[:seen, at(2 * sh, slot)], oth_ref[:seen, at(sh, slot)])
            scores = []
            for part in range(2):
                allowed = kpos_ref[part * rows : part * rows + seen] <= qpos
                scores.append(jnp.where(allowed, dot_t(keys[part], queries), MASKED))
            top = jnp.maximum(
                jnp.max(scores[0], axis=0, keepdims=True), jnp.max(scores[1], axis=0, keepdims=True)
            )
            total = jnp.zeros_like(top)
            weighted = jnp.zeros((HD, step), F32)
            exps = []
            for part in range(2):
                e = jnp.exp2((scores[part] - top) * power)
                total = total + jnp.sum(e, axis=0, keepdims=True)
                exps.append(e)
            inverse = 1.0 / total
            for part in range(2):
                probs = (exps[part] * inverse).astype(BF16)
                weighted = weighted + dot_n(values[part].T, probs)
            att_ref[at(0, slot), q_rows] = weighted
            low_ref[q_rows, at(0, slot)] = weighted.T.astype(BF16)
            lse_ref[slot : slot + 1, q_rows] = top * power + jnp.log(total) * LOG2E
            run_next(between)

    return chunk


def attend_kernel(n, slots, step, layer, io, *refs):
    kpos_ref, qpos_ref, carried, out_all, normed, qkv_all, qkv_bias = refs[:7]
    att_ref, low_ref, lse_ref, oth_ref, part_to, carried_to, own_ref = refs[7:14]
    kv_ss, kv_rs, out_weight, qkv_weight, load_sems = refs[14:19]
    qkv_load = fetch(qkv_all.at[layer], qkv_weight, load_sems.at[1])
    out_load = fetch(out_all.at[layer], out_weight, load_sems.at[0])
    p = Place(n)
    rows = own_ref.shape[0]
    sh = slots * HD
    greet(p, line=True, sibling=True)
    job = Gather(p, carried, carried_to, *refs[19:])
    job.start()
    qkv_load.wait()
    io.need(4)
    between = job.steps()

    def project(first, size):
        some = pl.ds(first, size)
        weight = qkv_weight[...].reshape(normed.shape[1], 3 * sh)
        own_ref[some] = (dot_n(normed[some], weight) + qkv_bias[layer]).astype(BF16)

    row_blocks(rows, project)
    swap = remote(own_ref.at[:, pl.ds(sh, 2 * sh)], oth_ref, kv_ss, kv_rs, p.sibling)
    swap.start()
    run_next(between)
    run_next(between)
    swap.wait_recv()
    chunk = attention(slots, step, own_ref, oth_ref, kpos_ref, qpos_ref, att_ref, low_ref, lse_ref)
    in_blocks(rows, step, chunk, between)
    out_load.wait()

    def give(first, size):
        some = pl.ds(first, size)
        part_to[some] = dot_n(low_ref[some], out_weight[...]).astype(BF16)

    row_blocks(rows, give)
    io.done(0, 1, 4, 6)
    for rest in between:
        rest()
    swap.wait_send()
    job.finish()


def attend_call(n, collective_id, slots, layer, kpos, qpos, carried, out_all, *source):
    rows = qpos.shape[1]
    sh = slots * HD
    full = out_all.shape[2]
    return staged_call(
        functools.partial(attend_kernel, n, slots, min(rows, 256), layer),
        "attend",
        collective_id,
        (kpos, qpos, carried, out_all, *source),
        [
            jax.ShapeDtypeStruct((sh, rows), F32),
            jax.ShapeDtypeStruct((rows, sh), BF16),
            jax.ShapeDtypeStruct((slots, rows), F32),
            jax.ShapeDtypeStruct((rows, 2 * sh), BF16),
            jax.ShapeDtypeStruct((rows, full), BF16),
            jax.ShapeDtypeStruct((n * carried.shape[0], full), BF16),
            jax.ShapeDtypeStruct((rows, 3 * sh), BF16),
        ],
        [
            DMA,
            DMA,
            pltpu.VMEM((sh, full), BF16),
            pltpu.VMEM(source[1].shape[1:], BF16),
            DMA((2,)),
        ]
        + gather_scratch(n),
        late=(4,),
        plain=(3, 5),
        early=(0, 1, 4, 6),
        raw=(5,),
    )


def attend_back_kernel(n, slots, step, layer, last, home, io, *refs):
    own_ref, oth_ref, resid, att_ref, lse_ref, kpos_ref, qpos_ref, out_all, qkv_all = refs[:9]
    refs = refs[9:]
    if last:
        part_ref, base_ref, feats = refs[:3]
        refs = refs[3:]
    if home:
        slim, refs = refs[0], refs[1:]
    triple_ref, part_to, refs = refs[0], refs[1], refs[2:]
    if last:
        value_ref, refs = refs[0], refs[1:]
    if home:
        slim_came, refs = refs[0], refs[1:]
    dq_t, dkv_own, dkv_oth, came, kv_ss, kv_rs = refs[:6]
    grad_ref, out_weight, qkv_weight, load_sems = refs[6:10]
    out_load = fetch(out_all.at[layer], out_weight, load_sems.at[0])
    qkv_load = fetch(qkv_all.at[layer], qkv_weight, load_sems.at[1])
    p = Place(n)
    rows = own_ref.shape[0]
    sh = slots * HD
    scale = HD**-0.5
    greet(p, line=last, sibling=True, over=home)
    between = []
    if last:
        scatter = Scatter(p, part_ref, *refs[10:])
        scatter.start()
        between = scatter.steps()
    if home:
        x_ss, x_rs = refs[10:]
        rows_first = slim.at[:, pl.ds(0, slim_came.shape[1])]
        cross = Cross(p, rows_first, slim_came, x_ss, x_rs, 1)
        cross.start()
    io.need(2)
    out_load.wait()

    def enter(first, size):
        some = pl.ds(first, size)
        grad_ref[some] = dot_t(resid[some], out_weight[...]).astype(BF16)

    row_blocks(rows, enter)
    io.need(0, 1, 3)

    def at(base, slot):
        return slice(base + slot * HD, base + (slot + 1) * HD)

    dq_t[...] = jnp.zeros_like(dq_t)
    swap = remote(dkv_oth, came, kv_ss, kv_rs, p.sibling)
    for part in (1, 0):
        dkv = (dkv_own, dkv_oth)[part]
        src = (own_ref, oth_ref)[part]
        base = (sh, 0)[part]
        dkv[...] = jnp.zeros_like(dkv)

        def chunk(first, seen, between):
            q_rows = pl.ds(first, step)
            qpos = qpos_ref[:, q_rows]
            for slot in range(slots):
                queries = own_ref[q_rows, at(0, slot)]
                grads = grad_ref[q_rows, at(0, slot)]
                keys, values = src[:seen, at(base, slot)], src[:seen, at(base + sh, slot)]
                lse = lse_ref[slot : slot + 1, q_rows]
                correction = jnp.sum(
                    grads.astype(F32).T * att_ref[at(0, slot), q_rows], axis=0, keepdims=True
                )
                allowed = kpos_ref[part * rows : part * rows + seen] <= qpos
                scores = dot_t(keys, queries)
                probs = jnp.where(allowed, jnp.exp2(scores * (scale * LOG2E) - lse), 0.0)
                prob_grad = dot_t(values, grads)
                score_grad = (probs * (prob_grad - correction)).astype(BF16)
                dkv[:seen, at(0, slot)] += dot_n(score_grad, queries) * scale
                dkv[:seen, at(sh, slot)] += dot_n(probs.astype(BF16), grads)
                dq_t[at(0, slot), q_rows] += dot_n(keys.T, score_grad)
                run_next(between)

        in_blocks(rows, step, chunk, between)
        if part:
            swap.start()
    triple_ref[:, :sh] = (dq_t[...].T * scale).astype(BF16)

    def finish_last():
        for rest in between:
            rest()
        hr = base_ref.shape[0] // HALVES
        for half in range(HALVES):
            part_rows = slice(half * hr, (half + 1) * hr)
            total = scatter.result(half)
            value_ref[part_rows] = base_ref[part_rows] + (total + feats[1, 5:6])
        scatter.finish()

    swap.wait_recv()
    triple_ref[:, sh:] = (dkv_own[...] + came[...]).astype(BF16)
    qkv_load.wait()

    def leave(first, size):
        some = pl.ds(first, size)
        weight = qkv_weight[...].reshape(part_to.shape[1], 3 * sh)
        part_to[some] = dot_t(triple_ref[some], weight).astype(BF16)

    io.done(0)
    row_blocks(rows, leave)
    io.done(1)
    if last:
        finish_last()
    if home:
        cross.finish()
    swap.wait_send()


def early_rows(rows):
    return rows * 2 // 5 // 16 * 16


def attend_back_call(n, collective_id, slots, layer, *args, last=(), home=()):
    qkv, out_all, qkv_all = args[0], args[7], args[8]
    rows = qkv.shape[0]
    sh = slots * HD
    full = out_all.shape[2]
    step = min(rows, 256)
    shapes = [
        jax.ShapeDtypeStruct((rows, 3 * sh), BF16),
        jax.ShapeDtypeStruct((rows, full), BF16),
    ]
    scratch = [pltpu.VMEM((sh, rows), F32)] + [pltpu.VMEM((rows, 2 * sh), F32)] * 3
    scratch += [DMA, DMA]
    scratch += [
        pltpu.VMEM((rows, sh), BF16),
        pltpu.VMEM((sh, full), BF16),
        pltpu.VMEM(qkv_all.shape[1:], BF16),
        DMA((2,)),
    ]
    if last:
        shapes.append(jax.ShapeDtypeStruct(last[1].shape, F32))
        scratch += scatter_scratch(n, *last[1].shape)
    if home:
        slim = home[0].shape
        shapes.append(jax.ShapeDtypeStruct((1, early_rows(slim[1]), full), BF16))
        scratch += [DMA, DMA]
    return staged_call(
        functools.partial(attend_back_kernel, n, slots, step, layer, bool(last), bool(home)),
        "attend_back",
        collective_id,
        args + tuple(last) + tuple(home),
        shapes,
        scratch,
        late=(0, 1, 2, 3),
        plain=(7, 8) + ((9,) if home else ()),
        early=(0, 1),
        raw=(2,) if home else (),
    )


def windows(width, n):
    share = width // n
    low = [j * share // HD for j in range(n)]
    slots = max(((j + 1) * share - 1) // HD - low[j] + 1 for j in range(n))
    return [min(first, HEADS - slots) for first in low], slots


def on_device(n, tokens, block_order, cotangent, *vectors_and_weights):
    (
        first_gain,
        first_shift,
        qkv_weight,
        input_bias,
        out_weight,
        out_bias,
        second_gain,
        second_shift,
        widen_weight,
        widen_bias,
        narrow_weight,
        narrow_bias,
    ) = (member[0] for member in vectors_and_weights)
    c = lax.axis_index("ctx")
    _, rows, width = tokens.shape
    hidden = widen_weight.shape[1]
    share = width // n
    hide = hidden // n
    padded = -(-share // 16) * 16
    full = n * padded
    low, slots = windows(width, n)
    sh = slots * HD
    total_rows = n * rows
    half_rows = rows // HALVES

    mask = jnp.asarray(np.arange(full)[None] % padded < share, F32)
    order = block_order.reshape(2, n, HALVES).transpose(0, 2, 1)
    places = order[..., None] * half_rows + jnp.arange(half_rows, dtype=jnp.int32)
    places = places.reshape(2, total_rows)
    own_places = jnp.where(c == 0, places[0], places[1])
    oth_places = jnp.where(c == 0, places[1], places[0])
    kpos = jnp.concatenate([own_places, oth_places])[:, None]
    qpos = own_places[None, :]

    (
        x,
        own_cot,
        out_grad,
        out_sums,
        normed,
        qkv,
        qkv_all,
        out_all,
        feats,
        qkv_bias,
        widen_biases,
        att,
        att_low,
        lse,
        other,
        widen_all,
        *middle,
        narrow_all,
    ) = open_call(
        n,
        low,
        slots,
        padded,
        tokens,
        cotangent,
        [
            member[None]
            for member in (
                first_gain,
                first_shift,
                out_bias,
                second_gain,
                second_shift,
                narrow_bias,
                input_bias,
                widen_bias,
            )
        ],
        (qkv_weight, out_weight, widen_weight, narrow_weight),
        mask,
        kpos,
        qpos,
    )
    stored = []
    layer_outs = []
    for layer in range(2):
        if layer:
            att, att_low, lse, other, part, out_low_all, qkv = attend_call(
                n, 2, slots, 1, kpos, qpos, own_cot, out_all, normed, qkv_all, qkv_bias
            )
            middle = forward_call(
                n,
                4,
                width,
                part,
                x,
                feats,
                mask,
                layer=1,
                feed=(widen_all, narrow_all, widen_biases),
            )
        residual, normed_two, hidden_pre, hidden_low, part = middle
        stored.append((x, normed, qkv, other, att, att_low, lse, residual, normed_two))
        stored[-1] += (hidden_pre, hidden_low)
        if layer == 0:
            x, normed = forward_call(n, 5, width, part, residual, feats, mask)
            layer_outs.append(x)
        else:
            last = (part, residual, feats)

    found = {}
    for layer in (1, 0):
        x, normed, qkv, other, att, att_low, lse, residual, normed_two = stored[layer][:9]
        hidden_pre, hidden_low = stored[layer][9:]
        resid_grad, sums_two, resid_low_all, wide, wide_came, slim, pre_sums = resid_call(
            n,
            7 + layer,
            width,
            layer,
            hide,
            residual,
            out_grad,
            feats,
            mask,
            normed_two,
            hidden_pre,
            hidden_low,
            out_low_all,
            widen_all,
            narrow_all,
        )
        back = attend_back_call(
            n,
            9 + layer,
            slots,
            layer,
            qkv,
            other,
            resid_low_all,
            att,
            lse,
            kpos,
            qpos,
            out_all,
            qkv_all,
            last=last if layer else (),
            home=() if layer else (slim,),
        )
        triple, part = back[:2]
        local = (part, x, resid_grad, feats, mask, normed, triple, att_low, resid_low_all)
        found[layer] = (wide, wide_came, slim, sums_two, pre_sums)
        if layer:
            layer_outs.append(back[2])
            upper_d_in, sums_one, out_low_all, qkv_grad, out_rows, slim_came, triple_sums = (
                input_call(n, 11, width, 0, low, *local, slim)
            )
            out_grad = upper_d_in
    lower, upper = found[0], found[1]
    d_in, narrow_back, qkv_back, out_back, vec, came, widen_back = finale_call(
        n,
        12,
        width,
        low,
        *local,
        lower[2],
        upper[2],
        back[2],
        slim_came,
        qkv_grad,
        out_rows,
        sums_one,
        lower[3],
        upper[3],
        triple_sums,
        lower[4],
        upper[4],
        out_sums,
        *layer_outs,
        upper_d_in,
        *lower[:2],
        *upper[:2],
    )
    settled = settle_call(
        low,
        share,
        hide,
        qkv_back,
        widen_back,
        out_back,
        narrow_back,
        vec,
        came,
        *layer_outs,
        d_in,
        upper_d_in,
    )
    qkv_out, widen_out, out_out, narrow_out, layer_out, d_out = (m[None] for m in settled[:6])
    gain1, shift1, out_b, gain2, shift2, narrow_b, input_b, widen_b = settled[6:]
    return (
        layer_out,
        d_out,
        gain1,
        shift1,
        qkv_out,
        input_b,
        out_out,
        out_b,
        gain2,
        shift2,
        widen_out,
        widen_b,
        narrow_out,
        narrow_b,
    )


def solution(mesh):
    rows = P(None, ("ctx", "shard"), None)
    vector = P("section", "shard")
    matrix = P("section", "shard", None)
    order = (
        vector,
        vector,
        matrix,
        vector,
        matrix,
        vector,
        vector,
        vector,
        matrix,
        vector,
        matrix,
        vector,
    )
    streams = P("section", None, ("ctx", "shard"), None)
    return jax.shard_map(
        functools.partial(on_device, mesh.shape["shard"]),
        mesh=mesh,
        in_specs=(rows, P(), rows) + order,
        out_specs=(streams, streams) + order,
        check_vma=False,
    )
```

```python
import functools

import jax
import jax.numpy as jnp
import numpy as np
from jax import lax
from jax.experimental import pallas as pl
from jax.experimental.pallas import tpu as pltpu
from jax.sharding import PartitionSpec as P

HEADS = 25
HD = 64
EPSILON = 1e-05
MASKED = -1e30
LOG2E = 1.4426950408889634
GELU_A = 0.7978845608028654
GELU_B = 0.044715
MESH = pl.DeviceIdType.MESH
F32 = jnp.float32
BF16 = jnp.bfloat16
VMEM_SPEC = pl.BlockSpec(memory_space=pltpu.VMEM)
ANY_SPEC = pl.BlockSpec(memory_space=pl.ANY)
DMA = pltpu.SemaphoreType.DMA
VMEM_LIMIT = 60 * 2**20
HALVES = 2


def params(collective_id=None):
    if collective_id is None:
        return pltpu.CompilerParams(vmem_limit_bytes=VMEM_LIMIT)
    return pltpu.CompilerParams(
        collective_id=collective_id, has_side_effects=True, vmem_limit_bytes=VMEM_LIMIT
    )


def remote(src, dst, send_sem, recv_sem, device):
    return pltpu.make_async_remote_copy(
        src_ref=src,
        dst_ref=dst,
        send_sem=send_sem,
        recv_sem=recv_sem,
        device_id=device,
        device_id_type=MESH,
    )


class Place:
    def __init__(self, n):
        self.s = lax.axis_index("section")
        self.c = lax.axis_index("ctx")
        self.h = lax.axis_index("shard")
        self.n = n
        self.zn = n // 2
        self.y = lax.rem(self.h, 2)
        self.z = lax.div(self.h, 2)
        self.far_y = self.y + self.c - 2 * self.y * self.c

    def flip(self, k):
        found = self.z
        for bit in range(self.zn.bit_length()):
            if k >> bit & 1:
                found = found + (1 - 2 * lax.rem(self.z // 2**bit, 2)) * 2**bit
        return found

    def dev(self, z, y):
        return (self.s, self.c, z * 2 + y)

    @property
    def pair(self):
        return self.dev(self.z, 1 - self.y)

    @property
    def above(self):
        return self.dev(self.z + 1, self.y)

    @property
    def below(self):
        return self.dev(self.z - 1, self.y)

    @property
    def over(self):
        return (1 - self.s, self.c, self.h)

    @property
    def sibling(self):
        return (self.s, 1 - self.c, self.h)


def greet(p, line=False, spread=False, over=False, sibling=False):
    bar = pltpu.get_barrier_semaphore()
    peers = 0

    def signal(device):
        pl.semaphore_signal(bar, inc=1, device_id=device, device_id_type=MESH)

    if line:
        signal(p.pair)

        @pl.when(p.z < p.zn - 1)
        def _():
            signal(p.above)

        @pl.when(p.z > 0)
        def _():
            signal(p.below)

        peers = 1 + (p.z + p.zn - 1) // p.zn + (2 * p.zn - 2 - p.z) // p.zn
    if spread:
        for dz in range(1, p.zn):
            signal(p.dev(lax.rem(p.z + dz, p.zn), p.far_y))

        @pl.when(p.c == 1)
        def _():
            signal(p.dev(p.z, p.far_y))

        peers = peers + p.zn - 1 + p.c
    if over:
        signal(p.over)
        peers = peers + 1
    if sibling:
        signal(p.sibling)
        peers = peers + 1
    pl.semaphore_wait(bar, peers)


class Gather:
    def __init__(self, p, own_ref, out_ref, ss, rs, ls):
        self.p, self.own_ref, self.out_ref = p, own_ref, out_ref
        self.ss, self.rs, self.ls = ss, rs, ls
        self.hr = own_ref.shape[0] // HALVES

    def blk(self, half, zz, yy):
        row = (half * self.p.n + zz * 2 + yy) * self.hr
        return self.out_ref.at[pl.ds(pl.multiple_of(row, 16), self.hr)]

    def own(self, half):
        return self.own_ref.at[pl.ds(half * self.hr, self.hr)]

    def up(self, t, half, src):
        p = self.p
        sems = (self.ss.at[0, t, half], self.rs.at[0, t, half])
        return remote(src, self.blk(half, p.z - (t - 1), p.y), *sems, p.above)

    def down(self, t, half, src):
        p = self.p
        sems = (self.ss.at[1, t, half], self.rs.at[1, t, half])
        return remote(src, self.blk(half, p.z + (t - 1), p.y), *sems, p.below)

    def across(self, kind, t, half, zz, src):
        p = self.p
        sems = (self.ss.at[2 + kind, t, half], self.rs.at[2 + kind, t, half])
        return remote(src, self.blk(half, zz, p.y), *sems, p.pair)

    def local(self, half):
        p = self.p
        return pltpu.make_async_copy(
            self.own(half), self.blk(half, p.z, p.y), self.ls.at[half]
        )

    def start(self, halves=range(HALVES)):
        p = self.p
        for half in halves:
            src = self.own(half)

            @pl.when(p.z < p.zn - 1)
            def _():
                self.up(1, half, src).start()

            @pl.when(p.z > 0)
            def _():
                self.down(1, half, src).start()

            self.across(0, 0, half, p.z, src).start()
            self.local(half).start()

    def step(self, t, half):
        p = self.p
        z, zn = p.z, p.zn

        @pl.when(z >= t)
        def _():
            block = self.blk(half, z - t, p.y)
            self.up(t, half, block).wait_recv()
            if t < zn - 1:

                @pl.when(z < zn - 1)
                def _():
                    self.up(t + 1, half, block).start()

            self.across(0, t, half, z - t, block).start()

        @pl.when(z <= zn - 1 - t)
        def _():
            block = self.blk(half, z + t, p.y)
            self.down(t, half, block).wait_recv()
            if t < zn - 1:

                @pl.when(z > 0)
                def _():
                    self.down(t + 1, half, block).start()

            self.across(1, t, half, z + t, block).start()

    def steps(self):
        return [
            functools.partial(self.step, t, half)
            for t in range(1, self.p.zn)
            for half in range(HALVES)
        ]

    def finish(self):
        p = self.p
        z, zn = p.z, p.zn
        for half in range(HALVES):
            self.across(0, 0, half, z, self.own(half)).wait_recv()
            for t in range(1, zn):

                @pl.when(z >= t)
                def _():
                    self.across(0, t, half, z - t, self.own(half)).wait_recv()

                @pl.when(z <= zn - 1 - t)
                def _():
                    self.across(1, t, half, z + t, self.own(half)).wait_recv()

        for half in range(HALVES):
            self.local(half).wait()
            self.across(0, 0, half, z, self.own(half)).wait_send()
            for t in range(1, zn):

                @pl.when((z < zn - 1) & (z >= t - 1))
                def _():
                    self.up(t, half, self.own(half)).wait_send()

                @pl.when((z > 0) & (z <= zn - t))
                def _():
                    self.down(t, half, self.own(half)).wait_send()

                @pl.when(z >= t)
                def _():
                    self.across(0, t, half, z - t, self.own(half)).wait_send()

                @pl.when(z <= zn - 1 - t)
                def _():
                    self.across(1, t, half, z + t, self.own(half)).wait_send()


class Scatter:
    def __init__(self, p, part_ref, ybuf, rbuf, sbuf, ss, rs):
        self.p, self.part_ref = p, part_ref
        self.ybuf, self.rbuf, self.sbuf, self.ss, self.rs = ybuf, rbuf, sbuf, ss, rs
        self.hr = ybuf.shape[2]

    def blk(self, half, zz, yy):
        row = (half * self.p.n + zz * 2 + yy) * self.hr
        return self.part_ref.at[pl.ds(pl.multiple_of(row, 16), self.hr)]

    def goal(self, k, t):
        return self.p.z + t if k == 0 else self.p.z - t

    def across(self, k, t, half):
        p = self.p
        zz = self.goal(k, t)
        sems = (self.ss.at[k, t, half], self.rs.at[k, t, half])
        return remote(self.blk(half, zz, 1 - p.y), self.ybuf.at[zz, half], *sems, p.pair)

    def along(self, k, t, half, slot):
        p = self.p
        zz = self.goal(k, t)
        sems = (self.ss.at[2 + k, t, half], self.rs.at[2 + k, slot, half])
        target = p.above if k == 0 else p.below
        return remote(self.sbuf.at[zz, half], self.rbuf.at[zz + 1 - k, half], *sems, target)

    def ok(self, k, t):
        return self.p.z <= self.p.zn - 1 - t if k == 0 else self.p.z >= t

    def has(self, k):
        return self.p.z > 0 if k == 0 else self.p.z < self.p.zn - 1

    def start(self):
        for t in range(self.p.zn - 1, 0, -1):
            for half in range(HALVES):
                for k in range(2):

                    @pl.when(self.ok(k, t))
                    def _():
                        self.across(k, t, half).start()

        for half in range(HALVES):
            self.across(0, 0, half).start()

    def step(self, t, half, k):
        p = self.p
        zz = self.goal(k, t)

        @pl.when(self.ok(k, t))
        def _():
            self.across(k, t, half).wait_recv()
            total = self.blk(half, zz, p.y)[...].astype(F32)
            total = total + self.ybuf[zz, half].astype(F32)
            if t < p.zn - 1:

                @pl.when(self.has(k))
                def _():
                    self.along(k, t, half, t).wait_recv()
                    more = total + self.rbuf[zz + 1 - k, half].astype(F32)
                    self.sbuf[zz, half] = more.astype(BF16)

                @pl.when(jnp.logical_not(self.has(k)))
                def _():
                    self.sbuf[zz, half] = total.astype(BF16)

            else:
                self.sbuf[zz, half] = total.astype(BF16)
            self.along(k, t, half, t - 1).start()

    def steps(self):
        return [
            functools.partial(self.step, t, half, k)
            for t in range(self.p.zn - 1, 0, -1)
            for half in range(HALVES)
            for k in range(2)
        ]

    def result(self, half):
        p = self.p
        z = p.z
        self.across(0, 0, half).wait_recv()
        for k in range(2):

            @pl.when(self.has(k))
            def _():
                self.along(k, 0, half, 0).wait_recv()

            @pl.when(jnp.logical_not(self.has(k)))
            def _():
                self.rbuf[z + 1 - k, half] = jnp.zeros(self.rbuf.shape[2:], BF16)

        total = self.blk(half, z, p.y)[...].astype(F32) + self.ybuf[z, half].astype(F32)
        return total + self.rbuf[z + 1, half].astype(F32) + self.rbuf[z, half].astype(F32)

    def finish(self):
        for half in range(HALVES):
            self.across(0, 0, half).wait_send()
            for t in range(1, self.p.zn):
                for k in range(2):

                    @pl.when(self.ok(k, t))
                    def _():
                        self.across(k, t, half).wait_send()
                        self.along(k, t, half, t - 1).wait_send()


class Spread:
    def __init__(self, p, src, dst, ss, rs, ls):
        self.p, self.src, self.dst, self.ss, self.rs, self.ls = p, src, dst, ss, rs, ls

    def source(self, dz):
        return self.p.flip(dz) * 2 + self.p.far_y

    def out(self, dz):
        p = self.p
        target = self.source(dz)
        sems = (self.ss.at[0, dz], self.rs.at[0, dz])
        return remote(self.src.at[target], self.dst.at[p.s, p.h], *sems, (p.s, p.c, target))

    def aside(self, dz):
        block = self.dst.at[self.p.s, self.source(dz)]
        return remote(block, block, self.ss.at[1, dz], self.rs.at[1, dz], self.p.sibling)

    def cross(self, dz):
        block = self.dst.at[self.p.s, self.source(dz)]
        return remote(block, block, self.ss.at[2, dz], self.rs.at[2, dz], self.p.over)

    def cross_own(self):
        p = self.p
        sems = (self.ss.at[2, 0], self.rs.at[2, 0])
        return remote(self.src.at[p.h], self.dst.at[p.s, p.h], *sems, p.over)

    def cross_aside(self, dz):
        block = self.dst.at[1 - self.p.s, self.source(dz)]
        return remote(block, block, self.ss.at[3, dz], self.rs.at[3, dz], self.p.sibling)

    def local(self):
        p = self.p
        return pltpu.make_async_copy(self.src.at[p.h], self.dst.at[p.s, p.h], self.ls)

    def start(self):
        @pl.when(self.p.c == 1)
        def _():
            self.out(0).start()

        @pl.when(self.p.c == 0)
        def _():
            self.cross_own().start()

        for dz in range(1, min(3, self.p.zn)):
            self.out(dz).start()
        self.local().start()

    def arrived(self, dz):
        if 3 <= dz + 2 < self.p.zn:
            self.out(dz + 1).wait_send()
            self.out(dz + 2).start()
        self.out(dz).wait_recv()
        self.cross(dz).start()
        self.aside(dz).start()

    def crossed(self, dz):
        self.cross(dz).wait_recv()
        self.cross_aside(dz).start()

    def first(self):
        @pl.when(self.p.c == 1)
        def _():
            self.arrived(0)

    def steps(self):
        found = [self.first]
        found += [functools.partial(self.arrived, dz) for dz in range(1, self.p.zn)]
        return found + [functools.partial(self.crossed, dz) for dz in range(self.p.zn)]

    def finish(self):
        self.local().wait()

        @pl.when(self.p.c == 0)
        def _():
            self.aside(0).wait_recv()
            self.cross_own().wait_send()

        @pl.when(self.p.c == 1)
        def _():
            self.out(0).wait_send()
            self.aside(0).wait_send()
            self.cross(0).wait_send()

        for dz in range(self.p.zn):
            if dz:
                self.aside(dz).wait_recv()
                self.aside(dz).wait_send()
                if dz == 1 or dz == self.p.zn - 1:
                    self.out(dz).wait_send()
                self.cross(dz).wait_send()
            self.cross_aside(dz).wait_recv()
            self.cross_aside(dz).wait_send()


class RowSwap:
    def __init__(self, p, src, dst, ss, rs, ls):
        self.p, self.src, self.dst, self.ss, self.rs, self.ls = p, src, dst, ss, rs, ls
        self.split = src.shape[0] % 32 == 0

    def piece(self, which):
        count = self.src.shape[0]
        if not self.split:
            return self.src, self.dst.at[which, pl.ds(0, count)]
        half = count // 2
        rows = pl.ds(pl.multiple_of(self.p.c * half, 16), half)
        return self.src.at[rows], self.dst.at[which, rows]

    def cross(self):
        src, dst = self.piece(self.p.s)
        return remote(src, dst, self.ss.at[0], self.rs.at[0], self.p.over)

    def aside(self):
        block = self.piece(1 - self.p.s)[1]
        return remote(block, block, self.ss.at[1], self.rs.at[1], self.p.sibling)

    def local(self):
        rows = pl.ds(0, self.src.shape[0])
        return pltpu.make_async_copy(self.src, self.dst.at[self.p.s, rows], self.ls)

    def start(self):
        self.cross().start()
        self.local().start()

    def step(self):
        self.cross().wait_recv()
        if self.split:
            self.aside().start()

    def finish(self):
        self.local().wait()
        self.cross().wait_send()
        if self.split:
            self.aside().wait_recv()
            self.aside().wait_send()


class Cross:
    def __init__(self, p, src, dst, ss, rs, source):
        self.p, self.source = p, source
        self.copy = remote(src, dst, ss, rs, p.over)

    def start(self):
        @pl.when(self.p.s == self.source)
        def _():
            self.copy.start()

    def finish(self):
        @pl.when(self.p.s == self.source)
        def _():
            self.copy.wait_send()

        @pl.when(self.p.s != self.source)
        def _():
            self.copy.wait_recv()


class Home:
    def __init__(self, p, src, dst, ss, rs, ls):
        self.p, self.src, self.dst, self.ss, self.rs, self.ls = p, src, dst, ss, rs, ls

    def send(self, k):
        p = self.p
        far = p.flip(k)
        target = (p.s, p.c, far * 2 + p.far_y)
        sems = (self.ss.at[0, k], self.rs.at[0, k])
        return remote(self.src.at[far], self.dst.at[p.h], *sems, target)

    def keep(self):
        return pltpu.make_async_copy(self.src.at[self.p.z], self.dst.at[self.p.h], self.ls)

    def aside(self, k):
        block = self.dst.at[self.p.flip(k) * 2 + self.p.far_y]
        return remote(block, block, self.ss.at[1, k], self.rs.at[1, k], self.p.sibling)

    def start(self, k):
        if k:
            self.send(k).start()
            return

        @pl.when(self.p.c == 1)
        def _():
            self.send(0).start()

        @pl.when(self.p.c == 0)
        def _():
            self.keep().start()

    def arrived(self, k):
        if k:
            self.send(k).wait_recv()
        else:

            @pl.when(self.p.c == 1)
            def _():
                self.send(0).wait_recv()

            @pl.when(self.p.c == 0)
            def _():
                self.keep().wait()

        self.aside(k).start()

    def steps(self):
        return [functools.partial(self.arrived, k) for k in range(self.p.zn)]

    def finish(self):
        @pl.when(self.p.c == 1)
        def _():
            self.send(0).wait_send()

        for k in range(self.p.zn):
            if k:
                self.send(k).wait_send()
            self.aside(k).wait_recv()
            self.aside(k).wait_send()


def add_home(p, to, index, first, first_came, second, second_came):
    pairs = ((first, first_came), (second, second_came))
    for section, (own, came) in enumerate(pairs):

        @pl.when(p.s == section)
        def _():
            to[index] = (own[index].astype(F32) + came[index].astype(F32)).astype(BF16)


class Fold:
    def __init__(self, p, src, came, out, ss, rs):
        self.p, self.src, self.came, self.out, self.ss, self.rs = p, src, came, out, ss, rs
        self.count = out.shape[0]
        self.size = out.shape[1]

    def rows(self, item, near):
        p = self.p
        if self.count == 1:
            index = 1 - p.c if near else p.c
        else:
            index = item * 2 + (1 - p.far_y if near else p.far_y)
        return pl.ds(pl.multiple_of(index * self.size, 16), self.size)

    def copy(self, item):
        src = self.src.at[self.rows(item, True)]
        sems = (self.ss.at[item], self.rs.at[item])
        return remote(src, self.came.at[item], *sems, self.p.sibling)

    def start(self):
        for item in range(self.count):
            self.copy(item).start()

    def step(self, item):
        self.copy(item).wait_recv()
        own = self.src[self.rows(item, False)].astype(F32)
        self.out[item] = (own + self.came[item].astype(F32)).astype(BF16)

    def steps(self):
        return [functools.partial(self.step, item) for item in range(self.count)]

    def finish(self):
        for item in range(self.count):
            self.copy(item).wait_send()


def fold_scratch(source, out):
    return [pltpu.VMEM(source, BF16), pltpu.VMEM(out, BF16), DMA((out[0],)), DMA((out[0],))]


def product(a_ref, b_ref, to_ref):
    rows = to_ref.shape[0]

    def step(first, size):
        found = lax.dot_general(
            a_ref[:, first : first + size],
            b_ref[...],
            (((0,), (0,)), ((), ())),
            preferred_element_type=F32,
        )
        to_ref[first : first + size] = found.astype(BF16)

    return [
        functools.partial(step, first, min(256, rows - first)) for first in range(0, rows, 256)
    ]


def home_rows(a_ref, b_ref, to_ref, low, share):
    found = lax.dot_general(
        a_ref[...], b_ref[...], (((0,), (0,)), ((), ())), preferred_element_type=F32
    )
    h = lax.axis_index("shard")
    shift = 0
    for j, first in enumerate(low):
        shift = shift + jnp.where(h == j, (HD * first - j * share) % found.shape[0], 0)
    to_ref[...] = pltpu.roll(found, shift, 0).astype(BF16)


def in_turn(steps, work, each=1):
    for step in steps:
        for _ in range(each):
            run_next(work)
        step()


def by_halves(scatter, gather, rows_step, work, each=1):
    in_turn(scatter.steps(), work, each)
    for half in range(HALVES):
        rows_step(half)
        if gather is not None:
            gather.start([half])
    if gather is not None:
        in_turn(gather.steps(), work, each)


def fetch(src, dst, sem):
    copy = pltpu.make_async_copy(src, dst, sem)
    copy.start()
    return copy


class Staging:
    greeted, extra = False, {}

    def __init__(self):
        self.loads, self.stores, self.running = {}, {}, []

    def need(self, *items):
        for item in items:
            self.loads.pop(item).wait()

    def done(self, *items):
        for item in items:
            self.running.append(fetch(*self.stores.pop(item)))

    def end(self):
        self.done(*list(self.stores))
        for copy in self.running:
            copy.wait()


def staged_call(
    body, name, collective_id, args, shapes, scratch, late=(), plain=(), early=(), raw=(), layers={}
):
    late, early = tuple(late), tuple(early)
    n_in, n_out, n_scratch = len(args), len(shapes), len(scratch)

    def run(*refs):
        ins, outs = list(refs[:n_in]), list(refs[n_in : n_in + n_out])
        rest = refs[n_in + n_out :]
        own, rest = rest[:n_scratch], rest[n_scratch:]
        staged_in, rest = rest[: len(late)], rest[len(late) :]
        staged_out, sems = rest[: len(early)], rest[len(early) :]
        io = Staging()
        for x, item in enumerate(late):
            src = ins[item].at[layers[item]] if item in layers else ins[item]
            io.loads[item] = fetch(src, staged_in[x], sems[0].at[x])
            ins[item] = staged_in[x]
        for x, item in enumerate(early):
            io.stores[item] = (staged_out[x], outs[item], sems[1].at[x])
            outs[item] = staged_out[x]
        body(io, *ins, *outs, *own)
        io.end()

    stages = [
        pltpu.VMEM(args[item].shape[1 if item in layers else 0 :], args[item].dtype) for item in late
    ]
    stages += [pltpu.VMEM(shapes[item].shape, shapes[item].dtype) for item in early]
    stages += [DMA((max(len(late), 1),)), DMA((max(len(early), 1),))]
    return pl.pallas_call(
        run,
        out_shape=shapes,
        in_specs=[ANY_SPEC if i in late + tuple(plain) else VMEM_SPEC for i in range(n_in)],
        out_specs=[ANY_SPEC if i in early + tuple(raw) else VMEM_SPEC for i in range(n_out)],
        scratch_shapes=list(scratch) + stages,
        compiler_params=params(collective_id),
        name=name,
    )(*args)


class Mapped:
    def __init__(self, io, loads, stores, greeted=True, extra={}):
        self.io, self.loads, self.stores = io, loads, stores
        self.greeted, self.extra = greeted, extra

    def need(self, *items):
        for item in items:
            if self.loads.get(item) in self.io.loads:
                self.io.need(self.loads[item])

    def done(self, *items):
        for item in items:
            if self.stores.get(item) in self.io.stores:
                self.io.done(self.stores[item])


class Result:
    def __init__(self, step, index):
        self.step, self.index = step, index
        self.shape, self.dtype = step.shapes[index].shape, step.shapes[index].dtype


class Step:
    def __init__(self, body, name, collective_id, args, shapes, scratch, greets, **staging):
        self.body, self.name, self.collective_id = body, name, collective_id
        self.args, self.shapes, self.scratch, self.greets = tuple(args), shapes, scratch, greets
        self.late = tuple(staging.get("late", ()))
        self.plain = tuple(staging.get("plain", ()))
        self.early = tuple(staging.get("early", ()))
        self.raw = tuple(staging.get("raw", ()))
        self.layers = staging.get("layers", {})


def run_steps(steps):
    args, arg_of, out_of, first_out = [], {}, {}, []
    shapes, scratch, early, raw = [], [], [], []
    linked = {
        (id(arg.step), arg.index) for step in steps for arg in step.args if isinstance(arg, Result)
    }
    for k, step in enumerate(steps):
        for i, arg in enumerate(step.args):
            if isinstance(arg, Result):
                continue
            spots = [x for x, known in enumerate(args) if known is arg]
            if not spots:
                args.append(arg)
                spots = [len(args) - 1]
            arg_of[k, i] = spots[0]
        first_out.append(len(shapes))
        for o, shape in enumerate(step.shapes):
            out_of[k, o] = len(shapes)
            keep = (id(step), o) in linked
            if o in step.early or (o in step.raw and keep):
                early.append(len(shapes))
            elif o in step.raw:
                raw.append(len(shapes))
            shapes.append(shape)
        scratch += step.scratch
    direct = {
        arg_of[k, i]
        for k, step in enumerate(steps)
        for i in range(len(step.args))
        if (k, i) in arg_of and i not in step.late and i not in step.plain
    }
    late, layers = [], {}
    for k, step in enumerate(steps):
        for i in step.late:
            spot = arg_of.get((k, i))
            if spot is not None and spot not in direct and spot not in late:
                late.append(spot)
                if i in step.layers:
                    layers[spot] = step.layers[i]
    plain = [x for x in range(len(args)) if x not in direct and x not in late]
    extra = {}
    for step in steps:
        extra.update(step.greets)

    def body(io, *refs):
        ins, outs = refs[: len(args)], refs[len(args) : len(args) + len(shapes)]
        rest = refs[len(args) + len(shapes) :]
        for k, step in enumerate(steps):
            mine = []
            for i, arg in enumerate(step.args):
                if isinstance(arg, Result):
                    mine.append(outs[out_of[steps.index(arg.step), arg.index]])
                else:
                    mine.append(ins[arg_of[k, i]])
            loads = {i: arg_of[k, i] for i in range(len(step.args)) if (k, i) in arg_of}
            stores = {o: out_of[k, o] for o in range(len(step.shapes))}
            own = outs[first_out[k] : first_out[k] + len(step.shapes)]
            count = len(step.scratch)
            part = Mapped(io, loads, stores, k > 0, extra)
            step.body(part, *mine, *own, *rest[:count])
            part.done(*stores)
            rest = rest[count:]

    found = staged_call(
        body,
        "_".join(step.name for step in steps),
        steps[0].collective_id,
        args,
        shapes,
        scratch,
        late=late,
        plain=plain,
        early=early,
        raw=raw,
        layers=layers,
    )
    return [
        found[first : first + len(step.shapes)] for first, step in zip(first_out, steps)
    ]


def follow(merge, first, make_second):
    if merge:
        results = [Result(first, i) for i in range(len(first.shapes))]
        return run_steps([first, make_second(results)])
    (found,) = run_steps([first])
    return found, run_steps([make_second(found)])[0]


def row_blocks(rows, step):
    size = min(rows, 256)
    count = rows // size
    if count <= 2:
        for b in range(count):
            step(b * size, size)
    else:

        def body(b, carry):
            step(pl.multiple_of(b * size, size), size)
            return carry

        lax.fori_loop(0, count, body, 0)


def enter(io, p, **greets):
    if not io.greeted:
        greets.update(io.extra)
        greet(p, **greets)


def gelu_parts(values):
    square = values * values
    return jnp.tanh(GELU_A * (values + GELU_B * values * square)), square


def greet_all(p):
    bar = pltpu.get_barrier_semaphore()
    for a in range(2):
        for b in range(p.n):
            if (a, b) != (0, 0):
                other = (lax.rem(p.s + a, 2), p.c, lax.rem(p.h + b, p.n))
                pl.semaphore_signal(bar, inc=1, device_id=other, device_id_type=MESH)
    pl.semaphore_signal(bar, inc=1, device_id=p.sibling, device_id_type=MESH)
    pl.semaphore_wait(bar, 2 * p.n)


def others(n):
    return [(a, b) for a in range(2) for b in range(n) if (a, b) != (0, 0)]


def with_gaps(values, n, padded):
    rows, width = values.shape
    share = width // n
    pieces = []
    for j in range(n):
        pieces.append(values[:, j * share : (j + 1) * share])
        if padded > share:
            pieces.append(jnp.zeros((rows, padded - share), values.dtype))
    return jnp.concatenate(pieces, axis=1)


def lay_vectors(vectors, pack_to):
    lanes = pack_to.shape[1]
    members = []
    for ref in vectors:
        member = ref[...].astype(F32)
        members.append(
            jnp.concatenate([member, jnp.zeros((1, lanes - member.shape[1]), F32)], axis=1)
        )
    members.append(jnp.zeros((8, lanes), F32))
    pack_to[...] = jnp.concatenate(members, axis=0).astype(BF16)


def lay_first(low, qkv_ref, qkv_to):
    n, padded, triple = qkv_to.shape
    share = qkv_ref.shape[0]
    width = qkv_ref.shape[1] // 3
    sh = triple // 3
    for j in range(n):
        for t in range(3):
            first = t * width + HD * low[j]
            qkv_to[j, :share, t * sh : (t + 1) * sh] = qkv_ref[:, first : first + sh]
        if padded > share:
            qkv_to[j, share:] = jnp.zeros((padded - share, triple), BF16)


def lay_rows(low, out_ref, out_to):
    share = out_ref.shape[0]
    sh, full = out_to.shape
    n = len(low)
    h = lax.axis_index("shard")
    offset = 0
    for j in range(n):
        offset = offset + jnp.where(h == j, j * share - HD * low[j], 0)
    rows = with_gaps(out_ref[...].astype(F32), n, full // n)
    rows = jnp.concatenate([rows, jnp.zeros((sh - share, full), F32)], axis=0)
    out_to[...] = pltpu.roll(rows, offset, 0).astype(BF16)


def lay_widen(j, widen_ref, widen_to):
    n, padded, hide_full = widen_to.shape
    share, hidden = widen_ref.shape
    hide = hidden // n
    widen_to[j, :share, :hide] = widen_ref[:, j * hide : (j + 1) * hide]
    if hide_full > hide:
        widen_to[j, :share, hide:] = jnp.zeros((share, hide_full - hide), BF16)
    if padded > share:
        widen_to[j, share:] = jnp.zeros((padded - share, hide_full), BF16)


def lay_narrow(first, size, n, narrow_ref, narrow_to):
    rows = slice(first, first + size)
    narrow_to[rows] = with_gaps(narrow_ref[rows], n, narrow_to.shape[1] // n)


def spread_vectors(n, low, width, pack_all, feats_to, qkv_bias, widen_bias):
    h = lax.axis_index("shard")
    sh = qkv_bias.shape[2] // 3
    share = width // n
    padded = feats_to.shape[2] // n
    for layer in range(2):
        pieces = [pack_all[layer, j] for j in range(n)]
        feats_to[layer] = jnp.concatenate([m[:, :padded] for m in pieces], axis=1).astype(F32)
        bias = jnp.concatenate([m[6:7, : 2 * share] for m in pieces], axis=1).astype(F32)
        found = jnp.zeros((1, 2 * sh), F32)
        wide = jnp.zeros((1, widen_bias.shape[2]), F32)
        for j in range(n):
            first = HD * low[j]
            spots = [bias[:, k * width + first : k * width + first + sh] for k in range(2)]
            found = jnp.where(h == j, jnp.concatenate(spots, axis=1), found)
            own = pieces[j][7:8, : wide.shape[1]].astype(F32)
            wide = jnp.where(h == j, own, wide)
        qkv_bias[layer] = jnp.concatenate(
            [found[:, :sh], jnp.zeros((1, sh), F32), found[:, sh:]], axis=1
        )
        widen_bias[layer] = wide


def feed_forward(low_all, widen, narrow, widen_bias, pre_to, hidden_to, part_to):
    def block(first, size):
        rows = pl.ds(first, size)
        weight = widen[...].reshape(low_all.shape[1], widen.shape[2])
        pre = dot_n(low_all[rows], weight) + widen_bias
        pre_to[rows] = pre
        hidden = (0.5 * pre * (1.0 + gelu_parts(pre)[0])).astype(BF16)
        hidden_to[rows] = hidden
        part_to[rows] = dot_n(hidden, narrow[...]).astype(BF16)

    row_blocks(low_all.shape[0], block)


def open_kernel(n, low, width, slots, step, io, *refs):
    tok_ref, cot_ref, vectors, refs = refs[0], refs[1], refs[2:10], refs[10:]
    qkv_ref, out_ref, widen_ref, narrow_ref, mask, kpos_ref, qpos_ref = refs[:7]
    refs = refs[7:]
    x_to, cot_to, grad_to, sums_to, normed_to, own_ref, qkv_all, out_all = refs[:8]
    feats_to, qkv_bias, widen_bias, att_ref, low_ref, lse_ref, oth_ref, widen_all = refs[8:16]
    value_to, tok_all, pre_to, hidden_to, part_to, narrow_all = refs[16:22]
    refs = refs[22:]
    tok_own, pack, qkv_send, out_rows, widen_raw, narrow_raw, widen_send, narrow_to = refs[:8]
    pack_all, widen, refs = refs[8], refs[9], refs[10:]
    g_ss, g_rs, g_ls, p_ss, p_rs, a_ss, a_rs, w_ss, w_rs, o_ss, o_rs, l_sem = refs[:12]
    kv_ss, kv_rs, n_ss, n_rs, refs = refs[12], refs[13], refs[14], refs[15], refs[16:]
    scatter_refs, (second_ss, second_rs, second_ls) = refs[:5], refs[5:]
    p = Place(n)
    s, c, h = p.s, p.c, p.h
    widen_load = fetch(widen_ref, widen_raw, l_sem.at[4])
    narrow_load = fetch(narrow_ref, narrow_raw, l_sem.at[5])
    padded = qkv_send.shape[1]
    tok_own[...] = with_gaps(tok_ref[s], n, padded)
    greet_all(p)

    def pack_copy(a, b):
        target = (lax.rem(s + a, 2), c, lax.rem(h + b, n))
        return remote(pack, pack_all.at[s, h], p_ss.at[a, b], p_rs.at[a, b], target)

    tokens = Gather(p, tok_own, tok_all, g_ss, g_rs, g_ls)
    qkv = Spread(p, qkv_send, qkv_all, a_ss, a_rs, l_sem.at[1])
    wide = Spread(p, widen_send, widen_all, w_ss, w_rs, l_sem.at[3])
    narrow = RowSwap(p, narrow_to, narrow_all, n_ss, n_rs, l_sem.at[6])
    out = RowSwap(p, out_rows, out_all, o_ss, o_rs, l_sem.at[2])
    pack_own = pltpu.make_async_copy(pack, pack_all.at[s, h], l_sem.at[0])
    tokens.start()
    io.need(10)
    lay_first(low, qkv_ref, qkv_send)
    qkv.start()
    lay_vectors(vectors, pack)
    for a, b in others(n):
        pack_copy(a, b).start()
    pack_own.start()

    def start_out():
        io.need(1, 11)
        lay_rows(low, out_ref, out_rows)
        out.start()

    def lay_cot():
        values = with_gaps(cot_ref[s], n, padded)
        cot_to[...] = values
        grad_to[...] = values.astype(F32)
        sums_to[...] = jnp.sum(grad_to[...], axis=0, keepdims=True)
        x_to[...] = tok_own[...].astype(F32)

    hide = narrow_ref.shape[0]
    work = [start_out, widen_load.wait]
    work += [functools.partial(lay_widen, j, widen_raw, widen_send) for j in range(n)]
    work += [lay_cot, narrow_load.wait]
    work += [
        functools.partial(lay_narrow, first, min(208, hide - first), n, narrow_raw, narrow_to)
        for first in range(0, hide, 208)
    ]
    qkv_steps = qkv.steps()
    for token_step in tokens.steps():
        run_next(work)
        run_next(work)
        token_step()
        run_next(qkv_steps)
    for rest in work:
        rest()
    extra = narrow_to.shape[0] - hide
    if extra:
        narrow_to[hide:] = jnp.zeros((extra, n * padded), BF16)
    for member in range(2):
        if narrow_all.shape[1] > narrow_to.shape[0]:
            spare = (narrow_all.shape[1] - narrow_to.shape[0], n * padded)
            narrow_all[member, narrow_to.shape[0] :] = jnp.zeros(spare, BF16)
    tokens.finish()
    wide.start()
    pack_own.wait()
    for a, b in others(n):
        pack_copy(a, b).wait_recv()
    spread_vectors(n, low, width, pack_all, feats_to, qkv_bias, widen_bias)

    normed = part_to

    def first_norm(first, size):
        some = pl.ds(first, size)
        unit = unit_rows(tok_all[some].astype(F32), mask[...], width)[0]
        normed[some] = (unit * feats_to[0, 0:1] + feats_to[0, 1:2]).astype(BF16)

    rows = tok_all.shape[0]
    row_blocks(rows, first_norm)
    normed_store = fetch(normed, normed_to, l_sem.at[7])
    for rest in qkv_steps:
        rest()
    qkv.finish()
    narrow.start()
    io.done(6)
    sh = slots * HD

    def project(first, size):
        some = pl.ds(first, size)
        weight = qkv_all[0].reshape(n * padded, 3 * sh)
        own_ref[some] = (dot_n(normed[some], weight) + qkv_bias[0]).astype(BF16)

    row_blocks(rows, project)
    swap = remote(own_ref.at[:, pl.ds(sh, 2 * sh)], oth_ref, kv_ss, kv_rs, p.sibling)
    swap.start()
    swap.wait_recv()
    out.step()
    wide_steps = wide.steps()
    chunk = attention(slots, step, own_ref, oth_ref, kpos_ref, qpos_ref, att_ref, low_ref, lse_ref)
    in_blocks(rows, step, chunk, [])
    out.finish()
    io.done(5, 7, 11, 12, 14)
    normed_store.wait()

    def give(first, size):
        some = pl.ds(first, size)
        part_to[some] = dot_n(low_ref[some], out_all[0]).astype(BF16)

    row_blocks(rows, give)

    scatter = Scatter(p, part_to, *scatter_refs)
    scatter.start()
    arrivals, crossings = wide_steps[: p.zn], wide_steps[p.zn :]
    early = len(arrivals) // 2
    for arrive in arrivals[:early]:
        arrive()
    second = Gather(p, tok_own, tok_all, second_ss, second_rs, second_ls)
    hr = tok_own.shape[0] // HALVES

    def rows_step(half):
        some = slice(half * hr, (half + 1) * hr)
        value = x_to[some] + (scatter.result(half) + feats_to[0, 2:3])
        value_to[some] = value
        unit = unit_rows(value, mask[...], width)[0]
        tok_own[some] = (unit * feats_to[0, 3:4] + feats_to[0, 4:5]).astype(BF16)

    by_halves(scatter, None, lambda half: None, [])
    for arrive in arrivals[early:]:
        arrive()
    for half in range(HALVES):
        rows_step(half)
        second.start([half])
    for second_step in second.steps():
        second_step()
    narrow.step()
    for crossing in crossings:
        crossing()
    second.finish()
    scatter.finish()
    for a, b in others(n):
        pack_copy(a, b).wait_send()
    swap.wait_send()
    narrow.finish()
    wide.finish()
    load = fetch(widen_all.at[0], widen, l_sem.at[4])
    io.done(17, 21)
    load.wait()
    feed_forward(tok_all, widen, narrow_all.at[0], widen_bias[0], pre_to, hidden_to, part_to)


def open_call(n, low, slots, padded, tokens, cotangent, vectors, weights, mask, kpos, qpos):
    qkv, out, widen, narrow = weights
    share, hidden = widen.shape
    width = n * share
    hide = hidden // n
    hide_full = -(-hide // 128) * 128
    sh = slots * HD
    full = n * padded
    rows = tokens.shape[1]
    total = n * rows
    zn = n // 2
    lanes = max(hide_full, -(-2 * share // 128) * 128)
    blocks = (n, padded, 3 * sh)
    wide = (n, padded, hide_full)

    def low_type(*shape):
        return jax.ShapeDtypeStruct(shape, BF16)

    def full_type(*shape):
        return jax.ShapeDtypeStruct(shape, F32)

    return staged_call(
        functools.partial(open_kernel, n, low, width, slots, min(total, 256)),
        "open",
        0,
        (tokens, cotangent, *vectors, qkv, out, widen, narrow, mask, kpos, qpos),
        [
            full_type(rows, full),
            low_type(rows, full),
            full_type(rows, full),
            full_type(1, full),
            low_type(total, full),
            low_type(total, 3 * sh),
            low_type(2, *blocks),
            low_type(2, sh, full),
            full_type(2, 16, full),
            full_type(2, 1, 3 * sh),
            full_type(2, 1, hide_full),
            full_type(sh, total),
            low_type(total, sh),
            full_type(slots, total),
            low_type(total, 2 * sh),
            low_type(2, *wide),
            full_type(rows, full),
            low_type(total, full),
            full_type(total, hide_full),
            low_type(total, hide_full),
            low_type(total, full),
            low_type(2, hide_full, full),
        ],
        [
            pltpu.VMEM((rows, full), BF16),
            pltpu.VMEM((16, lanes), BF16),
            pltpu.VMEM(blocks, BF16),
            pltpu.VMEM((sh, full), BF16),
            pltpu.VMEM(widen.shape, BF16),
            pltpu.VMEM(narrow.shape, BF16),
            pltpu.VMEM(wide, BF16),
            pltpu.VMEM((-(-hide // 16) * 16, full), BF16),
            pltpu.VMEM((2, n, 16, lanes), BF16),
            pltpu.VMEM(wide, BF16),
        ]
        + gather_scratch(n)
        + [DMA((2, n))] * 2
        + [DMA((4, zn))] * 4
        + [DMA((2,))] * 2
        + [DMA((8,)), DMA, DMA, DMA((2,)), DMA((2,))]
        + scatter_scratch(n, rows, full)
        + gather_scratch(n),
        late=(1, 10, 11),
        plain=(12, 13),
        early=(5, 6, 7, 11, 12, 14, 17, 18, 19, 20, 21),
        raw=(4, 15),
    )


def settle_kernel(low, sizes, *refs):
    sources, vec_ref, came_ref, streams, refs = refs[:4], refs[4], refs[5], refs[6:10], refs[10:]
    outs, stream_to, vectors, refs = refs[:4], refs[4:6], refs[6:14], refs[14:]
    loaded, made, in_sem, out_sem = refs[:4], refs[4:8], refs[8], refs[9]
    qkv_ref, widen_ref, out_ref, narrow_ref = loaded
    qkv_to, widen_to, out_to, narrow_to = made
    order = (3, 1, 0, 2)
    loads = {i: fetch(sources[i], loaded[i], in_sem.at[i]) for i in order}
    n, padded, _ = widen_ref.shape
    share = out_to.shape[0]
    hide = narrow_to.shape[0]
    width = qkv_to.shape[1] // 3
    sh = qkv_ref.shape[2] // 3
    s = lax.axis_index("section")

    def without_gaps(values):
        pieces = [values[:, j * padded : j * padded + share] for j in range(n)]
        return jnp.concatenate(pieces, axis=1)

    def lay_rows_back(ref, to):
        to[...] = without_gaps(ref[: to.shape[0]]).astype(F32)

    def lay_qkv_back():
        qkv_to[...] = jnp.zeros_like(qkv_to)
        for j in range(n):
            for t in range(3):
                first = t * width + HD * low[j]
                block = qkv_ref[j, :share, t * sh : (t + 1) * sh]
                qkv_to[:, first : first + sh] += block.astype(F32)

    def lay_widen_back():
        pieces = [widen_ref[j, :share, :hide] for j in range(n)]
        widen_to[...] = jnp.concatenate(pieces, axis=1).astype(F32)

    makers = (
        lay_qkv_back,
        lay_widen_back,
        functools.partial(lay_rows_back, out_ref, out_to),
        functools.partial(lay_rows_back, narrow_ref, narrow_to),
    )
    for item, to in enumerate(stream_to):
        first, second = (ref[...] for ref in streams[2 * item : 2 * item + 2])
        to[s] = without_gaps(jnp.where(s == 0, first, second))
        to[1 - s] = without_gaps(came_ref[item].astype(F32))
    for row, (size, to) in enumerate(zip(sizes, vectors)):
        to[...] = vec_ref[row : row + 1, :size]
    stores = []
    for i in order:
        loads[i].wait()
        makers[i]()
        stores.append(fetch(made[i], outs[i], out_sem.at[i]))
    for store in stores:
        store.wait()


def settle_call(low, share, hide, qkv, widen, out, narrow, vec, came, *streams):
    n = widen.shape[0]
    width = n * share
    rows = came.shape[1]
    sizes = [share] * 6 + [2 * share, hide]
    big = [(share, 3 * width), (share, n * hide), (share, width), (hide, width)]
    return pl.pallas_call(
        functools.partial(settle_kernel, low, sizes),
        out_shape=[jax.ShapeDtypeStruct(shape, F32) for shape in big]
        + [
            jax.ShapeDtypeStruct((2, rows, width), F32),
            jax.ShapeDtypeStruct((2, rows, width), F32),
        ]
        + [jax.ShapeDtypeStruct((1, size), F32) for size in sizes],
        in_specs=[ANY_SPEC] * 4 + [VMEM_SPEC] * 6,
        out_specs=[ANY_SPEC] * 4 + [VMEM_SPEC] * 10,
        scratch_shapes=[pltpu.VMEM(m.shape, BF16) for m in (qkv, widen, out, narrow)]
        + [pltpu.VMEM(shape, F32) for shape in big]
        + [DMA((4,)), DMA((4,))],
        compiler_params=params(),
        name="settle",
    )(qkv, widen, out, narrow, vec, came, *streams)


def unit_rows(values, mask, width):
    center = (values - jnp.sum(values, axis=-1, keepdims=True) * (1.0 / width)) * mask
    spread = jnp.sum(center * center, axis=-1, keepdims=True) * (1.0 / width)
    scale = lax.rsqrt(spread + EPSILON)
    return center * scale, scale


def norm_back(grad, unit, scale, gain, width):
    inner = grad * gain
    mean = jnp.sum(inner, axis=-1, keepdims=True) * (1.0 / width)
    along = jnp.sum(inner * unit, axis=-1, keepdims=True) * (1.0 / width)
    return (inner - mean - unit * along) * scale


def forward_kernel(n, width, layer, io, *refs):
    middle = layer is not None
    part, base, feats, mask = refs[:4]
    refs = refs[4:]
    if middle:
        bias, gain, shift = (feats[layer, row : row + 1] for row in (2, 3, 4))
        widen, narrow, widen_bias, refs = refs[0], refs[1], refs[2], refs[3:]
    else:
        bias, gain, shift = feats[0, 5:6], feats[1, 0:1], feats[1, 1:2]
    value_to, low_all, refs = refs[0], refs[1], refs[2:]
    if middle:
        pre_to, hidden_to, part_to, refs = refs[0], refs[1], refs[2], refs[3:]
    own, g_ss, g_rs, g_ls = refs[5:9]
    p = Place(n)
    enter(io, p, line=True)
    scatter = Scatter(p, part, *refs[:5])
    scatter.start()
    gather = Gather(p, own, low_all, g_ss, g_rs, g_ls)
    hr = own.shape[0] // HALVES

    def rows_step(half):
        rows = slice(half * hr, (half + 1) * hr)
        value = base[rows] + (scatter.result(half) + bias)
        value_to[rows] = value
        own[rows] = (unit_rows(value, mask[...], width)[0] * gain + shift).astype(BF16)

    by_halves(scatter, gather, rows_step, [])
    gather.finish()
    if middle:
        io.done(1)
        io.need(4, 5)
        feed_forward(low_all, widen, narrow, widen_bias[layer], pre_to, hidden_to, part_to)
    scatter.finish()


def scatter_scratch(n, rows, full):
    zn = n // 2
    piece = (HALVES, rows // HALVES, full)
    return [
        pltpu.VMEM((zn,) + piece, BF16),
        pltpu.VMEM((zn + 1,) + piece, BF16),
        pltpu.VMEM((zn,) + piece, BF16),
        DMA((4, zn, HALVES)),
        DMA((4, zn, HALVES)),
    ]


def gather_scratch(n):
    zn = n // 2
    return [DMA((4, zn, HALVES)), DMA((4, zn, HALVES)), DMA((HALVES,))]


def forward_step(n, collective_id, width, part, *local, layer=None, feed=()):
    total_rows, full = part.shape
    rows = total_rows // n
    shapes = [
        jax.ShapeDtypeStruct((rows, full), F32),
        jax.ShapeDtypeStruct((total_rows, full), BF16),
    ]
    scratch = scatter_scratch(n, rows, full)
    scratch += [pltpu.VMEM((rows, full), BF16)] + gather_scratch(n)
    middle = layer is not None
    if middle:
        widen, narrow, _ = feed
        hide = widen.shape[3]
        shapes += [
            jax.ShapeDtypeStruct((total_rows, hide), F32),
            jax.ShapeDtypeStruct((total_rows, hide), BF16),
            jax.ShapeDtypeStruct((total_rows, full), BF16),
        ]
    return Step(
        functools.partial(forward_kernel, n, width, layer),
        "forward_rows",
        collective_id,
        (part, *local, *feed),
        shapes,
        scratch,
        dict(line=True),
        late=(4, 5) if middle else (),
        layers={4: layer, 5: layer} if middle else {},
        early=(1, 2, 3, 4) if middle else (),
        raw=() if middle else (1,),
    )


def back_rows(scatter, half, base, grad, gain, mask, width):
    hr = scatter.hr
    rows = slice(half * hr, (half + 1) * hr)
    total = scatter.result(half)
    unit, scale = unit_rows(base[rows], mask[...], width)
    value = grad[rows] + norm_back(total, unit, scale, gain, width)
    low = value.astype(BF16)
    terms = (total * unit, total, low.astype(F32))
    return rows, value, low, [jnp.sum(term, axis=0, keepdims=True) for term in terms]


def resid_kernel(n, width, layer, io, *refs):
    base, grad, feats, mask, normed, hidden_pre, hidden, outs, widen, narrow = refs[:10]
    gain = feats[layer, 3:4]
    value_to, sums_to, low_all, wide_to, wide_came, slim_to, pre_sums = refs[10:17]
    refs = refs[17:]
    own, g_ss, g_rs, g_ls = refs[5:9]
    wide, wide_in, wide_ss, wide_rs, slim, slim_in, slim_ss, slim_rs, x_ss, x_rs = refs[9:19]
    part, pre = refs[19:]
    p = Place(n)
    enter(io, p, line=True, over=True, sibling=True)
    io.need(9, 7, 5)

    def inner(first, size):
        rows = pl.ds(first, size)
        values = hidden_pre[rows]
        act, square = gelu_parts(values)
        slope = 0.5 * (1.0 + act) + 0.5 * values * (1.0 - act * act) * GELU_A * (
            1.0 + 3.0 * GELU_B * square
        )
        found = (dot_t(outs[rows], narrow[...]) * slope).astype(BF16)
        pre[rows] = found

    def outer(first, size):
        rows = pl.ds(first, size)
        weight = widen[...].reshape(part.shape[1], widen.shape[2])
        part[rows] = dot_t(pre[rows], weight).astype(BF16)

    row_blocks(part.shape[0], inner)
    io.need(8)
    row_blocks(part.shape[0], outer)
    scatter = Scatter(p, part, *refs[:5])
    scatter.start()
    gather = Gather(p, own, low_all, g_ss, g_rs, g_ls)
    wide_fold = Fold(p, wide, wide_in, wide_to, wide_ss, wide_rs)
    slim_fold = Fold(p, slim, slim_in, slim_to, slim_ss, slim_rs)
    cross = Cross(p, wide_to, wide_came, x_ss, x_rs, 1 - layer)

    def pre_sum():
        pre_sums[...] = jnp.sum(pre[...].astype(F32), axis=0, keepdims=True)

    io.need(4, 6)
    for step in product(normed, pre, wide):
        step()
    wide_fold.start()

    def wide_done():
        cross.start()
        io.done(3)

    work = product(hidden, outs, slim) + wide_fold.steps() + [wide_done, slim_fold.start, pre_sum]
    work += slim_fold.steps() + [functools.partial(io.done, 5)]
    sums = []

    def rows_step(half):
        rows, value, low, terms = back_rows(scatter, half, base, grad, gain, mask, width)
        value_to[rows] = value
        own[rows] = low
        sums.append(jnp.concatenate(terms, axis=0))

    by_halves(scatter, gather, rows_step, work, 3)
    sums_to[...] = sum(sums)
    for rest in work:
        rest()
    gather.finish()
    scatter.finish()
    for job in (wide_fold, slim_fold, cross):
        job.finish()


def resid_step(n, collective_id, width, layer, hide, *args):
    base, normed, hidden = args[0], args[4], args[6]
    rows = base.shape[0]
    total_rows, full = normed.shape
    zn = n // 2
    wide = (zn, full // n, hidden.shape[1])
    half = -(-hide // 32) * 16
    slim = (1, half, full)
    return Step(
        functools.partial(resid_kernel, n, width, layer),
        "back_resid",
        collective_id,
        args,
        [
            jax.ShapeDtypeStruct((rows, full), F32),
            jax.ShapeDtypeStruct((3, full), F32),
            jax.ShapeDtypeStruct((total_rows, full), BF16),
            jax.ShapeDtypeStruct(wide, BF16),
            jax.ShapeDtypeStruct(wide, BF16),
            jax.ShapeDtypeStruct(slim, BF16),
            jax.ShapeDtypeStruct((1, hidden.shape[1]), F32),
        ],
        scatter_scratch(n, rows, full)
        + [pltpu.VMEM((rows, full), BF16)]
        + gather_scratch(n)
        + fold_scratch((full, hidden.shape[1]), wide)
        + fold_scratch((2 * half, full), slim)
        + [DMA, DMA]
        + [
            pltpu.VMEM((total_rows, full), BF16),
            pltpu.VMEM(hidden.shape, BF16),
        ],
        dict(line=True, over=True, sibling=True),
        late=(9, 7, 5, 8, 4, 6),
        layers={8: layer, 9: layer},
        early=(3, 5),
        raw=(2, 4),
    )


def input_kernel(n, width, source, low, io, *refs):
    part, base, grad, feats, mask, normed, triple, att, resid, slim = refs[:10]
    gain = feats[1, 0:1]
    value_to, sums_to, low_all, qkv_to, out_to, slim_came, triple_sums = refs[10:17]
    refs = refs[17:]
    own, g_ss, g_rs, g_ls = refs[5:9]
    qkv, qkv_in, qkv_ss, qkv_rs, out, out_in, out_ss, out_rs, x_ss, x_rs = refs[9:]
    p = Place(n)
    enter(io, p, line=True, over=True, sibling=True)
    scatter = Scatter(p, part, *refs[:5])
    scatter.start()
    cross = Cross(p, slim, slim_came, x_ss, x_rs, source)
    cross.start()
    gather = Gather(p, own, low_all, g_ss, g_rs, g_ls)
    qkv_fold = Fold(p, qkv, qkv_in, qkv_to, qkv_ss, qkv_rs)
    out_fold = Fold(p, out, out_in, out_to, out_ss, out_rs)

    def triple_sum():
        triple_sums[...] = jnp.sum(triple[...].astype(F32), axis=0, keepdims=True)

    work = [functools.partial(io.need, 5, 6)] + product(normed, triple, qkv)
    work += [qkv_fold.start, functools.partial(io.need, 7, 8)]
    work += [functools.partial(home_rows, att, resid, out, low, width // n), out_fold.start]
    work += qkv_fold.steps() + [functools.partial(io.done, 3), triple_sum]
    work += out_fold.steps() + [functools.partial(io.done, 4)]
    sums = []

    def rows_step(half):
        rows, value, lower, terms = back_rows(scatter, half, base, grad, gain, mask, width)
        value_to[rows] = value
        own[rows] = lower
        sums.append(jnp.concatenate(terms, axis=0))

    by_halves(scatter, gather, rows_step, work, 2)
    sums_to[...] = sum(sums)
    for rest in work:
        rest()
    gather.finish()
    scatter.finish()
    for job in (qkv_fold, out_fold, cross):
        job.finish()


def input_step(n, collective_id, width, source, low, part, base, grad, feats, mask, *operands):
    normed, triple, att, resid, slim = operands
    total_rows, full = part.shape
    rows = total_rows // n
    zn = n // 2
    qkv = (zn, full // n, triple.shape[1])
    out = (1, att.shape[1] // 2, full)
    return Step(
        functools.partial(input_kernel, n, width, source, low),
        "back_input",
        collective_id,
        (part, base, grad, feats, mask) + operands,
        [
            jax.ShapeDtypeStruct((rows, full), F32),
            jax.ShapeDtypeStruct((3, full), F32),
            jax.ShapeDtypeStruct((total_rows, full), BF16),
            jax.ShapeDtypeStruct(qkv, BF16),
            jax.ShapeDtypeStruct(out, BF16),
            jax.ShapeDtypeStruct(slim.shape, BF16),
            jax.ShapeDtypeStruct((1, triple.shape[1]), F32),
        ],
        scatter_scratch(n, rows, full)
        + [pltpu.VMEM((rows, full), BF16)]
        + gather_scratch(n)
        + fold_scratch((full, triple.shape[1]), qkv)
        + fold_scratch((att.shape[1], full), out)
        + [DMA, DMA],
        dict(line=True, over=True, sibling=True),
        late=(5, 6, 7, 8),
        plain=(9,),
        early=(3, 4),
        raw=(2, 5),
    )


def finale_kernel(n, width, low, between, io, *refs):
    part, base, grad, feats, mask, normed, triple, att, resid = refs[:9]
    slims, slim_came, qkv_far, out_far, vecs = refs[9:11], refs[11], refs[12], refs[13], refs[14:21]
    layer_outs, upper_d_in, wides, refs = refs[21:23], refs[23], refs[24:28], refs[28:]
    value_to, slim_to, qkv_to, out_to, vec_to, streams_to, wide_to = refs[:7]
    refs = refs[7:]
    qkv, qkv_fold_in, qkv_ss, qkv_rs, out, out_fold_in, out_ss, out_rs = refs[5:13]
    qkv_own, qkv_in, qkv_sum, out_own, out_in, out_sum = refs[13:19]
    slim_sum, slim_pair, vec, vec_in, vec_sum, vec_sib, streams = refs[19:26]
    a_ss, a_rs, x_ss, x_rs, v_ss, v_rs, r_ss, r_rs, ls = refs[26:35]
    wide_sum, wide_pair, w_ss, w_rs = refs[35:]
    p = Place(n)
    s, c, h, z, zn = p.s, p.c, p.h, p.z, p.zn
    share = width // n
    greet_all(p)
    choices = (
        (
            (wides[0], wide_pair.at[0], 5),
            (wides[1], wide_pair.at[1], 6),
            (slims[0], slim_pair.at[0], 1),
        ),
        (
            (wides[2], wide_pair.at[0], 5),
            (wides[3], wide_pair.at[1], 6),
            (slims[1], slim_pair.at[0], 1),
            (slim_came, slim_pair.at[1], 4),
        ),
    )
    for section, chosen in enumerate(choices):

        @pl.when(s == section)
        def _():
            for src, dst, item in chosen:
                pltpu.make_async_copy(src, dst, ls.at[item]).start()

    def chosen_wait(item):
        src, dst, sem = choices[1][item]
        pltpu.make_async_copy(src, dst, ls.at[sem]).wait()

    slim_cross = Cross(p, slims[0], slim_pair.at[1], x_ss.at[zn + 2], x_rs.at[zn + 2], 1)
    slim_cross.start()
    wide_back = Home(p, wide_sum, wide_to, w_ss, w_rs, ls.at[8])
    chosen_wait(0)
    chosen_wait(1)
    for k in list(range(1, zn)) + [0]:
        far = p.flip(k)
        total = wide_pair[0, far].astype(F32) + wide_pair[1, far].astype(F32)
        wide_sum[far] = total.astype(BF16)
        wide_back.start(k)
    if between is not None:
        between()
    scatter = Scatter(p, part, *refs[:5])
    scatter.start()
    back = Home(p, qkv_sum, qkv_to, a_ss, a_rs, ls.at[0])

    def x_block(k, src=qkv_far):
        far = p.flip(k)
        return remote(src.at[far], qkv_in.at[far], x_ss.at[k], x_rs.at[k], p.over)

    def out_cross(src=out_far):
        return remote(src, out_in, x_ss.at[zn], x_rs.at[zn], p.over)

    stream_cross = remote(streams, streams_to, x_ss.at[zn + 1], x_rs.at[zn + 1], p.over)

    def start_far():
        @pl.when(s == 0)
        def _():
            for k in range(zn):
                x_block(k).start()
            out_cross().start()

    def start_own(k):
        @pl.when(s == 1)
        def _():
            x_block(k, qkv_own).start()

    def start_own_out():
        @pl.when(s == 1)
        def _():
            out_cross(out_own).start()

    qkv_fold = Fold(p, qkv, qkv_fold_in, qkv_own, qkv_ss, qkv_rs)
    out_fold = Fold(p, out, out_fold_in, out_own, out_ss, out_rs)

    io.need(12, 13)
    start_far()
    io.need(5, 6)
    for step in product(normed, triple, qkv):
        step()
    qkv_fold.start()
    io.need(7, 8)
    work = [functools.partial(home_rows, att, resid, out, low, share), out_fold.start]
    work += qkv_fold.steps()
    work += [functools.partial(start_own, k) for k in list(range(1, zn)) + [0]]
    work += out_fold.steps() + [start_own_out]
    sums = []

    def rows_step(half):
        rows, value, lower, terms = back_rows(scatter, half, base, grad, feats[0, 0:1], mask, width)
        value_to[rows] = value
        sums.append(jnp.concatenate(terms, axis=0))

    by_halves(scatter, None, rows_step, work, 3)
    for rest in work:
        rest()

    io.need(21, 22, 23)
    streams[0] = jnp.where(s == 0, layer_outs[1][...], layer_outs[0][...]).astype(BF16)
    streams[1] = jnp.where(s == 0, upper_d_in[...], value_to[...]).astype(BF16)
    io.done(0)
    stream_cross.start()

    ones = (sum(sums), vecs[0][...])
    twos, triples, pres = vecs[1:3], (None, vecs[3]), vecs[4:6]
    lanes = vec.shape[3]
    padded = base.shape[1] // n
    sh = triple.shape[1] // 3
    for layer in range(2):
        one, two = ones[layer], twos[layer][...]
        outs = vecs[6][...] if layer else ones[1][2:3]
        features = jnp.concatenate([one[0:2], two[2:3], two[0:2], outs], axis=0)
        if layer:
            found = triples[1][...]
        else:
            found = jnp.sum(triple[...].astype(F32), axis=0, keepdims=True)
        bias = jnp.zeros((1, 2 * width), F32)
        for j, first in enumerate(low):
            spots = []
            for begin in (0, 2 * sh):
                spots += [
                    jnp.zeros((1, HD * first), F32),
                    found[:, begin : begin + sh],
                    jnp.zeros((1, width - sh - HD * first), F32),
                ]
            spots = [spot for spot in spots if spot.shape[1]]
            bias = jnp.where(h == j, jnp.concatenate(spots, axis=1), bias)
        for i in range(n):
            pieces = [
                features[:, i * padded : (i + 1) * padded],
                bias[:, i * 2 * share : (i + 1) * 2 * share],
                jnp.where(h == i, pres[layer][...], 0.0),
            ]
            wide_pieces = []
            for piece in pieces:
                rows, size = piece.shape
                if size < lanes:
                    piece = jnp.concatenate([piece, jnp.zeros((rows, lanes - size), F32)], axis=1)
                wide_pieces.append(piece)
            vec[layer, i] = jnp.concatenate(wide_pieces, axis=0)

    def vec_copy(a, b):
        l, i = lax.rem(s + a, 2), lax.rem(h + b, n)
        return remote(vec.at[l, i], vec_in.at[s, h], v_ss.at[a, b], v_rs.at[a, b], (l, c, i))

    for a, b in others(n):
        vec_copy(a, b).start()

    for k in list(range(1, zn)) + [0]:
        x_block(k).wait_recv()
        add_home(p, qkv_sum, p.flip(k), qkv_own, qkv_in, qkv_far, qkv_in)
        back.start(k)
    out_cross().wait_recv()
    add_home(p, out_sum, 0, out_own, out_in, out_far, out_in)
    for k in range(zn):
        x_block(k).wait_send()
    chosen_wait(2)

    @pl.when(s == 1)
    def _():
        chosen_wait(3)

    for step in wide_back.steps():
        step()
    slim_cross.finish()
    slim_sum[0] = (slim_pair[0, 0].astype(F32) + slim_pair[1, 0].astype(F32)).astype(BF16)

    def row_copies(w, src, dst):
        half = src.shape[1]
        piece = dst.at[pl.ds(pl.multiple_of(c * half, 16), half)]
        return (
            pltpu.make_async_copy(src.at[0], piece, ls.at[2 + w]),
            remote(src.at[0], piece, r_ss.at[w], r_rs.at[w], p.sibling),
        )

    copies = row_copies(0, slim_sum, slim_to) + row_copies(1, out_sum, out_to)
    for copy in copies:
        copy.start()
    total = vec[s, h]
    for a, b in others(n):
        vec_copy(a, b).wait_recv()
        total = total + vec_in[lax.rem(s + a, 2), lax.rem(h + n - b, n)]
    vec_sum[...] = total
    vec_share = remote(vec_sum, vec_sib, r_ss.at[2], r_rs.at[2], p.sibling)
    vec_share.start()
    for step in back.steps():
        step()
    vec_share.wait_recv()
    vec_to[...] = total + vec_sib[...]
    vec_share.wait_send()
    back.finish()
    wide_back.finish()
    for w in range(2):
        copies[2 * w].wait()
        copies[2 * w + 1].wait_recv()
        copies[2 * w + 1].wait_send()
    for a, b in others(n):
        vec_copy(a, b).wait_send()
    out_cross().wait_send()
    stream_cross.wait_recv()
    stream_cross.wait_send()
    for job in (scatter, qkv_fold, out_fold):
        job.finish()


def finale_parts(n, *args):
    part, triple, att = args[0], args[6], args[7]
    slim, lanes, wide = args[9].shape, args[18].shape[1], args[24].shape
    total_rows, full = part.shape
    rows = total_rows // n
    zn = n // 2
    qkv = (zn, full // n, triple.shape[1])
    out = (1, att.shape[1] // 2, full)
    shapes = [
            jax.ShapeDtypeStruct((rows, full), F32),
            jax.ShapeDtypeStruct((2 * slim[1], full), BF16),
            jax.ShapeDtypeStruct((n,) + qkv[1:], BF16),
            jax.ShapeDtypeStruct((2 * out[1], full), BF16),
            jax.ShapeDtypeStruct((8, lanes), F32),
            jax.ShapeDtypeStruct((2, rows, full), BF16),
            jax.ShapeDtypeStruct((n,) + wide[1:], BF16),
        ]
    scratch = (
        scatter_scratch(n, rows, full)
        + fold_scratch((full, triple.shape[1]), qkv)
        + fold_scratch((att.shape[1], full), out)
        + [pltpu.VMEM(qkv, BF16)] * 3
        + [pltpu.VMEM(out, BF16)] * 3
        + [
            pltpu.VMEM(slim, BF16),
            pltpu.VMEM((2,) + slim, BF16),
            pltpu.VMEM((2, n, 8, lanes), F32),
            pltpu.VMEM((2, n, 8, lanes), F32),
            pltpu.VMEM((8, lanes), F32),
            pltpu.VMEM((8, lanes), F32),
            pltpu.VMEM((2, rows, full), BF16),
            DMA((2, zn)),
            DMA((2, zn)),
            DMA((zn + 3,)),
            DMA((zn + 3,)),
            DMA((2, n)),
            DMA((2, n)),
            DMA((3,)),
            DMA((3,)),
            DMA((9,)),
            pltpu.VMEM(wide, BF16),
            pltpu.VMEM((2,) + wide, BF16),
            DMA((2, zn)),
            DMA((2, zn)),
        ]
    )
    return shapes, scratch


def finale_call(n, collective_id, width, low, *args):
    shapes, scratch = finale_parts(n, *args)
    return staged_call(
        functools.partial(finale_kernel, n, width, low, None),
        "finale",
        collective_id,
        args,
        shapes,
        scratch,
        late=(5, 6, 7, 8, 12, 13, 21, 22, 23),
        plain=(9, 10, 11, 24, 25, 26, 27),
        early=(0,),
        raw=(1, 2, 3, 5, 6),
    )


def dot_t(a, b):
    return lax.dot_general(a, b, (((1,), (1,)), ((), ())), preferred_element_type=F32)


def dot_n(a, b):
    return lax.dot_general(a, b, (((1,), (0,)), ((), ())), preferred_element_type=F32)


def in_blocks(rows, step, chunk, between):
    count = rows // step
    if count <= 2:
        for b in range(count):
            chunk(b * step, rows // 2 if (b + 1) * step <= rows // 2 else rows, between)
    else:

        def body(b, carry, keys):
            chunk(pl.multiple_of(b * step, step), keys, [])
            return carry

        middle = count // 2 if count % 2 == 0 else 0
        lax.fori_loop(0, middle, functools.partial(body, keys=rows // 2), 0)
        lax.fori_loop(middle, count, functools.partial(body, keys=rows), 0)


def run_next(between):
    if between:
        between.pop(0)()


def attention(slots, step, own_ref, oth_ref, kpos_ref, qpos_ref, att_ref, low_ref, lse_ref):
    rows = own_ref.shape[0]
    sh = slots * HD
    power = HD**-0.5 * LOG2E

    def at(base, slot):
        return slice(base + slot * HD, base + (slot + 1) * HD)

    def chunk(first, seen, between):
        q_rows = pl.ds(first, step)
        qpos = qpos_ref[:, q_rows]
        for slot in range(slots):
            queries = own_ref[q_rows, at(0, slot)]
            keys = (own_ref[:seen, at(sh, slot)], oth_ref[:seen, at(0, slot)])
            values = (own_ref[:seen, at(2 * sh, slot)], oth_ref[:seen, at(sh, slot)])
            scores = []
            for part in range(2):
                allowed = kpos_ref[part * rows : part * rows + seen] <= qpos
                scores.append(jnp.where(allowed, dot_t(keys[part], queries), MASKED))
            top = jnp.maximum(
                jnp.max(scores[0], axis=0, keepdims=True), jnp.max(scores[1], axis=0, keepdims=True)
            )
            total = jnp.zeros_like(top)
            weighted = jnp.zeros((HD, step), F32)
            exps = []
            for part in range(2):
                e = jnp.exp2((scores[part] - top) * power)
                total = total + jnp.sum(e, axis=0, keepdims=True)
                exps.append(e)
            inverse = 1.0 / total
            for part in range(2):
                probs = (exps[part] * inverse).astype(BF16)
                weighted = weighted + dot_n(values[part].T, probs)
            att_ref[at(0, slot), q_rows] = weighted
            low_ref[q_rows, at(0, slot)] = weighted.T.astype(BF16)
            lse_ref[slot : slot + 1, q_rows] = top * power + jnp.log(total) * LOG2E
            run_next(between)

    return chunk


def attend_kernel(n, slots, step, layer, io, *refs):
    kpos_ref, qpos_ref, carried, out_all, normed, qkv_all, qkv_bias = refs[:7]
    att_ref, low_ref, lse_ref, oth_ref, part_to, carried_to, own_ref = refs[7:14]
    kv_ss, kv_rs, out_weight, qkv_weight, load_sems = refs[14:19]
    qkv_load = fetch(qkv_all.at[layer], qkv_weight, load_sems.at[1])
    out_load = fetch(out_all.at[layer], out_weight, load_sems.at[0])
    p = Place(n)
    rows = own_ref.shape[0]
    sh = slots * HD
    enter(io, p, line=True, sibling=True)
    job = Gather(p, carried, carried_to, *refs[19:])
    job.start()
    qkv_load.wait()
    io.need(4)
    between = job.steps()

    def project(first, size):
        some = pl.ds(first, size)
        weight = qkv_weight[...].reshape(normed.shape[1], 3 * sh)
        own_ref[some] = (dot_n(normed[some], weight) + qkv_bias[layer]).astype(BF16)

    row_blocks(rows, project)
    swap = remote(own_ref.at[:, pl.ds(sh, 2 * sh)], oth_ref, kv_ss, kv_rs, p.sibling)
    swap.start()
    run_next(between)
    run_next(between)
    swap.wait_recv()
    chunk = attention(slots, step, own_ref, oth_ref, kpos_ref, qpos_ref, att_ref, low_ref, lse_ref)
    in_blocks(rows, step, chunk, between)
    out_load.wait()

    def give(first, size):
        some = pl.ds(first, size)
        part_to[some] = dot_n(low_ref[some], out_weight[...]).astype(BF16)

    row_blocks(rows, give)
    io.done(0, 1, 4, 6)
    for rest in between:
        rest()
    swap.wait_send()
    job.finish()


def attend_step(n, collective_id, slots, layer, kpos, qpos, carried, out_all, *source):
    rows = qpos.shape[1]
    sh = slots * HD
    full = out_all.shape[2]
    return Step(
        functools.partial(attend_kernel, n, slots, min(rows, 256), layer),
        "attend",
        collective_id,
        (kpos, qpos, carried, out_all, *source),
        [
            jax.ShapeDtypeStruct((sh, rows), F32),
            jax.ShapeDtypeStruct((rows, sh), BF16),
            jax.ShapeDtypeStruct((slots, rows), F32),
            jax.ShapeDtypeStruct((rows, 2 * sh), BF16),
            jax.ShapeDtypeStruct((rows, full), BF16),
            jax.ShapeDtypeStruct((n * carried.shape[0], full), BF16),
            jax.ShapeDtypeStruct((rows, 3 * sh), BF16),
        ],
        [
            DMA,
            DMA,
            pltpu.VMEM((sh, full), BF16),
            pltpu.VMEM(source[1].shape[1:], BF16),
            DMA((2,)),
        ]
        + gather_scratch(n),
        dict(line=True, sibling=True),
        late=(4,),
        plain=(3, 5),
        early=(0, 1, 4, 6),
        raw=(5,),
    )


def attend_back_kernel(n, slots, step, layer, last, greeted, io, *refs):
    own_ref, oth_ref, resid, att_ref, lse_ref, kpos_ref, qpos_ref, out_all, qkv_all = refs[:9]
    refs = refs[9:]
    if last:
        part_ref, base_ref, feats = refs[:3]
        refs = refs[3:]
    triple_ref, part_to, refs = refs[0], refs[1], refs[2:]
    if last:
        value_ref, refs = refs[0], refs[1:]
    dq_t, dkv_own, dkv_oth, came, kv_ss, kv_rs = refs[:6]
    grad_ref, out_weight, qkv_weight, load_sems = refs[6:10]
    out_load = fetch(out_all.at[layer], out_weight, load_sems.at[0])
    qkv_load = fetch(qkv_all.at[layer], qkv_weight, load_sems.at[1])
    p = Place(n)
    rows = own_ref.shape[0]
    sh = slots * HD
    scale = HD**-0.5
    if not greeted:
        greet(p, line=last, sibling=True)
    between = []
    if last:
        scatter = Scatter(p, part_ref, *refs[10:])
        scatter.start()
        between = scatter.steps()
    io.need(2)
    out_load.wait()

    def enter(first, size):
        some = pl.ds(first, size)
        grad_ref[some] = dot_t(resid[some], out_weight[...]).astype(BF16)

    row_blocks(rows, enter)
    io.need(0, 1, 3)

    def at(base, slot):
        return slice(base + slot * HD, base + (slot + 1) * HD)

    dq_t[...] = jnp.zeros_like(dq_t)
    swap = remote(dkv_oth, came, kv_ss, kv_rs, p.sibling)
    for part in (1, 0):
        dkv = (dkv_own, dkv_oth)[part]
        src = (own_ref, oth_ref)[part]
        base = (sh, 0)[part]
        dkv[...] = jnp.zeros_like(dkv)

        def chunk(first, seen, between):
            q_rows = pl.ds(first, step)
            qpos = qpos_ref[:, q_rows]
            for slot in range(slots):
                queries = own_ref[q_rows, at(0, slot)]
                grads = grad_ref[q_rows, at(0, slot)]
                keys, values = src[:seen, at(base, slot)], src[:seen, at(base + sh, slot)]
                lse = lse_ref[slot : slot + 1, q_rows]
                correction = jnp.sum(
                    grads.astype(F32).T * att_ref[at(0, slot), q_rows], axis=0, keepdims=True
                )
                allowed = kpos_ref[part * rows : part * rows + seen] <= qpos
                scores = dot_t(keys, queries)
                probs = jnp.where(allowed, jnp.exp2(scores * (scale * LOG2E) - lse), 0.0)
                prob_grad = dot_t(values, grads)
                score_grad = (probs * (prob_grad - correction)).astype(BF16)
                dkv[:seen, at(0, slot)] += dot_n(score_grad, queries) * scale
                dkv[:seen, at(sh, slot)] += dot_n(probs.astype(BF16), grads)
                dq_t[at(0, slot), q_rows] += dot_n(keys.T, score_grad)
                run_next(between)

        in_blocks(rows, step, chunk, between)
        if part:
            swap.start()
    triple_ref[:, :sh] = (dq_t[...].T * scale).astype(BF16)

    def finish_last():
        for rest in between:
            rest()
        hr = base_ref.shape[0] // HALVES
        for half in range(HALVES):
            part_rows = slice(half * hr, (half + 1) * hr)
            total = scatter.result(half)
            value_ref[part_rows] = base_ref[part_rows] + (total + feats[1, 5:6])
        scatter.finish()

    swap.wait_recv()
    triple_ref[:, sh:] = (dkv_own[...] + came[...]).astype(BF16)
    qkv_load.wait()

    def leave(first, size):
        some = pl.ds(first, size)
        weight = qkv_weight[...].reshape(part_to.shape[1], 3 * sh)
        part_to[some] = dot_t(triple_ref[some], weight).astype(BF16)

    io.done(0)
    row_blocks(rows, leave)
    io.done(1)
    if last:
        finish_last()
    swap.wait_send()


def attend_back_scratch(rows, sh, full, qkv_all):
    scratch = [pltpu.VMEM((sh, rows), F32)] + [pltpu.VMEM((rows, 2 * sh), F32)] * 3
    scratch += [DMA, DMA]
    return scratch + [
        pltpu.VMEM((rows, sh), BF16),
        pltpu.VMEM((sh, full), BF16),
        pltpu.VMEM(qkv_all.shape[1:], BF16),
        DMA((2,)),
    ]


def closing_kernel(n, width, low, slots, step, io, *refs):
    back, rest, refs = refs[:9], refs[9 : 9 + 25], refs[34:]
    outs, refs = refs[:7], refs[7:]
    back_scratch, triple, part, refs = refs[:10], refs[10], refs[11], refs[12:]

    def between():
        mapped = Mapped(io, {i: i for i in range(9)}, {})
        attend_back_kernel(
            n, slots, step, 0, False, True, mapped, *back, triple, part, *back_scratch
        )

    numbers = [i for i in range(28) if i not in (0, 6, 8)]
    places = {i: 9 + x for x, i in enumerate(numbers)}
    places[8] = 2
    operands = dict(zip(numbers, rest))
    operands.update({0: part, 6: triple, 8: back[2]})
    finale_kernel(
        n,
        width,
        low,
        between,
        Mapped(io, places, {i: i for i in range(7)}),
        *(operands[i] for i in range(28)),
        *outs,
        *refs,
    )


def closing_call(n, collective_id, width, low, slots, back, args):
    qkv, out_all, qkv_all = back[0], back[7], back[8]
    rows = qkv.shape[0]
    full = out_all.shape[2]
    triple = jax.ShapeDtypeStruct((rows, qkv.shape[1]), BF16)
    part = jax.ShapeDtypeStruct((rows, full), BF16)
    args = [part] + list(args[:5]) + [triple] + list(args[5:6]) + [back[2]] + list(args[6:])
    shapes, scratch = finale_parts(n, *args)
    numbers = [i for i in range(28) if i not in (0, 6, 8)]
    places = {i: 9 + x for x, i in enumerate(numbers)}
    return staged_call(
        functools.partial(closing_kernel, n, width, low, slots, min(rows, 256)),
        "closing",
        collective_id,
        tuple(back) + tuple(args[i] for i in numbers),
        shapes,
        attend_back_scratch(rows, slots * HD, full, qkv_all)
        + [pltpu.VMEM(triple.shape, BF16), pltpu.VMEM(part.shape, BF16)]
        + scratch,
        late=(2, 0, 1, 3) + tuple(places[i] for i in (5, 7, 12, 13, 21, 22, 23)),
        plain=(7, 8) + tuple(places[i] for i in (9, 10, 11, 24, 25, 26, 27)),
        early=(0,),
        raw=(1, 2, 3, 5, 6),
    )


def attend_back_call(n, collective_id, slots, layer, *args, last=()):
    qkv, out_all, qkv_all = args[0], args[7], args[8]
    rows = qkv.shape[0]
    sh = slots * HD
    full = out_all.shape[2]
    step = min(rows, 256)
    shapes = [
        jax.ShapeDtypeStruct((rows, 3 * sh), BF16),
        jax.ShapeDtypeStruct((rows, full), BF16),
    ]
    scratch = attend_back_scratch(rows, sh, full, qkv_all)
    if last:
        shapes.append(jax.ShapeDtypeStruct(last[1].shape, F32))
        scratch += scatter_scratch(n, *last[1].shape)
    return staged_call(
        functools.partial(attend_back_kernel, n, slots, step, layer, bool(last), False),
        "attend_back",
        collective_id,
        args + tuple(last),
        shapes,
        scratch,
        late=(0, 1, 2, 3),
        plain=(7, 8),
        early=(0, 1),
    )


def windows(width, n):
    share = width // n
    low = [j * share // HD for j in range(n)]
    slots = max(((j + 1) * share - 1) // HD - low[j] + 1 for j in range(n))
    return [min(first, HEADS - slots) for first in low], slots


def on_device(n, tokens, block_order, cotangent, *vectors_and_weights):
    (
        first_gain,
        first_shift,
        qkv_weight,
        input_bias,
        out_weight,
        out_bias,
        second_gain,
        second_shift,
        widen_weight,
        widen_bias,
        narrow_weight,
        narrow_bias,
    ) = (member[0] for member in vectors_and_weights)
    c = lax.axis_index("ctx")
    _, rows, width = tokens.shape
    hidden = widen_weight.shape[1]
    share = width // n
    hide = hidden // n
    padded = -(-share // 16) * 16
    full = n * padded
    low, slots = windows(width, n)
    sh = slots * HD
    total_rows = n * rows
    half_rows = rows // HALVES

    mask = jnp.asarray(np.arange(full)[None] % padded < share, F32)
    order = block_order.reshape(2, n, HALVES).transpose(0, 2, 1)
    places = order[..., None] * half_rows + jnp.arange(half_rows, dtype=jnp.int32)
    places = places.reshape(2, total_rows)
    own_places = jnp.where(c == 0, places[0], places[1])
    oth_places = jnp.where(c == 0, places[1], places[0])
    kpos = jnp.concatenate([own_places, oth_places])[:, None]
    qpos = own_places[None, :]

    (
        x,
        own_cot,
        out_grad,
        out_sums,
        normed,
        qkv,
        qkv_all,
        out_all,
        feats,
        qkv_bias,
        widen_biases,
        att,
        att_low,
        lse,
        other,
        widen_all,
        *middle,
        narrow_all,
    ) = open_call(
        n,
        low,
        slots,
        padded,
        tokens,
        cotangent,
        [
            member[None]
            for member in (
                first_gain,
                first_shift,
                out_bias,
                second_gain,
                second_shift,
                narrow_bias,
                input_bias,
                widen_bias,
            )
        ],
        (qkv_weight, out_weight, widen_weight, narrow_weight),
        mask,
        kpos,
        qpos,
    )
    stored = []
    layer_outs = []
    merge = total_rows * full <= 2**20
    residual, normed_two, hidden_pre, hidden_low, part = middle
    stored.append((x, normed, qkv, other, att, att_low, lse, residual, normed_two))
    stored[-1] += (hidden_pre, hidden_low)
    (x, normed), attended = follow(
        merge,
        forward_step(n, 5, width, part, residual, feats, mask),
        lambda ended: attend_step(
            n, 2, slots, 1, kpos, qpos, own_cot, out_all, ended[1], qkv_all, qkv_bias
        ),
    )
    layer_outs.append(x)
    att, att_low, lse, other, part, out_low_all, qkv = attended
    second_middle = forward_step(
        n,
        4,
        width,
        part,
        x,
        feats,
        mask,
        layer=1,
        feed=(widen_all, narrow_all, widen_biases),
    )

    def back_middle(layer, residual, grad, normed_two, hidden_pre, hidden_low, low_all):
        return resid_step(
            n,
            7 + layer,
            width,
            layer,
            hide,
            residual,
            grad,
            feats,
            mask,
            normed_two,
            hidden_pre,
            hidden_low,
            low_all,
            widen_all,
            narrow_all,
        )

    middle, back = follow(
        merge,
        second_middle,
        lambda made: back_middle(1, made[0], out_grad, *made[1:4], out_low_all),
    )
    residual, normed_two, hidden_pre, hidden_low, part = middle
    stored.append((x, normed, qkv, other, att, att_low, lse, residual, normed_two))
    stored[-1] += (hidden_pre, hidden_low)
    last = (part, residual, feats)

    found = {}
    for layer in (1, 0):
        x, normed, qkv, other, att, att_low, lse, residual, normed_two = stored[layer][:9]
        hidden_pre, hidden_low = stored[layer][9:]
        resid_grad, sums_two, resid_low_all, wide, wide_came, slim, pre_sums = back
        operands = (qkv, other, resid_low_all, att, lse, kpos, qpos, out_all, qkv_all)
        found[layer] = (wide, wide_came, slim, sums_two, pre_sums)
        if layer:
            triple, part, last_out = attend_back_call(n, 10, slots, 1, *operands, last=last)
            layer_outs.append(last_out)
            upper_step = input_step(
                n,
                11,
                width,
                0,
                low,
                part,
                x,
                resid_grad,
                feats,
                mask,
                normed,
                triple,
                att_low,
                resid_low_all,
                slim,
            )
            below = stored[0]
            ended, back = follow(
                merge,
                upper_step,
                lambda ended: back_middle(0, below[7], ended[0], *below[8:], ended[2]),
            )
            upper_d_in, sums_one, _, qkv_grad, out_rows, slim_came, triple_sums = ended
    lower, upper = found[0], found[1]
    streams = (
        lower[2],
        upper[2],
        slim_came,
        qkv_grad,
        out_rows,
        sums_one,
        lower[3],
        upper[3],
        triple_sums,
        lower[4],
        upper[4],
        out_sums,
        *layer_outs,
        upper_d_in,
        *lower[:2],
        *upper[:2],
    )
    own = (x, resid_grad, feats, mask, normed)
    if merge:
        ended = closing_call(n, 12, width, low, slots, operands, (*own, att_low, *streams))
    else:
        triple, part = attend_back_call(n, 9, slots, 0, *operands)
        ended = finale_call(
            n, 12, width, low, part, *own, triple, att_low, resid_low_all, *streams
        )
    d_in, narrow_back, qkv_back, out_back, vec, came, widen_back = ended
    settled = settle_call(
        low,
        share,
        hide,
        qkv_back,
        widen_back,
        out_back,
        narrow_back,
        vec,
        came,
        *layer_outs,
        d_in,
        upper_d_in,
    )
    qkv_out, widen_out, out_out, narrow_out, layer_out, d_out = (m[None] for m in settled[:6])
    gain1, shift1, out_b, gain2, shift2, narrow_b, input_b, widen_b = settled[6:]
    return (
        layer_out,
        d_out,
        gain1,
        shift1,
        qkv_out,
        input_b,
        out_out,
        out_b,
        gain2,
        shift2,
        widen_out,
        widen_b,
        narrow_out,
        narrow_b,
    )


def solution(mesh):
    rows = P(None, ("ctx", "shard"), None)
    vector = P("section", "shard")
    matrix = P("section", "shard", None)
    order = (
        vector,
        vector,
        matrix,
        vector,
        matrix,
        vector,
        vector,
        vector,
        matrix,
        vector,
        matrix,
        vector,
    )
    streams = P("section", None, ("ctx", "shard"), None)
    return jax.shard_map(
        functools.partial(on_device, mesh.shape["shard"]),
        mesh=mesh,
        in_specs=(rows, P(), rows) + order,
        out_specs=(streams, streams) + order,
        check_vma=False,
    )
```

```python
import functools

import jax
import jax.numpy as jnp
import numpy as np
from jax import lax
from jax.experimental import pallas as pl
from jax.experimental.pallas import tpu as pltpu
from jax.sharding import PartitionSpec as P

HEADS = 25
HD = 64
EPSILON = 1e-05
MASKED = -1e30
LOG2E = 1.4426950408889634
GELU_A = 0.7978845608028654
GELU_B = 0.044715
MESH = pl.DeviceIdType.MESH
F32 = jnp.float32
BF16 = jnp.bfloat16
VMEM_SPEC = pl.BlockSpec(memory_space=pltpu.VMEM)
ANY_SPEC = pl.BlockSpec(memory_space=pl.ANY)
DMA = pltpu.SemaphoreType.DMA
VMEM_LIMIT = 60 * 2**20
HALVES = 2


def params(collective_id=None):
    if collective_id is None:
        return pltpu.CompilerParams(vmem_limit_bytes=VMEM_LIMIT)
    return pltpu.CompilerParams(
        collective_id=collective_id, has_side_effects=True, vmem_limit_bytes=VMEM_LIMIT
    )


def remote(src, dst, send_sem, recv_sem, device):
    return pltpu.make_async_remote_copy(
        src_ref=src,
        dst_ref=dst,
        send_sem=send_sem,
        recv_sem=recv_sem,
        device_id=device,
        device_id_type=MESH,
    )


class Place:
    def __init__(self, n):
        self.s = lax.axis_index("section")
        self.c = lax.axis_index("ctx")
        self.h = lax.axis_index("shard")
        self.n = n
        self.zn = n // 2
        self.y = lax.rem(self.h, 2)
        self.z = lax.div(self.h, 2)
        self.far_y = self.y + self.c - 2 * self.y * self.c

    def flip(self, k):
        found = self.z
        for bit in range(self.zn.bit_length()):
            if k >> bit & 1:
                found = found + (1 - 2 * lax.rem(self.z // 2**bit, 2)) * 2**bit
        return found

    def dev(self, z, y):
        return (self.s, self.c, z * 2 + y)

    @property
    def pair(self):
        return self.dev(self.z, 1 - self.y)

    @property
    def above(self):
        return self.dev(self.z + 1, self.y)

    @property
    def below(self):
        return self.dev(self.z - 1, self.y)

    @property
    def over(self):
        return (1 - self.s, self.c, self.h)

    @property
    def sibling(self):
        return (self.s, 1 - self.c, self.h)


def greet(p, line=False, spread=False, over=False, sibling=False):
    bar = pltpu.get_barrier_semaphore()
    peers = 0

    def signal(device):
        pl.semaphore_signal(bar, inc=1, device_id=device, device_id_type=MESH)

    if line:
        signal(p.pair)

        @pl.when(p.z < p.zn - 1)
        def _():
            signal(p.above)

        @pl.when(p.z > 0)
        def _():
            signal(p.below)

        peers = 1 + (p.z + p.zn - 1) // p.zn + (2 * p.zn - 2 - p.z) // p.zn
    if spread:
        for dz in range(1, p.zn):
            signal(p.dev(lax.rem(p.z + dz, p.zn), p.far_y))

        @pl.when(p.c == 1)
        def _():
            signal(p.dev(p.z, p.far_y))

        peers = peers + p.zn - 1 + p.c
    if over:
        signal(p.over)
        peers = peers + 1
    if sibling:
        signal(p.sibling)
        peers = peers + 1
    pl.semaphore_wait(bar, peers)


class Gather:
    def __init__(self, p, own_ref, out_ref, ss, rs, ls):
        self.p, self.own_ref, self.out_ref = p, own_ref, out_ref
        self.ss, self.rs, self.ls = ss, rs, ls
        self.hr = own_ref.shape[0] // HALVES

    def blk(self, half, zz, yy):
        row = (half * self.p.n + zz * 2 + yy) * self.hr
        return self.out_ref.at[pl.ds(pl.multiple_of(row, 16), self.hr)]

    def own(self, half):
        return self.own_ref.at[pl.ds(half * self.hr, self.hr)]

    def up(self, t, half, src):
        p = self.p
        sems = (self.ss.at[0, t, half], self.rs.at[0, t, half])
        return remote(src, self.blk(half, p.z - (t - 1), p.y), *sems, p.above)

    def down(self, t, half, src):
        p = self.p
        sems = (self.ss.at[1, t, half], self.rs.at[1, t, half])
        return remote(src, self.blk(half, p.z + (t - 1), p.y), *sems, p.below)

    def across(self, kind, t, half, zz, src):
        p = self.p
        sems = (self.ss.at[2 + kind, t, half], self.rs.at[2 + kind, t, half])
        return remote(src, self.blk(half, zz, p.y), *sems, p.pair)

    def local(self, half):
        p = self.p
        return pltpu.make_async_copy(
            self.own(half), self.blk(half, p.z, p.y), self.ls.at[half]
        )

    def start(self, halves=range(HALVES)):
        p = self.p
        for half in halves:
            src = self.own(half)

            @pl.when(p.z < p.zn - 1)
            def _():
                self.up(1, half, src).start()

            @pl.when(p.z > 0)
            def _():
                self.down(1, half, src).start()

            self.across(0, 0, half, p.z, src).start()
            self.local(half).start()

    def step(self, t, half):
        p = self.p
        z, zn = p.z, p.zn

        @pl.when(z >= t)
        def _():
            block = self.blk(half, z - t, p.y)
            self.up(t, half, block).wait_recv()
            if t < zn - 1:

                @pl.when(z < zn - 1)
                def _():
                    self.up(t + 1, half, block).start()

            self.across(0, t, half, z - t, block).start()

        @pl.when(z <= zn - 1 - t)
        def _():
            block = self.blk(half, z + t, p.y)
            self.down(t, half, block).wait_recv()
            if t < zn - 1:

                @pl.when(z > 0)
                def _():
                    self.down(t + 1, half, block).start()

            self.across(1, t, half, z + t, block).start()

    def steps(self):
        return [
            functools.partial(self.step, t, half)
            for t in range(1, self.p.zn)
            for half in range(HALVES)
        ]

    def finish(self):
        p = self.p
        z, zn = p.z, p.zn
        for half in range(HALVES):
            self.across(0, 0, half, z, self.own(half)).wait_recv()
            for t in range(1, zn):

                @pl.when(z >= t)
                def _():
                    self.across(0, t, half, z - t, self.own(half)).wait_recv()

                @pl.when(z <= zn - 1 - t)
                def _():
                    self.across(1, t, half, z + t, self.own(half)).wait_recv()

        for half in range(HALVES):
            self.local(half).wait()
            self.across(0, 0, half, z, self.own(half)).wait_send()
            for t in range(1, zn):

                @pl.when((z < zn - 1) & (z >= t - 1))
                def _():
                    self.up(t, half, self.own(half)).wait_send()

                @pl.when((z > 0) & (z <= zn - t))
                def _():
                    self.down(t, half, self.own(half)).wait_send()

                @pl.when(z >= t)
                def _():
                    self.across(0, t, half, z - t, self.own(half)).wait_send()

                @pl.when(z <= zn - 1 - t)
                def _():
                    self.across(1, t, half, z + t, self.own(half)).wait_send()


class Scatter:
    def __init__(self, p, part_ref, ybuf, rbuf, sbuf, ss, rs):
        self.p, self.part_ref = p, part_ref
        self.ybuf, self.rbuf, self.sbuf, self.ss, self.rs = ybuf, rbuf, sbuf, ss, rs
        self.hr = ybuf.shape[2]

    def blk(self, half, zz, yy):
        row = (half * self.p.n + zz * 2 + yy) * self.hr
        return self.part_ref.at[pl.ds(pl.multiple_of(row, 16), self.hr)]

    def goal(self, k, t):
        return self.p.z + t if k == 0 else self.p.z - t

    def across(self, k, t, half):
        p = self.p
        zz = self.goal(k, t)
        sems = (self.ss.at[k, t, half], self.rs.at[k, t, half])
        return remote(self.blk(half, zz, 1 - p.y), self.ybuf.at[zz, half], *sems, p.pair)

    def along(self, k, t, half, slot):
        p = self.p
        zz = self.goal(k, t)
        sems = (self.ss.at[2 + k, t, half], self.rs.at[2 + k, slot, half])
        target = p.above if k == 0 else p.below
        return remote(self.sbuf.at[zz, half], self.rbuf.at[zz + 1 - k, half], *sems, target)

    def ok(self, k, t):
        return self.p.z <= self.p.zn - 1 - t if k == 0 else self.p.z >= t

    def has(self, k):
        return self.p.z > 0 if k == 0 else self.p.z < self.p.zn - 1

    def start(self):
        for t in range(self.p.zn - 1, 0, -1):
            for half in range(HALVES):
                for k in range(2):

                    @pl.when(self.ok(k, t))
                    def _():
                        self.across(k, t, half).start()

        for half in range(HALVES):
            self.across(0, 0, half).start()

    def step(self, t, half, k):
        p = self.p
        zz = self.goal(k, t)

        @pl.when(self.ok(k, t))
        def _():
            self.across(k, t, half).wait_recv()
            total = self.blk(half, zz, p.y)[...].astype(F32)
            total = total + self.ybuf[zz, half].astype(F32)
            if t < p.zn - 1:

                @pl.when(self.has(k))
                def _():
                    self.along(k, t, half, t).wait_recv()
                    more = total + self.rbuf[zz + 1 - k, half].astype(F32)
                    self.sbuf[zz, half] = more.astype(BF16)

                @pl.when(jnp.logical_not(self.has(k)))
                def _():
                    self.sbuf[zz, half] = total.astype(BF16)

            else:
                self.sbuf[zz, half] = total.astype(BF16)
            self.along(k, t, half, t - 1).start()

    def steps(self):
        return [
            functools.partial(self.step, t, half, k)
            for t in range(self.p.zn - 1, 0, -1)
            for half in range(HALVES)
            for k in range(2)
        ]

    def result(self, half):
        p = self.p
        z = p.z
        self.across(0, 0, half).wait_recv()
        for k in range(2):

            @pl.when(self.has(k))
            def _():
                self.along(k, 0, half, 0).wait_recv()

            @pl.when(jnp.logical_not(self.has(k)))
            def _():
                self.rbuf[z + 1 - k, half] = jnp.zeros(self.rbuf.shape[2:], BF16)

        total = self.blk(half, z, p.y)[...].astype(F32) + self.ybuf[z, half].astype(F32)
        return total + self.rbuf[z + 1, half].astype(F32) + self.rbuf[z, half].astype(F32)

    def finish(self):
        for half in range(HALVES):
            self.across(0, 0, half).wait_send()
            for t in range(1, self.p.zn):
                for k in range(2):

                    @pl.when(self.ok(k, t))
                    def _():
                        self.across(k, t, half).wait_send()
                        self.along(k, t, half, t - 1).wait_send()


class Spread:
    def __init__(self, p, src, dst, ss, rs, ls):
        self.p, self.src, self.dst, self.ss, self.rs, self.ls = p, src, dst, ss, rs, ls

    def source(self, dz):
        return self.p.flip(dz) * 2 + self.p.far_y

    def out(self, dz):
        p = self.p
        target = self.source(dz)
        sems = (self.ss.at[0, dz], self.rs.at[0, dz])
        return remote(self.src.at[target], self.dst.at[p.s, p.h], *sems, (p.s, p.c, target))

    def aside(self, dz):
        block = self.dst.at[self.p.s, self.source(dz)]
        return remote(block, block, self.ss.at[1, dz], self.rs.at[1, dz], self.p.sibling)

    def cross(self, dz):
        block = self.dst.at[self.p.s, self.source(dz)]
        return remote(block, block, self.ss.at[2, dz], self.rs.at[2, dz], self.p.over)

    def cross_own(self):
        p = self.p
        sems = (self.ss.at[2, 0], self.rs.at[2, 0])
        return remote(self.src.at[p.h], self.dst.at[p.s, p.h], *sems, p.over)

    def cross_aside(self, dz):
        block = self.dst.at[1 - self.p.s, self.source(dz)]
        return remote(block, block, self.ss.at[3, dz], self.rs.at[3, dz], self.p.sibling)

    def local(self):
        p = self.p
        return pltpu.make_async_copy(self.src.at[p.h], self.dst.at[p.s, p.h], self.ls)

    def start(self):
        @pl.when(self.p.c == 1)
        def _():
            self.out(0).start()

        @pl.when(self.p.c == 0)
        def _():
            self.cross_own().start()

        for dz in range(1, min(3, self.p.zn)):
            self.out(dz).start()
        self.local().start()

    def arrived(self, dz):
        if 3 <= dz + 2 < self.p.zn:
            self.out(dz + 1).wait_send()
            self.out(dz + 2).start()
        self.out(dz).wait_recv()
        self.cross(dz).start()
        self.aside(dz).start()

    def crossed(self, dz):
        self.cross(dz).wait_recv()
        self.cross_aside(dz).start()

    def first(self):
        @pl.when(self.p.c == 1)
        def _():
            self.arrived(0)

    def steps(self):
        found = [self.first]
        found += [functools.partial(self.arrived, dz) for dz in range(1, self.p.zn)]
        return found + [functools.partial(self.crossed, dz) for dz in range(self.p.zn)]

    def finish(self):
        self.local().wait()

        @pl.when(self.p.c == 0)
        def _():
            self.aside(0).wait_recv()
            self.cross_own().wait_send()

        @pl.when(self.p.c == 1)
        def _():
            self.out(0).wait_send()
            self.aside(0).wait_send()
            self.cross(0).wait_send()

        for dz in range(self.p.zn):
            if dz:
                self.aside(dz).wait_recv()
                self.aside(dz).wait_send()
                if dz == 1 or dz == self.p.zn - 1:
                    self.out(dz).wait_send()
                self.cross(dz).wait_send()
            self.cross_aside(dz).wait_recv()
            self.cross_aside(dz).wait_send()


class RowSwap:
    def __init__(self, p, src, dst, ss, rs, ls):
        self.p, self.src, self.dst, self.ss, self.rs, self.ls = p, src, dst, ss, rs, ls
        self.split = src.shape[0] % 32 == 0

    def piece(self, which):
        count = self.src.shape[0]
        if not self.split:
            return self.src, self.dst.at[which, pl.ds(0, count)]
        half = count // 2
        rows = pl.ds(pl.multiple_of(self.p.c * half, 16), half)
        return self.src.at[rows], self.dst.at[which, rows]

    def cross(self):
        src, dst = self.piece(self.p.s)
        return remote(src, dst, self.ss.at[0], self.rs.at[0], self.p.over)

    def aside(self):
        block = self.piece(1 - self.p.s)[1]
        return remote(block, block, self.ss.at[1], self.rs.at[1], self.p.sibling)

    def local(self):
        rows = pl.ds(0, self.src.shape[0])
        return pltpu.make_async_copy(self.src, self.dst.at[self.p.s, rows], self.ls)

    def start(self):
        self.cross().start()
        self.local().start()

    def step(self):
        self.cross().wait_recv()
        if self.split:
            self.aside().start()

    def finish(self):
        self.local().wait()
        self.cross().wait_send()
        if self.split:
            self.aside().wait_recv()
            self.aside().wait_send()


class Cross:
    def __init__(self, p, src, dst, ss, rs, source):
        self.p, self.source = p, source
        self.copy = remote(src, dst, ss, rs, p.over)

    def start(self):
        @pl.when(self.p.s == self.source)
        def _():
            self.copy.start()

    def finish(self):
        @pl.when(self.p.s == self.source)
        def _():
            self.copy.wait_send()

        @pl.when(self.p.s != self.source)
        def _():
            self.copy.wait_recv()


class Home:
    def __init__(self, p, src, dst, ss, rs, ls):
        self.p, self.src, self.dst, self.ss, self.rs, self.ls = p, src, dst, ss, rs, ls

    def send(self, k):
        p = self.p
        far = p.flip(k)
        target = (p.s, p.c, far * 2 + p.far_y)
        sems = (self.ss.at[0, k], self.rs.at[0, k])
        return remote(self.src.at[far], self.dst.at[p.h], *sems, target)

    def keep(self):
        return pltpu.make_async_copy(self.src.at[self.p.z], self.dst.at[self.p.h], self.ls)

    def aside(self, k):
        block = self.dst.at[self.p.flip(k) * 2 + self.p.far_y]
        return remote(block, block, self.ss.at[1, k], self.rs.at[1, k], self.p.sibling)

    def start(self, k):
        if k:
            self.send(k).start()
            return

        @pl.when(self.p.c == 1)
        def _():
            self.send(0).start()

        @pl.when(self.p.c == 0)
        def _():
            self.keep().start()

    def arrived(self, k):
        if k:
            self.send(k).wait_recv()
        else:

            @pl.when(self.p.c == 1)
            def _():
                self.send(0).wait_recv()

            @pl.when(self.p.c == 0)
            def _():
                self.keep().wait()

        self.aside(k).start()

    def steps(self):
        return [functools.partial(self.arrived, k) for k in range(self.p.zn)]

    def finish(self):
        @pl.when(self.p.c == 1)
        def _():
            self.send(0).wait_send()

        for k in range(self.p.zn):
            if k:
                self.send(k).wait_send()
            self.aside(k).wait_recv()
            self.aside(k).wait_send()


def add_home(p, to, index, first, first_came, second, second_came):
    pairs = ((first, first_came), (second, second_came))
    for section, (own, came) in enumerate(pairs):

        @pl.when(p.s == section)
        def _():
            to[index] = (own[index].astype(F32) + came[index].astype(F32)).astype(BF16)


class Fold:
    def __init__(self, p, src, came, out, ss, rs):
        self.p, self.src, self.came, self.out, self.ss, self.rs = p, src, came, out, ss, rs
        self.count = out.shape[0]
        self.size = out.shape[1]

    def rows(self, item, near):
        p = self.p
        if self.count == 1:
            index = 1 - p.c if near else p.c
        else:
            index = item * 2 + (1 - p.far_y if near else p.far_y)
        return pl.ds(pl.multiple_of(index * self.size, 16), self.size)

    def copy(self, item):
        src = self.src.at[self.rows(item, True)]
        sems = (self.ss.at[item], self.rs.at[item])
        return remote(src, self.came.at[item], *sems, self.p.sibling)

    def start(self):
        for item in range(self.count):
            self.copy(item).start()

    def step(self, item):
        self.copy(item).wait_recv()
        own = self.src[self.rows(item, False)].astype(F32)
        self.out[item] = (own + self.came[item].astype(F32)).astype(BF16)

    def steps(self):
        return [functools.partial(self.step, item) for item in range(self.count)]

    def finish(self):
        for item in range(self.count):
            self.copy(item).wait_send()


def fold_scratch(source, out):
    return [pltpu.VMEM(source, BF16), pltpu.VMEM(out, BF16), DMA((out[0],)), DMA((out[0],))]


def product(a_ref, b_ref, to_ref):
    rows = to_ref.shape[0]

    def step(first, size):
        found = lax.dot_general(
            a_ref[:, first : first + size],
            b_ref[...],
            (((0,), (0,)), ((), ())),
            preferred_element_type=F32,
        )
        to_ref[first : first + size] = found.astype(BF16)

    return [
        functools.partial(step, first, min(256, rows - first)) for first in range(0, rows, 256)
    ]


def home_rows(a_ref, b_ref, to_ref, low, share):
    found = lax.dot_general(
        a_ref[...], b_ref[...], (((0,), (0,)), ((), ())), preferred_element_type=F32
    )
    h = lax.axis_index("shard")
    shift = 0
    for j, first in enumerate(low):
        shift = shift + jnp.where(h == j, (HD * first - j * share) % found.shape[0], 0)
    to_ref[...] = pltpu.roll(found, shift, 0).astype(BF16)


def in_turn(steps, work, each=1):
    for step in steps:
        for _ in range(each):
            run_next(work)
        step()


def by_halves(scatter, gather, rows_step, work, each=1):
    in_turn(scatter.steps(), work, each)
    for half in range(HALVES):
        rows_step(half)
        if gather is not None:
            gather.start([half])
    if gather is not None:
        in_turn(gather.steps(), work, each)


def fetch(src, dst, sem):
    copy = pltpu.make_async_copy(src, dst, sem)
    copy.start()
    return copy


class Staging:
    greeted, extra = False, {}

    def __init__(self):
        self.loads, self.stores, self.running = {}, {}, []

    def need(self, *items):
        for item in items:
            self.loads.pop(item).wait()

    def done(self, *items):
        for item in items:
            self.running.append(fetch(*self.stores.pop(item)))

    def end(self):
        self.done(*list(self.stores))
        for copy in self.running:
            copy.wait()


def staged_call(
    body,
    name,
    collective_id,
    args,
    shapes,
    scratch,
    late=(),
    plain=(),
    early=(),
    raw=(),
    layers={},
    scalars=(),
):
    late, early = tuple(late), tuple(early)
    n_in, n_out, n_scratch = len(args), len(shapes), len(scratch)

    def run(*refs):
        ins, outs = list(refs[:n_in]), list(refs[n_in : n_in + n_out])
        rest = refs[n_in + n_out :]
        own, rest = rest[:n_scratch], rest[n_scratch:]
        staged_in, rest = rest[: len(late)], rest[len(late) :]
        staged_out, sems = rest[: len(early)], rest[len(early) :]
        io = Staging()
        for x, item in enumerate(late):
            src = ins[item].at[layers[item]] if item in layers else ins[item]
            io.loads[item] = fetch(src, staged_in[x], sems[0].at[x])
            ins[item] = staged_in[x]
        for x, item in enumerate(early):
            io.stores[item] = (staged_out[x], outs[item], sems[1].at[x])
            outs[item] = staged_out[x]
        body(io, *ins, *outs, *own)
        io.end()

    def place(i):
        if i in scalars:
            return pl.BlockSpec(memory_space=pltpu.SMEM)
        return ANY_SPEC if i in late + tuple(plain) else VMEM_SPEC

    stages = [
        pltpu.VMEM(args[item].shape[1 if item in layers else 0 :], args[item].dtype) for item in late
    ]
    stages += [pltpu.VMEM(shapes[item].shape, shapes[item].dtype) for item in early]
    stages += [DMA((max(len(late), 1),)), DMA((max(len(early), 1),))]
    return pl.pallas_call(
        run,
        out_shape=shapes,
        in_specs=[place(i) for i in range(n_in)],
        out_specs=[ANY_SPEC if i in early + tuple(raw) else VMEM_SPEC for i in range(n_out)],
        scratch_shapes=list(scratch) + stages,
        compiler_params=params(collective_id),
        name=name,
    )(*args)


class Mapped:
    def __init__(self, io, loads, stores, greeted=True, extra={}):
        self.io, self.loads, self.stores = io, loads, stores
        self.greeted, self.extra = greeted, extra

    def need(self, *items):
        for item in items:
            if self.loads.get(item) in self.io.loads:
                self.io.need(self.loads[item])

    def done(self, *items):
        for item in items:
            if self.stores.get(item) in self.io.stores:
                self.io.done(self.stores[item])


class Result:
    def __init__(self, step, index):
        self.step, self.index = step, index
        self.shape, self.dtype = step.shapes[index].shape, step.shapes[index].dtype


class Step:
    def __init__(self, body, name, collective_id, args, shapes, scratch, greets, **staging):
        self.body, self.name, self.collective_id = body, name, collective_id
        self.args, self.shapes, self.scratch, self.greets = tuple(args), shapes, scratch, greets
        self.late = tuple(staging.get("late", ()))
        self.plain = tuple(staging.get("plain", ()))
        self.early = tuple(staging.get("early", ()))
        self.raw = tuple(staging.get("raw", ()))
        self.layers = staging.get("layers", {})


def run_steps(steps):
    args, arg_of, out_of, first_out = [], {}, {}, []
    shapes, scratch, early, raw = [], [], [], []
    linked = {
        (id(arg.step), arg.index) for step in steps for arg in step.args if isinstance(arg, Result)
    }
    for k, step in enumerate(steps):
        for i, arg in enumerate(step.args):
            if isinstance(arg, Result):
                continue
            spots = [x for x, known in enumerate(args) if known is arg]
            if not spots:
                args.append(arg)
                spots = [len(args) - 1]
            arg_of[k, i] = spots[0]
        first_out.append(len(shapes))
        for o, shape in enumerate(step.shapes):
            out_of[k, o] = len(shapes)
            keep = (id(step), o) in linked
            if o in step.early or (o in step.raw and keep):
                early.append(len(shapes))
            elif o in step.raw:
                raw.append(len(shapes))
            shapes.append(shape)
        scratch += step.scratch
    direct = {
        arg_of[k, i]
        for k, step in enumerate(steps)
        for i in range(len(step.args))
        if (k, i) in arg_of and i not in step.late and i not in step.plain
    }
    late, layers = [], {}
    for k, step in enumerate(steps):
        for i in step.late:
            spot = arg_of.get((k, i))
            if spot is not None and spot not in direct and spot not in late:
                late.append(spot)
                if i in step.layers:
                    layers[spot] = step.layers[i]
    plain = [x for x in range(len(args)) if x not in direct and x not in late]
    extra = {}
    for step in steps:
        extra.update(step.greets)

    def body(io, *refs):
        ins, outs = refs[: len(args)], refs[len(args) : len(args) + len(shapes)]
        rest = refs[len(args) + len(shapes) :]
        for k, step in enumerate(steps):
            mine = []
            for i, arg in enumerate(step.args):
                if isinstance(arg, Result):
                    mine.append(outs[out_of[steps.index(arg.step), arg.index]])
                else:
                    mine.append(ins[arg_of[k, i]])
            loads = {i: arg_of[k, i] for i in range(len(step.args)) if (k, i) in arg_of}
            stores = {o: out_of[k, o] for o in range(len(step.shapes))}
            own = outs[first_out[k] : first_out[k] + len(step.shapes)]
            count = len(step.scratch)
            part = Mapped(io, loads, stores, k > 0, extra)
            step.body(part, *mine, *own, *rest[:count])
            part.done(*stores)
            rest = rest[count:]

    found = staged_call(
        body,
        "_".join(step.name for step in steps),
        steps[0].collective_id,
        args,
        shapes,
        scratch,
        late=late,
        plain=plain,
        early=early,
        raw=raw,
        layers=layers,
    )
    return [
        found[first : first + len(step.shapes)] for first, step in zip(first_out, steps)
    ]


def follow(merge, first, *makers):
    if merge:
        steps, results = [first], [[Result(first, i) for i in range(len(first.shapes))]]
        for make in makers:
            step = make(*results)
            steps.append(step)
            results.append([Result(step, i) for i in range(len(step.shapes))])
        return run_steps(steps)
    found = run_steps([first])
    for make in makers:
        found += run_steps([make(*found)])
    return found


def row_blocks(rows, step):
    size = min(rows, 256)
    count = rows // size
    if count <= 2:
        for b in range(count):
            step(b * size, size)
    else:

        def body(b, carry):
            step(pl.multiple_of(b * size, size), size)
            return carry

        lax.fori_loop(0, count, body, 0)


def enter(io, p, **greets):
    if not io.greeted:
        greets.update(io.extra)
        greet(p, **greets)


def gelu_parts(values):
    square = values * values
    return jnp.tanh(GELU_A * (values + GELU_B * values * square)), square


def greet_all(p):
    bar = pltpu.get_barrier_semaphore()
    for a in range(2):
        for b in range(p.n):
            if (a, b) != (0, 0):
                other = (lax.rem(p.s + a, 2), p.c, lax.rem(p.h + b, p.n))
                pl.semaphore_signal(bar, inc=1, device_id=other, device_id_type=MESH)
    pl.semaphore_signal(bar, inc=1, device_id=p.sibling, device_id_type=MESH)
    pl.semaphore_wait(bar, 2 * p.n)


def others(n):
    return [(a, b) for a in range(2) for b in range(n) if (a, b) != (0, 0)]


def with_gaps(values, n, padded):
    rows, width = values.shape
    share = width // n
    pieces = []
    for j in range(n):
        pieces.append(values[:, j * share : (j + 1) * share])
        if padded > share:
            pieces.append(jnp.zeros((rows, padded - share), values.dtype))
    return jnp.concatenate(pieces, axis=1)


def lay_vectors(vectors, pack_to):
    lanes = pack_to.shape[1]
    members = []
    for ref in vectors:
        member = ref[...].astype(F32)
        members.append(
            jnp.concatenate([member, jnp.zeros((1, lanes - member.shape[1]), F32)], axis=1)
        )
    members.append(jnp.zeros((8, lanes), F32))
    pack_to[...] = jnp.concatenate(members, axis=0).astype(BF16)


def lay_first(low, qkv_ref, qkv_to):
    n, padded, triple = qkv_to.shape
    share = qkv_ref.shape[0]
    width = qkv_ref.shape[1] // 3
    sh = triple // 3
    for j in range(n):
        for t in range(3):
            first = t * width + HD * low[j]
            qkv_to[j, :share, t * sh : (t + 1) * sh] = qkv_ref[:, first : first + sh]
        if padded > share:
            qkv_to[j, share:] = jnp.zeros((padded - share, triple), BF16)


def lay_rows(low, out_ref, out_to):
    share = out_ref.shape[0]
    sh, full = out_to.shape
    n = len(low)
    h = lax.axis_index("shard")
    offset = 0
    for j in range(n):
        offset = offset + jnp.where(h == j, j * share - HD * low[j], 0)
    rows = with_gaps(out_ref[...].astype(F32), n, full // n)
    rows = jnp.concatenate([rows, jnp.zeros((sh - share, full), F32)], axis=0)
    out_to[...] = pltpu.roll(rows, offset, 0).astype(BF16)


def lay_widen(j, widen_ref, widen_to):
    n, padded, hide_full = widen_to.shape
    share, hidden = widen_ref.shape
    hide = hidden // n
    widen_to[j, :share, :hide] = widen_ref[:, j * hide : (j + 1) * hide]
    if hide_full > hide:
        widen_to[j, :share, hide:] = jnp.zeros((share, hide_full - hide), BF16)
    if padded > share:
        widen_to[j, share:] = jnp.zeros((padded - share, hide_full), BF16)


def lay_narrow(first, size, n, narrow_ref, narrow_to):
    rows = slice(first, first + size)
    narrow_to[rows] = with_gaps(narrow_ref[rows], n, narrow_to.shape[1] // n)


def spread_vectors(n, low, width, pack_all, feats_to, qkv_bias, widen_bias):
    h = lax.axis_index("shard")
    sh = qkv_bias.shape[2] // 3
    share = width // n
    padded = feats_to.shape[2] // n
    for layer in range(2):
        pieces = [pack_all[layer, j] for j in range(n)]
        feats_to[layer] = jnp.concatenate([m[:, :padded] for m in pieces], axis=1).astype(F32)
        bias = jnp.concatenate([m[6:7, : 2 * share] for m in pieces], axis=1).astype(F32)
        found = jnp.zeros((1, 2 * sh), F32)
        wide = jnp.zeros((1, widen_bias.shape[2]), F32)
        for j in range(n):
            first = HD * low[j]
            spots = [bias[:, k * width + first : k * width + first + sh] for k in range(2)]
            found = jnp.where(h == j, jnp.concatenate(spots, axis=1), found)
            own = pieces[j][7:8, : wide.shape[1]].astype(F32)
            wide = jnp.where(h == j, own, wide)
        qkv_bias[layer] = jnp.concatenate(
            [found[:, :sh], jnp.zeros((1, sh), F32), found[:, sh:]], axis=1
        )
        widen_bias[layer] = wide


def feed_forward(low_all, widen, narrow, widen_bias, pre_to, hidden_to, part_to):
    def block(first, size):
        rows = pl.ds(first, size)
        weight = widen[...].reshape(low_all.shape[1], widen.shape[2])
        pre = dot_n(low_all[rows], weight) + widen_bias
        pre_to[rows] = pre
        hidden = (0.5 * pre * (1.0 + gelu_parts(pre)[0])).astype(BF16)
        hidden_to[rows] = hidden
        part_to[rows] = dot_n(hidden, narrow[...]).astype(BF16)

    row_blocks(low_all.shape[0], block)


def open_kernel(n, low, width, slots, step, io, *refs):
    tok_ref, cot_ref, vectors, refs = refs[0], refs[1], refs[2:10], refs[10:]
    qkv_ref, out_ref, widen_ref, narrow_ref, mask, order_ref = refs[:6]
    refs = refs[6:]
    x_to, cot_to, grad_to, sums_to, normed_to, own_ref, qkv_all, out_all = refs[:8]
    feats_to, qkv_bias, widen_bias, att_ref, low_ref, lse_ref, oth_ref, widen_all = refs[8:16]
    value_to, tok_all, pre_to, hidden_to, part_to, narrow_all, kpos_ref, qpos_ref = refs[16:24]
    refs = refs[24:]
    tok_own, pack, qkv_send, out_rows, widen_raw, narrow_raw, widen_send, narrow_to = refs[:8]
    pack_all, widen, refs = refs[8], refs[9], refs[10:]
    g_ss, g_rs, g_ls, p_ss, p_rs, a_ss, a_rs, w_ss, w_rs, o_ss, o_rs, l_sem = refs[:12]
    kv_ss, kv_rs, n_ss, n_rs, refs = refs[12], refs[13], refs[14], refs[15], refs[16:]
    scatter_refs, (second_ss, second_rs, second_ls) = refs[:5], refs[5:]
    p = Place(n)
    s, c, h = p.s, p.c, p.h
    widen_load = fetch(widen_ref, widen_raw, l_sem.at[4])
    narrow_load = fetch(narrow_ref, narrow_raw, l_sem.at[5])
    padded = qkv_send.shape[1]
    tok_own[...] = with_gaps(tok_ref[s], n, padded)
    greet_all(p)

    def pack_copy(a, b):
        target = (lax.rem(s + a, 2), c, lax.rem(h + b, n))
        return remote(pack, pack_all.at[s, h], p_ss.at[a, b], p_rs.at[a, b], target)

    tokens = Gather(p, tok_own, tok_all, g_ss, g_rs, g_ls)
    qkv = Spread(p, qkv_send, qkv_all, a_ss, a_rs, l_sem.at[1])
    wide = Spread(p, widen_send, widen_all, w_ss, w_rs, l_sem.at[3])
    narrow = RowSwap(p, narrow_to, narrow_all, n_ss, n_rs, l_sem.at[6])
    out = RowSwap(p, out_rows, out_all, o_ss, o_rs, l_sem.at[2])
    pack_own = pltpu.make_async_copy(pack, pack_all.at[s, h], l_sem.at[0])
    tokens.start()
    io.need(10)
    lay_first(low, qkv_ref, qkv_send)
    qkv.start()
    lay_vectors(vectors, pack)
    for a, b in others(n):
        pack_copy(a, b).start()
    pack_own.start()

    def start_out():
        io.need(1, 11)
        lay_rows(low, out_ref, out_rows)
        out.start()

    def lay_places():
        size = tok_own.shape[0] // HALVES
        down = lax.broadcasted_iota(jnp.int32, (size, 1), 0)
        along = lax.broadcasted_iota(jnp.int32, (1, size), 1)
        found = []
        for part in range(2):
            core = 1 - c if part else c
            for half in range(HALVES):
                for j in range(n):
                    first = order_ref[core * n + j, half] * size
                    spot = ((part * HALVES + half) * n + j) * size
                    kpos_ref[spot : spot + size] = first + down
                    if not part:
                        found.append(first + along)
        qpos_ref[...] = jnp.concatenate(found, axis=1)

    def lay_cot():
        values = with_gaps(cot_ref[s], n, padded)
        cot_to[...] = values
        grad_to[...] = values.astype(F32)
        sums_to[...] = jnp.sum(grad_to[...], axis=0, keepdims=True)
        x_to[...] = tok_own[...].astype(F32)

    hide = narrow_ref.shape[0]
    work = [start_out, lay_places, widen_load.wait]
    work += [functools.partial(lay_widen, j, widen_raw, widen_send) for j in range(n)]
    work += [lay_cot, narrow_load.wait]
    work += [
        functools.partial(lay_narrow, first, min(208, hide - first), n, narrow_raw, narrow_to)
        for first in range(0, hide, 208)
    ]
    qkv_steps = qkv.steps()
    for token_step in tokens.steps():
        run_next(work)
        run_next(work)
        token_step()
        run_next(qkv_steps)
    for rest in work:
        rest()
    extra = narrow_to.shape[0] - hide
    if extra:
        narrow_to[hide:] = jnp.zeros((extra, n * padded), BF16)
    for member in range(2):
        if narrow_all.shape[1] > narrow_to.shape[0]:
            spare = (narrow_all.shape[1] - narrow_to.shape[0], n * padded)
            narrow_all[member, narrow_to.shape[0] :] = jnp.zeros(spare, BF16)
    tokens.finish()
    wide.start()
    pack_own.wait()
    for a, b in others(n):
        pack_copy(a, b).wait_recv()
    spread_vectors(n, low, width, pack_all, feats_to, qkv_bias, widen_bias)

    normed = part_to

    def first_norm(first, size):
        some = pl.ds(first, size)
        unit = unit_rows(tok_all[some].astype(F32), mask[...], width)[0]
        normed[some] = (unit * feats_to[0, 0:1] + feats_to[0, 1:2]).astype(BF16)

    rows = tok_all.shape[0]
    row_blocks(rows, first_norm)
    normed_store = fetch(normed, normed_to, l_sem.at[7])
    for rest in qkv_steps:
        rest()
    qkv.finish()
    narrow.start()
    io.done(6)
    sh = slots * HD

    def project(first, size):
        some = pl.ds(first, size)
        weight = qkv_all[0].reshape(n * padded, 3 * sh)
        own_ref[some] = (dot_n(normed[some], weight) + qkv_bias[0]).astype(BF16)

    row_blocks(rows, project)
    swap = remote(own_ref.at[:, pl.ds(sh, 2 * sh)], oth_ref, kv_ss, kv_rs, p.sibling)
    swap.start()
    swap.wait_recv()
    out.step()
    wide_steps = wide.steps()
    chunk = attention(slots, step, own_ref, oth_ref, kpos_ref, qpos_ref, att_ref, low_ref, lse_ref)
    in_blocks(rows, step, chunk, [])
    out.finish()
    io.done(5, 7, 11, 12, 14)
    normed_store.wait()

    def give(first, size):
        some = pl.ds(first, size)
        part_to[some] = dot_n(low_ref[some], out_all[0]).astype(BF16)

    row_blocks(rows, give)

    scatter = Scatter(p, part_to, *scatter_refs)
    scatter.start()
    arrivals, crossings = wide_steps[: p.zn], wide_steps[p.zn :]
    early = len(arrivals) // 2
    for arrive in arrivals[:early]:
        arrive()
    second = Gather(p, tok_own, tok_all, second_ss, second_rs, second_ls)
    hr = tok_own.shape[0] // HALVES

    def rows_step(half):
        some = slice(half * hr, (half + 1) * hr)
        value = x_to[some] + (scatter.result(half) + feats_to[0, 2:3])
        value_to[some] = value
        unit = unit_rows(value, mask[...], width)[0]
        tok_own[some] = (unit * feats_to[0, 3:4] + feats_to[0, 4:5]).astype(BF16)

    by_halves(scatter, None, lambda half: None, [])
    for arrive in arrivals[early:]:
        arrive()
    for half in range(HALVES):
        rows_step(half)
        second.start([half])
    for second_step in second.steps():
        second_step()
    narrow.step()
    for crossing in crossings:
        crossing()
    second.finish()
    scatter.finish()
    for a, b in others(n):
        pack_copy(a, b).wait_send()
    swap.wait_send()
    narrow.finish()
    wide.finish()
    load = fetch(widen_all.at[0], widen, l_sem.at[4])
    io.done(17, 21)
    load.wait()
    feed_forward(tok_all, widen, narrow_all.at[0], widen_bias[0], pre_to, hidden_to, part_to)


def open_call(n, low, slots, padded, tokens, cotangent, vectors, weights, mask, order):
    qkv, out, widen, narrow = weights
    share, hidden = widen.shape
    width = n * share
    hide = hidden // n
    hide_full = -(-hide // 128) * 128
    sh = slots * HD
    full = n * padded
    rows = tokens.shape[1]
    total = n * rows
    zn = n // 2
    lanes = max(hide_full, -(-2 * share // 128) * 128)
    blocks = (n, padded, 3 * sh)
    wide = (n, padded, hide_full)

    def low_type(*shape):
        return jax.ShapeDtypeStruct(shape, BF16)

    def full_type(*shape):
        return jax.ShapeDtypeStruct(shape, F32)

    return staged_call(
        functools.partial(open_kernel, n, low, width, slots, min(total, 256)),
        "open",
        0,
        (tokens, cotangent, *vectors, qkv, out, widen, narrow, mask, order),
        [
            full_type(rows, full),
            low_type(rows, full),
            full_type(rows, full),
            full_type(1, full),
            low_type(total, full),
            low_type(total, 3 * sh),
            low_type(2, *blocks),
            low_type(2, sh, full),
            full_type(2, 16, full),
            full_type(2, 1, 3 * sh),
            full_type(2, 1, hide_full),
            full_type(sh, total),
            low_type(total, sh),
            full_type(slots, total),
            low_type(total, 2 * sh),
            low_type(2, *wide),
            full_type(rows, full),
            low_type(total, full),
            full_type(total, hide_full),
            low_type(total, hide_full),
            low_type(total, full),
            low_type(2, hide_full, full),
            jax.ShapeDtypeStruct((2 * total, 1), jnp.int32),
            jax.ShapeDtypeStruct((1, total), jnp.int32),
        ],
        [
            pltpu.VMEM((rows, full), BF16),
            pltpu.VMEM((16, lanes), BF16),
            pltpu.VMEM(blocks, BF16),
            pltpu.VMEM((sh, full), BF16),
            pltpu.VMEM(widen.shape, BF16),
            pltpu.VMEM(narrow.shape, BF16),
            pltpu.VMEM(wide, BF16),
            pltpu.VMEM((-(-hide // 16) * 16, full), BF16),
            pltpu.VMEM((2, n, 16, lanes), BF16),
            pltpu.VMEM(wide, BF16),
        ]
        + gather_scratch(n)
        + [DMA((2, n))] * 2
        + [DMA((4, zn))] * 4
        + [DMA((2,))] * 2
        + [DMA((8,)), DMA, DMA, DMA((2,)), DMA((2,))]
        + scatter_scratch(n, rows, full)
        + gather_scratch(n),
        late=(1, 10, 11),
        plain=(12, 13),
        early=(5, 6, 7, 11, 12, 14, 17, 18, 19, 20, 21),
        raw=(4, 15),
        scalars=(15,),
    )


def settle_kernel(low, sizes, *refs):
    sources, vec_ref, came_ref, streams, refs = refs[:4], refs[4], refs[5], refs[6:10], refs[10:]
    outs, stream_to, vectors, refs = refs[:4], refs[4:6], refs[6:14], refs[14:]
    loaded, made, came, in_sem, out_sem = refs[:4], refs[4:8], refs[8], refs[9], refs[10]
    qkv_ref, widen_ref, out_ref, narrow_ref = loaded
    qkv_to, widen_to, out_to, narrow_to = made
    order = (3, 1, 0, 2)
    loads = {i: fetch(sources[i], loaded[i], in_sem.at[i]) for i in order}
    came_load = fetch(came_ref, came, in_sem.at[4])
    n, padded, _ = widen_ref.shape
    share = out_to.shape[0]
    hide = narrow_to.shape[0]
    width = qkv_to.shape[1] // 3
    sh = qkv_ref.shape[2] // 3
    s = lax.axis_index("section")

    def without_gaps(values):
        pieces = [values[:, j * padded : j * padded + share] for j in range(n)]
        return jnp.concatenate(pieces, axis=1)

    def lay_rows_back(ref, to, rows):
        to[rows] = without_gaps(ref[rows]).astype(F32)

    def lay_qkv_back(rows):
        qkv_to[rows] = jnp.zeros((rows.stop - rows.start, 3 * width), F32)
        for j in range(n):
            for t in range(3):
                first = t * width + HD * low[j]
                block = qkv_ref[j, rows, t * sh : (t + 1) * sh]
                qkv_to[rows, first : first + sh] += block.astype(F32)

    def lay_widen_back(rows):
        pieces = [widen_ref[j, rows, :hide] for j in range(n)]
        widen_to[rows] = jnp.concatenate(pieces, axis=1).astype(F32)

    makers = (
        lay_qkv_back,
        lay_widen_back,
        functools.partial(lay_rows_back, out_ref, out_to),
        functools.partial(lay_rows_back, narrow_ref, narrow_to),
    )
    stores = []
    for i in order:
        loads[i].wait()
        count = made[i].shape[0]
        middle = (count // 2 + 15) // 16 * 16 if count % 8 == 0 else count
        for x, (start, stop) in enumerate(((0, middle), (middle, count))):
            if stop > start:
                makers[i](slice(start, stop))
                part = pl.ds(start, stop - start)
                stores.append(fetch(made[i].at[part], outs[i].at[part], out_sem.at[2 * i + x]))
    came_load.wait()
    for item, to in enumerate(stream_to):
        first, second = (ref[...] for ref in streams[2 * item : 2 * item + 2])
        to[s] = without_gaps(jnp.where(s == 0, first, second))
        to[1 - s] = without_gaps(came[item].astype(F32))
    for row, (size, to) in enumerate(zip(sizes, vectors)):
        to[...] = vec_ref[row : row + 1, :size]
    for store in stores:
        store.wait()


def settle_call(low, share, hide, qkv, widen, out, narrow, vec, came, *streams):
    n = widen.shape[0]
    width = n * share
    rows = came.shape[1]
    sizes = [share] * 6 + [2 * share, hide]
    big = [(share, 3 * width), (share, n * hide), (share, width), (hide, width)]
    return pl.pallas_call(
        functools.partial(settle_kernel, low, sizes),
        out_shape=[jax.ShapeDtypeStruct(shape, F32) for shape in big]
        + [
            jax.ShapeDtypeStruct((2, rows, width), F32),
            jax.ShapeDtypeStruct((2, rows, width), F32),
        ]
        + [jax.ShapeDtypeStruct((1, size), F32) for size in sizes],
        in_specs=[ANY_SPEC] * 4 + [VMEM_SPEC, ANY_SPEC] + [VMEM_SPEC] * 4,
        out_specs=[ANY_SPEC] * 4 + [VMEM_SPEC] * 10,
        scratch_shapes=[pltpu.VMEM(m.shape, BF16) for m in (qkv, widen, out, narrow)]
        + [pltpu.VMEM(shape, F32) for shape in big]
        + [pltpu.VMEM(came.shape, BF16), DMA((5,)), DMA((8,))],
        compiler_params=params(),
        name="settle",
    )(qkv, widen, out, narrow, vec, came, *streams)


def unit_rows(values, mask, width):
    center = (values - jnp.sum(values, axis=-1, keepdims=True) * (1.0 / width)) * mask
    spread = jnp.sum(center * center, axis=-1, keepdims=True) * (1.0 / width)
    scale = lax.rsqrt(spread + EPSILON)
    return center * scale, scale


def norm_back(grad, unit, scale, gain, width):
    inner = grad * gain
    mean = jnp.sum(inner, axis=-1, keepdims=True) * (1.0 / width)
    along = jnp.sum(inner * unit, axis=-1, keepdims=True) * (1.0 / width)
    return (inner - mean - unit * along) * scale


def forward_kernel(n, width, layer, io, *refs):
    middle = layer is not None
    part, base, feats, mask = refs[:4]
    refs = refs[4:]
    if middle:
        bias, gain, shift = (feats[layer, row : row + 1] for row in (2, 3, 4))
        widen, narrow, widen_bias, refs = refs[0], refs[1], refs[2], refs[3:]
    else:
        bias, gain, shift = feats[0, 5:6], feats[1, 0:1], feats[1, 1:2]
    value_to, low_all, refs = refs[0], refs[1], refs[2:]
    if middle:
        pre_to, hidden_to, part_to, refs = refs[0], refs[1], refs[2], refs[3:]
    own, g_ss, g_rs, g_ls = refs[5:9]
    p = Place(n)
    enter(io, p, line=True)
    scatter = Scatter(p, part, *refs[:5])
    scatter.start()
    gather = Gather(p, own, low_all, g_ss, g_rs, g_ls)
    hr = own.shape[0] // HALVES

    def rows_step(half):
        rows = slice(half * hr, (half + 1) * hr)
        value = base[rows] + (scatter.result(half) + bias)
        value_to[rows] = value
        own[rows] = (unit_rows(value, mask[...], width)[0] * gain + shift).astype(BF16)

    by_halves(scatter, gather, rows_step, [])
    gather.finish()
    if middle:
        io.done(1)
        io.need(4, 5)
        feed_forward(low_all, widen, narrow, widen_bias[layer], pre_to, hidden_to, part_to)
    scatter.finish()


def scatter_scratch(n, rows, full):
    zn = n // 2
    piece = (HALVES, rows // HALVES, full)
    return [
        pltpu.VMEM((zn,) + piece, BF16),
        pltpu.VMEM((zn + 1,) + piece, BF16),
        pltpu.VMEM((zn,) + piece, BF16),
        DMA((4, zn, HALVES)),
        DMA((4, zn, HALVES)),
    ]


def gather_scratch(n):
    zn = n // 2
    return [DMA((4, zn, HALVES)), DMA((4, zn, HALVES)), DMA((HALVES,))]


def forward_step(n, collective_id, width, part, *local, layer=None, feed=()):
    total_rows, full = part.shape
    rows = total_rows // n
    shapes = [
        jax.ShapeDtypeStruct((rows, full), F32),
        jax.ShapeDtypeStruct((total_rows, full), BF16),
    ]
    scratch = scatter_scratch(n, rows, full)
    scratch += [pltpu.VMEM((rows, full), BF16)] + gather_scratch(n)
    middle = layer is not None
    if middle:
        widen, narrow, _ = feed
        hide = widen.shape[3]
        shapes += [
            jax.ShapeDtypeStruct((total_rows, hide), F32),
            jax.ShapeDtypeStruct((total_rows, hide), BF16),
            jax.ShapeDtypeStruct((total_rows, full), BF16),
        ]
    return Step(
        functools.partial(forward_kernel, n, width, layer),
        "forward_rows",
        collective_id,
        (part, *local, *feed),
        shapes,
        scratch,
        dict(line=True),
        late=(4, 5) if middle else (),
        layers={4: layer, 5: layer} if middle else {},
        early=(1, 2, 3, 4) if middle else (),
        raw=() if middle else (1,),
    )


def back_rows(scatter, half, base, grad, gain, mask, width):
    hr = scatter.hr
    rows = slice(half * hr, (half + 1) * hr)
    total = scatter.result(half)
    unit, scale = unit_rows(base[rows], mask[...], width)
    value = grad[rows] + norm_back(total, unit, scale, gain, width)
    low = value.astype(BF16)
    terms = (total * unit, total, low.astype(F32))
    return rows, value, low, [jnp.sum(term, axis=0, keepdims=True) for term in terms]


def resid_kernel(n, width, layer, io, *refs):
    base, grad, feats, mask, normed, hidden_pre, hidden, outs, widen, narrow = refs[:10]
    gain = feats[layer, 3:4]
    value_to, sums_to, low_all, wide_to, wide_came, slim_to, pre_sums = refs[10:17]
    refs = refs[17:]
    own, g_ss, g_rs, g_ls = refs[5:9]
    wide, wide_in, wide_ss, wide_rs, slim, slim_in, slim_ss, slim_rs, x_ss, x_rs = refs[9:19]
    part, pre = refs[19:]
    p = Place(n)
    enter(io, p, line=True, over=True, sibling=True)
    io.need(9, 7, 5)

    def inner(first, size):
        rows = pl.ds(first, size)
        values = hidden_pre[rows]
        act, square = gelu_parts(values)
        slope = 0.5 * (1.0 + act) + 0.5 * values * (1.0 - act * act) * GELU_A * (
            1.0 + 3.0 * GELU_B * square
        )
        found = (dot_t(outs[rows], narrow[...]) * slope).astype(BF16)
        pre[rows] = found

    def outer(first, size):
        rows = pl.ds(first, size)
        weight = widen[...].reshape(part.shape[1], widen.shape[2])
        part[rows] = dot_t(pre[rows], weight).astype(BF16)

    row_blocks(part.shape[0], inner)
    io.need(8)
    row_blocks(part.shape[0], outer)
    scatter = Scatter(p, part, *refs[:5])
    scatter.start()
    gather = Gather(p, own, low_all, g_ss, g_rs, g_ls)
    wide_fold = Fold(p, wide, wide_in, wide_to, wide_ss, wide_rs)
    slim_fold = Fold(p, slim, slim_in, slim_to, slim_ss, slim_rs)
    cross = Cross(p, wide_to, wide_came, x_ss, x_rs, 1 - layer)

    def pre_sum():
        pre_sums[...] = jnp.sum(pre[...].astype(F32), axis=0, keepdims=True)

    io.need(4, 6)
    for step in product(normed, pre, wide):
        step()
    wide_fold.start()

    def wide_done():
        cross.start()
        io.done(3)

    work = product(hidden, outs, slim) + wide_fold.steps() + [wide_done, slim_fold.start, pre_sum]
    work += slim_fold.steps() + [functools.partial(io.done, 5)]
    sums = []

    def rows_step(half):
        rows, value, low, terms = back_rows(scatter, half, base, grad, gain, mask, width)
        value_to[rows] = value
        own[rows] = low
        sums.append(jnp.concatenate(terms, axis=0))

    by_halves(scatter, gather, rows_step, work, 3)
    sums_to[...] = sum(sums)
    for rest in work:
        rest()
    gather.finish()
    scatter.finish()
    for job in (wide_fold, slim_fold, cross):
        job.finish()


def resid_step(n, collective_id, width, layer, hide, *args):
    base, normed, hidden = args[0], args[4], args[6]
    rows = base.shape[0]
    total_rows, full = normed.shape
    zn = n // 2
    wide = (zn, full // n, hidden.shape[1])
    half = -(-hide // 32) * 16
    slim = (1, half, full)
    return Step(
        functools.partial(resid_kernel, n, width, layer),
        "back_resid",
        collective_id,
        args,
        [
            jax.ShapeDtypeStruct((rows, full), F32),
            jax.ShapeDtypeStruct((3, full), F32),
            jax.ShapeDtypeStruct((total_rows, full), BF16),
            jax.ShapeDtypeStruct(wide, BF16),
            jax.ShapeDtypeStruct(wide, BF16),
            jax.ShapeDtypeStruct(slim, BF16),
            jax.ShapeDtypeStruct((1, hidden.shape[1]), F32),
        ],
        scatter_scratch(n, rows, full)
        + [pltpu.VMEM((rows, full), BF16)]
        + gather_scratch(n)
        + fold_scratch((full, hidden.shape[1]), wide)
        + fold_scratch((2 * half, full), slim)
        + [DMA, DMA]
        + [
            pltpu.VMEM((total_rows, full), BF16),
            pltpu.VMEM(hidden.shape, BF16),
        ],
        dict(line=True, over=True, sibling=True),
        late=(9, 7, 5, 8, 4, 6),
        layers={8: layer, 9: layer},
        early=(3, 5),
        raw=(2, 4),
    )


def input_kernel(n, width, source, low, io, *refs):
    part, base, grad, feats, mask, normed, triple, att, resid, slim = refs[:10]
    gain = feats[1, 0:1]
    value_to, sums_to, low_all, qkv_to, out_to, slim_came, triple_sums = refs[10:17]
    refs = refs[17:]
    own, g_ss, g_rs, g_ls = refs[5:9]
    qkv, qkv_in, qkv_ss, qkv_rs, out, out_in, out_ss, out_rs, x_ss, x_rs = refs[9:]
    p = Place(n)
    enter(io, p, line=True, over=True, sibling=True)
    scatter = Scatter(p, part, *refs[:5])
    scatter.start()
    cross = Cross(p, slim, slim_came, x_ss, x_rs, source)
    cross.start()
    gather = Gather(p, own, low_all, g_ss, g_rs, g_ls)
    qkv_fold = Fold(p, qkv, qkv_in, qkv_to, qkv_ss, qkv_rs)
    out_fold = Fold(p, out, out_in, out_to, out_ss, out_rs)

    def triple_sum():
        triple_sums[...] = jnp.sum(triple[...].astype(F32), axis=0, keepdims=True)

    work = [functools.partial(io.need, 5, 6)] + product(normed, triple, qkv)
    work += [qkv_fold.start, functools.partial(io.need, 7, 8)]
    work += [functools.partial(home_rows, att, resid, out, low, width // n), out_fold.start]
    work += qkv_fold.steps() + [functools.partial(io.done, 3), triple_sum]
    work += out_fold.steps() + [functools.partial(io.done, 4)]
    sums = []

    def rows_step(half):
        rows, value, lower, terms = back_rows(scatter, half, base, grad, gain, mask, width)
        value_to[rows] = value
        own[rows] = lower
        sums.append(jnp.concatenate(terms, axis=0))

    by_halves(scatter, gather, rows_step, work, 2)
    sums_to[...] = sum(sums)
    for rest in work:
        rest()
    gather.finish()
    scatter.finish()
    for job in (qkv_fold, out_fold, cross):
        job.finish()


def input_step(n, collective_id, width, source, low, part, base, grad, feats, mask, *operands):
    normed, triple, att, resid, slim = operands
    total_rows, full = part.shape
    rows = total_rows // n
    zn = n // 2
    qkv = (zn, full // n, triple.shape[1])
    out = (1, att.shape[1] // 2, full)
    return Step(
        functools.partial(input_kernel, n, width, source, low),
        "back_input",
        collective_id,
        (part, base, grad, feats, mask) + operands,
        [
            jax.ShapeDtypeStruct((rows, full), F32),
            jax.ShapeDtypeStruct((3, full), F32),
            jax.ShapeDtypeStruct((total_rows, full), BF16),
            jax.ShapeDtypeStruct(qkv, BF16),
            jax.ShapeDtypeStruct(out, BF16),
            jax.ShapeDtypeStruct(slim.shape, BF16),
            jax.ShapeDtypeStruct((1, triple.shape[1]), F32),
        ],
        scatter_scratch(n, rows, full)
        + [pltpu.VMEM((rows, full), BF16)]
        + gather_scratch(n)
        + fold_scratch((full, triple.shape[1]), qkv)
        + fold_scratch((att.shape[1], full), out)
        + [DMA, DMA],
        dict(line=True, over=True, sibling=True),
        late=(5, 6, 7, 8),
        plain=(9,),
        early=(3, 4),
        raw=(2, 5),
    )


def finale_kernel(n, width, low, between, io, *refs):
    part, base, grad, feats, mask, normed, triple, att, resid = refs[:9]
    slims, slim_came, qkv_far, out_far, vecs = refs[9:11], refs[11], refs[12], refs[13], refs[14:21]
    layer_outs, upper_d_in, wides, refs = refs[21:23], refs[23], refs[24:28], refs[28:]
    value_to, slim_to, qkv_to, out_to, vec_to, streams_to, wide_to = refs[:7]
    refs = refs[7:]
    qkv, qkv_fold_in, qkv_ss, qkv_rs, out, out_fold_in, out_ss, out_rs = refs[5:13]
    qkv_own, qkv_in, qkv_sum, out_own, out_in, out_sum = refs[13:19]
    slim_sum, slim_pair, vec, vec_in, vec_sum, vec_sib, streams = refs[19:26]
    a_ss, a_rs, x_ss, x_rs, v_ss, v_rs, r_ss, r_rs, ls = refs[26:35]
    wide_sum, wide_pair, w_ss, w_rs = refs[35:]
    p = Place(n)
    s, c, h, z, zn = p.s, p.c, p.h, p.z, p.zn
    share = width // n
    greet_all(p)
    choices = (
        (
            (wides[0], wide_pair.at[0], 5),
            (wides[1], wide_pair.at[1], 6),
            (slims[0], slim_pair.at[0], 1),
        ),
        (
            (wides[2], wide_pair.at[0], 5),
            (wides[3], wide_pair.at[1], 6),
            (slims[1], slim_pair.at[0], 1),
            (slim_came, slim_pair.at[1], 4),
        ),
    )
    for section, chosen in enumerate(choices):

        @pl.when(s == section)
        def _():
            for src, dst, item in chosen:
                pltpu.make_async_copy(src, dst, ls.at[item]).start()

    def chosen_wait(item):
        src, dst, sem = choices[1][item]
        pltpu.make_async_copy(src, dst, ls.at[sem]).wait()

    slim_cross = Cross(p, slims[0], slim_pair.at[1], x_ss.at[zn + 2], x_rs.at[zn + 2], 1)
    slim_cross.start()
    wide_back = Home(p, wide_sum, wide_to, w_ss, w_rs, ls.at[8])
    chosen_wait(0)
    chosen_wait(1)
    for k in list(range(1, zn)) + [0]:
        far = p.flip(k)
        total = wide_pair[0, far].astype(F32) + wide_pair[1, far].astype(F32)
        wide_sum[far] = total.astype(BF16)
        wide_back.start(k)
    leave = between() if between is not None else None
    scatter = Scatter(p, part, *refs[:5])
    back = Home(p, qkv_sum, qkv_to, a_ss, a_rs, ls.at[0])

    def x_block(k, src=qkv_far):
        far = p.flip(k)
        return remote(src.at[far], qkv_in.at[far], x_ss.at[k], x_rs.at[k], p.over)

    def out_cross(src=out_far):
        return remote(src, out_in, x_ss.at[zn], x_rs.at[zn], p.over)

    stream_cross = remote(streams, streams_to, x_ss.at[zn + 1], x_rs.at[zn + 1], p.over)

    def start_far():
        @pl.when(s == 0)
        def _():
            for k in range(zn):
                x_block(k).start()
            out_cross().start()

    def start_own(k):
        @pl.when(s == 1)
        def _():
            x_block(k, qkv_own).start()

    def start_own_out():
        @pl.when(s == 1)
        def _():
            out_cross(out_own).start()

    qkv_fold = Fold(p, qkv, qkv_fold_in, qkv_own, qkv_ss, qkv_rs)
    out_fold = Fold(p, out, out_fold_in, out_own, out_ss, out_rs)

    io.need(12, 13)
    start_far()
    io.need(5, 6)
    for step in product(normed, triple, qkv):
        step()
    qkv_fold.start()
    if leave is not None:
        leave()
    scatter.start()
    io.need(7, 8)
    work = [functools.partial(home_rows, att, resid, out, low, share), out_fold.start]
    work += qkv_fold.steps()
    work += [functools.partial(start_own, k) for k in list(range(1, zn)) + [0]]
    work += out_fold.steps() + [start_own_out]
    sums = []

    def rows_step(half):
        rows, value, lower, terms = back_rows(scatter, half, base, grad, feats[0, 0:1], mask, width)
        value_to[rows] = value
        sums.append(jnp.concatenate(terms, axis=0))

    by_halves(scatter, None, rows_step, work, 3)
    for rest in work:
        rest()

    io.need(21, 22, 23)
    streams[0] = jnp.where(s == 0, layer_outs[1][...], layer_outs[0][...]).astype(BF16)
    streams[1] = jnp.where(s == 0, upper_d_in[...], value_to[...]).astype(BF16)
    io.done(0)
    stream_cross.start()

    ones = (sum(sums), vecs[0][...])
    twos, triples, pres = vecs[1:3], (None, vecs[3]), vecs[4:6]
    lanes = vec.shape[3]
    padded = base.shape[1] // n
    sh = triple.shape[1] // 3
    for layer in range(2):
        one, two = ones[layer], twos[layer][...]
        outs = vecs[6][...] if layer else ones[1][2:3]
        features = jnp.concatenate([one[0:2], two[2:3], two[0:2], outs], axis=0)
        if layer:
            found = triples[1][...]
        else:
            found = jnp.sum(triple[...].astype(F32), axis=0, keepdims=True)
        bias = jnp.zeros((1, 2 * width), F32)
        for j, first in enumerate(low):
            spots = []
            for begin in (0, 2 * sh):
                spots += [
                    jnp.zeros((1, HD * first), F32),
                    found[:, begin : begin + sh],
                    jnp.zeros((1, width - sh - HD * first), F32),
                ]
            spots = [spot for spot in spots if spot.shape[1]]
            bias = jnp.where(h == j, jnp.concatenate(spots, axis=1), bias)
        for i in range(n):
            pieces = [
                features[:, i * padded : (i + 1) * padded],
                bias[:, i * 2 * share : (i + 1) * 2 * share],
                jnp.where(h == i, pres[layer][...], 0.0),
            ]
            wide_pieces = []
            for piece in pieces:
                rows, size = piece.shape
                if size < lanes:
                    piece = jnp.concatenate([piece, jnp.zeros((rows, lanes - size), F32)], axis=1)
                wide_pieces.append(piece)
            vec[layer, i] = jnp.concatenate(wide_pieces, axis=0)

    def vec_copy(a, b):
        l, i = lax.rem(s + a, 2), lax.rem(h + b, n)
        return remote(vec.at[l, i], vec_in.at[s, h], v_ss.at[a, b], v_rs.at[a, b], (l, c, i))

    for a, b in others(n):
        vec_copy(a, b).start()

    for k in list(range(1, zn)) + [0]:
        x_block(k).wait_recv()
        add_home(p, qkv_sum, p.flip(k), qkv_own, qkv_in, qkv_far, qkv_in)
        back.start(k)
    out_cross().wait_recv()
    add_home(p, out_sum, 0, out_own, out_in, out_far, out_in)
    for k in range(zn):
        x_block(k).wait_send()
    chosen_wait(2)

    @pl.when(s == 1)
    def _():
        chosen_wait(3)

    for step in wide_back.steps():
        step()
    slim_cross.finish()
    slim_sum[0] = (slim_pair[0, 0].astype(F32) + slim_pair[1, 0].astype(F32)).astype(BF16)

    def row_copies(w, src, dst):
        half = src.shape[1]
        piece = dst.at[pl.ds(pl.multiple_of(c * half, 16), half)]
        return (
            pltpu.make_async_copy(src.at[0], piece, ls.at[2 + w]),
            remote(src.at[0], piece, r_ss.at[w], r_rs.at[w], p.sibling),
        )

    copies = row_copies(0, slim_sum, slim_to) + row_copies(1, out_sum, out_to)
    for copy in copies:
        copy.start()
    total = vec[s, h]
    for a, b in others(n):
        vec_copy(a, b).wait_recv()
        total = total + vec_in[lax.rem(s + a, 2), lax.rem(h + n - b, n)]
    vec_sum[...] = total
    vec_share = remote(vec_sum, vec_sib, r_ss.at[2], r_rs.at[2], p.sibling)
    vec_share.start()
    for step in back.steps():
        step()
    vec_share.wait_recv()
    vec_to[...] = total + vec_sib[...]
    vec_share.wait_send()
    back.finish()
    wide_back.finish()
    for w in range(2):
        copies[2 * w].wait()
        copies[2 * w + 1].wait_recv()
        copies[2 * w + 1].wait_send()
    for a, b in others(n):
        vec_copy(a, b).wait_send()
    out_cross().wait_send()
    stream_cross.wait_recv()
    stream_cross.wait_send()
    for job in (scatter, qkv_fold, out_fold):
        job.finish()


def finale_parts(n, *args):
    part, triple, att = args[0], args[6], args[7]
    slim, lanes, wide = args[9].shape, args[18].shape[1], args[24].shape
    total_rows, full = part.shape
    rows = total_rows // n
    zn = n // 2
    qkv = (zn, full // n, triple.shape[1])
    out = (1, att.shape[1] // 2, full)
    shapes = [
            jax.ShapeDtypeStruct((rows, full), F32),
            jax.ShapeDtypeStruct((2 * slim[1], full), BF16),
            jax.ShapeDtypeStruct((n,) + qkv[1:], BF16),
            jax.ShapeDtypeStruct((2 * out[1], full), BF16),
            jax.ShapeDtypeStruct((8, lanes), F32),
            jax.ShapeDtypeStruct((2, rows, full), BF16),
            jax.ShapeDtypeStruct((n,) + wide[1:], BF16),
        ]
    scratch = (
        scatter_scratch(n, rows, full)
        + fold_scratch((full, triple.shape[1]), qkv)
        + fold_scratch((att.shape[1], full), out)
        + [pltpu.VMEM(qkv, BF16)] * 3
        + [pltpu.VMEM(out, BF16)] * 3
        + [
            pltpu.VMEM(slim, BF16),
            pltpu.VMEM((2,) + slim, BF16),
            pltpu.VMEM((2, n, 8, lanes), F32),
            pltpu.VMEM((2, n, 8, lanes), F32),
            pltpu.VMEM((8, lanes), F32),
            pltpu.VMEM((8, lanes), F32),
            pltpu.VMEM((2, rows, full), BF16),
            DMA((2, zn)),
            DMA((2, zn)),
            DMA((zn + 3,)),
            DMA((zn + 3,)),
            DMA((2, n)),
            DMA((2, n)),
            DMA((3,)),
            DMA((3,)),
            DMA((9,)),
            pltpu.VMEM(wide, BF16),
            pltpu.VMEM((2,) + wide, BF16),
            DMA((2, zn)),
            DMA((2, zn)),
        ]
    )
    return shapes, scratch


def finale_call(n, collective_id, width, low, *args):
    shapes, scratch = finale_parts(n, *args)
    return staged_call(
        functools.partial(finale_kernel, n, width, low, None),
        "finale",
        collective_id,
        args,
        shapes,
        scratch,
        late=(5, 6, 7, 8, 12, 13, 21, 22, 23),
        plain=(9, 10, 11, 24, 25, 26, 27),
        early=(0,),
        raw=(1, 2, 3, 5, 6),
    )


def dot_t(a, b):
    return lax.dot_general(a, b, (((1,), (1,)), ((), ())), preferred_element_type=F32)


def dot_n(a, b):
    return lax.dot_general(a, b, (((1,), (0,)), ((), ())), preferred_element_type=F32)


def in_blocks(rows, step, chunk, between):
    count = rows // step
    if count <= 2:
        for b in range(count):
            chunk(b * step, rows // 2 if (b + 1) * step <= rows // 2 else rows, between)
    else:

        def body(b, carry, keys):
            chunk(pl.multiple_of(b * step, step), keys, [])
            return carry

        middle = count // 2 if count % 2 == 0 else 0
        lax.fori_loop(0, middle, functools.partial(body, keys=rows // 2), 0)
        lax.fori_loop(middle, count, functools.partial(body, keys=rows), 0)


def run_next(between):
    if between:
        between.pop(0)()


def attention(slots, step, own_ref, oth_ref, kpos_ref, qpos_ref, att_ref, low_ref, lse_ref):
    rows = own_ref.shape[0]
    sh = slots * HD
    power = HD**-0.5 * LOG2E

    def at(base, slot):
        return slice(base + slot * HD, base + (slot + 1) * HD)

    def chunk(first, seen, between):
        q_rows = pl.ds(first, step)
        qpos = qpos_ref[:, q_rows]
        for slot in range(slots):
            queries = own_ref[q_rows, at(0, slot)]
            keys = (own_ref[:seen, at(sh, slot)], oth_ref[:seen, at(0, slot)])
            values = (own_ref[:seen, at(2 * sh, slot)], oth_ref[:seen, at(sh, slot)])
            scores = []
            for part in range(2):
                allowed = kpos_ref[part * rows : part * rows + seen] <= qpos
                scores.append(jnp.where(allowed, dot_t(keys[part], queries), MASKED))
            top = jnp.maximum(
                jnp.max(scores[0], axis=0, keepdims=True), jnp.max(scores[1], axis=0, keepdims=True)
            )
            total = jnp.zeros_like(top)
            weighted = jnp.zeros((HD, step), F32)
            exps = []
            for part in range(2):
                e = jnp.exp2((scores[part] - top) * power)
                total = total + jnp.sum(e, axis=0, keepdims=True)
                exps.append(e)
            inverse = 1.0 / total
            for part in range(2):
                probs = (exps[part] * inverse).astype(BF16)
                weighted = weighted + dot_n(values[part].T, probs)
            att_ref[at(0, slot), q_rows] = weighted
            low_ref[q_rows, at(0, slot)] = weighted.T.astype(BF16)
            lse_ref[slot : slot + 1, q_rows] = top * power + jnp.log(total) * LOG2E
            run_next(between)

    return chunk


def attend_kernel(n, slots, step, layer, io, *refs):
    kpos_ref, qpos_ref, carried, out_all, normed, qkv_all, qkv_bias = refs[:7]
    att_ref, low_ref, lse_ref, oth_ref, part_to, carried_to, own_ref = refs[7:14]
    kv_ss, kv_rs, out_weight, qkv_weight, load_sems = refs[14:19]
    qkv_load = fetch(qkv_all.at[layer], qkv_weight, load_sems.at[1])
    out_load = fetch(out_all.at[layer], out_weight, load_sems.at[0])
    p = Place(n)
    rows = own_ref.shape[0]
    sh = slots * HD
    enter(io, p, line=True, sibling=True)
    job = Gather(p, carried, carried_to, *refs[19:])
    job.start()
    qkv_load.wait()
    io.need(4)
    between = job.steps()

    def project(first, size):
        some = pl.ds(first, size)
        weight = qkv_weight[...].reshape(normed.shape[1], 3 * sh)
        own_ref[some] = (dot_n(normed[some], weight) + qkv_bias[layer]).astype(BF16)

    row_blocks(rows, project)
    swap = remote(own_ref.at[:, pl.ds(sh, 2 * sh)], oth_ref, kv_ss, kv_rs, p.sibling)
    swap.start()
    run_next(between)
    run_next(between)
    swap.wait_recv()
    chunk = attention(slots, step, own_ref, oth_ref, kpos_ref, qpos_ref, att_ref, low_ref, lse_ref)
    in_blocks(rows, step, chunk, between)
    out_load.wait()

    def give(first, size):
        some = pl.ds(first, size)
        part_to[some] = dot_n(low_ref[some], out_weight[...]).astype(BF16)

    row_blocks(rows, give)
    io.done(0, 1, 4, 6)
    for rest in between:
        rest()
    swap.wait_send()
    job.finish()


def attend_step(n, collective_id, slots, layer, kpos, qpos, carried, out_all, *source):
    rows = qpos.shape[1]
    sh = slots * HD
    full = out_all.shape[2]
    return Step(
        functools.partial(attend_kernel, n, slots, min(rows, 256), layer),
        "attend",
        collective_id,
        (kpos, qpos, carried, out_all, *source),
        [
            jax.ShapeDtypeStruct((sh, rows), F32),
            jax.ShapeDtypeStruct((rows, sh), BF16),
            jax.ShapeDtypeStruct((slots, rows), F32),
            jax.ShapeDtypeStruct((rows, 2 * sh), BF16),
            jax.ShapeDtypeStruct((rows, full), BF16),
            jax.ShapeDtypeStruct((n * carried.shape[0], full), BF16),
            jax.ShapeDtypeStruct((rows, 3 * sh), BF16),
        ],
        [
            DMA,
            DMA,
            pltpu.VMEM((sh, full), BF16),
            pltpu.VMEM(source[1].shape[1:], BF16),
            DMA((2,)),
        ]
        + gather_scratch(n),
        dict(line=True, sibling=True),
        late=(4,),
        plain=(3, 5),
        early=(0, 1, 4, 6),
        raw=(5,),
    )


def attend_back_kernel(n, slots, step, layer, last, greeted, io, *refs):
    own_ref, oth_ref, resid, att_ref, lse_ref, kpos_ref, qpos_ref, out_all, qkv_all = refs[:9]
    refs = refs[9:]
    if last:
        part_ref, base_ref, feats = refs[:3]
        refs = refs[3:]
    triple_ref, part_to, refs = refs[0], refs[1], refs[2:]
    if last:
        value_ref, refs = refs[0], refs[1:]
    dq_t, dkv_own, dkv_oth, came, kv_ss, kv_rs = refs[:6]
    grad_ref, out_weight, qkv_weight, load_sems = refs[6:10]
    out_load = fetch(out_all.at[layer], out_weight, load_sems.at[0])
    qkv_load = fetch(qkv_all.at[layer], qkv_weight, load_sems.at[1])
    p = Place(n)
    rows = own_ref.shape[0]
    sh = slots * HD
    scale = HD**-0.5
    if not greeted:
        enter(io, p, line=last, sibling=True)
    between = []
    if last:
        scatter = Scatter(p, part_ref, *refs[10:])
        scatter.start()
        between = scatter.steps()
    io.need(2)
    out_load.wait()

    def begin(first, size):
        some = pl.ds(first, size)
        grad_ref[some] = dot_t(resid[some], out_weight[...]).astype(BF16)

    row_blocks(rows, begin)
    io.need(0, 1, 3)

    def at(base, slot):
        return slice(base + slot * HD, base + (slot + 1) * HD)

    dq_t[...] = jnp.zeros_like(dq_t)
    swap = remote(dkv_oth, came, kv_ss, kv_rs, p.sibling)
    for part in (1, 0):
        dkv = (dkv_own, dkv_oth)[part]
        src = (own_ref, oth_ref)[part]
        base = (sh, 0)[part]
        dkv[...] = jnp.zeros_like(dkv)

        def chunk(first, seen, between):
            q_rows = pl.ds(first, step)
            qpos = qpos_ref[:, q_rows]
            for slot in range(slots):
                queries = own_ref[q_rows, at(0, slot)]
                grads = grad_ref[q_rows, at(0, slot)]
                keys, values = src[:seen, at(base, slot)], src[:seen, at(base + sh, slot)]
                lse = lse_ref[slot : slot + 1, q_rows]
                correction = jnp.sum(
                    grads.astype(F32).T * att_ref[at(0, slot), q_rows], axis=0, keepdims=True
                )
                allowed = kpos_ref[part * rows : part * rows + seen] <= qpos
                scores = dot_t(keys, queries)
                probs = jnp.where(allowed, jnp.exp2(scores * (scale * LOG2E) - lse), 0.0)
                prob_grad = dot_t(values, grads)
                score_grad = (probs * (prob_grad - correction)).astype(BF16)
                dkv[:seen, at(0, slot)] += dot_n(score_grad, queries) * scale
                dkv[:seen, at(sh, slot)] += dot_n(probs.astype(BF16), grads)
                dq_t[at(0, slot), q_rows] += dot_n(keys.T, score_grad)
                run_next(between)

        in_blocks(rows, step, chunk, between)
        if part:
            swap.start()
    triple_ref[:, :sh] = (dq_t[...].T * scale).astype(BF16)

    def finish_last():
        for rest in between:
            rest()
        hr = base_ref.shape[0] // HALVES
        for half in range(HALVES):
            part_rows = slice(half * hr, (half + 1) * hr)
            total = scatter.result(half)
            value_ref[part_rows] = base_ref[part_rows] + (total + feats[1, 5:6])
        scatter.finish()

    swap.wait_recv()
    triple_ref[:, sh:] = (dkv_own[...] + came[...]).astype(BF16)
    qkv_load.wait()

    def leave(first, size):
        some = pl.ds(first, size)
        weight = qkv_weight[...].reshape(part_to.shape[1], 3 * sh)
        part_to[some] = dot_t(triple_ref[some], weight).astype(BF16)

    io.done(0)
    if greeted:
        swap.wait_send()
        return functools.partial(row_blocks, rows, leave)
    row_blocks(rows, leave)
    io.done(1)
    if last:
        finish_last()
    swap.wait_send()


def attend_back_scratch(rows, sh, full, qkv_all):
    scratch = [pltpu.VMEM((sh, rows), F32)] + [pltpu.VMEM((rows, 2 * sh), F32)] * 3
    scratch += [DMA, DMA]
    return scratch + [
        pltpu.VMEM((rows, sh), BF16),
        pltpu.VMEM((sh, full), BF16),
        pltpu.VMEM(qkv_all.shape[1:], BF16),
        DMA((2,)),
    ]


def closing_kernel(n, width, low, slots, step, io, *refs):
    back, rest, refs = refs[:9], refs[9 : 9 + 25], refs[34:]
    outs, refs = refs[:7], refs[7:]
    back_scratch, triple, part, refs = refs[:10], refs[10], refs[11], refs[12:]

    def between():
        mapped = Mapped(io, {i: i for i in range(9)}, {})
        return attend_back_kernel(
            n, slots, step, 0, False, True, mapped, *back, triple, part, *back_scratch
        )

    numbers = [i for i in range(28) if i not in (0, 6, 8)]
    places = {i: 9 + x for x, i in enumerate(numbers)}
    places[8] = 2
    operands = dict(zip(numbers, rest))
    operands.update({0: part, 6: triple, 8: back[2]})
    finale_kernel(
        n,
        width,
        low,
        between,
        Mapped(io, places, {i: i for i in range(7)}),
        *(operands[i] for i in range(28)),
        *outs,
        *refs,
    )


def closing_call(n, collective_id, width, low, slots, back, args):
    qkv, out_all, qkv_all = back[0], back[7], back[8]
    rows = qkv.shape[0]
    full = out_all.shape[2]
    triple = jax.ShapeDtypeStruct((rows, qkv.shape[1]), BF16)
    part = jax.ShapeDtypeStruct((rows, full), BF16)
    args = [part] + list(args[:5]) + [triple] + list(args[5:6]) + [back[2]] + list(args[6:])
    shapes, scratch = finale_parts(n, *args)
    numbers = [i for i in range(28) if i not in (0, 6, 8)]
    places = {i: 9 + x for x, i in enumerate(numbers)}
    return staged_call(
        functools.partial(closing_kernel, n, width, low, slots, min(rows, 256)),
        "closing",
        collective_id,
        tuple(back) + tuple(args[i] for i in numbers),
        shapes,
        attend_back_scratch(rows, slots * HD, full, qkv_all)
        + [pltpu.VMEM(triple.shape, BF16), pltpu.VMEM(part.shape, BF16)]
        + scratch,
        late=(2, 0, 1, 3) + tuple(places[i] for i in (5, 7, 12, 13, 21, 22, 23)),
        plain=(7, 8) + tuple(places[i] for i in (9, 10, 11, 24, 25, 26, 27)),
        early=(0,),
        raw=(1, 2, 3, 5, 6),
    )


def attend_back_step(n, collective_id, slots, layer, *args, last=()):
    qkv, out_all, qkv_all = args[0], args[7], args[8]
    rows = qkv.shape[0]
    sh = slots * HD
    full = out_all.shape[2]
    step = min(rows, 256)
    shapes = [
        jax.ShapeDtypeStruct((rows, 3 * sh), BF16),
        jax.ShapeDtypeStruct((rows, full), BF16),
    ]
    scratch = attend_back_scratch(rows, sh, full, qkv_all)
    if last:
        shapes.append(jax.ShapeDtypeStruct(last[1].shape, F32))
        scratch += scatter_scratch(n, *last[1].shape)
    return Step(
        functools.partial(attend_back_kernel, n, slots, step, layer, bool(last), False),
        "attend_back",
        collective_id,
        args + tuple(last),
        shapes,
        scratch,
        dict(line=bool(last), sibling=True),
        late=(0, 1, 2, 3),
        plain=(7, 8),
        early=(0, 1),
    )


def windows(width, n):
    share = width // n
    low = [j * share // HD for j in range(n)]
    slots = max(((j + 1) * share - 1) // HD - low[j] + 1 for j in range(n))
    return [min(first, HEADS - slots) for first in low], slots


def on_device(n, tokens, block_order, cotangent, *vectors_and_weights):
    (
        first_gain,
        first_shift,
        qkv_weight,
        input_bias,
        out_weight,
        out_bias,
        second_gain,
        second_shift,
        widen_weight,
        widen_bias,
        narrow_weight,
        narrow_bias,
    ) = (member[0] for member in vectors_and_weights)
    _, rows, width = tokens.shape
    hidden = widen_weight.shape[1]
    share = width // n
    hide = hidden // n
    padded = -(-share // 16) * 16
    full = n * padded
    low, slots = windows(width, n)
    sh = slots * HD
    total_rows = n * rows

    mask = jnp.asarray(np.arange(full)[None] % padded < share, F32)
    (
        x,
        own_cot,
        out_grad,
        out_sums,
        normed,
        qkv,
        qkv_all,
        out_all,
        feats,
        qkv_bias,
        widen_biases,
        att,
        att_low,
        lse,
        other,
        widen_all,
        *middle,
        narrow_all,
        kpos,
        qpos,
    ) = open_call(
        n,
        low,
        slots,
        padded,
        tokens,
        cotangent,
        [
            member[None]
            for member in (
                first_gain,
                first_shift,
                out_bias,
                second_gain,
                second_shift,
                narrow_bias,
                input_bias,
                widen_bias,
            )
        ],
        (qkv_weight, out_weight, widen_weight, narrow_weight),
        mask,
        block_order,
    )
    stored = []
    layer_outs = []
    merge = total_rows * full <= 2**20
    residual, normed_two, hidden_pre, hidden_low, part = middle
    stored.append((x, normed, qkv, other, att, att_low, lse, residual, normed_two))
    stored[-1] += (hidden_pre, hidden_low)
    (x, normed), attended = follow(
        merge,
        forward_step(n, 5, width, part, residual, feats, mask),
        lambda ended: attend_step(
            n, 2, slots, 1, kpos, qpos, own_cot, out_all, ended[1], qkv_all, qkv_bias
        ),
    )
    layer_outs.append(x)
    att, att_low, lse, other, part, out_low_all, qkv = attended
    second_middle = forward_step(
        n,
        4,
        width,
        part,
        x,
        feats,
        mask,
        layer=1,
        feed=(widen_all, narrow_all, widen_biases),
    )

    def back_middle(layer, residual, grad, normed_two, hidden_pre, hidden_low, low_all):
        return resid_step(
            n,
            7 + layer,
            width,
            layer,
            hide,
            residual,
            grad,
            feats,
            mask,
            normed_two,
            hidden_pre,
            hidden_low,
            low_all,
            widen_all,
            narrow_all,
        )

    upper = (qkv, other, att, lse, kpos, qpos, out_all, qkv_all)
    middle, back, (triple, part, last_out) = follow(
        merge,
        second_middle,
        lambda made: back_middle(1, made[0], out_grad, *made[1:4], out_low_all),
        lambda made, back: attend_back_step(
            n, 10, slots, 1, *upper[:2], back[2], *upper[2:], last=(made[4], made[0], feats)
        ),
    )
    upper_part = part
    layer_outs.append(last_out)
    residual, normed_two, hidden_pre, hidden_low, _ = middle
    stored.append((x, normed, qkv, other, att, att_low, lse, residual, normed_two))
    stored[-1] += (hidden_pre, hidden_low)

    found = {}
    for layer in (1, 0):
        x, normed, qkv, other, att, att_low, lse, residual, normed_two = stored[layer][:9]
        hidden_pre, hidden_low = stored[layer][9:]
        resid_grad, sums_two, resid_low_all, wide, wide_came, slim, pre_sums = back
        operands = (qkv, other, resid_low_all, att, lse, kpos, qpos, out_all, qkv_all)
        found[layer] = (wide, wide_came, slim, sums_two, pre_sums)
        if layer:
            upper_step = input_step(
                n,
                11,
                width,
                0,
                low,
                upper_part,
                x,
                resid_grad,
                feats,
                mask,
                normed,
                triple,
                att_low,
                resid_low_all,
                slim,
            )
            below = stored[0]
            ended, back = follow(
                merge,
                upper_step,
                lambda ended: back_middle(0, below[7], ended[0], *below[8:], ended[2]),
            )
            upper_d_in, sums_one, _, qkv_grad, out_rows, slim_came, triple_sums = ended
    lower, upper = found[0], found[1]
    streams = (
        lower[2],
        upper[2],
        slim_came,
        qkv_grad,
        out_rows,
        sums_one,
        lower[3],
        upper[3],
        triple_sums,
        lower[4],
        upper[4],
        out_sums,
        *layer_outs,
        upper_d_in,
        *lower[:2],
        *upper[:2],
    )
    own = (x, resid_grad, feats, mask, normed)
    if merge:
        ended = closing_call(n, 12, width, low, slots, operands, (*own, att_low, *streams))
    else:
        ((triple, part),) = run_steps([attend_back_step(n, 9, slots, 0, *operands)])
        ended = finale_call(
            n, 12, width, low, part, *own, triple, att_low, resid_low_all, *streams
        )
    d_in, narrow_back, qkv_back, out_back, vec, came, widen_back = ended
    settled = settle_call(
        low,
        share,
        hide,
        qkv_back,
        widen_back,
        out_back,
        narrow_back,
        vec,
        came,
        *layer_outs,
        d_in,
        upper_d_in,
    )
    qkv_out, widen_out, out_out, narrow_out, layer_out, d_out = (m[None] for m in settled[:6])
    gain1, shift1, out_b, gain2, shift2, narrow_b, input_b, widen_b = settled[6:]
    return (
        layer_out,
        d_out,
        gain1,
        shift1,
        qkv_out,
        input_b,
        out_out,
        out_b,
        gain2,
        shift2,
        widen_out,
        widen_b,
        narrow_out,
        narrow_b,
    )


def solution(mesh):
    rows = P(None, ("ctx", "shard"), None)
    vector = P("section", "shard")
    matrix = P("section", "shard", None)
    order = (
        vector,
        vector,
        matrix,
        vector,
        matrix,
        vector,
        vector,
        vector,
        matrix,
        vector,
        matrix,
        vector,
    )
    streams = P("section", None, ("ctx", "shard"), None)
    return jax.shard_map(
        functools.partial(on_device, mesh.shape["shard"]),
        mesh=mesh,
        in_specs=(rows, P(), rows) + order,
        out_specs=(streams, streams) + order,
        check_vma=False,
    )
```

```python
import functools

import jax
import jax.numpy as jnp
import numpy as np
from jax import lax
from jax.experimental import pallas as pl
from jax.experimental.pallas import tpu as pltpu
from jax.sharding import PartitionSpec as P

HEADS = 25
HD = 64
EPSILON = 1e-05
MASKED = -1e30
LOG2E = 1.4426950408889634
GELU_A = 0.7978845608028654
GELU_B = 0.044715
MESH = pl.DeviceIdType.MESH
F32 = jnp.float32
BF16 = jnp.bfloat16
VMEM_SPEC = pl.BlockSpec(memory_space=pltpu.VMEM)
ANY_SPEC = pl.BlockSpec(memory_space=pl.ANY)
DMA = pltpu.SemaphoreType.DMA
VMEM_LIMIT = 60 * 2**20
HALVES = 2


def params(collective_id=None):
    if collective_id is None:
        return pltpu.CompilerParams(vmem_limit_bytes=VMEM_LIMIT)
    return pltpu.CompilerParams(
        collective_id=collective_id, has_side_effects=True, vmem_limit_bytes=VMEM_LIMIT
    )


def remote(src, dst, send_sem, recv_sem, device):
    return pltpu.make_async_remote_copy(
        src_ref=src,
        dst_ref=dst,
        send_sem=send_sem,
        recv_sem=recv_sem,
        device_id=device,
        device_id_type=MESH,
    )


class Place:
    def __init__(self, n):
        self.s = lax.axis_index("section")
        self.c = lax.axis_index("ctx")
        self.h = lax.axis_index("shard")
        self.n = n
        self.zn = n // 2
        self.y = lax.rem(self.h, 2)
        self.z = lax.div(self.h, 2)
        self.far_y = self.y + self.c - 2 * self.y * self.c

    def flip(self, k):
        found = self.z
        for bit in range(self.zn.bit_length()):
            if k >> bit & 1:
                found = found + (1 - 2 * lax.rem(self.z // 2**bit, 2)) * 2**bit
        return found

    def dev(self, z, y):
        return (self.s, self.c, z * 2 + y)

    @property
    def pair(self):
        return self.dev(self.z, 1 - self.y)

    @property
    def above(self):
        return self.dev(self.z + 1, self.y)

    @property
    def below(self):
        return self.dev(self.z - 1, self.y)

    @property
    def over(self):
        return (1 - self.s, self.c, self.h)

    @property
    def sibling(self):
        return (self.s, 1 - self.c, self.h)


def greet(p, line=False, spread=False, over=False, sibling=False):
    bar = pltpu.get_barrier_semaphore()
    peers = 0

    def signal(device):
        pl.semaphore_signal(bar, inc=1, device_id=device, device_id_type=MESH)

    if line:
        signal(p.pair)

        @pl.when(p.z < p.zn - 1)
        def _():
            signal(p.above)

        @pl.when(p.z > 0)
        def _():
            signal(p.below)

        peers = 1 + (p.z + p.zn - 1) // p.zn + (2 * p.zn - 2 - p.z) // p.zn
    if spread:
        for dz in range(1, p.zn):
            signal(p.dev(lax.rem(p.z + dz, p.zn), p.far_y))

        @pl.when(p.c == 1)
        def _():
            signal(p.dev(p.z, p.far_y))

        peers = peers + p.zn - 1 + p.c
    if over:
        signal(p.over)
        peers = peers + 1
    if sibling:
        signal(p.sibling)
        peers = peers + 1
    pl.semaphore_wait(bar, peers)


class Gather:
    def __init__(self, p, own_ref, out_ref, ss, rs, ls):
        self.p, self.own_ref, self.out_ref = p, own_ref, out_ref
        self.ss, self.rs, self.ls = ss, rs, ls
        self.hr = own_ref.shape[0] // HALVES

    def blk(self, half, zz, yy):
        row = (half * self.p.n + zz * 2 + yy) * self.hr
        return self.out_ref.at[pl.ds(pl.multiple_of(row, 16), self.hr)]

    def own(self, half):
        return self.own_ref.at[pl.ds(half * self.hr, self.hr)]

    def up(self, t, half, src):
        p = self.p
        sems = (self.ss.at[0, t, half], self.rs.at[0, t, half])
        return remote(src, self.blk(half, p.z - (t - 1), p.y), *sems, p.above)

    def down(self, t, half, src):
        p = self.p
        sems = (self.ss.at[1, t, half], self.rs.at[1, t, half])
        return remote(src, self.blk(half, p.z + (t - 1), p.y), *sems, p.below)

    def across(self, kind, t, half, zz, src):
        p = self.p
        sems = (self.ss.at[2 + kind, t, half], self.rs.at[2 + kind, t, half])
        return remote(src, self.blk(half, zz, p.y), *sems, p.pair)

    def local(self, half):
        p = self.p
        return pltpu.make_async_copy(
            self.own(half), self.blk(half, p.z, p.y), self.ls.at[half]
        )

    def start(self, halves=range(HALVES)):
        p = self.p
        for half in halves:
            src = self.own(half)

            @pl.when(p.z < p.zn - 1)
            def _():
                self.up(1, half, src).start()

            @pl.when(p.z > 0)
            def _():
                self.down(1, half, src).start()

            self.across(0, 0, half, p.z, src).start()
            self.local(half).start()

    def step(self, t, half):
        p = self.p
        z, zn = p.z, p.zn

        @pl.when(z >= t)
        def _():
            block = self.blk(half, z - t, p.y)
            self.up(t, half, block).wait_recv()
            if t < zn - 1:

                @pl.when(z < zn - 1)
                def _():
                    self.up(t + 1, half, block).start()

            self.across(0, t, half, z - t, block).start()

        @pl.when(z <= zn - 1 - t)
        def _():
            block = self.blk(half, z + t, p.y)
            self.down(t, half, block).wait_recv()
            if t < zn - 1:

                @pl.when(z > 0)
                def _():
                    self.down(t + 1, half, block).start()

            self.across(1, t, half, z + t, block).start()

    def steps(self):
        return [
            functools.partial(self.step, t, half)
            for t in range(1, self.p.zn)
            for half in range(HALVES)
        ]

    def finish(self):
        p = self.p
        z, zn = p.z, p.zn
        for half in range(HALVES):
            self.across(0, 0, half, z, self.own(half)).wait_recv()
            for t in range(1, zn):

                @pl.when(z >= t)
                def _():
                    self.across(0, t, half, z - t, self.own(half)).wait_recv()

                @pl.when(z <= zn - 1 - t)
                def _():
                    self.across(1, t, half, z + t, self.own(half)).wait_recv()

        for half in range(HALVES):
            self.local(half).wait()
            self.across(0, 0, half, z, self.own(half)).wait_send()
            for t in range(1, zn):

                @pl.when((z < zn - 1) & (z >= t - 1))
                def _():
                    self.up(t, half, self.own(half)).wait_send()

                @pl.when((z > 0) & (z <= zn - t))
                def _():
                    self.down(t, half, self.own(half)).wait_send()

                @pl.when(z >= t)
                def _():
                    self.across(0, t, half, z - t, self.own(half)).wait_send()

                @pl.when(z <= zn - 1 - t)
                def _():
                    self.across(1, t, half, z + t, self.own(half)).wait_send()


class Scatter:
    def __init__(self, p, part_ref, ybuf, rbuf, sbuf, ss, rs):
        self.p, self.part_ref = p, part_ref
        self.ybuf, self.rbuf, self.sbuf, self.ss, self.rs = ybuf, rbuf, sbuf, ss, rs
        self.hr = ybuf.shape[2]

    def blk(self, half, zz, yy):
        row = (half * self.p.n + zz * 2 + yy) * self.hr
        return self.part_ref.at[pl.ds(pl.multiple_of(row, 16), self.hr)]

    def goal(self, k, t):
        return self.p.z + t if k == 0 else self.p.z - t

    def across(self, k, t, half):
        p = self.p
        zz = self.goal(k, t)
        sems = (self.ss.at[k, t, half], self.rs.at[k, t, half])
        return remote(self.blk(half, zz, 1 - p.y), self.ybuf.at[zz, half], *sems, p.pair)

    def along(self, k, t, half, slot):
        p = self.p
        zz = self.goal(k, t)
        sems = (self.ss.at[2 + k, t, half], self.rs.at[2 + k, slot, half])
        target = p.above if k == 0 else p.below
        return remote(self.sbuf.at[zz, half], self.rbuf.at[zz + 1 - k, half], *sems, target)

    def ok(self, k, t):
        return self.p.z <= self.p.zn - 1 - t if k == 0 else self.p.z >= t

    def has(self, k):
        return self.p.z > 0 if k == 0 else self.p.z < self.p.zn - 1

    def start(self):
        for t in range(self.p.zn - 1, 0, -1):
            for half in range(HALVES):
                for k in range(2):

                    @pl.when(self.ok(k, t))
                    def _():
                        self.across(k, t, half).start()

        for half in range(HALVES):
            self.across(0, 0, half).start()

    def step(self, t, half, k):
        p = self.p
        zz = self.goal(k, t)

        @pl.when(self.ok(k, t))
        def _():
            self.across(k, t, half).wait_recv()
            total = self.blk(half, zz, p.y)[...].astype(F32)
            total = total + self.ybuf[zz, half].astype(F32)
            if t < p.zn - 1:

                @pl.when(self.has(k))
                def _():
                    self.along(k, t, half, t).wait_recv()
                    more = total + self.rbuf[zz + 1 - k, half].astype(F32)
                    self.sbuf[zz, half] = more.astype(BF16)

                @pl.when(jnp.logical_not(self.has(k)))
                def _():
                    self.sbuf[zz, half] = total.astype(BF16)

            else:
                self.sbuf[zz, half] = total.astype(BF16)
            self.along(k, t, half, t - 1).start()

    def steps(self):
        return [
            functools.partial(self.step, t, half, k)
            for t in range(self.p.zn - 1, 0, -1)
            for half in range(HALVES)
            for k in range(2)
        ]

    def result(self, half):
        p = self.p
        z = p.z
        self.across(0, 0, half).wait_recv()
        for k in range(2):

            @pl.when(self.has(k))
            def _():
                self.along(k, 0, half, 0).wait_recv()

            @pl.when(jnp.logical_not(self.has(k)))
            def _():
                self.rbuf[z + 1 - k, half] = jnp.zeros(self.rbuf.shape[2:], BF16)

        total = self.blk(half, z, p.y)[...].astype(F32) + self.ybuf[z, half].astype(F32)
        return total + self.rbuf[z + 1, half].astype(F32) + self.rbuf[z, half].astype(F32)

    def finish(self):
        for half in range(HALVES):
            self.across(0, 0, half).wait_send()
            for t in range(1, self.p.zn):
                for k in range(2):

                    @pl.when(self.ok(k, t))
                    def _():
                        self.across(k, t, half).wait_send()
                        self.along(k, t, half, t - 1).wait_send()


class Spread:
    def __init__(self, p, src, dst, ss, rs, ls):
        self.p, self.src, self.dst, self.ss, self.rs, self.ls = p, src, dst, ss, rs, ls

    def source(self, dz):
        return self.p.flip(dz) * 2 + self.p.far_y

    def out(self, dz):
        p = self.p
        target = self.source(dz)
        sems = (self.ss.at[0, dz], self.rs.at[0, dz])
        return remote(self.src.at[target], self.dst.at[p.s, p.h], *sems, (p.s, p.c, target))

    def aside(self, dz):
        block = self.dst.at[self.p.s, self.source(dz)]
        return remote(block, block, self.ss.at[1, dz], self.rs.at[1, dz], self.p.sibling)

    def cross(self, dz):
        block = self.dst.at[self.p.s, self.source(dz)]
        return remote(block, block, self.ss.at[2, dz], self.rs.at[2, dz], self.p.over)

    def cross_own(self):
        p = self.p
        sems = (self.ss.at[2, 0], self.rs.at[2, 0])
        return remote(self.src.at[p.h], self.dst.at[p.s, p.h], *sems, p.over)

    def cross_aside(self, dz):
        block = self.dst.at[1 - self.p.s, self.source(dz)]
        return remote(block, block, self.ss.at[3, dz], self.rs.at[3, dz], self.p.sibling)

    def local(self):
        p = self.p
        return pltpu.make_async_copy(self.src.at[p.h], self.dst.at[p.s, p.h], self.ls)

    def start(self):
        @pl.when(self.p.c == 1)
        def _():
            self.out(0).start()

        @pl.when(self.p.c == 0)
        def _():
            self.cross_own().start()

        for dz in range(1, min(3, self.p.zn)):
            self.out(dz).start()
        self.local().start()

    def arrived(self, dz):
        if 3 <= dz + 2 < self.p.zn:
            self.out(dz + 1).wait_send()
            self.out(dz + 2).start()
        self.out(dz).wait_recv()
        self.cross(dz).start()
        self.aside(dz).start()

    def crossed(self, dz):
        self.cross(dz).wait_recv()
        self.cross_aside(dz).start()

    def first(self):
        @pl.when(self.p.c == 1)
        def _():
            self.arrived(0)

    def steps(self):
        found = [self.first]
        found += [functools.partial(self.arrived, dz) for dz in range(1, self.p.zn)]
        return found + [functools.partial(self.crossed, dz) for dz in range(self.p.zn)]

    def finish(self):
        self.local().wait()

        @pl.when(self.p.c == 0)
        def _():
            self.aside(0).wait_recv()
            self.cross_own().wait_send()

        @pl.when(self.p.c == 1)
        def _():
            self.out(0).wait_send()
            self.aside(0).wait_send()
            self.cross(0).wait_send()

        for dz in range(self.p.zn):
            if dz:
                self.aside(dz).wait_recv()
                self.aside(dz).wait_send()
                if dz == 1 or dz == self.p.zn - 1:
                    self.out(dz).wait_send()
                self.cross(dz).wait_send()
            self.cross_aside(dz).wait_recv()
            self.cross_aside(dz).wait_send()


class RowSwap:
    def __init__(self, p, src, dst, ss, rs, ls):
        self.p, self.src, self.dst, self.ss, self.rs, self.ls = p, src, dst, ss, rs, ls
        self.split = src.shape[0] % 32 == 0

    def piece(self, which):
        count = self.src.shape[0]
        if not self.split:
            return self.src, self.dst.at[which, pl.ds(0, count)]
        half = count // 2
        rows = pl.ds(pl.multiple_of(self.p.c * half, 16), half)
        return self.src.at[rows], self.dst.at[which, rows]

    def cross(self):
        src, dst = self.piece(self.p.s)
        return remote(src, dst, self.ss.at[0], self.rs.at[0], self.p.over)

    def aside(self):
        block = self.piece(1 - self.p.s)[1]
        return remote(block, block, self.ss.at[1], self.rs.at[1], self.p.sibling)

    def local(self):
        rows = pl.ds(0, self.src.shape[0])
        return pltpu.make_async_copy(self.src, self.dst.at[self.p.s, rows], self.ls)

    def start(self):
        self.cross().start()
        self.local().start()

    def step(self):
        self.cross().wait_recv()
        if self.split:
            self.aside().start()

    def finish(self):
        self.local().wait()
        self.cross().wait_send()
        if self.split:
            self.aside().wait_recv()
            self.aside().wait_send()


class Cross:
    def __init__(self, p, src, dst, ss, rs, source):
        self.p, self.source = p, source
        self.copy = remote(src, dst, ss, rs, p.over)

    def start(self):
        @pl.when(self.p.s == self.source)
        def _():
            self.copy.start()

    def finish(self):
        @pl.when(self.p.s == self.source)
        def _():
            self.copy.wait_send()

        @pl.when(self.p.s != self.source)
        def _():
            self.copy.wait_recv()


class Home:
    def __init__(self, p, src, dst, ss, rs, ls):
        self.p, self.src, self.dst, self.ss, self.rs, self.ls = p, src, dst, ss, rs, ls

    def send(self, k):
        p = self.p
        far = p.flip(k)
        target = (p.s, p.c, far * 2 + p.far_y)
        sems = (self.ss.at[0, k], self.rs.at[0, k])
        return remote(self.src.at[far], self.dst.at[p.h], *sems, target)

    def keep(self):
        return pltpu.make_async_copy(self.src.at[self.p.z], self.dst.at[self.p.h], self.ls)

    def aside(self, k):
        block = self.dst.at[self.p.flip(k) * 2 + self.p.far_y]
        return remote(block, block, self.ss.at[1, k], self.rs.at[1, k], self.p.sibling)

    def start(self, k):
        if k:
            self.send(k).start()
            return

        @pl.when(self.p.c == 1)
        def _():
            self.send(0).start()

        @pl.when(self.p.c == 0)
        def _():
            self.keep().start()

    def arrived(self, k):
        if k:
            self.send(k).wait_recv()
        else:

            @pl.when(self.p.c == 1)
            def _():
                self.send(0).wait_recv()

            @pl.when(self.p.c == 0)
            def _():
                self.keep().wait()

        self.aside(k).start()

    def steps(self):
        return [functools.partial(self.arrived, k) for k in range(self.p.zn)]

    def finish(self):
        @pl.when(self.p.c == 1)
        def _():
            self.send(0).wait_send()

        for k in range(self.p.zn):
            if k:
                self.send(k).wait_send()
            self.aside(k).wait_recv()
            self.aside(k).wait_send()


def add_home(p, to, index, first, first_came, second, second_came):
    pairs = ((first, first_came), (second, second_came))
    for section, (own, came) in enumerate(pairs):

        @pl.when(p.s == section)
        def _():
            to[index] = (own[index].astype(F32) + came[index].astype(F32)).astype(BF16)


class Fold:
    def __init__(self, p, src, came, out, ss, rs):
        self.p, self.src, self.came, self.out, self.ss, self.rs = p, src, came, out, ss, rs
        self.count = out.shape[0]
        self.size = out.shape[1]

    def rows(self, item, near):
        p = self.p
        if self.count == 1:
            index = 1 - p.c if near else p.c
        else:
            index = item * 2 + (1 - p.far_y if near else p.far_y)
        return pl.ds(pl.multiple_of(index * self.size, 16), self.size)

    def copy(self, item):
        src = self.src.at[self.rows(item, True)]
        sems = (self.ss.at[item], self.rs.at[item])
        return remote(src, self.came.at[item], *sems, self.p.sibling)

    def start(self):
        for item in range(self.count):
            self.copy(item).start()

    def step(self, item):
        self.copy(item).wait_recv()
        own = self.src[self.rows(item, False)].astype(F32)
        self.out[item] = (own + self.came[item].astype(F32)).astype(BF16)

    def steps(self):
        return [functools.partial(self.step, item) for item in range(self.count)]

    def finish(self):
        for item in range(self.count):
            self.copy(item).wait_send()


def fold_scratch(source, out):
    return [pltpu.VMEM(source, BF16), pltpu.VMEM(out, BF16), DMA((out[0],)), DMA((out[0],))]


def product(a_ref, b_ref, to_ref):
    rows = to_ref.shape[0]

    def step(first, size):
        found = lax.dot_general(
            a_ref[:, first : first + size],
            b_ref[...],
            (((0,), (0,)), ((), ())),
            preferred_element_type=F32,
        )
        to_ref[first : first + size] = found.astype(BF16)

    return [
        functools.partial(step, first, min(256, rows - first)) for first in range(0, rows, 256)
    ]


def home_rows(a_ref, b_ref, to_ref, low, share):
    found = lax.dot_general(
        a_ref[...], b_ref[...], (((0,), (0,)), ((), ())), preferred_element_type=F32
    )
    h = lax.axis_index("shard")
    shift = 0
    for j, first in enumerate(low):
        shift = shift + jnp.where(h == j, (HD * first - j * share) % found.shape[0], 0)
    to_ref[...] = pltpu.roll(found, shift, 0).astype(BF16)


def in_turn(steps, work, each=1):
    for step in steps:
        for _ in range(each):
            run_next(work)
        step()


def by_halves(scatter, gather, rows_step, work, each=1):
    in_turn(scatter.steps(), work, each)
    for half in range(HALVES):
        rows_step(half)
        if gather is not None:
            gather.start([half])
    if gather is not None:
        in_turn(gather.steps(), work, each)


def fetch(src, dst, sem):
    copy = pltpu.make_async_copy(src, dst, sem)
    copy.start()
    return copy


class Staging:
    greeted, extra = False, {}

    def __init__(self):
        self.loads, self.stores, self.running = {}, {}, []

    def need(self, *items):
        for item in items:
            self.loads.pop(item).wait()

    def done(self, *items):
        for item in items:
            self.running.append(fetch(*self.stores.pop(item)))

    def end(self):
        self.done(*list(self.stores))
        for copy in self.running:
            copy.wait()


def staged_call(
    body,
    name,
    collective_id,
    args,
    shapes,
    scratch,
    late=(),
    plain=(),
    early=(),
    raw=(),
    layers={},
    scalars=(),
):
    late, early = tuple(late), tuple(early)
    n_in, n_out, n_scratch = len(args), len(shapes), len(scratch)

    def run(*refs):
        ins, outs = list(refs[:n_in]), list(refs[n_in : n_in + n_out])
        rest = refs[n_in + n_out :]
        own, rest = rest[:n_scratch], rest[n_scratch:]
        staged_in, rest = rest[: len(late)], rest[len(late) :]
        staged_out, sems = rest[: len(early)], rest[len(early) :]
        io = Staging()
        for x, item in enumerate(late):
            src = ins[item].at[layers[item]] if item in layers else ins[item]
            io.loads[item] = fetch(src, staged_in[x], sems[0].at[x])
            ins[item] = staged_in[x]
        for x, item in enumerate(early):
            io.stores[item] = (staged_out[x], outs[item], sems[1].at[x])
            outs[item] = staged_out[x]
        body(io, *ins, *outs, *own)
        io.end()

    def place(i):
        if i in scalars:
            return pl.BlockSpec(memory_space=pltpu.SMEM)
        return ANY_SPEC if i in late + tuple(plain) else VMEM_SPEC

    stages = [
        pltpu.VMEM(args[item].shape[1 if item in layers else 0 :], args[item].dtype) for item in late
    ]
    stages += [pltpu.VMEM(shapes[item].shape, shapes[item].dtype) for item in early]
    stages += [DMA((max(len(late), 1),)), DMA((max(len(early), 1),))]
    return pl.pallas_call(
        run,
        out_shape=shapes,
        in_specs=[place(i) for i in range(n_in)],
        out_specs=[ANY_SPEC if i in early + tuple(raw) else VMEM_SPEC for i in range(n_out)],
        scratch_shapes=list(scratch) + stages,
        compiler_params=params(collective_id),
        name=name,
    )(*args)


class Mapped:
    def __init__(self, io, loads, stores, greeted=True, extra={}):
        self.io, self.loads, self.stores = io, loads, stores
        self.greeted, self.extra = greeted, extra

    def need(self, *items):
        for item in items:
            if self.loads.get(item) in self.io.loads:
                self.io.need(self.loads[item])

    def done(self, *items):
        for item in items:
            if self.stores.get(item) in self.io.stores:
                self.io.done(self.stores[item])


class Result:
    def __init__(self, step, index):
        self.step, self.index = step, index
        self.shape, self.dtype = step.shapes[index].shape, step.shapes[index].dtype


class Step:
    def __init__(self, body, name, collective_id, args, shapes, scratch, greets, **staging):
        self.body, self.name, self.collective_id = body, name, collective_id
        self.args, self.shapes, self.scratch, self.greets = tuple(args), shapes, scratch, greets
        self.late = tuple(staging.get("late", ()))
        self.plain = tuple(staging.get("plain", ()))
        self.early = tuple(staging.get("early", ()))
        self.raw = tuple(staging.get("raw", ()))
        self.layers = staging.get("layers", {})


def run_steps(steps):
    args, arg_of, out_of, first_out = [], {}, {}, []
    shapes, scratch, early, raw = [], [], [], []
    linked = {
        (id(arg.step), arg.index) for step in steps for arg in step.args if isinstance(arg, Result)
    }
    for k, step in enumerate(steps):
        for i, arg in enumerate(step.args):
            if isinstance(arg, Result):
                continue
            spots = [x for x, known in enumerate(args) if known is arg]
            if not spots:
                args.append(arg)
                spots = [len(args) - 1]
            arg_of[k, i] = spots[0]
        first_out.append(len(shapes))
        for o, shape in enumerate(step.shapes):
            out_of[k, o] = len(shapes)
            keep = (id(step), o) in linked
            if o in step.early or (o in step.raw and keep):
                early.append(len(shapes))
            elif o in step.raw:
                raw.append(len(shapes))
            shapes.append(shape)
        scratch += step.scratch
    direct = {
        arg_of[k, i]
        for k, step in enumerate(steps)
        for i in range(len(step.args))
        if (k, i) in arg_of and i not in step.late and i not in step.plain
    }
    late, layers = [], {}
    for k, step in enumerate(steps):
        for i in step.late:
            spot = arg_of.get((k, i))
            if spot is not None and spot not in direct and spot not in late:
                late.append(spot)
                if i in step.layers:
                    layers[spot] = step.layers[i]
    plain = [x for x in range(len(args)) if x not in direct and x not in late]
    extra = {}
    for step in steps:
        extra.update(step.greets)

    def body(io, *refs):
        ins, outs = refs[: len(args)], refs[len(args) : len(args) + len(shapes)]
        rest = refs[len(args) + len(shapes) :]
        for k, step in enumerate(steps):
            mine = []
            for i, arg in enumerate(step.args):
                if isinstance(arg, Result):
                    mine.append(outs[out_of[steps.index(arg.step), arg.index]])
                else:
                    mine.append(ins[arg_of[k, i]])
            loads = {i: arg_of[k, i] for i in range(len(step.args)) if (k, i) in arg_of}
            stores = {o: out_of[k, o] for o in range(len(step.shapes))}
            own = outs[first_out[k] : first_out[k] + len(step.shapes)]
            count = len(step.scratch)
            part = Mapped(io, loads, stores, k > 0, extra)
            step.body(part, *mine, *own, *rest[:count])
            part.done(*stores)
            rest = rest[count:]

    found = staged_call(
        body,
        "_".join(step.name for step in steps),
        steps[0].collective_id,
        args,
        shapes,
        scratch,
        late=late,
        plain=plain,
        early=early,
        raw=raw,
        layers=layers,
    )
    return [
        found[first : first + len(step.shapes)] for first, step in zip(first_out, steps)
    ]


def follow(merge, first, *makers):
    if merge:
        steps, results = [first], [[Result(first, i) for i in range(len(first.shapes))]]
        for make in makers:
            step = make(*results)
            steps.append(step)
            results.append([Result(step, i) for i in range(len(step.shapes))])
        return run_steps(steps)
    found = run_steps([first])
    for make in makers:
        found += run_steps([make(*found)])
    return found


def row_blocks(rows, step):
    size = min(rows, 256)
    count = rows // size
    if count <= 2:
        for b in range(count):
            step(b * size, size)
    else:

        def body(b, carry):
            step(pl.multiple_of(b * size, size), size)
            return carry

        lax.fori_loop(0, count, body, 0)


def enter(io, p, **greets):
    if not io.greeted:
        greets.update(io.extra)
        greet(p, **greets)


def gelu_parts(values):
    square = values * values
    return jnp.tanh(GELU_A * (values + GELU_B * values * square)), square


def greet_all(p):
    bar = pltpu.get_barrier_semaphore()
    for a in range(2):
        for b in range(p.n):
            if (a, b) != (0, 0):
                other = (lax.rem(p.s + a, 2), p.c, lax.rem(p.h + b, p.n))
                pl.semaphore_signal(bar, inc=1, device_id=other, device_id_type=MESH)
    pl.semaphore_signal(bar, inc=1, device_id=p.sibling, device_id_type=MESH)
    pl.semaphore_wait(bar, 2 * p.n)


def others(n):
    return [(a, b) for a in range(2) for b in range(n) if (a, b) != (0, 0)]


def with_gaps(values, n, padded):
    rows, width = values.shape
    share = width // n
    pieces = []
    for j in range(n):
        pieces.append(values[:, j * share : (j + 1) * share])
        if padded > share:
            pieces.append(jnp.zeros((rows, padded - share), values.dtype))
    return jnp.concatenate(pieces, axis=1)


def lay_vectors(vectors, pack_to):
    lanes = pack_to.shape[1]
    members = []
    for ref in vectors:
        member = ref[...].astype(F32)
        members.append(
            jnp.concatenate([member, jnp.zeros((1, lanes - member.shape[1]), F32)], axis=1)
        )
    members.append(jnp.zeros((8, lanes), F32))
    pack_to[...] = jnp.concatenate(members, axis=0).astype(BF16)


def lay_first(low, qkv_ref, qkv_to):
    n, padded, triple = qkv_to.shape
    share = qkv_ref.shape[0]
    width = qkv_ref.shape[1] // 3
    sh = triple // 3
    for j in range(n):
        for t in range(3):
            first = t * width + HD * low[j]
            qkv_to[j, :share, t * sh : (t + 1) * sh] = qkv_ref[:, first : first + sh]
        if padded > share:
            qkv_to[j, share:] = jnp.zeros((padded - share, triple), BF16)


def lay_rows(low, out_ref, out_to):
    share = out_ref.shape[0]
    sh, full = out_to.shape
    n = len(low)
    h = lax.axis_index("shard")
    offset = 0
    for j in range(n):
        offset = offset + jnp.where(h == j, j * share - HD * low[j], 0)
    rows = with_gaps(out_ref[...].astype(F32), n, full // n)
    rows = jnp.concatenate([rows, jnp.zeros((sh - share, full), F32)], axis=0)
    out_to[...] = pltpu.roll(rows, offset, 0).astype(BF16)


def lay_widen(j, widen_ref, widen_to):
    n, padded, hide_full = widen_to.shape
    share, hidden = widen_ref.shape
    hide = hidden // n
    widen_to[j, :share, :hide] = widen_ref[:, j * hide : (j + 1) * hide]
    if hide_full > hide:
        widen_to[j, :share, hide:] = jnp.zeros((share, hide_full - hide), BF16)
    if padded > share:
        widen_to[j, share:] = jnp.zeros((padded - share, hide_full), BF16)


def lay_narrow(first, size, n, narrow_ref, narrow_to):
    rows = slice(first, first + size)
    narrow_to[rows] = with_gaps(narrow_ref[rows], n, narrow_to.shape[1] // n)


def spread_vectors(n, low, width, pack_all, feats_to, qkv_bias, widen_bias):
    h = lax.axis_index("shard")
    sh = qkv_bias.shape[2] // 3
    share = width // n
    padded = feats_to.shape[2] // n
    for layer in range(2):
        pieces = [pack_all[layer, j] for j in range(n)]
        feats_to[layer] = jnp.concatenate([m[:, :padded] for m in pieces], axis=1).astype(F32)
        bias = jnp.concatenate([m[6:7, : 2 * share] for m in pieces], axis=1).astype(F32)
        found = jnp.zeros((1, 2 * sh), F32)
        wide = jnp.zeros((1, widen_bias.shape[2]), F32)
        for j in range(n):
            first = HD * low[j]
            spots = [bias[:, k * width + first : k * width + first + sh] for k in range(2)]
            found = jnp.where(h == j, jnp.concatenate(spots, axis=1), found)
            own = pieces[j][7:8, : wide.shape[1]].astype(F32)
            wide = jnp.where(h == j, own, wide)
        qkv_bias[layer] = jnp.concatenate(
            [found[:, :sh], jnp.zeros((1, sh), F32), found[:, sh:]], axis=1
        )
        widen_bias[layer] = wide


def feed_forward(low_all, widen, narrow, widen_bias, pre_to, hidden_to, part_to):
    def block(first, size):
        rows = pl.ds(first, size)
        weight = widen[...].reshape(low_all.shape[1], widen.shape[2])
        pre = dot_n(low_all[rows], weight) + widen_bias
        pre_to[rows] = pre
        hidden = (0.5 * pre * (1.0 + gelu_parts(pre)[0])).astype(BF16)
        hidden_to[rows] = hidden
        part_to[rows] = dot_n(hidden, narrow[...]).astype(BF16)

    row_blocks(low_all.shape[0], block)


def open_kernel(n, low, width, slots, step, io, *refs):
    tok_ref, cot_ref, vectors, refs = refs[0], refs[1], refs[2:10], refs[10:]
    qkv_ref, out_ref, widen_ref, narrow_ref, mask, order_ref = refs[:6]
    refs = refs[6:]
    x_to, cot_to, grad_to, sums_to, normed_to, own_ref, qkv_all, out_all = refs[:8]
    feats_to, qkv_bias, widen_bias, att_ref, low_ref, lse_ref, oth_ref, widen_all = refs[8:16]
    value_to, tok_all, pre_to, hidden_to, part_to, narrow_all, kpos_ref, qpos_ref = refs[16:24]
    refs = refs[24:]
    tok_own, pack, qkv_send, out_rows, widen_raw, narrow_raw, widen_send, narrow_to = refs[:8]
    pack_all, widen, refs = refs[8], refs[9], refs[10:]
    g_ss, g_rs, g_ls, p_ss, p_rs, a_ss, a_rs, w_ss, w_rs, o_ss, o_rs, l_sem = refs[:12]
    kv_ss, kv_rs, n_ss, n_rs, refs = refs[12], refs[13], refs[14], refs[15], refs[16:]
    scatter_refs, (second_ss, second_rs, second_ls) = refs[:5], refs[5:]
    p = Place(n)
    s, c, h = p.s, p.c, p.h
    widen_load = fetch(widen_ref, widen_raw, l_sem.at[4])
    narrow_load = fetch(narrow_ref, narrow_raw, l_sem.at[5])
    padded = qkv_send.shape[1]
    tok_own[...] = with_gaps(tok_ref[s], n, padded)
    greet_all(p)

    def pack_copy(a, b):
        target = (lax.rem(s + a, 2), c, lax.rem(h + b, n))
        return remote(pack, pack_all.at[s, h], p_ss.at[a, b], p_rs.at[a, b], target)

    tokens = Gather(p, tok_own, tok_all, g_ss, g_rs, g_ls)
    qkv = Spread(p, qkv_send, qkv_all, a_ss, a_rs, l_sem.at[1])
    wide = Spread(p, widen_send, widen_all, w_ss, w_rs, l_sem.at[3])
    narrow = RowSwap(p, narrow_to, narrow_all, n_ss, n_rs, l_sem.at[6])
    out = RowSwap(p, out_rows, out_all, o_ss, o_rs, l_sem.at[2])
    pack_own = pltpu.make_async_copy(pack, pack_all.at[s, h], l_sem.at[0])
    tokens.start()
    io.need(10)
    lay_first(low, qkv_ref, qkv_send)
    qkv.start()
    lay_vectors(vectors, pack)
    for a, b in others(n):
        pack_copy(a, b).start()
    pack_own.start()

    def start_out():
        io.need(1, 11)
        lay_rows(low, out_ref, out_rows)
        out.start()

    def lay_places():
        size = tok_own.shape[0] // HALVES
        down = lax.broadcasted_iota(jnp.int32, (size, 1), 0)
        along = lax.broadcasted_iota(jnp.int32, (1, size), 1)
        found = []
        for part in range(2):
            core = 1 - c if part else c
            for half in range(HALVES):
                for j in range(n):
                    first = order_ref[core * n + j, half] * size
                    spot = ((part * HALVES + half) * n + j) * size
                    kpos_ref[spot : spot + size] = first + down
                    if not part:
                        found.append(first + along)
        qpos_ref[...] = jnp.concatenate(found, axis=1)

    def lay_cot():
        values = with_gaps(cot_ref[s], n, padded)
        cot_to[...] = values
        grad_to[...] = values.astype(F32)
        sums_to[...] = jnp.sum(grad_to[...], axis=0, keepdims=True)
        x_to[...] = tok_own[...].astype(F32)

    hide = narrow_ref.shape[0]
    work = [start_out, lay_places, widen_load.wait]
    work += [functools.partial(lay_widen, j, widen_raw, widen_send) for j in range(n)]
    work += [lay_cot, narrow_load.wait]
    work += [
        functools.partial(lay_narrow, first, min(208, hide - first), n, narrow_raw, narrow_to)
        for first in range(0, hide, 208)
    ]
    qkv_steps = qkv.steps()
    for token_step in tokens.steps():
        run_next(work)
        run_next(work)
        token_step()
        run_next(qkv_steps)
    for rest in work:
        rest()
    extra = narrow_to.shape[0] - hide
    if extra:
        narrow_to[hide:] = jnp.zeros((extra, n * padded), BF16)
    for member in range(2):
        if narrow_all.shape[1] > narrow_to.shape[0]:
            spare = (narrow_all.shape[1] - narrow_to.shape[0], n * padded)
            narrow_all[member, narrow_to.shape[0] :] = jnp.zeros(spare, BF16)
    tokens.finish()
    wide.start()
    pack_own.wait()
    for a, b in others(n):
        pack_copy(a, b).wait_recv()
    spread_vectors(n, low, width, pack_all, feats_to, qkv_bias, widen_bias)

    normed = part_to

    def first_norm(first, size):
        some = pl.ds(first, size)
        unit = unit_rows(tok_all[some].astype(F32), mask[...], width)[0]
        normed[some] = (unit * feats_to[0, 0:1] + feats_to[0, 1:2]).astype(BF16)

    rows = tok_all.shape[0]
    row_blocks(rows, first_norm)
    normed_store = fetch(normed, normed_to, l_sem.at[7])
    for rest in qkv_steps:
        rest()
    qkv.finish()
    narrow.start()
    io.done(6)
    sh = slots * HD

    def project(first, size):
        some = pl.ds(first, size)
        weight = qkv_all[0].reshape(n * padded, 3 * sh)
        own_ref[some] = (dot_n(normed[some], weight) + qkv_bias[0]).astype(BF16)

    row_blocks(rows, project)
    swap = remote(own_ref.at[:, pl.ds(sh, 2 * sh)], oth_ref, kv_ss, kv_rs, p.sibling)
    swap.start()
    swap.wait_recv()
    out.step()
    wide_steps = wide.steps()
    chunk = attention(slots, step, own_ref, oth_ref, kpos_ref, qpos_ref, att_ref, low_ref, lse_ref)
    in_blocks(rows, step, chunk, [])
    out.finish()
    io.done(5, 7, 11, 12, 14)
    normed_store.wait()

    def give(first, size):
        some = pl.ds(first, size)
        part_to[some] = dot_n(low_ref[some], out_all[0]).astype(BF16)

    row_blocks(rows, give)

    scatter = Scatter(p, part_to, *scatter_refs)
    scatter.start()
    arrivals, crossings = wide_steps[: p.zn], wide_steps[p.zn :]
    early = len(arrivals) // 2
    for arrive in arrivals[:early]:
        arrive()
    second = Gather(p, tok_own, tok_all, second_ss, second_rs, second_ls)
    hr = tok_own.shape[0] // HALVES

    def rows_step(half):
        some = slice(half * hr, (half + 1) * hr)
        value = x_to[some] + (scatter.result(half) + feats_to[0, 2:3])
        value_to[some] = value
        unit = unit_rows(value, mask[...], width)[0]
        tok_own[some] = (unit * feats_to[0, 3:4] + feats_to[0, 4:5]).astype(BF16)

    by_halves(scatter, None, lambda half: None, [])
    for arrive in arrivals[early:]:
        arrive()
    for half in range(HALVES):
        rows_step(half)
        second.start([half])
    for second_step in second.steps():
        second_step()
    narrow.step()
    for crossing in crossings:
        crossing()
    second.finish()
    scatter.finish()
    for a, b in others(n):
        pack_copy(a, b).wait_send()
    swap.wait_send()
    narrow.finish()
    wide.finish()
    load = fetch(widen_all.at[0], widen, l_sem.at[4])
    io.done(17, 21)
    load.wait()
    feed_forward(tok_all, widen, narrow_all.at[0], widen_bias[0], pre_to, hidden_to, part_to)


def open_call(n, low, slots, padded, tokens, cotangent, vectors, weights, mask, order):
    qkv, out, widen, narrow = weights
    share, hidden = widen.shape
    width = n * share
    hide = hidden // n
    hide_full = -(-hide // 128) * 128
    sh = slots * HD
    full = n * padded
    rows = tokens.shape[1]
    total = n * rows
    zn = n // 2
    lanes = max(hide_full, -(-2 * share // 128) * 128)
    blocks = (n, padded, 3 * sh)
    wide = (n, padded, hide_full)

    def low_type(*shape):
        return jax.ShapeDtypeStruct(shape, BF16)

    def full_type(*shape):
        return jax.ShapeDtypeStruct(shape, F32)

    return staged_call(
        functools.partial(open_kernel, n, low, width, slots, min(total, 256)),
        "open",
        0,
        (tokens, cotangent, *vectors, qkv, out, widen, narrow, mask, order),
        [
            full_type(rows, full),
            low_type(rows, full),
            full_type(rows, full),
            full_type(1, full),
            low_type(total, full),
            low_type(total, 3 * sh),
            low_type(2, *blocks),
            low_type(2, sh, full),
            full_type(2, 16, full),
            full_type(2, 1, 3 * sh),
            full_type(2, 1, hide_full),
            full_type(sh, total),
            low_type(total, sh),
            full_type(slots, total),
            low_type(total, 2 * sh),
            low_type(2, *wide),
            full_type(rows, full),
            low_type(total, full),
            full_type(total, hide_full),
            low_type(total, hide_full),
            low_type(total, full),
            low_type(2, hide_full, full),
            jax.ShapeDtypeStruct((2 * total, 1), jnp.int32),
            jax.ShapeDtypeStruct((1, total), jnp.int32),
        ],
        [
            pltpu.VMEM((rows, full), BF16),
            pltpu.VMEM((16, lanes), BF16),
            pltpu.VMEM(blocks, BF16),
            pltpu.VMEM((sh, full), BF16),
            pltpu.VMEM(widen.shape, BF16),
            pltpu.VMEM(narrow.shape, BF16),
            pltpu.VMEM(wide, BF16),
            pltpu.VMEM((-(-hide // 16) * 16, full), BF16),
            pltpu.VMEM((2, n, 16, lanes), BF16),
            pltpu.VMEM(wide, BF16),
        ]
        + gather_scratch(n)
        + [DMA((2, n))] * 2
        + [DMA((4, zn))] * 4
        + [DMA((2,))] * 2
        + [DMA((8,)), DMA, DMA, DMA((2,)), DMA((2,))]
        + scatter_scratch(n, rows, full)
        + gather_scratch(n),
        late=(1, 10, 11),
        plain=(12, 13),
        early=(5, 6, 7, 11, 12, 14, 17, 18, 19, 20, 21),
        raw=(4, 15),
        scalars=(15,),
    )


def settle_kernel(low, sizes, *refs):
    sources, vec_ref, came_ref, streams, refs = refs[:4], refs[4], refs[5], refs[6:10], refs[10:]
    outs, stream_to, vectors, refs = refs[:4], refs[4:6], refs[6:14], refs[14:]
    loaded, made, came, in_sem, out_sem = refs[:4], refs[4:8], refs[8], refs[9], refs[10]
    qkv_ref, widen_ref, out_ref, narrow_ref = loaded
    qkv_to, widen_to, out_to, narrow_to = made
    order = (3, 1, 0, 2)
    loads = {i: fetch(sources[i], loaded[i], in_sem.at[i]) for i in order}
    came_load = fetch(came_ref, came, in_sem.at[4])
    n, padded, _ = widen_ref.shape
    share = out_to.shape[0]
    hide = narrow_to.shape[0]
    width = qkv_to.shape[1] // 3
    sh = qkv_ref.shape[2] // 3
    s = lax.axis_index("section")

    def without_gaps(values):
        pieces = [values[:, j * padded : j * padded + share] for j in range(n)]
        return jnp.concatenate(pieces, axis=1)

    def lay_rows_back(ref, to, rows):
        to[rows] = without_gaps(ref[rows]).astype(F32)

    def lay_qkv_back(rows):
        qkv_to[rows] = jnp.zeros((rows.stop - rows.start, 3 * width), F32)
        for j in range(n):
            for t in range(3):
                first = t * width + HD * low[j]
                block = qkv_ref[j, rows, t * sh : (t + 1) * sh]
                qkv_to[rows, first : first + sh] += block.astype(F32)

    def lay_widen_back(rows):
        pieces = [widen_ref[j, rows, :hide] for j in range(n)]
        widen_to[rows] = jnp.concatenate(pieces, axis=1).astype(F32)

    makers = (
        lay_qkv_back,
        lay_widen_back,
        functools.partial(lay_rows_back, out_ref, out_to),
        functools.partial(lay_rows_back, narrow_ref, narrow_to),
    )
    stores = []
    for i in order:
        loads[i].wait()
        count = made[i].shape[0]
        middle = (count // 2 + 15) // 16 * 16 if count % 8 == 0 else count
        for x, (start, stop) in enumerate(((0, middle), (middle, count))):
            if stop > start:
                makers[i](slice(start, stop))
                part = pl.ds(start, stop - start)
                stores.append(fetch(made[i].at[part], outs[i].at[part], out_sem.at[2 * i + x]))
    came_load.wait()
    for item, to in enumerate(stream_to):
        first, second = (ref[...] for ref in streams[2 * item : 2 * item + 2])
        to[s] = without_gaps(jnp.where(s == 0, first, second))
        to[1 - s] = without_gaps(came[item].astype(F32))
    for row, (size, to) in enumerate(zip(sizes, vectors)):
        to[...] = vec_ref[row : row + 1, :size]
    for store in stores:
        store.wait()


def settle_call(low, share, hide, qkv, widen, out, narrow, vec, came, *streams):
    n = widen.shape[0]
    width = n * share
    rows = came.shape[1]
    sizes = [share] * 6 + [2 * share, hide]
    big = [(share, 3 * width), (share, n * hide), (share, width), (hide, width)]
    return pl.pallas_call(
        functools.partial(settle_kernel, low, sizes),
        out_shape=[jax.ShapeDtypeStruct(shape, F32) for shape in big]
        + [
            jax.ShapeDtypeStruct((2, rows, width), F32),
            jax.ShapeDtypeStruct((2, rows, width), F32),
        ]
        + [jax.ShapeDtypeStruct((1, size), F32) for size in sizes],
        in_specs=[ANY_SPEC] * 4 + [VMEM_SPEC, ANY_SPEC] + [VMEM_SPEC] * 4,
        out_specs=[ANY_SPEC] * 4 + [VMEM_SPEC] * 10,
        scratch_shapes=[pltpu.VMEM(m.shape, BF16) for m in (qkv, widen, out, narrow)]
        + [pltpu.VMEM(shape, F32) for shape in big]
        + [pltpu.VMEM(came.shape, BF16), DMA((5,)), DMA((8,))],
        compiler_params=params(),
        name="settle",
    )(qkv, widen, out, narrow, vec, came, *streams)


def unit_rows(values, mask, width):
    center = (values - jnp.sum(values, axis=-1, keepdims=True) * (1.0 / width)) * mask
    spread = jnp.sum(center * center, axis=-1, keepdims=True) * (1.0 / width)
    scale = lax.rsqrt(spread + EPSILON)
    return center * scale, scale


def norm_back(grad, unit, scale, gain, width):
    inner = grad * gain
    mean = jnp.sum(inner, axis=-1, keepdims=True) * (1.0 / width)
    along = jnp.sum(inner * unit, axis=-1, keepdims=True) * (1.0 / width)
    return (inner - mean - unit * along) * scale


def forward_kernel(n, width, layer, io, *refs):
    middle = layer is not None
    part, base, feats, mask = refs[:4]
    refs = refs[4:]
    if middle:
        bias, gain, shift = (feats[layer, row : row + 1] for row in (2, 3, 4))
        widen, narrow, widen_bias, refs = refs[0], refs[1], refs[2], refs[3:]
    else:
        bias, gain, shift = feats[0, 5:6], feats[1, 0:1], feats[1, 1:2]
    value_to, low_all, refs = refs[0], refs[1], refs[2:]
    if middle:
        pre_to, hidden_to, part_to, refs = refs[0], refs[1], refs[2], refs[3:]
    own, g_ss, g_rs, g_ls = refs[5:9]
    p = Place(n)
    enter(io, p, line=True)
    scatter = Scatter(p, part, *refs[:5])
    scatter.start()
    gather = Gather(p, own, low_all, g_ss, g_rs, g_ls)
    hr = own.shape[0] // HALVES

    def rows_step(half):
        rows = slice(half * hr, (half + 1) * hr)
        value = base[rows] + (scatter.result(half) + bias)
        value_to[rows] = value
        own[rows] = (unit_rows(value, mask[...], width)[0] * gain + shift).astype(BF16)

    by_halves(scatter, gather, rows_step, [])
    gather.finish()
    if middle:
        io.done(1)
        io.need(4, 5)
        feed_forward(low_all, widen, narrow, widen_bias[layer], pre_to, hidden_to, part_to)
    scatter.finish()


def scatter_scratch(n, rows, full):
    zn = n // 2
    piece = (HALVES, rows // HALVES, full)
    return [
        pltpu.VMEM((zn,) + piece, BF16),
        pltpu.VMEM((zn + 1,) + piece, BF16),
        pltpu.VMEM((zn,) + piece, BF16),
        DMA((4, zn, HALVES)),
        DMA((4, zn, HALVES)),
    ]


def gather_scratch(n):
    zn = n // 2
    return [DMA((4, zn, HALVES)), DMA((4, zn, HALVES)), DMA((HALVES,))]


def forward_step(n, collective_id, width, part, *local, layer=None, feed=()):
    total_rows, full = part.shape
    rows = total_rows // n
    shapes = [
        jax.ShapeDtypeStruct((rows, full), F32),
        jax.ShapeDtypeStruct((total_rows, full), BF16),
    ]
    scratch = scatter_scratch(n, rows, full)
    scratch += [pltpu.VMEM((rows, full), BF16)] + gather_scratch(n)
    middle = layer is not None
    if middle:
        widen, narrow, _ = feed
        hide = widen.shape[3]
        shapes += [
            jax.ShapeDtypeStruct((total_rows, hide), F32),
            jax.ShapeDtypeStruct((total_rows, hide), BF16),
            jax.ShapeDtypeStruct((total_rows, full), BF16),
        ]
    return Step(
        functools.partial(forward_kernel, n, width, layer),
        "forward_rows",
        collective_id,
        (part, *local, *feed),
        shapes,
        scratch,
        dict(line=True),
        late=(4, 5) if middle else (),
        layers={4: layer, 5: layer} if middle else {},
        early=(1, 2, 3, 4) if middle else (),
        raw=() if middle else (1,),
    )


def back_rows(scatter, half, base, grad, gain, mask, width):
    hr = scatter.hr
    rows = slice(half * hr, (half + 1) * hr)
    total = scatter.result(half)
    unit, scale = unit_rows(base[rows], mask[...], width)
    value = grad[rows] + norm_back(total, unit, scale, gain, width)
    low = value.astype(BF16)
    terms = (total * unit, total, low.astype(F32))
    return rows, value, low, [jnp.sum(term, axis=0, keepdims=True) for term in terms]


def resid_kernel(n, width, layer, io, *refs):
    base, grad, feats, mask, normed, hidden_pre, hidden, outs, widen, narrow = refs[:10]
    gain = feats[layer, 3:4]
    value_to, sums_to, low_all, wide_to, wide_came, slim_to, pre_sums = refs[10:17]
    refs = refs[17:]
    own, g_ss, g_rs, g_ls = refs[5:9]
    wide, wide_in, wide_ss, wide_rs, slim, slim_in, slim_ss, slim_rs, x_ss, x_rs = refs[9:19]
    part, pre = refs[19:]
    p = Place(n)
    enter(io, p, line=True, over=True, sibling=True)
    io.need(9, 7, 5)

    def inner(first, size):
        rows = pl.ds(first, size)
        values = hidden_pre[rows]
        act, square = gelu_parts(values)
        slope = 0.5 * (1.0 + act) + 0.5 * values * (1.0 - act * act) * GELU_A * (
            1.0 + 3.0 * GELU_B * square
        )
        found = (dot_t(outs[rows], narrow[...]) * slope).astype(BF16)
        pre[rows] = found

    def outer(first, size):
        rows = pl.ds(first, size)
        weight = widen[...].reshape(part.shape[1], widen.shape[2])
        part[rows] = dot_t(pre[rows], weight).astype(BF16)

    row_blocks(part.shape[0], inner)
    io.need(8)
    row_blocks(part.shape[0], outer)
    scatter = Scatter(p, part, *refs[:5])
    scatter.start()
    gather = Gather(p, own, low_all, g_ss, g_rs, g_ls)
    wide_fold = Fold(p, wide, wide_in, wide_to, wide_ss, wide_rs)
    slim_fold = Fold(p, slim, slim_in, slim_to, slim_ss, slim_rs)
    cross = Cross(p, wide_to, wide_came, x_ss, x_rs, 1 - layer)

    def pre_sum():
        pre_sums[...] = jnp.sum(pre[...].astype(F32), axis=0, keepdims=True)

    io.need(4, 6)
    for step in product(normed, pre, wide):
        step()
    wide_fold.start()

    def wide_done():
        cross.start()
        io.done(3)

    work = product(hidden, outs, slim) + wide_fold.steps() + [wide_done, slim_fold.start, pre_sum]
    work += slim_fold.steps() + [functools.partial(io.done, 5)]
    sums = []

    def rows_step(half):
        rows, value, low, terms = back_rows(scatter, half, base, grad, gain, mask, width)
        value_to[rows] = value
        own[rows] = low
        sums.append(jnp.concatenate(terms, axis=0))

    by_halves(scatter, gather, rows_step, work, 3)
    sums_to[...] = sum(sums)
    for rest in work:
        rest()
    gather.finish()
    scatter.finish()
    for job in (wide_fold, slim_fold, cross):
        job.finish()


def resid_step(n, collective_id, width, layer, hide, *args):
    base, normed, hidden = args[0], args[4], args[6]
    rows = base.shape[0]
    total_rows, full = normed.shape
    zn = n // 2
    wide = (zn, full // n, hidden.shape[1])
    half = -(-hide // 32) * 16
    slim = (1, half, full)
    return Step(
        functools.partial(resid_kernel, n, width, layer),
        "back_resid",
        collective_id,
        args,
        [
            jax.ShapeDtypeStruct((rows, full), F32),
            jax.ShapeDtypeStruct((3, full), F32),
            jax.ShapeDtypeStruct((total_rows, full), BF16),
            jax.ShapeDtypeStruct(wide, BF16),
            jax.ShapeDtypeStruct(wide, BF16),
            jax.ShapeDtypeStruct(slim, BF16),
            jax.ShapeDtypeStruct((1, hidden.shape[1]), F32),
        ],
        scatter_scratch(n, rows, full)
        + [pltpu.VMEM((rows, full), BF16)]
        + gather_scratch(n)
        + fold_scratch((full, hidden.shape[1]), wide)
        + fold_scratch((2 * half, full), slim)
        + [DMA, DMA]
        + [
            pltpu.VMEM((total_rows, full), BF16),
            pltpu.VMEM(hidden.shape, BF16),
        ],
        dict(line=True, over=True, sibling=True),
        late=(9, 7, 5, 8, 4, 6),
        layers={8: layer, 9: layer},
        early=(3, 5),
        raw=(2, 4),
    )


def input_kernel(n, width, source, low, io, *refs):
    part, base, grad, feats, mask, normed, triple, att, resid, slim = refs[:10]
    gain = feats[1, 0:1]
    value_to, sums_to, low_all, qkv_to, out_to, slim_came, triple_sums = refs[10:17]
    refs = refs[17:]
    own, g_ss, g_rs, g_ls = refs[5:9]
    qkv, qkv_in, qkv_ss, qkv_rs, out, out_in, out_ss, out_rs, x_ss, x_rs = refs[9:]
    p = Place(n)
    enter(io, p, line=True, over=True, sibling=True)
    scatter = Scatter(p, part, *refs[:5])
    scatter.start()
    cross = Cross(p, slim, slim_came, x_ss, x_rs, source)
    cross.start()
    gather = Gather(p, own, low_all, g_ss, g_rs, g_ls)
    qkv_fold = Fold(p, qkv, qkv_in, qkv_to, qkv_ss, qkv_rs)
    out_fold = Fold(p, out, out_in, out_to, out_ss, out_rs)

    def triple_sum():
        triple_sums[...] = jnp.sum(triple[...].astype(F32), axis=0, keepdims=True)

    work = [functools.partial(io.need, 5, 6)] + product(normed, triple, qkv)
    work += [qkv_fold.start, functools.partial(io.need, 7, 8)]
    work += [functools.partial(home_rows, att, resid, out, low, width // n), out_fold.start]
    work += qkv_fold.steps() + [functools.partial(io.done, 3), triple_sum]
    work += out_fold.steps() + [functools.partial(io.done, 4)]
    sums = []

    def rows_step(half):
        rows, value, lower, terms = back_rows(scatter, half, base, grad, gain, mask, width)
        value_to[rows] = value
        own[rows] = lower
        sums.append(jnp.concatenate(terms, axis=0))

    by_halves(scatter, gather, rows_step, work, 2)
    sums_to[...] = sum(sums)
    for rest in work:
        rest()
    gather.finish()
    scatter.finish()
    for job in (qkv_fold, out_fold, cross):
        job.finish()


def input_step(n, collective_id, width, source, low, part, base, grad, feats, mask, *operands):
    normed, triple, att, resid, slim = operands
    total_rows, full = part.shape
    rows = total_rows // n
    zn = n // 2
    qkv = (zn, full // n, triple.shape[1])
    out = (1, att.shape[1] // 2, full)
    return Step(
        functools.partial(input_kernel, n, width, source, low),
        "back_input",
        collective_id,
        (part, base, grad, feats, mask) + operands,
        [
            jax.ShapeDtypeStruct((rows, full), F32),
            jax.ShapeDtypeStruct((3, full), F32),
            jax.ShapeDtypeStruct((total_rows, full), BF16),
            jax.ShapeDtypeStruct(qkv, BF16),
            jax.ShapeDtypeStruct(out, BF16),
            jax.ShapeDtypeStruct(slim.shape, BF16),
            jax.ShapeDtypeStruct((1, triple.shape[1]), F32),
        ],
        scatter_scratch(n, rows, full)
        + [pltpu.VMEM((rows, full), BF16)]
        + gather_scratch(n)
        + fold_scratch((full, triple.shape[1]), qkv)
        + fold_scratch((att.shape[1], full), out)
        + [DMA, DMA],
        dict(line=True, over=True, sibling=True),
        late=(5, 6, 7, 8),
        plain=(9,),
        early=(3, 4),
        raw=(2, 5),
    )


def finale_kernel(n, width, low, between, io, *refs):
    part, base, grad, feats, mask, normed, triple, att, resid = refs[:9]
    slims, slim_came, qkv_far, out_far, vecs = refs[9:11], refs[11], refs[12], refs[13], refs[14:21]
    layer_outs, upper_d_in, wides, refs = refs[21:23], refs[23], refs[24:28], refs[28:]
    value_to, slim_to, qkv_to, out_to, vec_to, streams_to, wide_to = refs[:7]
    refs = refs[7:]
    qkv, qkv_fold_in, qkv_ss, qkv_rs, out, out_fold_in, out_ss, out_rs = refs[5:13]
    qkv_own, qkv_in, qkv_sum, out_own, out_in, out_sum = refs[13:19]
    slim_sum, slim_pair, vec, vec_in, vec_sum, vec_sib, streams = refs[19:26]
    a_ss, a_rs, x_ss, x_rs, v_ss, v_rs, r_ss, r_rs, ls = refs[26:35]
    wide_sum, wide_pair, w_ss, w_rs = refs[35:]
    p = Place(n)
    s, c, h, z, zn = p.s, p.c, p.h, p.z, p.zn
    share = width // n
    greet_all(p)
    choices = (
        (
            (wides[0], wide_pair.at[0], 5),
            (wides[1], wide_pair.at[1], 6),
            (slims[0], slim_pair.at[0], 1),
        ),
        (
            (wides[2], wide_pair.at[0], 5),
            (wides[3], wide_pair.at[1], 6),
            (slims[1], slim_pair.at[0], 1),
            (slim_came, slim_pair.at[1], 4),
        ),
    )
    for section, chosen in enumerate(choices):

        @pl.when(s == section)
        def _():
            for src, dst, item in chosen:
                pltpu.make_async_copy(src, dst, ls.at[item]).start()

    def chosen_wait(item):
        src, dst, sem = choices[1][item]
        pltpu.make_async_copy(src, dst, ls.at[sem]).wait()

    count = slims[0].shape[1]
    first = count * 3 // 5 // 16 * 16

    def slim_rows(item, start, size):
        rows = pl.ds(start, size)
        sems = (x_ss.at[zn + 2 + item], x_rs.at[zn + 2 + item])
        return Cross(p, slims[0].at[:, rows], slim_pair.at[1, :, rows], *sems, 1)

    slim_crosses = (slim_rows(0, 0, first), slim_rows(1, first, count - first))
    slim_crosses[0].start()
    wide_back = Home(p, wide_sum, wide_to, w_ss, w_rs, ls.at[8])
    chosen_wait(0)
    chosen_wait(1)
    for k in list(range(1, zn)) + [0]:
        far = p.flip(k)
        total = wide_pair[0, far].astype(F32) + wide_pair[1, far].astype(F32)
        wide_sum[far] = total.astype(BF16)
        wide_back.start(k)
    leave = between() if between is not None else None
    scatter = Scatter(p, part, *refs[:5])
    back = Home(p, qkv_sum, qkv_to, a_ss, a_rs, ls.at[0])

    def x_block(k, src=qkv_far):
        far = p.flip(k)
        return remote(src.at[far], qkv_in.at[far], x_ss.at[k], x_rs.at[k], p.over)

    def out_cross(src=out_far):
        return remote(src, out_in, x_ss.at[zn], x_rs.at[zn], p.over)

    stream_cross = remote(streams, streams_to, x_ss.at[zn + 1], x_rs.at[zn + 1], p.over)

    def start_far():
        @pl.when(s == 0)
        def _():
            for k in range(zn):
                x_block(k).start()
            out_cross().start()

    def start_own(k):
        @pl.when(s == 1)
        def _():
            x_block(k, qkv_own).start()

    def start_own_out():
        @pl.when(s == 1)
        def _():
            out_cross(out_own).start()

    qkv_fold = Fold(p, qkv, qkv_fold_in, qkv_own, qkv_ss, qkv_rs)
    out_fold = Fold(p, out, out_fold_in, out_own, out_ss, out_rs)

    io.need(12, 13)
    start_far()
    io.need(5, 6)
    for step in product(normed, triple, qkv):
        step()
    qkv_fold.start()
    if leave is not None:
        leave()
    scatter.start()
    io.need(7, 8)
    work = [functools.partial(home_rows, att, resid, out, low, share), out_fold.start]
    work += qkv_fold.steps()
    work += [functools.partial(start_own, k) for k in list(range(1, zn)) + [0]]
    work += out_fold.steps() + [start_own_out]
    sums = []

    def rows_step(half):
        rows, value, lower, terms = back_rows(scatter, half, base, grad, feats[0, 0:1], mask, width)
        value_to[rows] = value
        sums.append(jnp.concatenate(terms, axis=0))

    by_halves(scatter, None, rows_step, work, 3)
    for rest in work:
        rest()

    io.need(21, 22, 23)
    streams[0] = jnp.where(s == 0, layer_outs[1][...], layer_outs[0][...]).astype(BF16)
    streams[1] = jnp.where(s == 0, upper_d_in[...], value_to[...]).astype(BF16)
    io.done(0)
    stream_cross.start()

    ones = (sum(sums), vecs[0][...])
    twos, triples, pres = vecs[1:3], (None, vecs[3]), vecs[4:6]
    lanes = vec.shape[3]
    padded = base.shape[1] // n
    sh = triple.shape[1] // 3
    for layer in range(2):
        one, two = ones[layer], twos[layer][...]
        outs = vecs[6][...] if layer else ones[1][2:3]
        features = jnp.concatenate([one[0:2], two[2:3], two[0:2], outs], axis=0)
        if layer:
            found = triples[1][...]
        else:
            found = jnp.sum(triple[...].astype(F32), axis=0, keepdims=True)
        bias = jnp.zeros((1, 2 * width), F32)
        for j, first in enumerate(low):
            spots = []
            for begin in (0, 2 * sh):
                spots += [
                    jnp.zeros((1, HD * first), F32),
                    found[:, begin : begin + sh],
                    jnp.zeros((1, width - sh - HD * first), F32),
                ]
            spots = [spot for spot in spots if spot.shape[1]]
            bias = jnp.where(h == j, jnp.concatenate(spots, axis=1), bias)
        for i in range(n):
            pieces = [
                features[:, i * padded : (i + 1) * padded],
                bias[:, i * 2 * share : (i + 1) * 2 * share],
                jnp.where(h == i, pres[layer][...], 0.0),
            ]
            wide_pieces = []
            for piece in pieces:
                rows, size = piece.shape
                if size < lanes:
                    piece = jnp.concatenate([piece, jnp.zeros((rows, lanes - size), F32)], axis=1)
                wide_pieces.append(piece)
            vec[layer, i] = jnp.concatenate(wide_pieces, axis=0)

    def vec_copy(a, b):
        l, i = lax.rem(s + a, 2), lax.rem(h + b, n)
        return remote(vec.at[l, i], vec_in.at[s, h], v_ss.at[a, b], v_rs.at[a, b], (l, c, i))

    for a, b in others(n):
        vec_copy(a, b).start()

    for k in list(range(1, zn)) + [0]:
        x_block(k).wait_recv()
        add_home(p, qkv_sum, p.flip(k), qkv_own, qkv_in, qkv_far, qkv_in)
        back.start(k)
    out_cross().wait_recv()
    add_home(p, out_sum, 0, out_own, out_in, out_far, out_in)
    for k in range(zn):
        x_block(k).wait_send()
    slim_crosses[1].start()
    chosen_wait(2)

    @pl.when(s == 1)
    def _():
        chosen_wait(3)

    for step in wide_back.steps():
        step()
    for cross in slim_crosses:
        cross.finish()
    slim_sum[0] = (slim_pair[0, 0].astype(F32) + slim_pair[1, 0].astype(F32)).astype(BF16)

    def row_copies(w, src, dst):
        half = src.shape[1]
        piece = dst.at[pl.ds(pl.multiple_of(c * half, 16), half)]
        return (
            pltpu.make_async_copy(src.at[0], piece, ls.at[2 + w]),
            remote(src.at[0], piece, r_ss.at[w], r_rs.at[w], p.sibling),
        )

    copies = row_copies(0, slim_sum, slim_to) + row_copies(1, out_sum, out_to)
    for copy in copies:
        copy.start()
    total = vec[s, h]
    for a, b in others(n):
        vec_copy(a, b).wait_recv()
        total = total + vec_in[lax.rem(s + a, 2), lax.rem(h + n - b, n)]
    vec_sum[...] = total
    vec_share = remote(vec_sum, vec_sib, r_ss.at[2], r_rs.at[2], p.sibling)
    vec_share.start()
    for step in back.steps():
        step()
    vec_share.wait_recv()
    vec_to[...] = total + vec_sib[...]
    vec_share.wait_send()
    back.finish()
    wide_back.finish()
    for w in range(2):
        copies[2 * w].wait()
        copies[2 * w + 1].wait_recv()
        copies[2 * w + 1].wait_send()
    for a, b in others(n):
        vec_copy(a, b).wait_send()
    out_cross().wait_send()
    stream_cross.wait_recv()
    stream_cross.wait_send()
    for job in (scatter, qkv_fold, out_fold):
        job.finish()


def finale_parts(n, *args):
    part, triple, att = args[0], args[6], args[7]
    slim, lanes, wide = args[9].shape, args[18].shape[1], args[24].shape
    total_rows, full = part.shape
    rows = total_rows // n
    zn = n // 2
    qkv = (zn, full // n, triple.shape[1])
    out = (1, att.shape[1] // 2, full)
    shapes = [
            jax.ShapeDtypeStruct((rows, full), F32),
            jax.ShapeDtypeStruct((2 * slim[1], full), BF16),
            jax.ShapeDtypeStruct((n,) + qkv[1:], BF16),
            jax.ShapeDtypeStruct((2 * out[1], full), BF16),
            jax.ShapeDtypeStruct((8, lanes), F32),
            jax.ShapeDtypeStruct((2, rows, full), BF16),
            jax.ShapeDtypeStruct((n,) + wide[1:], BF16),
        ]
    scratch = (
        scatter_scratch(n, rows, full)
        + fold_scratch((full, triple.shape[1]), qkv)
        + fold_scratch((att.shape[1], full), out)
        + [pltpu.VMEM(qkv, BF16)] * 3
        + [pltpu.VMEM(out, BF16)] * 3
        + [
            pltpu.VMEM(slim, BF16),
            pltpu.VMEM((2,) + slim, BF16),
            pltpu.VMEM((2, n, 8, lanes), F32),
            pltpu.VMEM((2, n, 8, lanes), F32),
            pltpu.VMEM((8, lanes), F32),
            pltpu.VMEM((8, lanes), F32),
            pltpu.VMEM((2, rows, full), BF16),
            DMA((2, zn)),
            DMA((2, zn)),
            DMA((zn + 4,)),
            DMA((zn + 4,)),
            DMA((2, n)),
            DMA((2, n)),
            DMA((3,)),
            DMA((3,)),
            DMA((9,)),
            pltpu.VMEM(wide, BF16),
            pltpu.VMEM((2,) + wide, BF16),
            DMA((2, zn)),
            DMA((2, zn)),
        ]
    )
    return shapes, scratch


def finale_call(n, collective_id, width, low, *args):
    shapes, scratch = finale_parts(n, *args)
    return staged_call(
        functools.partial(finale_kernel, n, width, low, None),
        "finale",
        collective_id,
        args,
        shapes,
        scratch,
        late=(5, 6, 7, 8, 12, 13, 21, 22, 23),
        plain=(9, 10, 11, 24, 25, 26, 27),
        early=(0,),
        raw=(1, 2, 3, 5, 6),
    )


def dot_t(a, b):
    return lax.dot_general(a, b, (((1,), (1,)), ((), ())), preferred_element_type=F32)


def dot_n(a, b):
    return lax.dot_general(a, b, (((1,), (0,)), ((), ())), preferred_element_type=F32)


def in_blocks(rows, step, chunk, between):
    count = rows // step
    if count <= 2:
        for b in range(count):
            chunk(b * step, rows // 2 if (b + 1) * step <= rows // 2 else rows, between)
    else:

        def body(b, carry, keys):
            chunk(pl.multiple_of(b * step, step), keys, [])
            return carry

        middle = count // 2 if count % 2 == 0 else 0
        lax.fori_loop(0, middle, functools.partial(body, keys=rows // 2), 0)
        lax.fori_loop(middle, count, functools.partial(body, keys=rows), 0)


def run_next(between):
    if between:
        between.pop(0)()


def attention(slots, step, own_ref, oth_ref, kpos_ref, qpos_ref, att_ref, low_ref, lse_ref):
    rows = own_ref.shape[0]
    sh = slots * HD
    power = HD**-0.5 * LOG2E

    def at(base, slot):
        return slice(base + slot * HD, base + (slot + 1) * HD)

    def chunk(first, seen, between):
        q_rows = pl.ds(first, step)
        qpos = qpos_ref[:, q_rows]
        for slot in range(slots):
            queries = own_ref[q_rows, at(0, slot)]
            keys = (own_ref[:seen, at(sh, slot)], oth_ref[:seen, at(0, slot)])
            values = (own_ref[:seen, at(2 * sh, slot)], oth_ref[:seen, at(sh, slot)])
            scores = []
            for part in range(2):
                allowed = kpos_ref[part * rows : part * rows + seen] <= qpos
                scores.append(jnp.where(allowed, dot_t(keys[part], queries), MASKED))
            top = jnp.maximum(
                jnp.max(scores[0], axis=0, keepdims=True), jnp.max(scores[1], axis=0, keepdims=True)
            )
            total = jnp.zeros_like(top)
            weighted = jnp.zeros((HD, step), F32)
            exps = []
            for part in range(2):
                e = jnp.exp2((scores[part] - top) * power)
                total = total + jnp.sum(e, axis=0, keepdims=True)
                exps.append(e)
            inverse = 1.0 / total
            for part in range(2):
                probs = (exps[part] * inverse).astype(BF16)
                weighted = weighted + dot_n(values[part].T, probs)
            att_ref[at(0, slot), q_rows] = weighted
            low_ref[q_rows, at(0, slot)] = weighted.T.astype(BF16)
            lse_ref[slot : slot + 1, q_rows] = top * power + jnp.log(total) * LOG2E
            run_next(between)

    return chunk


def attend_kernel(n, slots, step, layer, io, *refs):
    kpos_ref, qpos_ref, carried, out_all, normed, qkv_all, qkv_bias = refs[:7]
    att_ref, low_ref, lse_ref, oth_ref, part_to, carried_to, own_ref = refs[7:14]
    kv_ss, kv_rs, out_weight, qkv_weight, load_sems = refs[14:19]
    qkv_load = fetch(qkv_all.at[layer], qkv_weight, load_sems.at[1])
    out_load = fetch(out_all.at[layer], out_weight, load_sems.at[0])
    p = Place(n)
    rows = own_ref.shape[0]
    sh = slots * HD
    enter(io, p, line=True, sibling=True)
    job = Gather(p, carried, carried_to, *refs[19:])
    job.start()
    qkv_load.wait()
    io.need(4)
    between = job.steps()

    def project(first, size):
        some = pl.ds(first, size)
        weight = qkv_weight[...].reshape(normed.shape[1], 3 * sh)
        own_ref[some] = (dot_n(normed[some], weight) + qkv_bias[layer]).astype(BF16)

    row_blocks(rows, project)
    swap = remote(own_ref.at[:, pl.ds(sh, 2 * sh)], oth_ref, kv_ss, kv_rs, p.sibling)
    swap.start()
    run_next(between)
    run_next(between)
    swap.wait_recv()
    chunk = attention(slots, step, own_ref, oth_ref, kpos_ref, qpos_ref, att_ref, low_ref, lse_ref)
    in_blocks(rows, step, chunk, between)
    out_load.wait()

    def give(first, size):
        some = pl.ds(first, size)
        part_to[some] = dot_n(low_ref[some], out_weight[...]).astype(BF16)

    row_blocks(rows, give)
    io.done(0, 1, 4, 6)
    for rest in between:
        rest()
    swap.wait_send()
    job.finish()


def attend_step(n, collective_id, slots, layer, kpos, qpos, carried, out_all, *source):
    rows = qpos.shape[1]
    sh = slots * HD
    full = out_all.shape[2]
    return Step(
        functools.partial(attend_kernel, n, slots, min(rows, 256), layer),
        "attend",
        collective_id,
        (kpos, qpos, carried, out_all, *source),
        [
            jax.ShapeDtypeStruct((sh, rows), F32),
            jax.ShapeDtypeStruct((rows, sh), BF16),
            jax.ShapeDtypeStruct((slots, rows), F32),
            jax.ShapeDtypeStruct((rows, 2 * sh), BF16),
            jax.ShapeDtypeStruct((rows, full), BF16),
            jax.ShapeDtypeStruct((n * carried.shape[0], full), BF16),
            jax.ShapeDtypeStruct((rows, 3 * sh), BF16),
        ],
        [
            DMA,
            DMA,
            pltpu.VMEM((sh, full), BF16),
            pltpu.VMEM(source[1].shape[1:], BF16),
            DMA((2,)),
        ]
        + gather_scratch(n),
        dict(line=True, sibling=True),
        late=(4,),
        plain=(3, 5),
        early=(0, 1, 4, 6),
        raw=(5,),
    )


def attend_back_kernel(n, slots, step, layer, last, greeted, io, *refs):
    own_ref, oth_ref, resid, att_ref, lse_ref, kpos_ref, qpos_ref, out_all, qkv_all = refs[:9]
    refs = refs[9:]
    if last:
        part_ref, base_ref, feats = refs[:3]
        refs = refs[3:]
    triple_ref, part_to, refs = refs[0], refs[1], refs[2:]
    if last:
        value_ref, refs = refs[0], refs[1:]
    dq_t, dkv_own, dkv_oth, came, kv_ss, kv_rs = refs[:6]
    grad_ref, out_weight, qkv_weight, load_sems = refs[6:10]
    out_load = fetch(out_all.at[layer], out_weight, load_sems.at[0])
    qkv_load = fetch(qkv_all.at[layer], qkv_weight, load_sems.at[1])
    p = Place(n)
    rows = own_ref.shape[0]
    sh = slots * HD
    scale = HD**-0.5
    if not greeted:
        enter(io, p, line=last, sibling=True)
    between = []
    if last:
        scatter = Scatter(p, part_ref, *refs[10:])
        scatter.start()
        between = scatter.steps()
    io.need(2)
    out_load.wait()

    def begin(first, size):
        some = pl.ds(first, size)
        grad_ref[some] = dot_t(resid[some], out_weight[...]).astype(BF16)

    row_blocks(rows, begin)
    io.need(0, 1, 3)

    def at(base, slot):
        return slice(base + slot * HD, base + (slot + 1) * HD)

    dq_t[...] = jnp.zeros_like(dq_t)
    swap = remote(dkv_oth, came, kv_ss, kv_rs, p.sibling)
    for part in (1, 0):
        dkv = (dkv_own, dkv_oth)[part]
        src = (own_ref, oth_ref)[part]
        base = (sh, 0)[part]
        dkv[...] = jnp.zeros_like(dkv)

        def chunk(first, seen, between):
            q_rows = pl.ds(first, step)
            qpos = qpos_ref[:, q_rows]
            for slot in range(slots):
                queries = own_ref[q_rows, at(0, slot)]
                grads = grad_ref[q_rows, at(0, slot)]
                keys, values = src[:seen, at(base, slot)], src[:seen, at(base + sh, slot)]
                lse = lse_ref[slot : slot + 1, q_rows]
                correction = jnp.sum(
                    grads.astype(F32).T * att_ref[at(0, slot), q_rows], axis=0, keepdims=True
                )
                allowed = kpos_ref[part * rows : part * rows + seen] <= qpos
                scores = dot_t(keys, queries)
                probs = jnp.where(allowed, jnp.exp2(scores * (scale * LOG2E) - lse), 0.0)
                prob_grad = dot_t(values, grads)
                score_grad = (probs * (prob_grad - correction)).astype(BF16)
                dkv[:seen, at(0, slot)] += dot_n(score_grad, queries) * scale
                dkv[:seen, at(sh, slot)] += dot_n(probs.astype(BF16), grads)
                dq_t[at(0, slot), q_rows] += dot_n(keys.T, score_grad)
                run_next(between)

        in_blocks(rows, step, chunk, between)
        if part:
            swap.start()
    triple_ref[:, :sh] = (dq_t[...].T * scale).astype(BF16)

    def finish_last():
        for rest in between:
            rest()
        hr = base_ref.shape[0] // HALVES
        for half in range(HALVES):
            part_rows = slice(half * hr, (half + 1) * hr)
            total = scatter.result(half)
            value_ref[part_rows] = base_ref[part_rows] + (total + feats[1, 5:6])
        scatter.finish()

    swap.wait_recv()
    triple_ref[:, sh:] = (dkv_own[...] + came[...]).astype(BF16)
    qkv_load.wait()

    def leave(first, size):
        some = pl.ds(first, size)
        weight = qkv_weight[...].reshape(part_to.shape[1], 3 * sh)
        part_to[some] = dot_t(triple_ref[some], weight).astype(BF16)

    io.done(0)
    if greeted:
        swap.wait_send()
        return functools.partial(row_blocks, rows, leave)
    row_blocks(rows, leave)
    io.done(1)
    if last:
        finish_last()
    swap.wait_send()


def attend_back_scratch(rows, sh, full, qkv_all):
    scratch = [pltpu.VMEM((sh, rows), F32)] + [pltpu.VMEM((rows, 2 * sh), F32)] * 3
    scratch += [DMA, DMA]
    return scratch + [
        pltpu.VMEM((rows, sh), BF16),
        pltpu.VMEM((sh, full), BF16),
        pltpu.VMEM(qkv_all.shape[1:], BF16),
        DMA((2,)),
    ]


def closing_kernel(n, width, low, slots, step, io, *refs):
    back, rest, refs = refs[:9], refs[9 : 9 + 25], refs[34:]
    outs, refs = refs[:7], refs[7:]
    back_scratch, triple, part, refs = refs[:10], refs[10], refs[11], refs[12:]

    def between():
        mapped = Mapped(io, {i: i for i in range(9)}, {})
        return attend_back_kernel(
            n, slots, step, 0, False, True, mapped, *back, triple, part, *back_scratch
        )

    numbers = [i for i in range(28) if i not in (0, 6, 8)]
    places = {i: 9 + x for x, i in enumerate(numbers)}
    places[8] = 2
    operands = dict(zip(numbers, rest))
    operands.update({0: part, 6: triple, 8: back[2]})
    finale_kernel(
        n,
        width,
        low,
        between,
        Mapped(io, places, {i: i for i in range(7)}),
        *(operands[i] for i in range(28)),
        *outs,
        *refs,
    )


def closing_call(n, collective_id, width, low, slots, back, args):
    qkv, out_all, qkv_all = back[0], back[7], back[8]
    rows = qkv.shape[0]
    full = out_all.shape[2]
    triple = jax.ShapeDtypeStruct((rows, qkv.shape[1]), BF16)
    part = jax.ShapeDtypeStruct((rows, full), BF16)
    args = [part] + list(args[:5]) + [triple] + list(args[5:6]) + [back[2]] + list(args[6:])
    shapes, scratch = finale_parts(n, *args)
    numbers = [i for i in range(28) if i not in (0, 6, 8)]
    places = {i: 9 + x for x, i in enumerate(numbers)}
    return staged_call(
        functools.partial(closing_kernel, n, width, low, slots, min(rows, 256)),
        "closing",
        collective_id,
        tuple(back) + tuple(args[i] for i in numbers),
        shapes,
        attend_back_scratch(rows, slots * HD, full, qkv_all)
        + [pltpu.VMEM(triple.shape, BF16), pltpu.VMEM(part.shape, BF16)]
        + scratch,
        late=(2, 0, 1, 3) + tuple(places[i] for i in (5, 7, 12, 13, 21, 22, 23)),
        plain=(7, 8) + tuple(places[i] for i in (9, 10, 11, 24, 25, 26, 27)),
        early=(0,),
        raw=(1, 2, 3, 5, 6),
    )


def attend_back_step(n, collective_id, slots, layer, *args, last=()):
    qkv, out_all, qkv_all = args[0], args[7], args[8]
    rows = qkv.shape[0]
    sh = slots * HD
    full = out_all.shape[2]
    step = min(rows, 256)
    shapes = [
        jax.ShapeDtypeStruct((rows, 3 * sh), BF16),
        jax.ShapeDtypeStruct((rows, full), BF16),
    ]
    scratch = attend_back_scratch(rows, sh, full, qkv_all)
    if last:
        shapes.append(jax.ShapeDtypeStruct(last[1].shape, F32))
        scratch += scatter_scratch(n, *last[1].shape)
    return Step(
        functools.partial(attend_back_kernel, n, slots, step, layer, bool(last), False),
        "attend_back",
        collective_id,
        args + tuple(last),
        shapes,
        scratch,
        dict(line=bool(last), sibling=True),
        late=(0, 1, 2, 3),
        plain=(7, 8),
        early=(0, 1),
    )


def windows(width, n):
    share = width // n
    low = [j * share // HD for j in range(n)]
    slots = max(((j + 1) * share - 1) // HD - low[j] + 1 for j in range(n))
    return [min(first, HEADS - slots) for first in low], slots


def on_device(n, tokens, block_order, cotangent, *vectors_and_weights):
    (
        first_gain,
        first_shift,
        qkv_weight,
        input_bias,
        out_weight,
        out_bias,
        second_gain,
        second_shift,
        widen_weight,
        widen_bias,
        narrow_weight,
        narrow_bias,
    ) = (member[0] for member in vectors_and_weights)
    _, rows, width = tokens.shape
    hidden = widen_weight.shape[1]
    share = width // n
    hide = hidden // n
    padded = -(-share // 16) * 16
    full = n * padded
    low, slots = windows(width, n)
    sh = slots * HD
    total_rows = n * rows

    mask = jnp.asarray(np.arange(full)[None] % padded < share, F32)
    (
        x,
        own_cot,
        out_grad,
        out_sums,
        normed,
        qkv,
        qkv_all,
        out_all,
        feats,
        qkv_bias,
        widen_biases,
        att,
        att_low,
        lse,
        other,
        widen_all,
        *middle,
        narrow_all,
        kpos,
        qpos,
    ) = open_call(
        n,
        low,
        slots,
        padded,
        tokens,
        cotangent,
        [
            member[None]
            for member in (
                first_gain,
                first_shift,
                out_bias,
                second_gain,
                second_shift,
                narrow_bias,
                input_bias,
                widen_bias,
            )
        ],
        (qkv_weight, out_weight, widen_weight, narrow_weight),
        mask,
        block_order,
    )
    stored = []
    layer_outs = []
    merge = total_rows * full <= 2**20
    residual, normed_two, hidden_pre, hidden_low, part = middle
    stored.append((x, normed, qkv, other, att, att_low, lse, residual, normed_two))
    stored[-1] += (hidden_pre, hidden_low)
    (x, normed), attended = follow(
        merge,
        forward_step(n, 5, width, part, residual, feats, mask),
        lambda ended: attend_step(
            n, 2, slots, 1, kpos, qpos, own_cot, out_all, ended[1], qkv_all, qkv_bias
        ),
    )
    layer_outs.append(x)
    att, att_low, lse, other, part, out_low_all, qkv = attended
    second_middle = forward_step(
        n,
        4,
        width,
        part,
        x,
        feats,
        mask,
        layer=1,
        feed=(widen_all, narrow_all, widen_biases),
    )

    def back_middle(layer, residual, grad, normed_two, hidden_pre, hidden_low, low_all):
        return resid_step(
            n,
            7 + layer,
            width,
            layer,
            hide,
            residual,
            grad,
            feats,
            mask,
            normed_two,
            hidden_pre,
            hidden_low,
            low_all,
            widen_all,
            narrow_all,
        )

    upper = (qkv, other, att, lse, kpos, qpos, out_all, qkv_all)
    middle, back, (triple, part, last_out) = follow(
        merge,
        second_middle,
        lambda made: back_middle(1, made[0], out_grad, *made[1:4], out_low_all),
        lambda made, back: attend_back_step(
            n, 10, slots, 1, *upper[:2], back[2], *upper[2:], last=(made[4], made[0], feats)
        ),
    )
    upper_part = part
    layer_outs.append(last_out)
    residual, normed_two, hidden_pre, hidden_low, _ = middle
    stored.append((x, normed, qkv, other, att, att_low, lse, residual, normed_two))
    stored[-1] += (hidden_pre, hidden_low)

    found = {}
    for layer in (1, 0):
        x, normed, qkv, other, att, att_low, lse, residual, normed_two = stored[layer][:9]
        hidden_pre, hidden_low = stored[layer][9:]
        resid_grad, sums_two, resid_low_all, wide, wide_came, slim, pre_sums = back
        operands = (qkv, other, resid_low_all, att, lse, kpos, qpos, out_all, qkv_all)
        found[layer] = (wide, wide_came, slim, sums_two, pre_sums)
        if layer:
            upper_step = input_step(
                n,
                11,
                width,
                0,
                low,
                upper_part,
                x,
                resid_grad,
                feats,
                mask,
                normed,
                triple,
                att_low,
                resid_low_all,
                slim,
            )
            below = stored[0]
            ended, back = follow(
                merge,
                upper_step,
                lambda ended: back_middle(0, below[7], ended[0], *below[8:], ended[2]),
            )
            upper_d_in, sums_one, _, qkv_grad, out_rows, slim_came, triple_sums = ended
    lower, upper = found[0], found[1]
    streams = (
        lower[2],
        upper[2],
        slim_came,
        qkv_grad,
        out_rows,
        sums_one,
        lower[3],
        upper[3],
        triple_sums,
        lower[4],
        upper[4],
        out_sums,
        *layer_outs,
        upper_d_in,
        *lower[:2],
        *upper[:2],
    )
    own = (x, resid_grad, feats, mask, normed)
    if merge:
        ended = closing_call(n, 12, width, low, slots, operands, (*own, att_low, *streams))
    else:
        ((triple, part),) = run_steps([attend_back_step(n, 9, slots, 0, *operands)])
        ended = finale_call(
            n, 12, width, low, part, *own, triple, att_low, resid_low_all, *streams
        )
    d_in, narrow_back, qkv_back, out_back, vec, came, widen_back = ended
    settled = settle_call(
        low,
        share,
        hide,
        qkv_back,
        widen_back,
        out_back,
        narrow_back,
        vec,
        came,
        *layer_outs,
        d_in,
        upper_d_in,
    )
    qkv_out, widen_out, out_out, narrow_out, layer_out, d_out = (m[None] for m in settled[:6])
    gain1, shift1, out_b, gain2, shift2, narrow_b, input_b, widen_b = settled[6:]
    return (
        layer_out,
        d_out,
        gain1,
        shift1,
        qkv_out,
        input_b,
        out_out,
        out_b,
        gain2,
        shift2,
        widen_out,
        widen_b,
        narrow_out,
        narrow_b,
    )


def solution(mesh):
    rows = P(None, ("ctx", "shard"), None)
    vector = P("section", "shard")
    matrix = P("section", "shard", None)
    order = (
        vector,
        vector,
        matrix,
        vector,
        matrix,
        vector,
        vector,
        vector,
        matrix,
        vector,
        matrix,
        vector,
    )
    streams = P("section", None, ("ctx", "shard"), None)
    return jax.shard_map(
        functools.partial(on_device, mesh.shape["shard"]),
        mesh=mesh,
        in_specs=(rows, P(), rows) + order,
        out_specs=(streams, streams) + order,
        check_vma=False,
    )
```
